32 devices in a mesh: rep: 4 (over x, core), fsdp: 8 (over z, y).
Axes of the slice: x: 2, y: 2, z: 4, core: 2. Of those that a mesh axis runs over, the one named last changes fastest.
Arguments:
- block_in: bfloat16 [32, 1024, 1152], P(('rep', 'fsdp')), may hold values from -6 to 6
- condition: bfloat16 [32, 8, 1152], P(('rep', 'fsdp')), may hold values from -6 to 6
- item_lengths: int32 [32, 8], P(('rep', 'fsdp')), may hold values from 1 to 256, 1024 in all within a row
- item_widths: int32 [32, 8], P(('rep', 'fsdp')), may hold values from 2 to 32
- ada_weight: bfloat16 [1152, 6912], P('fsdp'), may hold values from -0.1875 to 0.1875
- ada_bias: bfloat16 [6912], P('fsdp'), may hold values from -3 to 3
- qkv_weight: bfloat16 [1152, 3456], P('fsdp'), may hold values from -0.1875 to 0.1875
- query_gain: bfloat16 [72], replicated, may hold values from 0.099609375 to 1.8984375
- key_gain: bfloat16 [72], replicated, may hold values from 0.099609375 to 1.8984375
- proj_weight: bfloat16 [1152, 1152], P('fsdp'), may hold values from -1.5 to 1.5
- gate_up_weight: bfloat16 [1152, 6144], P('fsdp'), may hold values from -0.1875 to 0.1875
- down_weight: bfloat16 [3072, 1152], P('fsdp'), may hold values from -0.109375 to 0.109375
- out_grad: bfloat16 [32, 1024, 1152], P(('rep', 'fsdp')), may hold values from -6 to 6
Outputs:
- block_out: bfloat16 [32, 1024, 1152], P(('rep', 'fsdp'))
- grad_input: float32 [32, 1024, 1152], P(('rep', 'fsdp'))
- grad_condition: float32 [32, 8, 1152], P(('rep', 'fsdp'))
- grad_ada_weight: float32 [1152, 6912], P('fsdp')
- grad_ada_bias: float32 [6912], P('fsdp')
- grad_qkv: float32 [1152, 3456], P('fsdp')
- grad_query_gain: float32 [72], replicated
- grad_key_gain: float32 [72], replicated
- grad_proj: float32 [1152, 1152], P('fsdp')
- grad_gate_up: float32 [1152, 6144], P('fsdp')
- grad_down: float32 [3072, 1152], P('fsdp')
The draws below stay inside these ranges and needn't reach their ends.
Inputs may be any that keep to these rules, and one draw needn't show every extreme that they name: `item_lengths`: each row: the lengths of 7 items and last that of the padding, summing to 1024.
All inputs are finite; a program needn't handle non-finite values.
Results may differ from the reference program's by a relative error of at most 0.019.
Values may be sent and summed in bfloat16 or wider, within the bound.
No kernel may reach another device: no remote copies, remote signals or barrier semaphores. Data moves between devices by JAX's collectives and lax.ppermute only.
A program may use at most 448 MiB of HBM per device.

```python
import math
import jax
import jax.numpy as jnp
import numpy as np
from jax import lax

D = 1152
HEADS = 16
HD = 72
FF = 3072
LEN = 1024
SEGS = 8
SEQS = 32


def set_ends(entries, stream_key, smallest, largest):
    longest = entries.shape.index(max(entries.shape))
    spots = []
    for shift in (0, 1):
        where = [jax.random.randint(jax.random.fold_in(stream_key, axis), (), 0, length) for axis, length in enumerate(entries.shape)]
        where[longest] = (where[longest] + shift) % entries.shape[longest]
        spots.append(tuple(where))
    return entries.at[spots[0]].set(smallest).at[spots[1]].set(largest)


def steps_of(stream_key, shape, pieces, low, largest):
    gain = 1.0
    for dim, shards_of in pieces:
        steps = jax.random.uniform(jax.random.fold_in(jax.random.fold_in(stream_key, 6), dim), (shards_of,), jnp.float32, low / len(pieces), largest / len(pieces))
        gain = gain * jnp.repeat(jnp.exp(steps), shape[dim] // shards_of).reshape((-1,) + (1,) * (len(shape) - 1 - dim))
    return gain


def profile(count, total, limit, lean):
    weights = [(1 << 20) // math.isqrt(rank ** lean) + 1 for rank in range(2, count + 1)]
    spare, counts = total - limit - (count - 1), [1] * (count - 1)
    while spare > 0:
        free = [i for i in range(count - 1) if counts[i] < limit]
        pool, left = sum([weights[i] for i in free]), spare
        for i in free:
            addition = min(limit - counts[i], max(1, left * weights[i] // pool), spare)
            counts[i] = counts[i] + addition
            spare = spare - addition
    return np.array([limit] + counts)


def uneven(rng, count, total, bound, skew):
    if count == 2:
        one = jax.random.randint(rng, (), max(1, total - bound), min(bound, total - 1) + 1)
        return jnp.stack([one, total - one])
    tallies = jnp.asarray(profile(count, total, bound, skew), jnp.int32)
    couples = (count - 1) // 2
    donor, receiver = tallies[1:1 + 2 * couples:2], tallies[2:2 + 2 * couples:2]
    room = jnp.minimum(donor - 1, bound - receiver)
    passed = jax.random.randint(jax.random.fold_in(rng, 1), (couples,), 0, 1 << 20) % (room + 1)
    tallies = tallies.at[1:1 + 2 * couples:2].set(donor - passed).at[2:2 + 2 * couples:2].set(receiver + passed)
    return tallies[jax.random.permutation(jax.random.fold_in(rng, 2), count)]


def normal_values(key, shape, spread, most, pieces=(), kind=jnp.bfloat16):
    array = jax.random.normal(key, shape, jnp.float32) * spread
    if len(pieces) > 0:
        array = steps_of(key, shape, pieces, -0.22, 0.18) * array
    return jnp.clip(array, min=-most, max=most).astype(kind)


def setup_inputs(seed: int = 0) -> dict:
    key_list = jax.random.split(jax.random.key(seed), 14)
    return {
        "block_in": normal_values(key_list[0], (SEQS, LEN, D), 1.0, 6.0, ((0, 32),)),
        "condition": normal_values(key_list[1], (SEQS, SEGS, D), 1.0, 6.0, ((0, 32),)),
        "item_lengths": jax.vmap(lambda own: uneven(own, SEGS, LEN, LEN // 4, 2))(jax.random.split(key_list[2], SEQS)).reshape((SEQS, SEGS)).astype(jnp.int32),
        "item_widths": set_ends(jax.random.randint(key_list[3], (SEQS, SEGS), 2, 33), jax.random.fold_in(key_list[3], 1), 2, 32).astype(jnp.int32),
        "ada_weight": normal_values(key_list[4], (D, 6 * D), D ** -0.5, 0.1875, ((0, 8),)),
        "ada_bias": normal_values(key_list[5], (6 * D,), 0.5, 3.0, ((0, 8),)),
        "qkv_weight": normal_values(key_list[6], (D, 3 * D), D ** -0.5, 0.1875, ((0, 8),)),
        "query_gain": jnp.clip(1.0 + 0.18 * jax.random.normal(key_list[7], (HD,), jnp.float32), 0.099609375, 1.8984375).astype(jnp.bfloat16),
        "key_gain": jnp.clip(1.0 + 0.18 * jax.random.normal(key_list[8], (HD,), jnp.float32), 0.099609375, 1.8984375).astype(jnp.bfloat16),
        "proj_weight": normal_values(key_list[9], (D, D), (D * 16 // LEN) ** -0.5, 1.5, ((0, 8),)),
        "gate_up_weight": normal_values(key_list[10], (D, 2 * FF), D ** -0.5, 0.1875, ((0, 8),)),
        "down_weight": normal_values(key_list[11], (FF, D), FF ** -0.5, 0.109375, ((0, 8),)),
        "out_grad": normal_values(key_list[12], (SEQS, LEN, D), 1.0, 6.0, ((0, 32),)),
    }


@jax.custom_vjp
def low(v):
    return lax.optimization_barrier(v.astype(jnp.bfloat16)).astype(jnp.float32)

@jax.custom_vjp
def low_back(v):
    return v

def low_keep(v):
    return (low(v), None)

def low_pass(kept, grad):
    return (grad,)

def back_keep(v):
    return (v, None)

def back_low(kept, grad):
    return (low(grad),)
low.defvjp(low_keep, low_pass)
low_back.defvjp(back_keep, back_low)
HIGHEST_PRECISION = lax.Precision.HIGHEST
EPSILON = 1e-06

def matmul(left, right):
    return jnp.dot(left, right, precision=HIGHEST_PRECISION, preferred_element_type=jnp.float32)

def layer_norm(values):
    centred = values - lax.optimization_barrier(jnp.mean(values, axis=-1, keepdims=True))
    return centred * lax.rsqrt(lax.optimization_barrier(jnp.mean(centred * centred, axis=-1, keepdims=True)) + EPSILON)

def rms_norm(values, gain_part):
    return values * lax.rsqrt(lax.optimization_barrier(jnp.mean(values * values, axis=-1, keepdims=True)) + EPSILON) * gain_part

def turn_pairs(values, angle_part):
    quarter = values.shape[-1] // 2
    leading = values[..., :quarter]
    trailing = values[..., quarter:]
    cosine = jnp.cos(angle_part)[:, None, :]
    sine_part = jnp.sin(angle_part)[:, None, :]
    return jnp.concatenate([leading * cosine - trailing * sine_part, leading * sine_part + trailing * cosine], axis=-1)

def rotate(values, row_angle, column_angle):
    half_dim = values.shape[-1] // 2
    return jnp.concatenate([turn_pairs(values[..., :half_dim], row_angle), turn_pairs(values[..., half_dim:], column_angle)], axis=-1)

def angles(row_place, column_place):
    quarter = HD // 4
    inverse = 10000.0 ** (-jnp.arange(quarter, dtype=jnp.float32) / quarter)
    return (row_place.astype(jnp.float32)[:, None] * inverse[None, :], column_place.astype(jnp.float32)[:, None] * inverse[None, :])

def layout(lengths_row, widths_row):
    item_ends = jnp.cumsum(lengths_row).astype(jnp.int32)
    item_starts = (item_ends - lengths_row).astype(jnp.int32)
    token_place = jnp.arange(LEN, dtype=jnp.int32)[:, None]
    member = ((token_place >= item_starts[None, :]) & (token_place < item_ends[None, :])).astype(jnp.int32)
    segment = lax.optimization_barrier(jnp.sum(member * jnp.arange(SEGS, dtype=jnp.int32)[None, :], axis=1)).astype(jnp.int32)
    offset = (token_place[:, 0] - lax.optimization_barrier(jnp.sum(member * item_starts[None, :], axis=1))).astype(jnp.int32)
    across = lax.optimization_barrier(jnp.sum(member * widths_row[None, :], axis=1)).astype(jnp.int32)
    return (segment, offset // across, offset % across)

def block_forward(tokens_in, cond_in, weights, segment, row_place, column_place, keep):
    ada_weight, ada_bias, qkv_weight, query_gain, key_gain, proj_weight, gate_up_weight, down_weight = weights
    cond_act = low(jax.nn.silu(cond_in))
    modulation = low_back(matmul(cond_act, ada_weight)) + ada_bias
    token_mod = jnp.take(modulation, segment, axis=0)
    shift_a, scale_a, gate_a, shift_b, scale_b, gate_b = jnp.split(token_mod, 6, axis=1)
    normed_a = low(layer_norm(tokens_in) * (1.0 + scale_a) + shift_a)
    joint = low_back(matmul(normed_a, qkv_weight))
    query_raw, key_raw, value_raw = jnp.split(joint, 3, axis=1)
    row_angle, column_angle = angles(row_place, column_place)
    query = low(rotate(rms_norm(query_raw.reshape(LEN, HEADS, HD), query_gain), row_angle, column_angle))
    key_rot = low(rotate(rms_norm(key_raw.reshape(LEN, HEADS, HD), key_gain), row_angle, column_angle))
    value = low(value_raw.reshape(LEN, HEADS, HD))
    scores = low_back(jnp.einsum('qhd,khd->hqk', query, key_rot, precision=HIGHEST_PRECISION) * HD ** (-0.5))
    same_item = segment[:, None] == segment[None, :]
    probs = low(jax.nn.softmax(jnp.where(same_item[None], scores, -1e+30), axis=-1))
    mixed = low(low_back(jnp.einsum('hqk,khd->qhd', probs, value, precision=HIGHEST_PRECISION))).reshape(LEN, D)
    attended = low_back(matmul(mixed, proj_weight))
    middle = tokens_in + keep * gate_a * attended
    normed_b = low(layer_norm(middle) * (1.0 + scale_b) + shift_b)
    hidden = low_back(matmul(normed_b, gate_up_weight))
    gate_part, up_part = jnp.split(hidden, 2, axis=1)
    inner = low(jax.nn.silu(gate_part) * up_part)
    returned = low_back(matmul(inner, down_weight))
    return middle + keep * gate_b * returned

def reference(block_in, condition, item_lengths, item_widths, ada_weight, ada_bias, qkv_weight, query_gain, key_gain, proj_weight, gate_up_weight, down_weight, out_grad):
    weights = tuple((matrix.astype(jnp.float32) for matrix in (ada_weight, ada_bias, qkv_weight, query_gain, key_gain, proj_weight, gate_up_weight, down_weight)))

    def per_sequence(totals, sequence_data):
        tokens_in, cond_in, lengths_row, widths_row, cotangent = sequence_data
        segment, row_place, column_place = layout(lengths_row, widths_row)
        keep = (segment < SEGS - 1).astype(jnp.float32)[:, None]

        def forward(tokens_arg, cond_arg, *weight_args):
            return block_forward(tokens_arg, cond_arg, weight_args, segment, row_place, column_place, keep)
        output, pullback = jax.vjp(forward, tokens_in.astype(jnp.float32), cond_in.astype(jnp.float32), *weights)
        grads = pullback(cotangent.astype(jnp.float32))
        new_totals = tuple((running + piece for running, piece in zip(totals, grads[2:])))
        return (new_totals, (output.astype(jnp.bfloat16), grads[0], grads[1]))
    zeros = tuple((jnp.zeros(matrix.shape, jnp.float32) for matrix in weights))
    sums, stacked = lax.scan(per_sequence, zeros, (block_in, condition, item_lengths, item_widths, out_grad))
    return (stacked[0], stacked[1], stacked[2], sums[0], sums[1], sums[2], sums[3], sums[4], sums[5], sums[6], sums[7])
```

```python
from functools import partial

import jax
import jax.numpy as jnp
from jax import lax
from jax.experimental import pallas as pl
from jax.experimental.pallas import tpu as pltpu
from jax.sharding import PartitionSpec as P

HIGHEST_PRECISION = lax.Precision.HIGHEST
EPSILON = 1e-06


def matmul(left, right):
    return jnp.dot(left, right, preferred_element_type=jnp.float32)


def matmul_left(left, right):
    return lax.dot_general(
        left, right, (((0,), (0,)), ((), ())), preferred_element_type=jnp.float32
    )


def matmul_right(left, right):
    return lax.dot_general(
        left, right, (((1,), (1,)), ((), ())), preferred_element_type=jnp.float32
    )


def layer_norm(values):
    centred = values - jnp.mean(values, axis=-1, keepdims=True)
    return centred * lax.rsqrt(jnp.mean(centred * centred, axis=-1, keepdims=True) + EPSILON)


def modulated(values, shift_part, scale_part):
    return layer_norm(values) * (1.0 + scale_part) + shift_part


def rms_norm(values, gain_part):
    return (
        values * lax.rsqrt(jnp.mean(values * values, axis=-1, keepdims=True) + EPSILON) * gain_part
    )


def turn_pairs(values, angle_part):
    quarter = values.shape[-1] // 2
    leading = values[..., :quarter]
    trailing = values[..., quarter:]
    cosine = jnp.cos(angle_part)[:, None, :]
    sine_part = jnp.sin(angle_part)[:, None, :]
    return jnp.concatenate(
        [leading * cosine - trailing * sine_part, leading * sine_part + trailing * cosine], axis=-1
    )


def rotate(values, row_angle, column_angle):
    half_dim = values.shape[-1] // 2
    return jnp.concatenate(
        [
            turn_pairs(values[..., :half_dim], row_angle),
            turn_pairs(values[..., half_dim:], column_angle),
        ],
        axis=-1,
    )


def prepared(raw_part, gain_part, row_angle, column_angle, head_count):
    shaped = raw_part.reshape(raw_part.shape[0], head_count, -1)
    return rotate(rms_norm(shaped, gain_part), row_angle, column_angle)


def swiglu(paired):
    gate_part, up_part = jnp.split(paired, 2, axis=1)
    return jax.nn.silu(gate_part) * up_part


def angles(row_place, column_place, head_dim):
    quarter = head_dim // 4
    inverse = 10000.0 ** (-jnp.arange(quarter, dtype=jnp.float32) / quarter)
    return (
        row_place.astype(jnp.float32)[:, None] * inverse[None, :],
        column_place.astype(jnp.float32)[:, None] * inverse[None, :],
    )


def layout(lengths_row, widths_row, length):
    seg_count = lengths_row.shape[0]
    item_ends = jnp.cumsum(lengths_row)
    item_starts = item_ends - lengths_row
    token_place = jnp.arange(length, dtype=jnp.int32)[:, None]
    member = ((token_place >= item_starts[None, :]) & (token_place < item_ends[None, :])).astype(
        jnp.int32
    )
    segment = jnp.sum(member * jnp.arange(seg_count, dtype=jnp.int32)[None, :], axis=1)
    offset = token_place[:, 0] - jnp.sum(member * item_starts[None, :], axis=1)
    across = jnp.sum(member * widths_row[None, :], axis=1)
    return (member, segment, offset // across, offset % across)


AXES = ("rep", "fsdp")
HIGH_Z = 4
PARTS = 3


def device_index(x, core, z, y):
    return (x * 2 + core) * 8 + z * 2 + y


PLACES = [(x, c, z, y) for x in range(2) for c in range(2) for z in range(4) for y in range(2)]
TO_CORE = [(device_index(x, c, z, y), device_index(x, 1 - c, z, y)) for x, c, z, y in PLACES]
TO_X = [(device_index(x, c, z, y), device_index(1 - x, c, z, y)) for x, c, z, y in PLACES]
TO_Y = [(device_index(x, c, z, y), device_index(x, c, z, 1 - y)) for x, c, z, y in PLACES]
Z_GROUPS = [[0, 2, 4, 6], [1, 3, 5, 7]]


def coordinates():
    replica = lax.axis_index("rep")
    shard = lax.axis_index("fsdp")
    return replica // 2, replica % 2, shard // 2, shard % 2


def pick(operand, index, axis):
    return lax.dynamic_index_in_dim(operand, index, axis, keepdims=False)


def place_kernel(where, a0, a1, ax, b0, b1, bx, out, sems):
    x, core, y = where[0], where[1], where[2]
    copies = []
    for p0, p1, px, c in ((a0, a1, ax, core), (b0, b1, bx, 1 - core)):
        for q in range(HIGH_Z):
            for source, target in (
                (p0.at[q, 0], out.at[q, y, c, x]),
                (p0.at[q, 1], out.at[q, y, c, 2]),
                (p1.at[q, 0], out.at[q, 1 - y, c, x]),
                (p1.at[q, 1], out.at[q, 1 - y, c, 2]),
                (px.at[q, 0], out.at[q, y, c, 1 - x]),
                (px.at[q, 1], out.at[q, 1 - y, c, 1 - x]),
            ):
                copy = pltpu.make_async_copy(source, target, sems.at[len(copies)])
                copy.start()
                copies.append(copy)
    for copy in copies:
        copy.wait()


def gather_fast(weight):
    x, core, z, y = coordinates()
    rows, width = weight.shape
    h = rows // 6
    mine = pick(weight.reshape(2, PARTS, h, width), core, 0)
    base = jnp.stack([pick(mine, x, 0), mine[2]], 0)
    own = lax.all_to_all(
        jnp.broadcast_to(base, (HIGH_Z, 2, h, width)), "fsdp", 0, 0, axis_index_groups=Z_GROUPS
    )
    over_y = lax.ppermute(own, AXES, TO_Y)
    over_x = lax.ppermute(jnp.stack([own[:, 0], over_y[:, 0]], 1), AXES, TO_X)
    pieces = (own, over_y, over_x)
    others = tuple(lax.ppermute(piece, AXES, TO_CORE) for piece in pieces)
    where = jnp.stack([x, core, y]).astype(jnp.int32)
    full = pl.pallas_call(
        place_kernel,
        out_shape=jax.ShapeDtypeStruct((HIGH_Z, 2, 2, PARTS, h, width), weight.dtype),
        in_specs=[pl.BlockSpec(memory_space=pltpu.SMEM)] + [pl.BlockSpec(memory_space=pl.ANY)] * 6,
        out_specs=pl.BlockSpec(memory_space=pltpu.VMEM),
        scratch_shapes=[pltpu.SemaphoreType.DMA((48,))],
        compiler_params=pltpu.CompilerParams(vmem_limit_bytes=40 * 2**20),
        cost_estimate=pl.CostEstimate(
            flops=0, bytes_accessed=2 * 48 * h * width * 2, transcendentals=0
        ),
        name="place",
    )(where, *pieces, *others)
    return full.reshape(8 * rows, width)


def scatter_fast(grad):
    x, core, z, y = coordinates()
    total, width = grad.shape
    h = total // 48
    low = jnp.bfloat16
    wide = jnp.float32
    views = grad.reshape(HIGH_Z, 2, 2, PARTS, h, width)
    kept = pick(views, core, 2)
    got = lax.ppermute(pick(views, 1 - core, 2), AXES, TO_CORE)

    def pair(t):
        first = pick(kept, t, 2) if not isinstance(t, int) else kept[:, :, t]
        second = pick(got, t, 2) if not isinstance(t, int) else got[:, :, t]
        return first.astype(wide) + second.astype(wide)

    from_x = lax.ppermute(pair(1 - x).astype(low), AXES, TO_X)
    own = (pair(x) + from_x.astype(wide)).astype(low)
    both = pair(2).astype(low)
    halves = jnp.stack([own, both], 2)
    from_y = lax.ppermute(pick(halves, 1 - y, 1), AXES, TO_Y)
    line = (pick(halves, y, 1).astype(wide) + from_y.astype(wide)).astype(low)
    spread = lax.all_to_all(line, "fsdp", 0, 0, axis_index_groups=Z_GROUPS)
    part = jnp.sum(spread.astype(wide), axis=0).astype(low)
    other = lax.ppermute(part, AXES, TO_X)
    shared = (part[1].astype(wide) + other[1].astype(wide)).astype(low)
    first = jnp.where(x == 0, part[0], other[0])
    second = jnp.where(x == 0, other[0], part[0])
    done = jnp.stack([first, second, shared], 0)
    twin = lax.ppermute(done, AXES, TO_CORE)
    whole = jnp.stack([jnp.where(core == 0, done, twin), jnp.where(core == 0, twin, done)], 0)
    return whole.reshape(total // 8, width).astype(wide)


def is_fast():
    return lax.axis_size("rep") == 4 and lax.axis_size("fsdp") == 8


def gather_weight(weight):
    if is_fast() and weight.shape[0] % 48 == 0:
        return gather_fast(weight)
    return lax.all_gather(weight, "fsdp", axis=0, tiled=True)


def scatter_grad(grad):
    shards = lax.axis_size("fsdp")
    replicas = lax.axis_size("rep")
    if is_fast() and grad.shape[0] % 384 == 0:
        return scatter_fast(grad)
    part = lax.psum_scatter(grad, "fsdp", scatter_dimension=0, tiled=True)
    return lax.psum(part, "rep").astype(jnp.float32)


def gather_rows(rows):
    shards = lax.axis_size("fsdp")
    count, width = rows.shape
    group = lax.all_to_all(jnp.broadcast_to(rows, (shards, count, width)), "fsdp", 0, 0)
    group = group.reshape(shards * count, width)
    if not is_fast():
        return group, lax.all_gather(group, "rep", axis=0, tiled=True)
    x, core, z, y = coordinates()
    twin = lax.ppermute(group, AXES, TO_CORE)
    chip = jnp.stack([jnp.where(core == 0, group, twin), jnp.where(core == 0, twin, group)], 0)
    far = lax.ppermute(chip, AXES, TO_X)
    every = jnp.stack([jnp.where(x == 0, chip, far), jnp.where(x == 0, far, chip)], 0)
    return group, every.reshape(4 * shards * count, width)


def exchange(rows):
    shards = lax.axis_size("fsdp")
    count, width = rows.shape
    shaped = rows.reshape(count, shards, width // shards).swapaxes(0, 1)
    return lax.all_to_all(shaped, "fsdp", 0, 0).reshape(shards * count, width // shards)


def sum_back(partial_rows, count):
    shards = lax.axis_size("fsdp")
    shaped = partial_rows.astype(jnp.bfloat16).reshape(shards, count, -1)
    got = lax.all_to_all(shaped, "fsdp", 0, 0)
    return jnp.sum(got.astype(jnp.float32), axis=0)


def local(
    block_in,
    condition,
    item_lengths,
    item_widths,
    ada_weight,
    ada_bias,
    qkv_weight,
    query_gain,
    key_gain,
    proj_weight,
    gate_up_weight,
    down_weight,
    out_grad,
):
    seq_count, seq_len, model_width = block_in.shape
    seg_count = item_lengths.shape[1]
    head_dim = query_gain.shape[0]
    head_count = model_width // head_dim
    row_count = seq_count * seq_len
    query_block = min(512, seq_len)
    score_scale = float(head_dim) ** (-0.5)
    shards = lax.axis_size("fsdp")
    member, segment, row_place, column_place = jax.vmap(partial(layout, length=seq_len))(
        item_lengths, item_widths
    )
    keep_mask = (segment < seg_count - 1).astype(jnp.float32).reshape(row_count, 1)
    row_angle, column_angle = angles(row_place.reshape(-1), column_place.reshape(-1), head_dim)
    qkv_full = gather_weight(qkv_weight)
    proj_full = gather_weight(proj_weight)
    gate_up_full = gather_weight(gate_up_weight)
    down_full = gather_weight(down_weight)
    cond_float = condition.astype(jnp.float32).reshape(seq_count * seg_count, model_width)
    cond_silu, silu_pull = jax.vjp(jax.nn.silu, cond_float)
    cond_act = cond_silu.astype(jnp.bfloat16)
    mod_width = ada_weight.shape[1]
    item_count = seq_count * seg_count
    fsdp_place = lax.axis_index("fsdp")
    group_act = exchange(cond_act)
    bias_row = lax.dynamic_update_slice(
        jnp.zeros((mod_width,), jnp.float32),
        ada_bias.astype(jnp.float32),
        (fsdp_place * ada_bias.shape[0],),
    )
    mod_part = matmul(group_act, ada_weight) + bias_row[None, :]
    early = 2 * model_width
    modulation = jnp.concatenate(
        [
            sum_back(mod_part[:, :early], item_count),
            sum_back(mod_part[:, early:], item_count),
        ],
        axis=1,
    )
    mod_high = modulation.astype(jnp.bfloat16)
    mod_rest = (modulation - mod_high.astype(jnp.float32)).astype(jnp.bfloat16)
    member_low = member.astype(jnp.bfloat16).reshape(row_count, seg_count)
    token_mod = matmul(
        jnp.concatenate([member_low, member_low], axis=1),
        jnp.concatenate([mod_high, mod_rest], axis=0),
    )
    shift_a, scale_a, gate_a, shift_b, scale_b, gate_b = jnp.split(token_mod, 6, axis=1)
    inputs = block_in.astype(jnp.float32).reshape(row_count, model_width)
    normed_float, norm_pull_a = jax.vjp(modulated, inputs, shift_a, scale_a)
    normed_a = normed_float.astype(jnp.bfloat16)
    joint = matmul(normed_a, qkv_full)
    query_raw, key_raw, value_raw = jnp.split(joint, 3, axis=1)
    head_prep = partial(
        prepared, row_angle=row_angle, column_angle=column_angle, head_count=head_count
    )
    query_float, query_pull = jax.vjp(head_prep, query_raw, query_gain.astype(jnp.float32))
    key_float, key_pull = jax.vjp(head_prep, key_raw, key_gain.astype(jnp.float32))
    queries = query_float.astype(jnp.bfloat16)
    keys_low = key_float.astype(jnp.bfloat16)
    values_low = value_raw.reshape(row_count, head_count, head_dim).astype(jnp.bfloat16)
    mixed_parts = []
    log_totals = []
    sequence = 0
    first_row = sequence * seq_len
    segment_seq = segment[sequence]
    for offset_row in range(0, seq_len, query_block):
        query_part = queries[first_row + offset_row : first_row + offset_row + query_block]
        allowed = (
            segment_seq[offset_row : offset_row + query_block][:, None] == segment_seq[None, :]
        )
        scores = (
            jnp.einsum("qhd,khd->hqk", query_part, keys_low, preferred_element_type=jnp.float32)
            * score_scale
        )
        scores = jnp.where(allowed[None], scores, -1e30)
        row_peak = jnp.max(scores, axis=-1, keepdims=True)
        exponent = jnp.exp(scores - row_peak)
        totals = jnp.sum(exponent, axis=-1, keepdims=True)
        probs_low = (exponent / totals).astype(jnp.bfloat16)
        mixed_parts.append(
            jnp.einsum("hqk,khd->qhd", probs_low, values_low, preferred_element_type=jnp.float32)
        )
        log_totals.append(row_peak + jnp.log(totals))
    mixed = (
        jnp.concatenate(mixed_parts, axis=0).astype(jnp.bfloat16).reshape(row_count, model_width)
    )
    attended = matmul(mixed, proj_full)
    middle = inputs + keep_mask * gate_a * attended
    normed_b_float, norm_pull_b = jax.vjp(modulated, middle, shift_b, scale_b)
    normed_b = normed_b_float.astype(jnp.bfloat16)
    hidden = matmul(normed_b, gate_up_full)
    inner_float, swiglu_pull = jax.vjp(swiglu, hidden)
    inner = inner_float.astype(jnp.bfloat16)
    returned = matmul(inner, down_full)
    block_out = (
        (middle + keep_mask * gate_b * returned)
        .astype(jnp.bfloat16)
        .reshape(seq_count, seq_len, model_width)
    )
    upstream = out_grad.astype(jnp.float32).reshape(row_count, model_width)
    grad_gate_b = upstream * keep_mask * returned
    grad_returned = (upstream * keep_mask * gate_b).astype(jnp.bfloat16)
    grad_down = matmul_left(inner, grad_returned)
    grad_inner = matmul_right(grad_returned, down_full)
    grad_hidden = swiglu_pull(grad_inner)[0].astype(jnp.bfloat16)
    grad_gate_up = matmul_left(normed_b, grad_hidden)
    grad_normed_b = matmul_right(grad_hidden, gate_up_full)
    grad_middle_part, grad_shift_b, grad_scale_b = norm_pull_b(grad_normed_b)
    grad_middle = upstream + grad_middle_part
    grad_gate_a = grad_middle * keep_mask * attended
    grad_attended = (grad_middle * keep_mask * gate_a).astype(jnp.bfloat16)
    grad_proj = matmul_left(mixed, grad_attended)
    grad_mixed = (
        matmul_right(grad_attended, proj_full)
        .astype(jnp.bfloat16)
        .reshape(row_count, head_count, head_dim)
    )
    grad_query_parts = []
    block_number = 0
    sequence = 0
    first_row = sequence * seq_len
    segment_seq = segment[sequence]
    grad_key_seq = jnp.zeros((seq_len, head_count, head_dim), jnp.float32)
    grad_value_seq = jnp.zeros((seq_len, head_count, head_dim), jnp.float32)
    for offset_row in range(0, seq_len, query_block):
        query_part = queries[first_row + offset_row : first_row + offset_row + query_block]
        grad_out_part = grad_mixed[first_row + offset_row : first_row + offset_row + query_block]
        allowed = (
            segment_seq[offset_row : offset_row + query_block][:, None] == segment_seq[None, :]
        )
        scores = (
            jnp.einsum("qhd,khd->hqk", query_part, keys_low, preferred_element_type=jnp.float32)
            * score_scale
        )
        scores = jnp.where(allowed[None], scores, -1e30)
        probs_float = jnp.exp(scores - log_totals[block_number])
        block_number = block_number + 1
        probs_low = probs_float.astype(jnp.bfloat16)
        grad_value_seq = grad_value_seq + jnp.einsum(
            "hqk,qhd->khd", probs_low, grad_out_part, preferred_element_type=jnp.float32
        )
        grad_probs = jnp.einsum(
            "qhd,khd->hqk", grad_out_part, values_low, preferred_element_type=jnp.float32
        )
        row_delta = jnp.sum(grad_probs * probs_float, axis=-1, keepdims=True)
        grad_scores = (probs_float * (grad_probs - row_delta)).astype(jnp.bfloat16)
        grad_query_parts.append(
            jnp.einsum("hqk,khd->qhd", grad_scores, keys_low, preferred_element_type=jnp.float32)
            * score_scale
        )
        grad_key_seq = (
            grad_key_seq
            + jnp.einsum(
                "hqk,qhd->khd", grad_scores, query_part, preferred_element_type=jnp.float32
            )
            * score_scale
        )
    grad_query_raw, grad_query_gain = query_pull(jnp.concatenate(grad_query_parts, axis=0))
    grad_key_raw, grad_key_gain = key_pull(grad_key_seq)
    grad_value = grad_value_seq.reshape(row_count, model_width)
    grad_joint = jnp.concatenate([grad_query_raw, grad_key_raw, grad_value], axis=1).astype(
        jnp.bfloat16
    )
    grad_qkv = matmul_left(normed_a, grad_joint)
    grad_normed_a = matmul_right(grad_joint, qkv_full)
    grad_input_part, grad_shift_a, grad_scale_a = norm_pull_a(grad_normed_a)
    grad_input = (grad_middle + grad_input_part).reshape(seq_count, seq_len, model_width)
    def segment_sums(parts):
        stacked = jnp.concatenate([part.astype(jnp.bfloat16) for part in parts], axis=1)
        return matmul_left(member_low, stacked)

    late_sums = segment_sums([grad_gate_a, grad_shift_b, grad_scale_b, grad_gate_b])
    early_sums = segment_sums([grad_shift_a, grad_scale_a])
    gain_row = jnp.concatenate([grad_query_gain, grad_key_gain], axis=0)
    gain_high = gain_row.astype(jnp.bfloat16).astype(jnp.float32)
    gain_block = jnp.zeros((item_count, 256), jnp.float32)
    gain_block = gain_block.at[0, : 2 * head_dim].set(gain_high)
    gain_block = gain_block.at[1, : 2 * head_dim].set(gain_row - gain_high)
    ada_group = []
    ada_every = []
    for block in (late_sums, jnp.concatenate([early_sums, gain_block], axis=1)):
        group_rows, every_rows = gather_rows(block.astype(jnp.bfloat16))
        ada_group.append(group_rows)
        ada_every.append(every_rows)
    if is_fast():
        x, core, _, _ = coordinates()
        twin = lax.ppermute(group_act, AXES, TO_CORE)
        chip = jnp.stack(
            [jnp.where(core == 0, group_act, twin), jnp.where(core == 0, twin, group_act)], 0
        )
        far = lax.ppermute(chip, AXES, TO_X)
        every_act = jnp.stack([jnp.where(x == 0, chip, far), jnp.where(x == 0, far, chip)], 0)
        every_act = every_act.reshape(-1, group_act.shape[1])
    else:
        every_act = lax.all_gather(group_act, "rep", axis=0, tiled=True)
    early_every = ada_every[1][:, :early]
    early_group = ada_group[1][:, :early]
    shard_ada = jnp.concatenate(
        [matmul_left(every_act, early_every), matmul_left(every_act, ada_every[0])], axis=1
    )
    bias_sums = jnp.concatenate(
        [
            jnp.sum(early_every.astype(jnp.float32), axis=0),
            jnp.sum(ada_every[0].astype(jnp.float32), axis=0),
        ],
        axis=0,
    )
    shard_bias = lax.dynamic_slice(
        bias_sums, (fsdp_place * ada_bias.shape[0],), (ada_bias.shape[0],)
    )
    gain_sums = jnp.sum(ada_every[1][:, early:].astype(jnp.float32), axis=0)[: 2 * head_dim]
    cond_part = matmul_right(early_group, ada_weight[:, :early]) + matmul_right(
        ada_group[0], ada_weight[:, early:]
    )
    cond_back = lax.all_to_all(
        cond_part.astype(jnp.bfloat16).reshape(shards, item_count, -1), "fsdp", 0, 0
    )
    grad_cond_act = (
        cond_back.swapaxes(0, 1).reshape(item_count, model_width).astype(jnp.float32)
    )
    grad_condition = silu_pull(grad_cond_act)[0].reshape(seq_count, seg_count, model_width)
    shard_qkv = scatter_grad(grad_qkv.astype(jnp.bfloat16))
    shard_proj = scatter_grad(grad_proj.astype(jnp.bfloat16))
    shard_gate_up = scatter_grad(grad_gate_up.astype(jnp.bfloat16))
    shard_down = scatter_grad(grad_down.astype(jnp.bfloat16))
    return (
        block_out,
        grad_input,
        grad_condition,
        shard_ada,
        shard_bias,
        shard_qkv,
        gain_sums[:head_dim],
        gain_sums[head_dim:],
        shard_proj,
        shard_gate_up,
        shard_down,
    )


def solution(mesh):
    return jax.shard_map(
        local,
        mesh=mesh,
        in_specs=(
            P(("rep", "fsdp"), None, None),
            P(("rep", "fsdp"), None, None),
            P(("rep", "fsdp"), None),
            P(("rep", "fsdp"), None),
            P("fsdp", None),
            P("fsdp"),
            P("fsdp", None),
            P(),
            P(),
            P("fsdp", None),
            P("fsdp", None),
            P("fsdp", None),
            P(("rep", "fsdp"), None, None),
        ),
        out_specs=(
            P(("rep", "fsdp"), None, None),
            P(("rep", "fsdp"), None, None),
            P(("rep", "fsdp"), None, None),
            P("fsdp", None),
            P("fsdp"),
            P("fsdp", None),
            P(),
            P(),
            P("fsdp", None),
            P("fsdp", None),
            P("fsdp", None),
        ),
        check_vma=False,
    )
```

```python
import functools
from functools import partial

import jax
import jax.numpy as jnp
from jax import lax
from jax.experimental import pallas as pl
from jax.experimental.pallas import tpu as pltpu
from jax.sharding import PartitionSpec as P

EPSILON = 1e-06
WIDE = jnp.float32
LOW = jnp.bfloat16
AXES = ("rep", "fsdp")
HIGH_Z = 4
PARTS = 3
BLOCK = 256
LANES = 128
GROUP = 4
MASK = 4096.0
MIB = 2**20


def dot(left, right):
    return jnp.dot(left, right, preferred_element_type=WIDE)


def dot_left(left, right):
    return lax.dot_general(left, right, (((0,), (0,)), ((), ())), preferred_element_type=WIDE)


def dot_right(left, right):
    return lax.dot_general(left, right, (((1,), (1,)), ((), ())), preferred_element_type=WIDE)


def layer_norm(values):
    centred = values - jnp.mean(values, axis=-1, keepdims=True)
    return centred * lax.rsqrt(jnp.mean(centred * centred, axis=-1, keepdims=True) + EPSILON)


def modulated(values, shift_part, scale_part):
    return layer_norm(values) * (1.0 + scale_part) + shift_part


def layout(lengths_row, widths_row, length):
    seg_count = lengths_row.shape[0]
    item_ends = jnp.cumsum(lengths_row)
    item_starts = item_ends - lengths_row
    token_place = jnp.arange(length, dtype=jnp.int32)[:, None]
    member = ((token_place >= item_starts[None, :]) & (token_place < item_ends[None, :])).astype(
        jnp.int32
    )
    segment = jnp.sum(member * jnp.arange(seg_count, dtype=jnp.int32)[None, :], axis=1)
    offset = token_place[:, 0] - jnp.sum(member * item_starts[None, :], axis=1)
    across = jnp.sum(member * widths_row[None, :], axis=1)
    return (member, segment, offset // across, offset % across)


def device_index(x, core, z, y):
    return (x * 2 + core) * 8 + z * 2 + y


PLACES = [(x, c, z, y) for x in range(2) for c in range(2) for z in range(4) for y in range(2)]
TO_CORE = [(device_index(x, c, z, y), device_index(x, 1 - c, z, y)) for x, c, z, y in PLACES]
TO_X = [(device_index(x, c, z, y), device_index(1 - x, c, z, y)) for x, c, z, y in PLACES]
TO_Y = [(device_index(x, c, z, y), device_index(x, c, z, 1 - y)) for x, c, z, y in PLACES]
Z_GROUPS = [[0, 2, 4, 6], [1, 3, 5, 7]]


def coordinates():
    replica = lax.axis_index("rep")
    shard = lax.axis_index("fsdp")
    return replica // 2, replica % 2, shard // 2, shard % 2


def is_fast():
    return lax.axis_size("rep") == 4 and lax.axis_size("fsdp") == 8


def pick(operand, index, axis):
    return lax.dynamic_index_in_dim(operand, index, axis, keepdims=False)


def over_z(operand):
    return lax.all_to_all(operand, "fsdp", 0, 0, axis_index_groups=Z_GROUPS)


def hold(plans, values):
    flat, tree = jax.tree.flatten(([plan.live for plan in plans], values))
    flat = lax.optimization_barrier(flat)
    lives, values = jax.tree.unflatten(tree, flat)
    for plan, live in zip(plans, lives):
        plan.live = live
    return values


def place_kernel(rows, half, where, a0, a1, ax, b0, b1, bx, out, sems):
    x, core, y = where[0], where[1], where[2]
    h = rows // PARTS
    copies = []
    for p0, p1, px, c in ((a0, a1, ax, core), (b0, b1, bx, 1 - core)):
        for q in range(HIGH_Z):
            for source, yy, third in (
                (p0.at[q, 0], y, x),
                (p0.at[q, 1], y, 2),
                (p1.at[q, 0], 1 - y, x),
                (p1.at[q, 1], 1 - y, 2),
                (px.at[q, 0], y, 1 - x),
                (px.at[q, 1], 1 - y, 1 - x),
            ):
                row = pl.multiple_of((2 * q + yy) * rows + third * h, 16)
                column = pl.multiple_of(c * half, LANES)
                target = out.at[pl.ds(row, h), pl.ds(column, half)]
                copy = pltpu.make_async_copy(source, target, sems.at[len(copies)])
                copy.start()
                copies.append(copy)
    for copy in copies:
        copy.wait()


class Gather:
    def __init__(self, weight):
        self.rows, self.width = weight.shape
        self.live = {"weight": weight}
        self.fast = is_fast() and self.rows % 48 == 0

    def z(self):
        if not self.fast:
            return
        x, core, _, _ = coordinates()
        h, half = self.rows // PARTS, self.width // 2
        weight = self.live.pop("weight")
        mine = lax.dynamic_slice_in_dim(weight, core * half, half, 1).reshape(PARTS, h, half)
        base = jnp.stack([pick(mine, x, 0), mine[2]], 0)
        self.live["own"] = over_z(jnp.broadcast_to(base, (HIGH_Z, 2, h, half)))

    def y(self):
        if self.fast:
            self.live["far"] = lax.ppermute(self.live["own"], AXES, TO_Y)

    def x(self, early=False, late=False):
        if not self.fast:
            return
        own = None if late else self.live["own"][:, 0]
        far = None if early else self.live["far"][:, 0]
        if early:
            self.live["side"] = lax.ppermute(own, AXES, TO_X)
        elif late:
            self.live["side_far"] = lax.ppermute(far, AXES, TO_X)
        else:
            self.live["both"] = lax.ppermute(jnp.stack([own, far], 1), AXES, TO_X)

    def core(self, *names):
        if self.fast:
            for name in names:
                self.live["twin_" + name] = lax.ppermute(self.live[name], AXES, TO_CORE)

    def whole(self):
        if not self.fast:
            return lax.all_gather(self.live["weight"], "fsdp", axis=0, tiled=True)
        x, core, _, y = coordinates()
        live = self.live
        if "both" not in live:
            live["both"] = jnp.stack([live["side"], live["side_far"]], 1)
            live["twin_both"] = jnp.stack([live["twin_side"], live["twin_side_far"]], 1)
        where = jnp.stack([x, core, y]).astype(jnp.int32)
        any_space = pl.BlockSpec(memory_space=pl.ANY)
        shape = (8 * self.rows, self.width)
        return pl.pallas_call(
            partial(place_kernel, self.rows, self.width // 2),
            out_shape=jax.ShapeDtypeStruct(shape, LOW),
            in_specs=[pl.BlockSpec(memory_space=pltpu.SMEM)] + [any_space] * 6,
            out_specs=pl.BlockSpec(memory_space=pltpu.VMEM),
            scratch_shapes=[pltpu.SemaphoreType.DMA((48,))],
            compiler_params=pltpu.CompilerParams(vmem_limit_bytes=40 * MIB),
            cost_estimate=pl.CostEstimate(
                flops=0, bytes_accessed=4 * shape[0] * shape[1], transcendentals=0
            ),
            name="place",
        )(
            where,
            live["own"],
            live["far"],
            live["both"],
            live["twin_own"],
            live["twin_far"],
            live["twin_both"],
        )


class Scatter:
    def __init__(self, left, send, keep):
        self.left, self.fast = None, is_fast() and left.shape[1] % 384 == 0
        self.live = {"left": left, "send": send, "keep": keep}

    def first(self):
        live = self.live
        if self.fast:
            live["out"] = dot_left(live["left"], live.pop("send")).astype(LOW)

    def core(self):
        if self.fast:
            self.live["got"] = lax.ppermute(self.live.pop("out"), AXES, TO_CORE)

    def second(self):
        live = self.live
        if self.fast:
            product = dot_left(live.pop("left"), live.pop("keep"))
            live["kept"] = (product + live.pop("got").astype(WIDE)).astype(LOW)

    def view(self):
        rows, half = self.live["kept"].shape
        return self.live["kept"].reshape(HIGH_Z, 2, PARTS, rows // 24, half)

    def x(self):
        if self.fast:
            x, _, _, _ = coordinates()
            self.live["side"] = lax.ppermute(pick(self.view(), 1 - x, 2), AXES, TO_X)

    def row(self, index):
        x, _, _, _ = coordinates()
        view = pick(self.view(), index, 1)
        own = pick(view, x, 1).astype(WIDE) + pick(self.live["side"], index, 1).astype(WIDE)
        return jnp.stack([own.astype(LOW), view[:, 2]], 1)

    def y(self):
        if self.fast:
            _, _, _, y = coordinates()
            self.live["far"] = lax.ppermute(self.row(1 - y), AXES, TO_Y)

    def z(self):
        if self.fast:
            _, _, _, y = coordinates()
            line = self.row(y).astype(WIDE) + self.live["far"].astype(WIDE)
            self.live = {"line": over_z(line.astype(LOW))}

    def last_x(self):
        if self.fast:
            part = jnp.sum(self.live["line"].astype(WIDE), axis=0).astype(LOW)
            self.live = {"part": part, "other": lax.ppermute(part, AXES, TO_X)}

    def last_core(self):
        if self.fast:
            x, _, _, _ = coordinates()
            part, other = self.live["part"], self.live["other"]
            shared = (part[1].astype(WIDE) + other[1].astype(WIDE)).astype(LOW)
            first = jnp.where(x == 0, part[0], other[0])
            second = jnp.where(x == 0, other[0], part[0])
            done = jnp.concatenate([first, second, shared], 0)
            self.live = {"done": done, "twin": lax.ppermute(done, AXES, TO_CORE)}

    def halves(self):
        if self.fast:
            _, core, _, _ = coordinates()
            done, twin = self.live["done"], self.live["twin"]
            first = jnp.where(core == 0, done, twin)
            second = jnp.where(core == 0, twin, done)
            return first.astype(WIDE), second.astype(WIDE)
        _, core, _, _ = coordinates()
        left = self.live["left"]
        keep, send = self.live["keep"], self.live["send"]
        first = jnp.where(core == 0, keep, send)
        second = jnp.where(core == 0, send, keep)
        sums = []
        for columns in (first, second):
            grad = dot_left(left, columns).astype(LOW)
            part = lax.psum_scatter(grad, "fsdp", scatter_dimension=0, tiled=True)
            sums.append(lax.psum(part, "rep").astype(WIDE))
        return sums[0], sums[1]


def mine_and_other(first, second):
    _, core, _, _ = coordinates()
    return jnp.where(core == 0, second, first), jnp.where(core == 0, first, second)


def column_halves(array):
    _, core, _, _ = coordinates()
    half = array.shape[1] // 2
    send = lax.dynamic_slice_in_dim(array, (1 - core) * half, half, 1)
    keep = lax.dynamic_slice_in_dim(array, core * half, half, 1)
    return send, keep


def across_replicas(rows):
    if not is_fast():
        return lax.all_gather(rows, "rep", axis=0, tiled=True)
    x, core, _, _ = coordinates()
    count, width = rows.shape
    twin = lax.ppermute(rows, AXES, TO_CORE)
    chip = jnp.stack([jnp.where(core == 0, rows, twin), jnp.where(core == 0, twin, rows)], 0)
    far = lax.ppermute(chip, AXES, TO_X)
    every = jnp.stack([jnp.where(x == 0, chip, far), jnp.where(x == 0, far, chip)], 0)
    return every.reshape(4 * count, width)


def gather_rows(rows):
    shards = lax.axis_size("fsdp")
    count, width = rows.shape
    group = lax.all_to_all(jnp.broadcast_to(rows, (shards, count, width)), "fsdp", 0, 0)
    return group.reshape(shards * count, width)


def exchange(rows):
    shards = lax.axis_size("fsdp")
    count, width = rows.shape
    shaped = rows.reshape(count, shards, width // shards).swapaxes(0, 1)
    return lax.all_to_all(shaped, "fsdp", 0, 0).reshape(shards * count, width // shards)


def sum_back(partial_rows, count):
    shards = lax.axis_size("fsdp")
    shaped = partial_rows.astype(LOW).reshape(shards, count, -1)
    got = lax.all_to_all(shaped, "fsdp", 0, 0)
    return jnp.sum(got.astype(WIDE), axis=0)


def whole_block(array):
    return pl.BlockSpec(
        array.shape, lambda i: (0,) * array.ndim, pipeline_mode=pl.Buffered(1)
    )


def part_width(hd):
    return -(-3 * GROUP * hd // LANES) * LANES


def prepare_kernel(
    heads, hd, x_ref, hot_ref, mod_ref, w_ref, gq_ref, gk_ref, rot_ref, qt_ref, kt_ref, vt_ref,
    normed_ref, q_ref, k_ref, v_ref, rq_ref, rk_ref, wide_ref,
):
    width = heads * hd
    step = part_width(hd)
    x = x_ref[...].astype(WIDE)
    hot = hot_ref[...]
    shift = dot(hot, mod_ref[:, :width])
    scale = dot(hot, mod_ref[:, width:])
    mean = jnp.mean(x, axis=-1, keepdims=True)
    centred = x - mean
    var = jnp.mean(centred * centred, axis=-1, keepdims=True)
    normed = (centred * lax.rsqrt(var + EPSILON) * (1.0 + scale) + shift).astype(LOW)
    normed_ref[...] = normed
    cosine, plus, minus = rot_ref[0], rot_ref[1], rot_ref[2]
    lane = lax.broadcasted_iota(jnp.int32, (BLOCK, LANES), 1)
    inside = lane < hd
    ones = jnp.full((LANES, LANES), 1.0, LOW)
    wide_ref[:, step:] = jnp.zeros((BLOCK, LANES), WIDE)
    for part in range(heads // GROUP):
        wide_ref[:, :step] = dot(normed, w_ref[:, part * step : (part + 1) * step])
        for kind, (g_ref, t_ref, o_ref, r_ref) in enumerate(
            (
                (gq_ref, qt_ref, q_ref, rq_ref),
                (gk_ref, kt_ref, k_ref, rk_ref),
                (None, vt_ref, v_ref, None),
            )
        ):
            tail = t_ref[...]
            for g in range(GROUP):
                h = part * GROUP + g
                at = (kind * GROUP + g) * hd
                raw = jnp.where(inside, wide_ref[:, at : at + LANES], 0.0)
                if kind < 2:
                    r_ref[h] = raw.astype(LOW)
                    total = dot((raw * raw).astype(LOW), ones)
                    u = raw * lax.rsqrt(total * (1.0 / hd) + EPSILON) * g_ref[...]
                    up = pltpu.roll(u, LANES - hd // 4, 1)
                    down = pltpu.roll(u, hd // 4, 1)
                    raw = u * cosine + up * plus + down * minus
                o_ref[h] = raw.astype(LOW) + tail


def prepare(x, hot, mod, w, gq, gk, rot, qt, kt, vt, heads, hd):
    n = x.shape[0]
    width = heads * hd
    rows = pl.BlockSpec((BLOCK, width), lambda i: (i, 0))
    head_spec = pl.BlockSpec((heads, BLOCK, LANES), lambda i: (0, i, 0))
    tail = pl.BlockSpec((BLOCK, LANES), lambda i: (i, 0))
    return pl.pallas_call(
        partial(prepare_kernel, heads, hd),
        grid=(n // BLOCK,),
        in_specs=[
            rows,
            pl.BlockSpec((BLOCK, hot.shape[1]), lambda i: (i, 0)),
            whole_block(mod),
            whole_block(w),
            whole_block(gq),
            whole_block(gk),
            pl.BlockSpec((3, BLOCK, LANES), lambda i: (0, i, 0)),
            tail,
            tail,
            pl.BlockSpec((1, LANES), lambda i: (0, 0)),
        ],
        out_specs=[rows] + [head_spec] * 5,
        out_shape=[jax.ShapeDtypeStruct((n, width), LOW)]
        + [jax.ShapeDtypeStruct((heads, n, LANES), LOW)] * 5,
        scratch_shapes=[pltpu.VMEM((BLOCK, part_width(hd) + LANES), WIDE)],
        compiler_params=pltpu.CompilerParams(vmem_limit_bytes=56 * MIB),
        cost_estimate=pl.CostEstimate(
            flops=2 * n * width * w.shape[1], bytes_accessed=40 * MIB, transcendentals=0
        ),
        name="prepare",
    )(x, hot, mod, w, gq, gk, rot, qt, kt, vt)


def near_blocks(run):
    i = pl.program_id(0)
    n = pl.num_programs(0)

    @pl.when(i == 0)
    def _():
        run((0, 1))

    @pl.when(i == n - 1)
    def _():
        run((-1, 0))

    @pl.when((i > 0) & (i < n - 1))
    def _():
        run((-1, 0, 1))


def attend_kernel(hd, c, q_ref, k_ref, v_ref, mix_ref, q2_ref):
    i = pl.program_id(0)
    heads = q_ref.shape[0]
    lane = lax.broadcasted_iota(jnp.int32, (BLOCK, LANES), 1)

    def run(blocks):
        for h in range(heads):
            q = q_ref[h]
            total = None
            for j in blocks:
                at = pl.ds(pl.multiple_of((i + j) * BLOCK, BLOCK), BLOCK)
                p = jnp.exp2(dot_right(q, k_ref[h, at]) * c).astype(LOW)
                term = dot(p, v_ref[h, at])
                total = term if total is None else total + term
            norm = total[:, hd : hd + 1]
            out = (total * (1.0 / norm)).astype(LOW)
            mix_ref[:, hd * h : hd * (h + 1)] = out[:, :hd]
            rest = jnp.log2(norm) * (1.0 / c)
            first = rest.astype(LOW).astype(WIDE)
            rest = rest - first
            second = rest.astype(LOW).astype(WIDE)
            third = rest - second
            logs = jnp.where(lane == hd + 8, first, jnp.where(lane == hd + 9, second, third))
            q2_ref[h] = jnp.where((lane >= hd + 8) & (lane < hd + 11), logs.astype(LOW), q)

    near_blocks(run)


def attend(q, k, v, hd, c):
    heads, n, _ = q.shape
    full = pl.BlockSpec((heads, n, LANES), lambda i: (0, 0, 0), pipeline_mode=pl.Buffered(1))
    block = pl.BlockSpec((heads, BLOCK, LANES), lambda i: (0, i, 0))
    return pl.pallas_call(
        partial(attend_kernel, hd, c),
        grid=(n // BLOCK,),
        in_specs=[block, full, full],
        out_specs=[pl.BlockSpec((BLOCK, heads * hd), lambda i: (i, 0)), block],
        out_shape=[
            jax.ShapeDtypeStruct((n, heads * hd), LOW),
            jax.ShapeDtypeStruct((heads, n, LANES), LOW),
        ],
        compiler_params=pltpu.CompilerParams(vmem_limit_bytes=56 * MIB),
        cost_estimate=pl.CostEstimate(
            flops=4 * n * 640 * LANES * heads,
            bytes_accessed=20 * MIB,
            transcendentals=heads * n * 640,
        ),
        name="attend",
    )(q, k, v)


def spread_kernel(heads, hd, ga_ref, w_ref, mix_ref, out_ref, grad_scr, mix_scr):
    width = heads * hd
    grad_scr[:, width:] = jnp.zeros((BLOCK, LANES), WIDE)
    mix_scr[:, width:] = jnp.zeros((BLOCK, LANES), WIDE)
    grad_scr[:, :width] = dot_right(ga_ref[...], w_ref[:, :width]).astype(LOW).astype(WIDE)
    mix_scr[:, :width] = mix_ref[...].astype(WIDE)
    lane = lax.broadcasted_iota(jnp.int32, (BLOCK, LANES), 1)
    ones = jnp.full((LANES, LANES), 1.0, LOW)
    for h in range(heads):
        at = hd * h
        grad = jnp.where(lane < hd, grad_scr[:, at : at + LANES], 0.0)
        product = grad * mix_scr[:, at : at + LANES]
        high = product.astype(LOW)
        rest = (product - high.astype(WIDE)).astype(LOW)
        delta = -(dot(high, ones) + dot(rest, ones))
        first = delta.astype(LOW)
        second = (delta - first.astype(WIDE)).astype(LOW)
        out_ref[h] = jnp.where(
            lane == hd, first, jnp.where(lane == hd + 1, second, grad.astype(LOW))
        )


def spread(ga, w, mix, heads, hd):
    n = ga.shape[0]
    width = heads * hd
    row = pl.BlockSpec((BLOCK, width), lambda i: (i, 0))
    return pl.pallas_call(
        partial(spread_kernel, heads, hd),
        grid=(n // BLOCK,),
        in_specs=[row, whole_block(w), row],
        out_specs=pl.BlockSpec((heads, BLOCK, LANES), lambda i: (0, i, 0)),
        out_shape=jax.ShapeDtypeStruct((heads, n, LANES), LOW),
        scratch_shapes=[
            pltpu.VMEM((BLOCK, width + LANES), WIDE),
            pltpu.VMEM((BLOCK, width + LANES), WIDE),
        ],
        compiler_params=pltpu.CompilerParams(vmem_limit_bytes=56 * MIB),
        cost_estimate=pl.CostEstimate(
            flops=2 * n * width * width, bytes_accessed=12 * MIB, transcendentals=0
        ),
        name="spread",
    )(ga, w, mix)


def back_kernel(
    hd, c, score_scale, q_ref, k_ref, v_ref, do_ref, rq_ref, rk_ref, rot_ref, gq_ref, gk_ref,
    joint_ref, gain_ref, dq_scr, dk_scr, dv_scr, gain_scr,
):
    i = pl.program_id(0)
    n = pl.num_programs(0)
    heads = q_ref.shape[0]
    tail = joint_ref.shape[1] - 3 * heads * hd

    @pl.when(i == 0)
    def _():
        dq_scr[...] = jnp.zeros(dq_scr.shape, WIDE)
        gain_scr[...] = jnp.zeros(gain_scr.shape, WIDE)

    ones = jnp.full((LANES, LANES), 1.0, LOW)

    def run(blocks):
        def body(h, carry):
            kk = k_ref[h]
            vv = v_ref[h]
            dk = dv = None
            for j in blocks:
                at = pl.ds(pl.multiple_of((i + j) * BLOCK, BLOCK), BLOCK)
                q = q_ref[h, at]
                do = do_ref[h, at]
                p = jnp.exp2(dot_right(kk, q) * c)
                term = dot(p.astype(LOW), do)
                dv = term if dv is None else dv + term
                ds = (p * dot_right(vv, do)).astype(LOW)
                term = dot(ds, q)
                dk = term if dk is None else dk + term
                dq_scr[h, at] += dot_left(ds, kk)
            dk_scr[h] = dk
            dv_scr[h] = dv
            return carry

        lax.fori_loop(0, heads, body, 0, unroll=2)

    near_blocks(run)

    def finish(dy, raw, rot, gain, row):
        raw = raw.astype(WIDE)
        dy = dy * score_scale
        up = pltpu.roll(dy, LANES - hd // 4, 1)
        down = pltpu.roll(dy, hd // 4, 1)
        d = dy * rot[0] - up * rot[1] - down * rot[2]
        r = lax.rsqrt(dot((raw * raw).astype(LOW), ones) * (1.0 / hd) + EPSILON)
        u = raw * r
        ud = u * d
        gain_scr[row] += jnp.sum(ud.reshape(BLOCK // 8, 8, LANES), axis=0)
        m = dot((ud * gain).astype(LOW), ones) * (1.0 / hd)
        return (r * (gain * d - u * m)).astype(LOW)

    here = pl.ds(pl.multiple_of(i * BLOCK, BLOCK), BLOCK)
    rot = [rot_ref[t, here] for t in range(3)]
    width = heads * hd
    joint_ref[here, 3 * width :] = jnp.zeros((BLOCK, tail), LOW)
    for h in range(heads):
        grad = finish(dk_scr[h], rk_ref[h], rot, gk_ref[...], 1)
        joint_ref[here, width + hd * h : width + hd * (h + 1)] = grad[:, :hd]
        value = dv_scr[h].astype(LOW)
        joint_ref[here, 2 * width + hd * h : 2 * width + hd * (h + 1)] = value[:, :hd]

    @pl.when(i == n - 1)
    def _():
        def rows(b, carry):
            at = pl.ds(pl.multiple_of(b * BLOCK, BLOCK), BLOCK)
            turn = [rot_ref[t, at] for t in range(3)]
            for h in range(heads):
                grad = finish(dq_scr[h, at], rq_ref[h, at], turn, gq_ref[...], 0)
                joint_ref[at, hd * h : hd * (h + 1)] = grad[:, :hd]
            return carry

        lax.fori_loop(0, n, rows, 0)
        gain_ref[...] = gain_scr[...]


def attend_back(part, q2, k, v, do, rq, rk, rot, gq, gk, hd, c, score_scale):
    _, n, _ = q2.shape
    one = pl.Buffered(1)
    full = pl.BlockSpec((GROUP, n, LANES), lambda i: (part, 0, 0), pipeline_mode=one)
    block = pl.BlockSpec((GROUP, BLOCK, LANES), lambda i: (part, i, 0))
    small = pl.BlockSpec((1, LANES), lambda i: (0, 0))
    width = part_width(hd)
    return pl.pallas_call(
        partial(back_kernel, hd, c, score_scale),
        grid=(n // BLOCK,),
        in_specs=[full, block, block, full, full, block, whole_block(rot), small, small],
        out_specs=[
            pl.BlockSpec((n, width), lambda i: (0, 0), pipeline_mode=one),
            pl.BlockSpec((2, 8, LANES), lambda i: (0, 0, 0)),
        ],
        out_shape=[
            jax.ShapeDtypeStruct((n, width), LOW),
            jax.ShapeDtypeStruct((2, 8, LANES), WIDE),
        ],
        scratch_shapes=[
            pltpu.VMEM((GROUP, n, LANES), WIDE),
            pltpu.VMEM((GROUP, BLOCK, LANES), WIDE),
            pltpu.VMEM((GROUP, BLOCK, LANES), WIDE),
            pltpu.VMEM((2, 8, LANES), WIDE),
        ],
        compiler_params=pltpu.CompilerParams(vmem_limit_bytes=56 * MIB),
        cost_estimate=pl.CostEstimate(
            flops=10 * n * 640 * LANES * GROUP,
            bytes_accessed=10 * MIB,
            transcendentals=GROUP * n * 640,
        ),
        name="attend_back",
    )(q2, k, v, do, rq, rk, rot, gq, gk)


def turn_tables(row_place, column_place, hd):
    quarter = hd // 4
    inverse = 10000.0 ** (-jnp.arange(quarter, dtype=WIDE) / quarter)
    row_angle = row_place.astype(WIDE)[:, None] * inverse[None, :]
    column_angle = column_place.astype(WIDE)[:, None] * inverse[None, :]
    rest = jnp.zeros((row_place.shape[0], LANES - hd), WIDE)
    none = jnp.zeros_like(row_angle)
    rc, rs = jnp.cos(row_angle), jnp.sin(row_angle)
    cc, cs = jnp.cos(column_angle), jnp.sin(column_angle)
    return jnp.stack(
        [
            jnp.concatenate([rc, rc, cc, cc, rest], 1),
            jnp.concatenate([-rs, none, -cs, none, rest], 1),
            jnp.concatenate([none, rs, none, cs, rest], 1),
        ],
        0,
    )


def pad_columns(array, width):
    return jnp.pad(array, ((0, 0), (0, width - array.shape[1])))


def to_parts(array, heads, hd):
    rows = array.shape[0]
    shaped = array.reshape(rows, 3, heads // GROUP, GROUP * hd).swapaxes(1, 2)
    shaped = shaped.reshape(rows, heads // GROUP, 3 * GROUP * hd)
    padded = jnp.pad(shaped, ((0, 0), (0, 0), (0, part_width(hd) - 3 * GROUP * hd)))
    return padded.reshape(rows, -1)


def from_parts(array, heads, hd):
    rows = array.shape[0]
    shaped = array.reshape(rows, heads // GROUP, -1)[:, :, : 3 * GROUP * hd]
    shaped = shaped.reshape(rows, heads // GROUP, 3, GROUP * hd).swapaxes(1, 2)
    return shaped.reshape(rows, -1)


def local(
    block_in,
    condition,
    item_lengths,
    item_widths,
    ada_weight,
    ada_bias,
    qkv_weight,
    query_gain,
    key_gain,
    proj_weight,
    gate_up_weight,
    down_weight,
    out_grad,
):
    _, n, width = block_in.shape
    items = item_lengths.shape[1]
    hd = query_gain.shape[0]
    heads = width // hd
    ff = down_weight.shape[0] * lax.axis_size("fsdp")
    score_scale = float(hd) ** (-0.5)
    c = score_scale * 1.4426950408889634
    shards = lax.axis_size("fsdp")
    fsdp_place = lax.axis_index("fsdp")
    odd = width + LANES if (width // LANES) % 2 else width

    g_qkv = Gather(to_parts(qkv_weight, heads, hd))
    g_proj = Gather(pad_columns(proj_weight, odd))
    g_gate = Gather(gate_up_weight[:, :ff])
    g_up = Gather(gate_up_weight[:, ff:])
    g_down = Gather(pad_columns(down_weight, odd))
    gathers = [g_qkv, g_proj, g_gate, g_up, g_down]

    cond_float = condition.astype(WIDE).reshape(items, width)
    cond_silu, silu_pull = jax.vjp(jax.nn.silu, cond_float)
    cond_act = cond_silu.astype(LOW)

    group_act = exchange(cond_act)
    g_qkv.z()
    member, segment, row_place, column_place = layout(item_lengths[0], item_widths[0], n)
    member_low = member.astype(LOW)
    keep_mask = (segment < items - 1).astype(WIDE).reshape(n, 1)
    rot = turn_tables(row_place, column_place, hd)
    spare = jnp.zeros((n, LANES - hd - items), LOW)
    ones_at = jnp.zeros((n, LANES - hd - items), LOW).at[:, :3].set(-1.0)
    blank = jnp.zeros((n, hd), LOW)
    query_tail = jnp.concatenate([blank, member_low, spare], 1)
    key_tail = jnp.concatenate([blank, (member_low - 1.0) * MASK, ones_at], 1)
    value_tail = jnp.zeros((1, LANES), LOW).at[:, hd : hd + 2].set(1.0)
    gain_q = pad_columns(query_gain.astype(WIDE)[None, :], LANES)
    gain_k = pad_columns(key_gain.astype(WIDE)[None, :], LANES)
    bias_row = lax.dynamic_update_slice(
        jnp.zeros((6 * width,), WIDE), ada_bias.astype(WIDE), (fsdp_place * ada_bias.shape[0],)
    )
    mod_part = (dot(group_act, ada_weight) + bias_row[None, :]).astype(LOW)
    tables = (rot, query_tail, key_tail)
    mod_part, tables, group_act = hold(gathers, (mod_part, tables, group_act))

    early = 2 * width
    mod_a = sum_back(mod_part[:, :early], items)
    g_qkv.y()
    g_qkv.x(early=True)
    g_qkv.core("own")
    g_proj.z()
    g_gate.z()
    mod_a, mod_part, tables, group_act = hold(gathers, (mod_a, mod_part, tables, group_act))

    mod_b = sum_back(mod_part[:, early:], items)
    g_qkv.x(late=True)
    g_qkv.core("far", "side")
    g_proj.y()
    g_up.z()
    every_act = across_replicas(group_act)
    mod_a, mod_b, tables = hold(gathers, (mod_a, mod_b, tables))

    g_qkv.core("side_far")
    modulation = jnp.concatenate([mod_a, mod_b], axis=1)
    mod_high = modulation.astype(LOW)
    mod_rest = (modulation - mod_high.astype(WIDE)).astype(LOW)
    mod_low = jnp.concatenate([mod_high, mod_rest], axis=0)
    hot = jnp.concatenate([member_low, member_low], axis=1)
    inputs_low = block_in[0]
    mod_low, tables, inputs_low = hold(gathers, (mod_low, tables, inputs_low))

    g_proj.x()
    g_gate.y()
    g_up.y()
    g_down.z()
    rot, query_tail, key_tail = tables
    qkv_full = g_qkv.whole()
    normed_a, q, k, v, raw_q, raw_k = prepare(
        inputs_low, hot, mod_low[:, :early], qkv_full, gain_q, gain_k, rot,
        query_tail, key_tail, value_tail, heads, hd,
    )
    gathers = gathers[1:]
    normed_a, q, k, v, raw_q, raw_k, qkv_full = hold(
        gathers, (normed_a, q, k, v, raw_q, raw_k, qkv_full)
    )

    g_proj.core("own", "far", "both")
    g_gate.x()
    g_down.y()
    mixed, q2 = attend(q, k, v, hd, c)
    mixed, q2 = hold(gathers, (mixed, q2))

    g_gate.core("own", "far", "both")
    g_up.x()
    proj_full = g_proj.whole()
    token_mod = dot(hot, mod_low)
    shift_a, scale_a, gate_a, shift_b, scale_b, gate_b = jnp.split(token_mod, 6, axis=1)
    inputs = inputs_low.astype(WIDE)
    attended = dot(mixed, proj_full[:, :width])
    middle = inputs + keep_mask * gate_a * attended
    normed_b = modulated(middle, shift_b, scale_b).astype(LOW)
    gathers = gathers[1:]
    middle, normed_b, attended, proj_full = hold(
        gathers, (middle, normed_b, attended, proj_full)
    )

    g_up.core("own", "far", "both")
    g_down.x()
    gate_full = g_gate.whole()
    gate = dot(normed_b, gate_full).astype(LOW)
    gathers = gathers[1:]
    gate, gate_full, normed_b = hold(gathers, (gate, gate_full, normed_b))

    g_down.core("own", "far", "both")
    up_full = g_up.whole()
    up = dot(normed_b, up_full)
    gate_wide = gate.astype(WIDE)
    inner = (jax.nn.silu(gate_wide) * up).astype(LOW)
    up = up.astype(LOW)
    gathers = gathers[1:]
    inner, up, gate, up_full, middle = hold(gathers, (inner, up, gate, up_full, middle))

    down_full = g_down.whole()
    returned = dot(inner, down_full[:, :width])
    block_out = (middle + keep_mask * gate_b * returned).astype(LOW)
    upstream = out_grad[0].astype(WIDE)
    grad_gate_b = upstream * keep_mask * returned
    grad_returned = (upstream * keep_mask * gate_b).astype(LOW)

    s_down = Scatter(inner, *column_halves(pad_columns(grad_returned, odd)))
    s_down.first()
    plans = [s_down]
    grad_returned, down_full, gate, up, gate_full, up_full, normed_b, middle, attended = hold(
        plans,
        (grad_returned, down_full, gate, up, gate_full, up_full, normed_b, middle, attended),
    )

    s_down.core()
    grad_inner = dot_right(grad_returned, down_full[:, :width])
    gate_wide = gate.astype(WIDE)
    sig = jax.nn.sigmoid(gate_wide)
    grad_gate = (grad_inner * up.astype(WIDE) * sig * (1.0 + gate_wide * (1.0 - sig))).astype(LOW)
    grad_up = (grad_inner * gate_wide * sig).astype(LOW)
    grad_gate, grad_up = hold(plans, (grad_gate, grad_up))

    s_down.second()
    chunk = ff // 2
    s_one = Scatter(normed_b, *mine_and_other(grad_gate[:, :chunk], grad_up[:, :chunk]))
    s_two = Scatter(normed_b, *mine_and_other(grad_gate[:, chunk:], grad_up[:, chunk:]))
    s_one.first()
    plans = [s_down, s_one, s_two]
    grad_gate, grad_up = hold(plans, (grad_gate, grad_up))

    s_down.x()
    s_one.core()
    s_two.first()
    grad_normed_b = dot_right(grad_gate, gate_full) + dot_right(grad_up, up_full)
    _, norm_pull_b = jax.vjp(modulated, middle, shift_b, scale_b)
    grad_middle_part, grad_shift_b, grad_scale_b = norm_pull_b(grad_normed_b)
    grad_middle = upstream + grad_middle_part
    grad_gate_a = grad_middle * keep_mask * attended
    grad_attended = (grad_middle * keep_mask * gate_a).astype(LOW)
    s_proj = Scatter(mixed, *column_halves(pad_columns(grad_attended, odd)))
    late = jnp.concatenate(
        [part.astype(LOW) for part in (grad_gate_a, grad_shift_b, grad_scale_b, grad_gate_b)],
        axis=1,
    )
    plans = [s_down, s_one, s_two, s_proj]
    grad_middle, grad_attended, late = hold(plans, (grad_middle, grad_attended, late))

    s_down.y()
    s_two.core()
    s_one.second()
    s_proj.first()
    late_sums = dot_left(member_low, late).astype(LOW)
    grad_mixed = spread(grad_attended, proj_full, mixed, heads, hd)
    late_sums, grad_mixed = hold(plans, (late_sums, grad_mixed))

    back = partial(
        attend_back, q2=q2, k=k, v=v, rq=raw_q, rk=raw_k, rot=rot, gq=gain_q, gk=gain_k,
        hd=hd, c=c, score_scale=score_scale,
    )
    s_down.z()
    s_one.x()
    s_proj.core()
    s_two.second()
    joint_0, gains_0 = back(0, do=grad_mixed)
    joint_0, gains_0, grad_mixed, late_sums = hold(
        plans, (joint_0, gains_0, grad_mixed, late_sums)
    )

    s_down.last_x()
    s_one.y()
    s_two.x()
    s_proj.second()
    late_group = gather_rows(late_sums)
    joint_1, gains_1 = back(1, do=grad_mixed)
    s_head = Scatter(normed_a, *mine_and_other(joint_0, joint_1))
    s_head.first()
    plans = plans + [s_head]
    joint_0, joint_1, gains_1, grad_mixed, late_group = hold(
        plans, (joint_0, joint_1, gains_1, grad_mixed, late_group)
    )

    s_down.last_core()
    s_one.z()
    s_two.y()
    s_proj.x()
    s_head.core()
    late_every = across_replicas(late_group)
    joint_2, gains_2 = back(2, do=grad_mixed)
    joint_2, gains_2, grad_mixed, late_every = hold(
        plans, (joint_2, gains_2, grad_mixed, late_every)
    )
    s_one.last_x()
    s_two.z()
    s_proj.y()
    s_head.second()
    joint_3, gains_3 = back(3, do=grad_mixed)
    s_tail = Scatter(normed_a, *mine_and_other(joint_2, joint_3))
    s_tail.first()
    plans = plans[1:] + [s_tail]
    joint_2, joint_3, gains_3 = hold(plans, (joint_2, joint_3, gains_3))

    s_one.last_core()
    s_two.last_x()
    s_proj.z()
    s_head.x()
    s_tail.core()
    joint = jnp.concatenate([joint_0, joint_1, joint_2, joint_3], axis=1)
    grad_normed_a = dot_right(joint, qkv_full)
    _, norm_pull_a = jax.vjp(modulated, inputs, shift_a, scale_a)
    grad_input_part, grad_shift_a, grad_scale_a = norm_pull_a(grad_normed_a)
    grad_input = grad_middle + grad_input_part
    soon = jnp.concatenate([grad_shift_a.astype(LOW), grad_scale_a.astype(LOW)], axis=1)
    plans = plans[1:]
    grad_input, soon = hold(plans, (grad_input, soon))

    s_two.last_core()
    s_proj.last_x()
    s_head.y()
    s_tail.second()
    early_sums = dot_left(member_low, soon)
    gain_row = jnp.sum(gains_0 + gains_1 + gains_2 + gains_3, axis=1)[:, :hd].reshape(1, 2 * hd)
    gain_high = gain_row.astype(LOW).astype(WIDE)
    gain_block = jnp.concatenate([gain_high, gain_row - gain_high], axis=0)
    gain_block = jnp.pad(gain_block, ((0, items - 2), (0, 2 * LANES - 2 * hd)))
    early_sums = jnp.concatenate([early_sums, gain_block], axis=1).astype(LOW)
    plans = plans[1:]
    early_sums, late_every = hold(plans, (early_sums, late_every))

    s_proj.last_core()
    s_head.z()
    s_tail.x()
    early_group = gather_rows(early_sums)
    shard_late = dot_left(every_act, late_every)
    early_group, shard_late = hold(plans, (early_group, shard_late))

    s_head.last_x()
    s_tail.y()
    early_every = across_replicas(early_group)
    cond_part = dot_right(early_group[:, :early], ada_weight[:, :early]) + dot_right(
        late_group, ada_weight[:, early:]
    )
    early_every, cond_part = hold(plans, (early_every, cond_part))

    s_head.last_core()
    s_tail.z()
    cond_back = lax.all_to_all(cond_part.astype(LOW).reshape(shards, items, -1), "fsdp", 0, 0)
    shard_early = dot_left(every_act, early_every[:, :early])
    cond_back, shard_early = hold(plans, (cond_back, shard_early))

    s_tail.last_x()
    grad_cond_act = cond_back.swapaxes(0, 1).reshape(items, width).astype(WIDE)
    grad_condition = silu_pull(grad_cond_act)[0]
    shard_ada = jnp.concatenate([shard_early, shard_late], axis=1)
    bias_sums = jnp.concatenate(
        [
            jnp.sum(early_every[:, :early].astype(WIDE), axis=0),
            jnp.sum(late_every.astype(WIDE), axis=0),
        ],
        axis=0,
    )
    shard_bias = lax.dynamic_slice(
        bias_sums, (fsdp_place * ada_bias.shape[0],), (ada_bias.shape[0],)
    )
    gain_sums = jnp.sum(early_every[:, early:].astype(WIDE), axis=0)[: 2 * hd]
    hold(plans, ())
    s_tail.last_core()
    shard_qkv = from_parts(
        jnp.concatenate(s_head.halves() + s_tail.halves(), axis=1), heads, hd
    )
    shard_proj = jnp.concatenate(s_proj.halves(), axis=1)[:, :width]
    gate_1, up_1 = s_one.halves()
    gate_2, up_2 = s_two.halves()
    shard_gate_up = jnp.concatenate([gate_1, gate_2, up_1, up_2], axis=1)
    shard_down = jnp.concatenate(s_down.halves(), axis=1)[:, :width]
    return (
        block_out[None],
        grad_input[None],
        grad_condition[None],
        shard_ada,
        shard_bias,
        shard_qkv,
        gain_sums[:hd],
        gain_sums[hd:],
        shard_proj,
        shard_gate_up,
        shard_down,
    )


def solution(mesh):
    return jax.shard_map(
        local,
        mesh=mesh,
        in_specs=(
            P(("rep", "fsdp"), None, None),
            P(("rep", "fsdp"), None, None),
            P(("rep", "fsdp"), None),
            P(("rep", "fsdp"), None),
            P("fsdp", None),
            P("fsdp"),
            P("fsdp", None),
            P(),
            P(),
            P("fsdp", None),
            P("fsdp", None),
            P("fsdp", None),
            P(("rep", "fsdp"), None, None),
        ),
        out_specs=(
            P(("rep", "fsdp"), None, None),
            P(("rep", "fsdp"), None, None),
            P(("rep", "fsdp"), None, None),
            P("fsdp", None),
            P("fsdp"),
            P("fsdp", None),
            P(),
            P(),
            P("fsdp", None),
            P("fsdp", None),
            P("fsdp", None),
        ),
        check_vma=False,
    )
```

```python
import functools
from functools import partial

import jax
import jax.numpy as jnp
from jax import lax
from jax.experimental import pallas as pl
from jax.experimental.pallas import tpu as pltpu
from jax.sharding import PartitionSpec as P

EPSILON = 1e-06
WIDE = jnp.float32
LOW = jnp.bfloat16
AXES = ("rep", "fsdp")
HIGH_Z = 4
PARTS = 3
BLOCK = 256
LANES = 128
GROUP = 4
MASK = 4096.0
MIB = 2**20


def dot(left, right):
    return jnp.dot(left, right, preferred_element_type=WIDE)


def dot_left(left, right):
    return lax.dot_general(left, right, (((0,), (0,)), ((), ())), preferred_element_type=WIDE)


def dot_right(left, right):
    return lax.dot_general(left, right, (((1,), (1,)), ((), ())), preferred_element_type=WIDE)


def layer_norm(values):
    centred = values - jnp.mean(values, axis=-1, keepdims=True)
    return centred * lax.rsqrt(jnp.mean(centred * centred, axis=-1, keepdims=True) + EPSILON)


def modulated(values, shift_part, scale_part):
    return layer_norm(values) * (1.0 + scale_part) + shift_part


def layout(lengths_row, widths_row, length):
    seg_count = lengths_row.shape[0]
    item_ends = jnp.cumsum(lengths_row)
    item_starts = item_ends - lengths_row
    token_place = jnp.arange(length, dtype=jnp.int32)[:, None]
    member = ((token_place >= item_starts[None, :]) & (token_place < item_ends[None, :])).astype(
        jnp.int32
    )
    segment = jnp.sum(member * jnp.arange(seg_count, dtype=jnp.int32)[None, :], axis=1)
    offset = token_place[:, 0] - jnp.sum(member * item_starts[None, :], axis=1)
    across = jnp.sum(member * widths_row[None, :], axis=1)
    return (member, segment, offset // across, offset % across)


def device_index(x, core, z, y):
    return (x * 2 + core) * 8 + z * 2 + y


PLACES = [(x, c, z, y) for x in range(2) for c in range(2) for z in range(4) for y in range(2)]
TO_CORE = [(device_index(x, c, z, y), device_index(x, 1 - c, z, y)) for x, c, z, y in PLACES]
TO_X = [(device_index(x, c, z, y), device_index(1 - x, c, z, y)) for x, c, z, y in PLACES]
TO_Y = [(device_index(x, c, z, y), device_index(x, c, z, 1 - y)) for x, c, z, y in PLACES]
Z_GROUPS = [[0, 2, 4, 6], [1, 3, 5, 7]]


def coordinates():
    replica = lax.axis_index("rep")
    shard = lax.axis_index("fsdp")
    return replica // 2, replica % 2, shard // 2, shard % 2


def is_fast():
    return lax.axis_size("rep") == 4 and lax.axis_size("fsdp") == 8


def pick(operand, index, axis):
    return lax.dynamic_index_in_dim(operand, index, axis, keepdims=False)


def over_z(operand):
    return lax.all_to_all(operand, "fsdp", 0, 0, axis_index_groups=Z_GROUPS)


def hold(plans, values):
    flat, tree = jax.tree.flatten(([plan.live for plan in plans], values))
    flat = lax.optimization_barrier(flat)
    lives, values = jax.tree.unflatten(tree, flat)
    for plan, live in zip(plans, lives):
        plan.live = live
    return values


def place_kernel(rows, half, where, a0, a1, ax, b0, b1, bx, out, sems):
    x, core, y = where[0], where[1], where[2]
    h = rows // PARTS
    copies = []
    for p0, p1, px, c in ((a0, a1, ax, core), (b0, b1, bx, 1 - core)):
        for q in range(HIGH_Z):
            for source, yy, third in (
                (p0.at[q, 0], y, x),
                (p0.at[q, 1], y, 2),
                (p1.at[q, 0], 1 - y, x),
                (p1.at[q, 1], 1 - y, 2),
                (px.at[q, 0], y, 1 - x),
                (px.at[q, 1], 1 - y, 1 - x),
            ):
                row = pl.multiple_of((2 * q + yy) * rows + third * h, 16)
                column = pl.multiple_of(c * half, LANES)
                target = out.at[pl.ds(row, h), pl.ds(column, half)]
                copy = pltpu.make_async_copy(source, target, sems.at[len(copies)])
                copy.start()
                copies.append(copy)
    for copy in copies:
        copy.wait()


class Gather:
    def __init__(self, weight):
        self.rows, self.width = weight.shape
        self.live = {"weight": weight}
        self.fast = is_fast() and self.rows % 48 == 0

    def z(self):
        if not self.fast:
            return
        x, core, _, _ = coordinates()
        h, half = self.rows // PARTS, self.width // 2
        weight = self.live.pop("weight")
        mine = lax.dynamic_slice_in_dim(weight, core * half, half, 1).reshape(PARTS, h, half)
        base = jnp.stack([pick(mine, x, 0), mine[2]], 0)
        self.live["own"] = over_z(jnp.broadcast_to(base, (HIGH_Z, 2, h, half)))

    def y(self):
        if self.fast:
            self.live["far"] = lax.ppermute(self.live["own"], AXES, TO_Y)

    def x(self, early=False, late=False):
        if not self.fast:
            return
        own = None if late else self.live["own"][:, 0]
        far = None if early else self.live["far"][:, 0]
        if early:
            self.live["side"] = lax.ppermute(own, AXES, TO_X)
        elif late:
            self.live["side_far"] = lax.ppermute(far, AXES, TO_X)
        else:
            self.live["both"] = lax.ppermute(jnp.stack([own, far], 1), AXES, TO_X)

    def core(self, *names):
        if self.fast:
            for name in names:
                self.live["twin_" + name] = lax.ppermute(self.live[name], AXES, TO_CORE)

    def whole(self):
        if not self.fast:
            return lax.all_gather(self.live["weight"], "fsdp", axis=0, tiled=True)
        x, core, _, y = coordinates()
        live = self.live
        if "both" not in live:
            live["both"] = jnp.stack([live["side"], live["side_far"]], 1)
            live["twin_both"] = jnp.stack([live["twin_side"], live["twin_side_far"]], 1)
        where = jnp.stack([x, core, y]).astype(jnp.int32)
        any_space = pl.BlockSpec(memory_space=pl.ANY)
        shape = (8 * self.rows, self.width)
        return pl.pallas_call(
            partial(place_kernel, self.rows, self.width // 2),
            out_shape=jax.ShapeDtypeStruct(shape, LOW),
            in_specs=[pl.BlockSpec(memory_space=pltpu.SMEM)] + [any_space] * 6,
            out_specs=pl.BlockSpec(memory_space=pltpu.VMEM),
            scratch_shapes=[pltpu.SemaphoreType.DMA((48,))],
            compiler_params=pltpu.CompilerParams(vmem_limit_bytes=40 * MIB),
            cost_estimate=pl.CostEstimate(
                flops=0, bytes_accessed=4 * shape[0] * shape[1], transcendentals=0
            ),
            name="place",
        )(
            where,
            live["own"],
            live["far"],
            live["both"],
            live["twin_own"],
            live["twin_far"],
            live["twin_both"],
        )


class Scatter:
    def __init__(self, left, send, keep):
        self.left, self.fast = None, is_fast() and left.shape[1] % 384 == 0
        self.live = {"left": left, "send": send, "keep": keep}

    def first(self):
        live = self.live
        if self.fast:
            live["out"] = dot_left(live["left"], live.pop("send")).astype(LOW)

    def core(self):
        if self.fast:
            self.live["got"] = lax.ppermute(self.live.pop("out"), AXES, TO_CORE)

    def second(self):
        live = self.live
        if self.fast:
            product = dot_left(live.pop("left"), live.pop("keep"))
            live["kept"] = (product + live.pop("got").astype(WIDE)).astype(LOW)

    def join(self, other):
        if self.fast:
            kept = [self.live["kept"], other.live.pop("kept")]
            self.live["kept"] = jnp.concatenate(kept, axis=1)

    def view(self):
        rows, half = self.live["kept"].shape
        return self.live["kept"].reshape(HIGH_Z, 2, PARTS, rows // 24, half)

    def x(self):
        if self.fast:
            x, _, _, _ = coordinates()
            self.live["side"] = lax.ppermute(pick(self.view(), 1 - x, 2), AXES, TO_X)

    def row(self, index):
        x, _, _, _ = coordinates()
        view = pick(self.view(), index, 1)
        own = pick(view, x, 1).astype(WIDE) + pick(self.live["side"], index, 1).astype(WIDE)
        return jnp.stack([own.astype(LOW), view[:, 2]], 1)

    def y(self):
        if self.fast:
            _, _, _, y = coordinates()
            self.live["far"] = lax.ppermute(self.row(1 - y), AXES, TO_Y)

    def z(self):
        if self.fast:
            _, _, _, y = coordinates()
            line = self.row(y).astype(WIDE) + self.live["far"].astype(WIDE)
            self.live = {"line": over_z(line.astype(LOW))}

    def last_x(self):
        if self.fast:
            part = jnp.sum(self.live["line"].astype(WIDE), axis=0).astype(LOW)
            self.live = {"part": part, "other": lax.ppermute(part, AXES, TO_X)}

    def last_core(self):
        if self.fast:
            x, _, _, _ = coordinates()
            part, other = self.live["part"], self.live["other"]
            shared = (part[1].astype(WIDE) + other[1].astype(WIDE)).astype(LOW)
            first = jnp.where(x == 0, part[0], other[0])
            second = jnp.where(x == 0, other[0], part[0])
            done = jnp.concatenate([first, second, shared], 0)
            self.live = {"done": done, "twin": lax.ppermute(done, AXES, TO_CORE)}

    def halves(self):
        if self.fast:
            _, core, _, _ = coordinates()
            done, twin = self.live["done"], self.live["twin"]
            first = jnp.where(core == 0, done, twin)
            second = jnp.where(core == 0, twin, done)
            return first.astype(WIDE), second.astype(WIDE)
        _, core, _, _ = coordinates()
        left = self.live["left"]
        keep, send = self.live["keep"], self.live["send"]
        first = jnp.where(core == 0, keep, send)
        second = jnp.where(core == 0, send, keep)
        sums = []
        for columns in (first, second):
            grad = dot_left(left, columns).astype(LOW)
            part = lax.psum_scatter(grad, "fsdp", scatter_dimension=0, tiled=True)
            sums.append(lax.psum(part, "rep").astype(WIDE))
        return sums[0], sums[1]


def mine_and_other(first, second):
    _, core, _, _ = coordinates()
    return jnp.where(core == 0, second, first), jnp.where(core == 0, first, second)


def column_halves(array):
    _, core, _, _ = coordinates()
    half = array.shape[1] // 2
    send = lax.dynamic_slice_in_dim(array, (1 - core) * half, half, 1)
    keep = lax.dynamic_slice_in_dim(array, core * half, half, 1)
    return send, keep


def across_replicas(rows):
    if not is_fast():
        return lax.all_gather(rows, "rep", axis=0, tiled=True)
    x, core, _, _ = coordinates()
    count, width = rows.shape
    twin = lax.ppermute(rows, AXES, TO_CORE)
    chip = jnp.stack([jnp.where(core == 0, rows, twin), jnp.where(core == 0, twin, rows)], 0)
    far = lax.ppermute(chip, AXES, TO_X)
    every = jnp.stack([jnp.where(x == 0, chip, far), jnp.where(x == 0, far, chip)], 0)
    return every.reshape(4 * count, width)


def gather_rows(rows):
    shards = lax.axis_size("fsdp")
    count, width = rows.shape
    group = lax.all_to_all(jnp.broadcast_to(rows, (shards, count, width)), "fsdp", 0, 0)
    return group.reshape(shards * count, width)


def exchange(rows):
    shards = lax.axis_size("fsdp")
    count, width = rows.shape
    shaped = rows.reshape(count, shards, width // shards).swapaxes(0, 1)
    return lax.all_to_all(shaped, "fsdp", 0, 0).reshape(shards * count, width // shards)


def sum_back(partial_rows, count):
    shards = lax.axis_size("fsdp")
    shaped = partial_rows.astype(LOW).reshape(shards, count, -1)
    got = lax.all_to_all(shaped, "fsdp", 0, 0)
    return jnp.sum(got.astype(WIDE), axis=0)


def whole_block(array):
    return pl.BlockSpec(
        array.shape, lambda i: (0,) * array.ndim, pipeline_mode=pl.Buffered(1)
    )


def part_width(hd):
    return -(-3 * GROUP * hd // LANES) * LANES


def prepare_kernel(
    heads, hd, x_ref, hot_ref, mod_ref, w_ref, gq_ref, gk_ref, rot_ref, qt_ref, kt_ref, vt_ref,
    normed_ref, q_ref, k_ref, v_ref, rq_ref, rk_ref, wide_ref,
):
    width = heads * hd
    step = part_width(hd)
    x = x_ref[...].astype(WIDE)
    hot = hot_ref[...]
    shift = dot(hot, mod_ref[:, :width])
    scale = dot(hot, mod_ref[:, width:])
    mean = jnp.mean(x, axis=-1, keepdims=True)
    centred = x - mean
    var = jnp.mean(centred * centred, axis=-1, keepdims=True)
    normed = (centred * lax.rsqrt(var + EPSILON) * (1.0 + scale) + shift).astype(LOW)
    normed_ref[...] = normed
    cosine, plus, minus = rot_ref[0], rot_ref[1], rot_ref[2]
    lane = lax.broadcasted_iota(jnp.int32, (BLOCK, LANES), 1)
    inside = lane < hd
    ones = jnp.full((LANES, LANES), 1.0, LOW)
    wide_ref[:, step:] = jnp.zeros((BLOCK, LANES), WIDE)
    for part in range(heads // GROUP):
        wide_ref[:, :step] = dot(normed, w_ref[:, part * step : (part + 1) * step])
        for kind, (g_ref, t_ref, o_ref, r_ref) in enumerate(
            (
                (gq_ref, qt_ref, q_ref, rq_ref),
                (gk_ref, kt_ref, k_ref, rk_ref),
                (None, vt_ref, v_ref, None),
            )
        ):
            tail = t_ref[...]
            for g in range(GROUP):
                h = part * GROUP + g
                at = (kind * GROUP + g) * hd
                raw = jnp.where(inside, wide_ref[:, at : at + LANES], 0.0)
                if kind < 2:
                    r_ref[h] = raw.astype(LOW)
                    total = dot((raw * raw).astype(LOW), ones)
                    u = raw * lax.rsqrt(total * (1.0 / hd) + EPSILON) * g_ref[...]
                    up = pltpu.roll(u, LANES - hd // 4, 1)
                    down = pltpu.roll(u, hd // 4, 1)
                    raw = u * cosine + up * plus + down * minus
                o_ref[h] = raw.astype(LOW) + tail


def prepare(x, hot, mod, w, gq, gk, rot, qt, kt, vt, heads, hd):
    n = x.shape[0]
    width = heads * hd
    rows = pl.BlockSpec((BLOCK, width), lambda i: (i, 0))
    head_spec = pl.BlockSpec((heads, BLOCK, LANES), lambda i: (0, i, 0))
    tail = pl.BlockSpec((BLOCK, LANES), lambda i: (i, 0))
    return pl.pallas_call(
        partial(prepare_kernel, heads, hd),
        grid=(n // BLOCK,),
        in_specs=[
            rows,
            pl.BlockSpec((BLOCK, hot.shape[1]), lambda i: (i, 0)),
            whole_block(mod),
            whole_block(w),
            whole_block(gq),
            whole_block(gk),
            pl.BlockSpec((3, BLOCK, LANES), lambda i: (0, i, 0)),
            tail,
            tail,
            pl.BlockSpec((1, LANES), lambda i: (0, 0)),
        ],
        out_specs=[rows] + [head_spec] * 5,
        out_shape=[jax.ShapeDtypeStruct((n, width), LOW)]
        + [jax.ShapeDtypeStruct((heads, n, LANES), LOW)] * 5,
        scratch_shapes=[pltpu.VMEM((BLOCK, part_width(hd) + LANES), WIDE)],
        compiler_params=pltpu.CompilerParams(vmem_limit_bytes=56 * MIB),
        cost_estimate=pl.CostEstimate(
            flops=2 * n * width * w.shape[1], bytes_accessed=40 * MIB, transcendentals=0
        ),
        name="prepare",
    )(x, hot, mod, w, gq, gk, rot, qt, kt, vt)


def near_blocks(run):
    i = pl.program_id(0)
    n = pl.num_programs(0)

    @pl.when(i == 0)
    def _():
        run((0, 1))

    @pl.when(i == n - 1)
    def _():
        run((-1, 0))

    @pl.when((i > 0) & (i < n - 1))
    def _():
        run((-1, 0, 1))


def attend_kernel(hd, c, q_ref, k_ref, v_ref, mix_ref, q2_ref):
    i = pl.program_id(0)
    heads = q_ref.shape[0]
    lane = lax.broadcasted_iota(jnp.int32, (BLOCK, LANES), 1)

    def run(blocks):
        for h in range(heads):
            q = q_ref[h]
            total = None
            for j in blocks:
                at = pl.ds(pl.multiple_of((i + j) * BLOCK, BLOCK), BLOCK)
                p = jnp.exp2(dot_right(q, k_ref[h, at]) * c).astype(LOW)
                term = dot(p, v_ref[h, at])
                total = term if total is None else total + term
            norm = total[:, hd : hd + 1]
            out = (total * (1.0 / norm)).astype(LOW)
            mix_ref[:, hd * h : hd * (h + 1)] = out[:, :hd]
            rest = jnp.log2(norm) * (1.0 / c)
            first = rest.astype(LOW).astype(WIDE)
            rest = rest - first
            second = rest.astype(LOW).astype(WIDE)
            third = rest - second
            logs = jnp.where(lane == hd + 8, first, jnp.where(lane == hd + 9, second, third))
            q2_ref[h] = jnp.where((lane >= hd + 8) & (lane < hd + 11), logs.astype(LOW), q)

    near_blocks(run)


def attend(q, k, v, hd, c):
    heads, n, _ = q.shape
    full = pl.BlockSpec((heads, n, LANES), lambda i: (0, 0, 0), pipeline_mode=pl.Buffered(1))
    block = pl.BlockSpec((heads, BLOCK, LANES), lambda i: (0, i, 0))
    return pl.pallas_call(
        partial(attend_kernel, hd, c),
        grid=(n // BLOCK,),
        in_specs=[block, full, full],
        out_specs=[pl.BlockSpec((BLOCK, heads * hd), lambda i: (i, 0)), block],
        out_shape=[
            jax.ShapeDtypeStruct((n, heads * hd), LOW),
            jax.ShapeDtypeStruct((heads, n, LANES), LOW),
        ],
        compiler_params=pltpu.CompilerParams(vmem_limit_bytes=56 * MIB),
        cost_estimate=pl.CostEstimate(
            flops=4 * n * 640 * LANES * heads,
            bytes_accessed=20 * MIB,
            transcendentals=heads * n * 640,
        ),
        name="attend",
    )(q, k, v)


def spread_kernel(heads, hd, ga_ref, w_ref, mix_ref, out_ref, grad_scr, mix_scr):
    width = heads * hd
    grad_scr[:, width:] = jnp.zeros((BLOCK, LANES), WIDE)
    mix_scr[:, width:] = jnp.zeros((BLOCK, LANES), WIDE)
    grad_scr[:, :width] = dot_right(ga_ref[:, :width], w_ref[:, :width]).astype(LOW).astype(WIDE)
    mix_scr[:, :width] = mix_ref[...].astype(WIDE)
    lane = lax.broadcasted_iota(jnp.int32, (BLOCK, LANES), 1)
    ones = jnp.full((LANES, LANES), 1.0, LOW)
    for h in range(heads):
        at = hd * h
        grad = jnp.where(lane < hd, grad_scr[:, at : at + LANES], 0.0)
        product = grad * mix_scr[:, at : at + LANES]
        high = product.astype(LOW)
        rest = (product - high.astype(WIDE)).astype(LOW)
        delta = -(dot(high, ones) + dot(rest, ones))
        first = delta.astype(LOW)
        second = (delta - first.astype(WIDE)).astype(LOW)
        out_ref[h] = jnp.where(
            lane == hd, first, jnp.where(lane == hd + 1, second, grad.astype(LOW))
        )


def spread(ga, w, mix, heads, hd):
    n = ga.shape[0]
    width = heads * hd
    row = pl.BlockSpec((BLOCK, width), lambda i: (i, 0))
    wide_row = pl.BlockSpec((BLOCK, ga.shape[1]), lambda i: (i, 0))
    return pl.pallas_call(
        partial(spread_kernel, heads, hd),
        grid=(n // BLOCK,),
        in_specs=[wide_row, whole_block(w), row],
        out_specs=pl.BlockSpec((heads, BLOCK, LANES), lambda i: (0, i, 0)),
        out_shape=jax.ShapeDtypeStruct((heads, n, LANES), LOW),
        scratch_shapes=[
            pltpu.VMEM((BLOCK, width + LANES), WIDE),
            pltpu.VMEM((BLOCK, width + LANES), WIDE),
        ],
        compiler_params=pltpu.CompilerParams(vmem_limit_bytes=56 * MIB),
        cost_estimate=pl.CostEstimate(
            flops=2 * n * width * width, bytes_accessed=12 * MIB, transcendentals=0
        ),
        name="spread",
    )(ga, w, mix)


def back_kernel(
    hd, c, score_scale, q_ref, k_ref, v_ref, do_ref, rq_ref, rk_ref, rot_ref, gq_ref, gk_ref,
    joint_0, joint_1, gain_ref, dq_scr, dk_scr, dv_scr, gain_scr,
):
    i = pl.program_id(0)
    n = pl.num_programs(0)
    heads = q_ref.shape[0]
    width = GROUP * hd
    tail = joint_0.shape[1] - 3 * width
    joints = (joint_0, joint_1)

    @pl.when(i == 0)
    def _():
        dq_scr[...] = jnp.zeros(dq_scr.shape, WIDE)
        gain_scr[...] = jnp.zeros(gain_scr.shape, WIDE)

    ones = jnp.full((LANES, LANES), 1.0, LOW)

    def run(blocks):
        def body(h, carry):
            kk = k_ref[h]
            vv = v_ref[h]
            dk = dv = None
            for j in blocks:
                at = pl.ds(pl.multiple_of((i + j) * BLOCK, BLOCK), BLOCK)
                q = q_ref[h, at]
                do = do_ref[h, at]
                p = jnp.exp2(dot_right(kk, q) * c)
                term = dot(p.astype(LOW), do)
                dv = term if dv is None else dv + term
                ds = (p * dot_right(vv, do)).astype(LOW)
                term = dot(ds, q)
                dk = term if dk is None else dk + term
                dq_scr[h, at] += dot_left(ds, kk)
            dk_scr[h] = dk
            dv_scr[h] = dv
            return carry

        lax.fori_loop(0, heads, body, 0, unroll=2)

    near_blocks(run)

    def finish(dy, raw, rot, gain, row):
        raw = raw.astype(WIDE)
        dy = dy * score_scale
        up = pltpu.roll(dy, LANES - hd // 4, 1)
        down = pltpu.roll(dy, hd // 4, 1)
        d = dy * rot[0] - up * rot[1] - down * rot[2]
        r = lax.rsqrt(dot((raw * raw).astype(LOW), ones) * (1.0 / hd) + EPSILON)
        u = raw * r
        ud = u * d
        gain_scr[row] += jnp.sum(ud.reshape(BLOCK // 8, 8, LANES), axis=0)
        m = dot((ud * gain).astype(LOW), ones) * (1.0 / hd)
        return (r * (gain * d - u * m)).astype(LOW)

    here = pl.ds(pl.multiple_of(i * BLOCK, BLOCK), BLOCK)
    rot = [rot_ref[t, here] for t in range(3)]
    for joint_ref in joints:
        joint_ref[here, 3 * width :] = jnp.zeros((BLOCK, tail), LOW)
    for h in range(heads):
        joint_ref, at = joints[h // GROUP], hd * (h % GROUP)
        grad = finish(dk_scr[h], rk_ref[h], rot, gk_ref[...], 1)
        joint_ref[here, width + at : width + at + hd] = grad[:, :hd]
        value = dv_scr[h].astype(LOW)
        joint_ref[here, 2 * width + at : 2 * width + at + hd] = value[:, :hd]

    @pl.when(i == n - 1)
    def _():
        def rows(b, carry):
            at = pl.ds(pl.multiple_of(b * BLOCK, BLOCK), BLOCK)
            turn = [rot_ref[t, at] for t in range(3)]
            for h in range(heads):
                start = hd * (h % GROUP)
                grad = finish(dq_scr[h, at], rq_ref[h, at], turn, gq_ref[...], 0)
                joints[h // GROUP][at, start : start + hd] = grad[:, :hd]
            return carry

        lax.fori_loop(0, n, rows, 0)
        gain_ref[...] = gain_scr[...]


def attend_back(part, q2, k, v, do, rq, rk, rot, gq, gk, hd, c, score_scale):
    _, n, _ = q2.shape
    one = pl.Buffered(1)
    full = pl.BlockSpec((2 * GROUP, n, LANES), lambda i: (part, 0, 0), pipeline_mode=one)
    block = pl.BlockSpec((2 * GROUP, BLOCK, LANES), lambda i: (part, i, 0))
    small = pl.BlockSpec((1, LANES), lambda i: (0, 0))
    width = part_width(hd)
    return pl.pallas_call(
        partial(back_kernel, hd, c, score_scale),
        grid=(n // BLOCK,),
        in_specs=[full, block, block, full, full, block, whole_block(rot), small, small],
        out_specs=[
            pl.BlockSpec((n, width), lambda i: (0, 0), pipeline_mode=one),
            pl.BlockSpec((n, width), lambda i: (0, 0), pipeline_mode=one),
            pl.BlockSpec((2, 8, LANES), lambda i: (0, 0, 0)),
        ],
        out_shape=[
            jax.ShapeDtypeStruct((n, width), LOW),
            jax.ShapeDtypeStruct((n, width), LOW),
            jax.ShapeDtypeStruct((2, 8, LANES), WIDE),
        ],
        scratch_shapes=[
            pltpu.VMEM((2 * GROUP, n, LANES), WIDE),
            pltpu.VMEM((2 * GROUP, BLOCK, LANES), WIDE),
            pltpu.VMEM((2 * GROUP, BLOCK, LANES), WIDE),
            pltpu.VMEM((2, 8, LANES), WIDE),
        ],
        compiler_params=pltpu.CompilerParams(vmem_limit_bytes=56 * MIB),
        cost_estimate=pl.CostEstimate(
            flops=10 * n * 640 * LANES * 2 * GROUP,
            bytes_accessed=20 * MIB,
            transcendentals=2 * GROUP * n * 640,
        ),
        name="attend_back",
    )(q2, k, v, do, rq, rk, rot, gq, gk)


def normed_rows(values):
    centred = values - jnp.mean(values, axis=-1, keepdims=True)
    scale = lax.rsqrt(jnp.mean(centred * centred, axis=-1, keepdims=True) + EPSILON)
    return centred * scale, scale


def norm_back(normed, scale, grad):
    inner = jnp.mean(grad * normed, axis=-1, keepdims=True)
    return scale * (grad - jnp.mean(grad, axis=-1, keepdims=True) - normed * inner)


def add_sums(out_ref, at, hot, values):
    width = values.shape[1]
    term = dot_left(hot, values.astype(LOW))
    here = (slice(None), slice(at * width, (at + 1) * width))

    @pl.when(pl.program_id(0) == 0)
    def _():
        out_ref[here] = term

    @pl.when(pl.program_id(0) > 0)
    def _():
        out_ref[here] += term


def rows_of(array):
    return pl.BlockSpec((BLOCK, array.shape[1]), lambda i: (i, 0))


def call_rows(kernel, name, streamed, fixed, outs, sums=()):
    n = streamed[0].shape[0]
    width_of = lambda a: a.shape[1] * a.dtype.itemsize
    work = sum(2 * n * a.shape[0] * a.shape[1] for a in fixed if a.shape[0] > 256)
    moved = sum(n * width_of(a) for a in streamed) + sum(a.shape[0] * width_of(a) for a in fixed)
    return pl.pallas_call(
        kernel,
        grid=(n // BLOCK,),
        in_specs=[rows_of(a) for a in streamed] + [whole_block(a) for a in fixed],
        out_specs=[pl.BlockSpec((BLOCK, w), lambda i: (i, 0)) for w, _ in outs]
        + [pl.BlockSpec(shape, lambda i: (0, 0)) for shape in sums],
        out_shape=[jax.ShapeDtypeStruct((n, w), t) for w, t in outs]
        + [jax.ShapeDtypeStruct(shape, WIDE) for shape in sums],
        compiler_params=pltpu.CompilerParams(vmem_limit_bytes=56 * MIB),
        cost_estimate=pl.CostEstimate(flops=work, bytes_accessed=moved, transcendentals=0),
        name=name,
    )(*streamed, *fixed)


def join_kernel(mix_ref, x_ref, hot_ref, keep_ref, w_ref, mod_ref, att_ref, mid_ref, norm_ref):
    width = x_ref.shape[1]
    hot = hot_ref[...]
    attended = dot(mix_ref[...], w_ref[:, :width])
    att_ref[...] = attended.astype(LOW)
    gate = dot(hot, mod_ref[:, :width]) * keep_ref[...]
    middle = x_ref[...].astype(WIDE) + gate * attended
    mid_ref[...] = middle
    normed, _ = normed_rows(middle)
    scale = dot(hot, mod_ref[:, 2 * width : 3 * width])
    shift = dot(hot, mod_ref[:, width : 2 * width])
    norm_ref[...] = (normed * (1.0 + scale) + shift).astype(LOW)


def gate_kernel(x_ref, w_ref, out_ref):
    out_ref[...] = dot(x_ref[...], w_ref[...]).astype(LOW)


def up_kernel(x_ref, gate_ref, w_ref, up_ref, inner_ref):
    up = dot(x_ref[...], w_ref[...])
    up_ref[...] = up.astype(LOW)
    gate = gate_ref[...].astype(WIDE)
    inner_ref[...] = (gate * jax.nn.sigmoid(gate) * up).astype(LOW)


def down_kernel(
    inner_ref, mid_ref, grad_ref, hot_ref, keep_ref, w_ref, mod_ref, out_ref, back_ref, sum_ref
):
    width = mid_ref.shape[1]
    hot = hot_ref[...]
    returned = dot(inner_ref[...], w_ref[:, :width])
    gate = dot(hot, mod_ref[...]) * keep_ref[...]
    out_ref[...] = (mid_ref[...] + gate * returned).astype(LOW)
    upstream = grad_ref[...].astype(WIDE)
    back_ref[:, :width] = (upstream * gate).astype(LOW)
    if back_ref.shape[1] > width:
        back_ref[:, width:] = jnp.zeros((BLOCK, back_ref.shape[1] - width), LOW)
    add_sums(sum_ref, 0, hot, upstream * keep_ref[...] * returned)


def inner_back_kernel(grad_ref, gate_ref, up_ref, w_ref, gg_ref, gu_ref):
    grad = dot_right(grad_ref[...], w_ref[...])
    gate = gate_ref[...].astype(WIDE)
    sig = jax.nn.sigmoid(gate)
    act = gate * sig
    gg_ref[...] = (grad * up_ref[...].astype(WIDE) * (sig + act * (1.0 - sig))).astype(LOW)
    gu_ref[...] = (grad * act).astype(LOW)


def middle_back_kernel(
    gg_ref, gu_ref, mid_ref, grad_ref, att_ref, hot_ref, keep_ref, wg_ref, wu_ref, mod_ref,
    out_ref, back_ref, sum_ref,
):
    width = mid_ref.shape[1]
    hot = hot_ref[...]
    keep = keep_ref[...]
    grad = dot_right(gg_ref[...], wg_ref[...]) + dot_right(gu_ref[...], wu_ref[...])
    normed, scale = normed_rows(mid_ref[...])
    turned = grad * (1.0 + dot(hot, mod_ref[:, 2 * width : 3 * width]))
    total = grad_ref[...].astype(WIDE) + norm_back(normed, scale, turned)
    out_ref[...] = total
    gate = dot(hot, mod_ref[:, :width]) * keep
    back_ref[:, :width] = (total * gate).astype(LOW)
    if back_ref.shape[1] > width:
        back_ref[:, width:] = jnp.zeros((BLOCK, back_ref.shape[1] - width), LOW)
    add_sums(sum_ref, 0, hot, total * keep * att_ref[...].astype(WIDE))
    add_sums(sum_ref, 1, hot, grad)
    add_sums(sum_ref, 2, hot, grad * normed)


def input_back_kernel(j0, j1, j2, j3, mid_ref, x_ref, hot_ref, w_ref, mod_ref, out_ref, sum_ref):
    width = x_ref.shape[1]
    hot = hot_ref[...]
    step = j0.shape[1]
    grad = None
    for part, ref in enumerate((j0, j1, j2, j3)):
        term = dot_right(ref[...], w_ref[:, part * step : (part + 1) * step])
        grad = term if grad is None else grad + term
    normed, scale = normed_rows(x_ref[...].astype(WIDE))
    turned = grad * (1.0 + dot(hot, mod_ref[:, width : 2 * width]))
    out_ref[...] = mid_ref[...] + norm_back(normed, scale, turned)
    add_sums(sum_ref, 0, hot, grad)
    add_sums(sum_ref, 1, hot, grad * normed)


def turn_tables(row_place, column_place, hd):
    quarter = hd // 4
    inverse = 10000.0 ** (-jnp.arange(quarter, dtype=WIDE) / quarter)
    row_angle = row_place.astype(WIDE)[:, None] * inverse[None, :]
    column_angle = column_place.astype(WIDE)[:, None] * inverse[None, :]
    rest = jnp.zeros((row_place.shape[0], LANES - hd), WIDE)
    none = jnp.zeros_like(row_angle)
    rc, rs = jnp.cos(row_angle), jnp.sin(row_angle)
    cc, cs = jnp.cos(column_angle), jnp.sin(column_angle)
    return jnp.stack(
        [
            jnp.concatenate([rc, rc, cc, cc, rest], 1),
            jnp.concatenate([-rs, none, -cs, none, rest], 1),
            jnp.concatenate([none, rs, none, cs, rest], 1),
        ],
        0,
    )


def high_and_rest(values):
    high = values.astype(LOW)
    return jnp.concatenate([high, (values - high.astype(WIDE)).astype(LOW)], axis=0)


def pad_columns(array, width):
    return jnp.pad(array, ((0, 0), (0, width - array.shape[1])))


def to_parts(array, heads, hd):
    rows = array.shape[0]
    shaped = array.reshape(rows, 3, heads // GROUP, GROUP * hd).swapaxes(1, 2)
    shaped = shaped.reshape(rows, heads // GROUP, 3 * GROUP * hd)
    padded = jnp.pad(shaped, ((0, 0), (0, 0), (0, part_width(hd) - 3 * GROUP * hd)))
    return padded.reshape(rows, -1)


def from_parts(array, heads, hd):
    rows = array.shape[0]
    shaped = array.reshape(rows, heads // GROUP, -1)[:, :, : 3 * GROUP * hd]
    shaped = shaped.reshape(rows, heads // GROUP, 3, GROUP * hd).swapaxes(1, 2)
    return shaped.reshape(rows, -1)


def local(
    block_in,
    condition,
    item_lengths,
    item_widths,
    ada_weight,
    ada_bias,
    qkv_weight,
    query_gain,
    key_gain,
    proj_weight,
    gate_up_weight,
    down_weight,
    out_grad,
):
    _, n, width = block_in.shape
    items = item_lengths.shape[1]
    hd = query_gain.shape[0]
    heads = width // hd
    ff = down_weight.shape[0] * lax.axis_size("fsdp")
    score_scale = float(hd) ** (-0.5)
    c = score_scale * 1.4426950408889634
    shards = lax.axis_size("fsdp")
    fsdp_place = lax.axis_index("fsdp")
    odd = width + LANES if (width // LANES) % 2 else width

    g_qkv = Gather(to_parts(qkv_weight, heads, hd))
    g_proj = Gather(pad_columns(proj_weight, odd))
    g_gate = Gather(gate_up_weight[:, :ff])
    g_up = Gather(gate_up_weight[:, ff:])
    g_down = Gather(pad_columns(down_weight, odd))
    gathers = [g_qkv, g_proj, g_gate, g_up, g_down]

    cond_float = condition.astype(WIDE).reshape(items, width)
    cond_silu, silu_pull = jax.vjp(jax.nn.silu, cond_float)
    cond_act = cond_silu.astype(LOW)

    g_qkv.z()
    group_act = exchange(cond_act)
    member, segment, row_place, column_place = layout(item_lengths[0], item_widths[0], n)
    member_low = member.astype(LOW)
    keep = (segment < items - 1).astype(WIDE).reshape(n, 1)
    rot = turn_tables(row_place, column_place, hd)
    spare = jnp.zeros((n, LANES - hd - items), LOW)
    ones_at = jnp.zeros((n, LANES - hd - items), LOW).at[:, :3].set(-1.0)
    blank = jnp.zeros((n, hd), LOW)
    query_tail = jnp.concatenate([blank, member_low, spare], 1)
    key_tail = jnp.concatenate([blank, (member_low - 1.0) * MASK, ones_at], 1)
    value_tail = jnp.zeros((1, LANES), LOW).at[:, hd : hd + 2].set(1.0)
    gain_q = pad_columns(query_gain.astype(WIDE)[None, :], LANES)
    gain_k = pad_columns(key_gain.astype(WIDE)[None, :], LANES)
    hot = jnp.concatenate([member_low, member_low], axis=1)
    tables = (rot, query_tail, key_tail, hot, keep)
    tables, group_act = hold(gathers, (tables, group_act))

    g_qkv.y()
    g_qkv.x(early=True)
    g_qkv.core("own")
    g_gate.z()
    bias_row = lax.dynamic_update_slice(
        jnp.zeros((6 * width,), WIDE), ada_bias.astype(WIDE), (fsdp_place * ada_bias.shape[0],)
    )
    mod_part = (dot(group_act, ada_weight) + bias_row[None, :]).astype(LOW)
    mod_part, group_act, tables = hold(gathers, (mod_part, group_act, tables))

    early = 2 * width
    modulation = high_and_rest(sum_back(mod_part, items))
    g_qkv.x(late=True)
    g_qkv.core("far", "side")
    g_proj.z()
    inputs_low = block_in[0]
    modulation, tables, inputs_low = hold(gathers, (modulation, tables, inputs_low))
    mod_a, mod_b = modulation[:, :early], modulation[:, early:]

    g_qkv.core("side_far")
    g_proj.y()
    g_gate.y()
    g_up.z()
    rot, query_tail, key_tail, hot, keep = tables
    qkv_full = g_qkv.whole()
    normed_a, q, k, v, raw_q, raw_k = prepare(
        inputs_low, hot, mod_a, qkv_full, gain_q, gain_k, rot,
        query_tail, key_tail, value_tail, heads, hd,
    )
    gathers = gathers[1:]
    normed_a, q, k, v, raw_q, raw_k, qkv_full, mod_b = hold(
        gathers, (normed_a, q, k, v, raw_q, raw_k, qkv_full, mod_b)
    )

    g_proj.x()
    g_proj.core("own", "far")
    g_gate.x()
    g_gate.core("own", "far")
    g_up.y()
    g_down.z()
    mixed, q2 = attend(q, k, v, hd, c)
    mixed, q2 = hold(gathers, (mixed, q2))

    g_proj.core("both")
    g_gate.core("both")
    g_up.x()
    g_up.core("own", "far")
    g_down.y()
    proj_full = g_proj.whole()
    mod_mid = mod_b[:, : 3 * width]
    attended, middle, normed_b = call_rows(
        join_kernel, "join", (mixed, inputs_low, hot, keep), (proj_full, mod_mid),
        ((width, LOW), (width, WIDE), (width, LOW)),
    )
    gathers = gathers[1:]
    middle, normed_b, attended, proj_full = hold(
        gathers, (middle, normed_b, attended, proj_full)
    )

    g_up.core("both")
    g_down.x()
    g_down.core("own", "far")
    gate_full = g_gate.whole()
    (gate,) = call_rows(gate_kernel, "gate", (normed_b,), (gate_full,), ((ff, LOW),))
    gathers = gathers[1:]
    gate, gate_full, normed_b = hold(gathers, (gate, gate_full, normed_b))

    g_down.core("both")
    up_full = g_up.whole()
    up, inner = call_rows(
        up_kernel, "up", (normed_b, gate), (up_full,), ((ff, LOW), (ff, LOW))
    )
    gathers = gathers[1:]
    inner, up, gate, up_full, middle = hold(gathers, (inner, up, gate, up_full, middle))

    down_full = g_down.whole()
    block_out, grad_returned, sums_gate_b = call_rows(
        down_kernel, "down", (inner, middle, out_grad[0], hot, keep),
        (down_full, mod_b[:, 3 * width :]), ((width, LOW), (odd, LOW)), ((2 * items, width),),
    )

    s_down = Scatter(inner, *column_halves(grad_returned))
    s_down.first()
    plans = [s_down]
    grad_returned, down_full, gate, up, gate_full, up_full, normed_b, middle, attended = hold(
        plans,
        (grad_returned, down_full, gate, up, gate_full, up_full, normed_b, middle, attended),
    )

    s_down.core()
    grad_gate, grad_up = call_rows(
        inner_back_kernel, "inner_back", (grad_returned, gate, up), (down_full,),
        ((ff, LOW), (ff, LOW)),
    )
    grad_gate, grad_up = hold(plans, (grad_gate, grad_up))

    s_down.second()
    s_wide = Scatter(normed_b, *mine_and_other(grad_gate, grad_up))
    s_wide.first()
    plans = [s_down, s_wide]
    grad_gate, grad_up = hold(plans, (grad_gate, grad_up))

    s_down.x()
    s_wide.core()
    grad_middle, grad_attended, sums_mid = call_rows(
        middle_back_kernel, "middle_back",
        (grad_gate, grad_up, middle, out_grad[0], attended, hot, keep),
        (gate_full, up_full, mod_mid), ((width, WIDE), (odd, LOW)), ((2 * items, 3 * width),),
    )
    s_proj = Scatter(mixed, *column_halves(grad_attended))
    plans = [s_down, s_wide, s_proj]
    grad_middle, grad_attended, sums_mid = hold(plans, (grad_middle, grad_attended, sums_mid))

    s_down.y()
    s_wide.second()
    s_proj.first()
    late_sums = jnp.concatenate([sums_mid[:items], sums_gate_b[:items]], axis=1).astype(LOW)
    grad_mixed = spread(grad_attended, proj_full, mixed, heads, hd)
    late_sums, grad_mixed = hold(plans, (late_sums, grad_mixed))

    back = partial(
        attend_back, q2=q2, k=k, v=v, rq=raw_q, rk=raw_k, rot=rot, gq=gain_q, gk=gain_k,
        hd=hd, c=c, score_scale=score_scale,
    )
    s_down.z()
    s_wide.x()
    s_proj.core()
    joint_0, joint_1, gains_0 = back(0, do=grad_mixed)
    s_head = Scatter(normed_a, *mine_and_other(joint_0, joint_1))
    s_head.first()
    plans = plans + [s_head]
    joint_0, joint_1, gains_0, grad_mixed, late_sums = hold(
        plans, (joint_0, joint_1, gains_0, grad_mixed, late_sums)
    )

    s_down.last_x()
    s_wide.y()
    s_head.core()
    late_group = gather_rows(late_sums)
    joint_2, joint_3, gains_1 = back(1, do=grad_mixed)
    s_tail = Scatter(normed_a, *mine_and_other(joint_2, joint_3))
    plans = plans + [s_tail]
    joint_0, joint_1, joint_2, joint_3, gains_1, late_group = hold(
        plans, (joint_0, joint_1, joint_2, joint_3, gains_1, late_group)
    )

    s_down.last_core()
    s_wide.z()
    s_tail.first()
    s_tail.core()
    s_proj.second()
    s_head.second()
    s_head.join(s_proj)
    s_head.x()
    late_every = across_replicas(late_group)
    grad_input, sums_early = call_rows(
        input_back_kernel, "input_back",
        (joint_0, joint_1, joint_2, joint_3, grad_middle, inputs_low, hot),
        (qkv_full, mod_a), ((width, WIDE),), ((2 * items, 2 * width),),
    )
    s_tail.second()
    plans = [s_down, s_wide, s_head, s_tail]
    grad_input, sums_early, late_every = hold(plans, (grad_input, sums_early, late_every))

    s_wide.last_x()
    s_head.y()
    s_tail.x()
    early_sums = sums_early[:items]
    gain_row = jnp.sum(gains_0 + gains_1, axis=1)[:, :hd].reshape(1, 2 * hd)
    gain_high = gain_row.astype(LOW).astype(WIDE)
    gain_block = jnp.concatenate([gain_high, gain_row - gain_high], axis=0)
    gain_block = jnp.pad(gain_block, ((0, items - 2), (0, 2 * LANES - 2 * hd)))
    early_sums = jnp.concatenate([early_sums, gain_block], axis=1).astype(LOW)
    early_group = gather_rows(early_sums)
    every_act = across_replicas(group_act)
    early_group, late_every, every_act = hold(plans, (early_group, late_every, every_act))

    s_wide.last_core()
    s_head.z()
    s_tail.y()
    early_every = across_replicas(early_group)
    shard_late = dot_left(every_act, late_every)
    cond_part = dot_right(early_group[:, :early], ada_weight[:, :early]) + dot_right(
        late_group, ada_weight[:, early:]
    )
    early_every, cond_part, shard_late, every_act = hold(
        plans, (early_every, cond_part, shard_late, every_act)
    )

    s_head.last_x()
    s_tail.z()
    shard_early = dot_left(every_act, early_every[:, :early])
    shard_early, cond_part = hold(plans, (shard_early, cond_part))

    s_head.last_core()
    s_tail.last_x()
    cond_back = lax.all_to_all(cond_part.astype(LOW).reshape(shards, items, -1), "fsdp", 0, 0)
    shard_ada = jnp.concatenate([shard_early, shard_late], axis=1)
    bias_sums = jnp.concatenate(
        [
            jnp.sum(early_every[:, :early].astype(WIDE), axis=0),
            jnp.sum(late_every.astype(WIDE), axis=0),
        ],
        axis=0,
    )
    shard_bias = lax.dynamic_slice(
        bias_sums, (fsdp_place * ada_bias.shape[0],), (ada_bias.shape[0],)
    )
    gain_sums = jnp.sum(early_every[:, early:].astype(WIDE), axis=0)[: 2 * hd]
    cond_back = hold(plans, cond_back)
    s_tail.last_core()
    grad_cond_act = cond_back.swapaxes(0, 1).reshape(items, width).astype(WIDE)
    grad_condition = silu_pull(grad_cond_act)[0]
    cut = part_width(hd)
    if s_head.fast:
        head_0, head_1 = s_head.halves()
        proj_halves = (head_0[:, cut:], head_1[:, cut:])
    else:
        head_0, head_1 = s_head.halves()
        proj_halves = s_proj.halves()
    shard_qkv = from_parts(
        jnp.concatenate((head_0[:, :cut], head_1[:, :cut]) + s_tail.halves(), axis=1), heads, hd
    )
    shard_proj = jnp.concatenate(proj_halves, axis=1)[:, :width]
    shard_gate_up = jnp.concatenate(s_wide.halves(), axis=1)
    shard_down = jnp.concatenate(s_down.halves(), axis=1)[:, :width]
    return (
        block_out[None],
        grad_input[None],
        grad_condition[None],
        shard_ada,
        shard_bias,
        shard_qkv,
        gain_sums[:hd],
        gain_sums[hd:],
        shard_proj,
        shard_gate_up,
        shard_down,
    )


def solution(mesh):
    return jax.shard_map(
        local,
        mesh=mesh,
        in_specs=(
            P(("rep", "fsdp"), None, None),
            P(("rep", "fsdp"), None, None),
            P(("rep", "fsdp"), None),
            P(("rep", "fsdp"), None),
            P("fsdp", None),
            P("fsdp"),
            P("fsdp", None),
            P(),
            P(),
            P("fsdp", None),
            P("fsdp", None),
            P("fsdp", None),
            P(("rep", "fsdp"), None, None),
        ),
        out_specs=(
            P(("rep", "fsdp"), None, None),
            P(("rep", "fsdp"), None, None),
            P(("rep", "fsdp"), None, None),
            P("fsdp", None),
            P("fsdp"),
            P("fsdp", None),
            P(),
            P(),
            P("fsdp", None),
            P("fsdp", None),
            P("fsdp", None),
        ),
        check_vma=False,
    )
```

```python
import functools
from functools import partial

import jax
import jax.numpy as jnp
from jax import lax
from jax.experimental import pallas as pl
from jax.experimental.pallas import tpu as pltpu
from jax.sharding import PartitionSpec as P

EPSILON = 1e-06
WIDE = jnp.float32
LOW = jnp.bfloat16
AXES = ("rep", "fsdp")
HIGH_Z = 4
PARTS = 3
BLOCK = 256
LANES = 128
GROUP = 4
MASK = 4096.0
MIB = 2**20


def dot(left, right):
    return jnp.dot(left, right, preferred_element_type=WIDE)


def dot_left(left, right):
    return lax.dot_general(left, right, (((0,), (0,)), ((), ())), preferred_element_type=WIDE)


def dot_right(left, right):
    return lax.dot_general(left, right, (((1,), (1,)), ((), ())), preferred_element_type=WIDE)


def layer_norm(values):
    centred = values - jnp.mean(values, axis=-1, keepdims=True)
    return centred * lax.rsqrt(jnp.mean(centred * centred, axis=-1, keepdims=True) + EPSILON)


def modulated(values, shift_part, scale_part):
    return layer_norm(values) * (1.0 + scale_part) + shift_part


def layout(lengths_row, widths_row, length):
    seg_count = lengths_row.shape[0]
    item_ends = jnp.cumsum(lengths_row)
    item_starts = item_ends - lengths_row
    token_place = jnp.arange(length, dtype=jnp.int32)[:, None]
    member = ((token_place >= item_starts[None, :]) & (token_place < item_ends[None, :])).astype(
        jnp.int32
    )
    segment = jnp.sum(member * jnp.arange(seg_count, dtype=jnp.int32)[None, :], axis=1)
    offset = token_place[:, 0] - jnp.sum(member * item_starts[None, :], axis=1)
    across = jnp.sum(member * widths_row[None, :], axis=1)
    return (member, segment, offset // across, offset % across)


def device_index(x, core, z, y):
    return (x * 2 + core) * 8 + z * 2 + y


PLACES = [(x, c, z, y) for x in range(2) for c in range(2) for z in range(4) for y in range(2)]
TO_CORE = [(device_index(x, c, z, y), device_index(x, 1 - c, z, y)) for x, c, z, y in PLACES]
TO_X = [(device_index(x, c, z, y), device_index(1 - x, c, z, y)) for x, c, z, y in PLACES]
TO_Y = [(device_index(x, c, z, y), device_index(x, c, z, 1 - y)) for x, c, z, y in PLACES]
TO_Z = [
    [(device_index(x, c, z, y), device_index(x, c, (z + k) % 4, y)) for x, c, z, y in PLACES]
    for k in range(4)
]
Z_GROUPS = [[0, 2, 4, 6], [1, 3, 5, 7]]


def coordinates():
    replica = lax.axis_index("rep")
    shard = lax.axis_index("fsdp")
    return replica // 2, replica % 2, shard // 2, shard % 2


def is_fast():
    return lax.axis_size("rep") == 4 and lax.axis_size("fsdp") == 8


def pick(operand, index, axis):
    return lax.dynamic_index_in_dim(operand, index, axis, keepdims=False)


def over_z(operand):
    return lax.all_to_all(operand, "fsdp", 0, 0, axis_index_groups=Z_GROUPS)


def hold(plans, values):
    flat, tree = jax.tree.flatten(([plan.live for plan in plans], values))
    flat = lax.optimization_barrier(flat)
    lives, values = jax.tree.unflatten(tree, flat)
    for plan, live in zip(plans, lives):
        plan.live = live
    return values


def place_kernel(rows, half, apart, where, a0, a1, ax, b0, b1, bx, out, sems):
    x, core, z, y = where[0], where[1], where[2], where[3]
    h = rows // PARTS
    copies = []
    for p0, p1, px, c in ((a0, a1, ax, core), (b0, b1, bx, 1 - core)):
        for q in range(HIGH_Z):
            for source, yy, third in (
                (p0.at[q, 0], y, x),
                (p0.at[q, 1], y, 2),
                (p1.at[q, 0], 1 - y, x),
                (p1.at[q, 1], 1 - y, 2),
                (px.at[q, 0], y, 1 - x),
                (px.at[q, 1], 1 - y, 1 - x),
            ):
                zz = (z + HIGH_Z - q) % HIGH_Z if apart else q
                row = pl.multiple_of((2 * zz + yy) * rows + third * h, 16)
                column = pl.multiple_of(c * half, LANES)
                target = out.at[pl.ds(row, h), pl.ds(column, half)]
                copy = pltpu.make_async_copy(source, target, sems.at[len(copies)])
                copy.start()
                copies.append(copy)
    for copy in copies:
        copy.wait()


class Gather:
    def __init__(self, weight):
        self.rows, self.width = weight.shape
        self.live = {"weight": weight}
        self.fast = is_fast() and self.rows % 48 == 0

    def z(self, apart=False):
        if not self.fast:
            return
        self.apart = apart
        x, core, _, _ = coordinates()
        h, half = self.rows // PARTS, self.width // 2
        weight = self.live.pop("weight")
        mine = lax.dynamic_slice_in_dim(weight, core * half, half, 1).reshape(PARTS, h, half)
        base = jnp.stack([pick(mine, x, 0), mine[2]], 0)
        if apart:
            lines = [base] + [lax.ppermute(base, AXES, TO_Z[k]) for k in (1, 2, 3)]
            self.live["own"] = jnp.stack(lines, 0)
            return
        self.live["own"] = over_z(jnp.broadcast_to(base, (HIGH_Z, 2, h, half)))

    def y(self):
        if self.fast:
            self.live["far"] = lax.ppermute(self.live["own"], AXES, TO_Y)

    def x(self):
        if self.fast:
            ends = jnp.stack([self.live["own"][:, 0], self.live["far"][:, 0]], 1)
            self.live["both"] = lax.ppermute(ends, AXES, TO_X)

    def core(self, *names):
        if self.fast:
            for name in names:
                self.live["twin_" + name] = lax.ppermute(self.live[name], AXES, TO_CORE)

    def whole(self):
        if not self.fast:
            return lax.all_gather(self.live["weight"], "fsdp", axis=0, tiled=True)
        live = self.live
        where = jnp.stack(coordinates()).astype(jnp.int32)
        any_space = pl.BlockSpec(memory_space=pl.ANY)
        shape = (8 * self.rows, self.width)
        return pl.pallas_call(
            partial(place_kernel, self.rows, self.width // 2, self.apart),
            out_shape=jax.ShapeDtypeStruct(shape, LOW),
            in_specs=[pl.BlockSpec(memory_space=pltpu.SMEM)] + [any_space] * 6,
            out_specs=pl.BlockSpec(memory_space=pltpu.VMEM),
            scratch_shapes=[pltpu.SemaphoreType.DMA((48,))],
            compiler_params=pltpu.CompilerParams(vmem_limit_bytes=40 * MIB),
            cost_estimate=pl.CostEstimate(
                flops=0, bytes_accessed=4 * shape[0] * shape[1], transcendentals=0
            ),
            name="place",
        )(
            where,
            live["own"],
            live["far"],
            live["both"],
            live["twin_own"],
            live["twin_far"],
            live["twin_both"],
        )


class Scatter:
    def __init__(self, left, send, keep):
        self.left, self.fast = None, is_fast() and left.shape[1] % 384 == 0
        self.live = {"left": left, "send": send, "keep": keep}

    def first(self):
        live = self.live
        if self.fast:
            live["out"] = dot_left(live["left"], live.pop("send")).astype(LOW)

    def core(self):
        if self.fast:
            self.live["got"] = lax.ppermute(self.live.pop("out"), AXES, TO_CORE)

    def second(self):
        live = self.live
        if self.fast:
            product = dot_left(live.pop("left"), live.pop("keep"))
            live["kept"] = (product + live.pop("got").astype(WIDE)).astype(LOW)

    def join(self, other):
        if self.fast:
            kept = [self.live["kept"], other.live.pop("kept")]
            self.live["kept"] = jnp.concatenate(kept, axis=1)

    def view(self):
        rows, half = self.live["kept"].shape
        return self.live["kept"].reshape(HIGH_Z, 2, PARTS, rows // 24, half)

    def x(self):
        if self.fast:
            x, _, _, _ = coordinates()
            self.live["side"] = lax.ppermute(pick(self.view(), 1 - x, 2), AXES, TO_X)

    def row(self, index):
        x, _, _, _ = coordinates()
        view = pick(self.view(), index, 1)
        own = pick(view, x, 1).astype(WIDE) + pick(self.live["side"], index, 1).astype(WIDE)
        return jnp.stack([own.astype(LOW), view[:, 2]], 1)

    def y(self):
        if self.fast:
            _, _, _, y = coordinates()
            self.live["far"] = lax.ppermute(self.row(1 - y), AXES, TO_Y)

    def z(self, apart=False):
        if self.fast:
            _, _, _, y = coordinates()
            line = (self.row(y).astype(WIDE) + self.live["far"].astype(WIDE)).astype(LOW)
            if apart:
                _, _, z, _ = coordinates()
                live = {"0": pick(line, z, 0)}
                for k in (2, 1, 3):
                    live[str(k)] = lax.ppermute(pick(line, (z + k) % 4, 0), AXES, TO_Z[k])
                self.live = {"lines": live}
            else:
                self.live = {"line": over_z(line)}

    def last_x(self):
        if self.fast:
            if "lines" in self.live:
                lines = [self.live["lines"][k].astype(WIDE) for k in ("0", "1", "2", "3")]
                part = (lines[0] + lines[1] + lines[2] + lines[3]).astype(LOW)
            else:
                part = jnp.sum(self.live["line"].astype(WIDE), axis=0).astype(LOW)
            self.live = {"part": part, "other": lax.ppermute(part, AXES, TO_X)}

    def last_core(self):
        if self.fast:
            x, _, _, _ = coordinates()
            part, other = self.live["part"], self.live["other"]
            shared = (part[1].astype(WIDE) + other[1].astype(WIDE)).astype(LOW)
            first = jnp.where(x == 0, part[0], other[0])
            second = jnp.where(x == 0, other[0], part[0])
            done = jnp.concatenate([first, second, shared], 0)
            self.live = {"done": done, "twin": lax.ppermute(done, AXES, TO_CORE)}

    def halves(self):
        if self.fast:
            _, core, _, _ = coordinates()
            done, twin = self.live["done"], self.live["twin"]
            first = jnp.where(core == 0, done, twin)
            second = jnp.where(core == 0, twin, done)
            return first.astype(WIDE), second.astype(WIDE)
        _, core, _, _ = coordinates()
        left = self.live["left"]
        keep, send = self.live["keep"], self.live["send"]
        first = jnp.where(core == 0, keep, send)
        second = jnp.where(core == 0, send, keep)
        sums = []
        for columns in (first, second):
            grad = dot_left(left, columns).astype(LOW)
            part = lax.psum_scatter(grad, "fsdp", scatter_dimension=0, tiled=True)
            sums.append(lax.psum(part, "rep").astype(WIDE))
        return sums[0], sums[1]


def column_halves(array):
    _, core, _, _ = coordinates()
    half = array.shape[1] // 2
    send = lax.dynamic_slice_in_dim(array, (1 - core) * half, half, 1)
    keep = lax.dynamic_slice_in_dim(array, core * half, half, 1)
    return send, keep


def across_x(rows):
    return lax.ppermute(rows, AXES, TO_X) if is_fast() else rows


def across_replicas(rows, far):
    if not is_fast():
        return lax.all_gather(rows, "rep", axis=0, tiled=True)
    x, core, _, _ = coordinates()
    count, width = rows.shape
    line = jnp.stack([jnp.where(x == 0, rows, far), jnp.where(x == 0, far, rows)], 0)
    twin = lax.ppermute(line, AXES, TO_CORE)
    every = [jnp.where(core == 0, line, twin), jnp.where(core == 0, twin, line)]
    return jnp.stack(every, 1).reshape(4 * count, width)


def gather_rows(rows):
    shards = lax.axis_size("fsdp")
    count, width = rows.shape
    group = lax.all_to_all(jnp.broadcast_to(rows, (shards, count, width)), "fsdp", 0, 0)
    return group.reshape(shards * count, width)


def exchange(rows):
    shards = lax.axis_size("fsdp")
    count, width = rows.shape
    shaped = rows.reshape(count, shards, width // shards).swapaxes(0, 1)
    return lax.all_to_all(shaped, "fsdp", 0, 0).reshape(shards * count, width // shards)


def sum_back(partial_rows, count):
    shards = lax.axis_size("fsdp")
    shaped = partial_rows.astype(LOW).reshape(shards, count, -1)
    got = lax.all_to_all(shaped, "fsdp", 0, 0)
    return jnp.sum(got.astype(WIDE), axis=0)


def whole_block(array):
    return pl.BlockSpec(
        array.shape, lambda i: (0,) * array.ndim, pipeline_mode=pl.Buffered(1)
    )


def part_width(hd):
    return -(-3 * GROUP * hd // LANES) * LANES


def prepare_kernel(
    first, heads, hd, x_ref, hot_ref, mod_ref, w_ref, gq_ref, gk_ref, rot_ref, qt_ref, kt_ref,
    vt_ref, *refs
):
    normed_ref, q_ref, k_ref, v_ref, rq_ref, rk_ref, wide_ref = refs if first else (x_ref, *refs)
    step = part_width(hd)
    if first:
        width = x_ref.shape[1]
        hot = hot_ref[...]
        shift = dot(hot, mod_ref[:, :width])
        scale = dot(hot, mod_ref[:, width:])
        normed, _ = normed_rows(x_ref[...].astype(WIDE))
        normed = (normed * (1.0 + scale) + shift).astype(LOW)
        normed_ref[...] = normed
    else:
        normed = x_ref[...]
    cosine, plus, minus = rot_ref[0], rot_ref[1], rot_ref[2]
    lane = lax.broadcasted_iota(jnp.int32, (BLOCK, LANES), 1)
    inside = lane < hd
    ones = jnp.full((LANES, LANES), 1.0, LOW)
    wide_ref[:, step:] = jnp.zeros((BLOCK, LANES), WIDE)
    for part in range(heads // GROUP):
        wide_ref[:, :step] = dot(normed, w_ref[:, part * step : (part + 1) * step])
        for kind, (g_ref, t_ref, o_ref, r_ref) in enumerate(
            (
                (gq_ref, qt_ref, q_ref, rq_ref),
                (gk_ref, kt_ref, k_ref, rk_ref),
                (None, vt_ref, v_ref, None),
            )
        ):
            tail = t_ref[...]
            for g in range(GROUP):
                h = part * GROUP + g
                at = (kind * GROUP + g) * hd
                raw = jnp.where(inside, wide_ref[:, at : at + LANES], 0.0)
                if kind < 2:
                    r_ref[h] = raw.astype(LOW)
                    total = dot((raw * raw).astype(LOW), ones)
                    u = raw * lax.rsqrt(total * (1.0 / hd) + EPSILON) * g_ref[...]
                    up = pltpu.roll(u, LANES - hd // 4, 1)
                    down = pltpu.roll(u, hd // 4, 1)
                    raw = u * cosine + up * plus + down * minus
                o_ref[h] = raw.astype(LOW) + tail


def prepare(first, x, hot, mod, w, gq, gk, rot, qt, kt, vt, heads, hd):
    n, width = x.shape
    rows = pl.BlockSpec((BLOCK, width), lambda i: (i, 0))
    head_spec = pl.BlockSpec((heads, BLOCK, LANES), lambda i: (0, i, 0))
    tail = pl.BlockSpec((BLOCK, LANES), lambda i: (i, 0))
    normed_spec, normed_shape = [rows], [jax.ShapeDtypeStruct((n, width), LOW)]
    return pl.pallas_call(
        partial(prepare_kernel, first, heads, hd),
        grid=(n // BLOCK,),
        in_specs=[
            rows,
            pl.BlockSpec((BLOCK, hot.shape[1]), lambda i: (i, 0)),
            whole_block(mod),
            whole_block(w),
            whole_block(gq),
            whole_block(gk),
            pl.BlockSpec((3, BLOCK, LANES), lambda i: (0, i, 0)),
            tail,
            tail,
            pl.BlockSpec((1, LANES), lambda i: (0, 0)),
        ],
        out_specs=(normed_spec if first else []) + [head_spec] * 5,
        out_shape=(normed_shape if first else [])
        + [jax.ShapeDtypeStruct((heads, n, LANES), LOW)] * 5,
        scratch_shapes=[pltpu.VMEM((BLOCK, part_width(hd) + LANES), WIDE)],
        compiler_params=pltpu.CompilerParams(vmem_limit_bytes=56 * MIB),
        cost_estimate=pl.CostEstimate(
            flops=2 * n * width * w.shape[1], bytes_accessed=20 * MIB, transcendentals=0
        ),
        name="prepare",
    )(x, hot, mod, w, gq, gk, rot, qt, kt, vt)


def near_blocks(run):
    i = pl.program_id(0)
    n = pl.num_programs(0)

    @pl.when(i == 0)
    def _():
        run((0, 1))

    @pl.when(i == n - 1)
    def _():
        run((-1, 0))

    @pl.when((i > 0) & (i < n - 1))
    def _():
        run((-1, 0, 1))


def attend_kernel(hd, c, *refs):
    i = pl.program_id(0)
    mix_ref = refs[6]
    lane = lax.broadcasted_iota(jnp.int32, (BLOCK, LANES), 1)
    heads = refs[0].shape[0]

    def run(blocks):
        for head in range(2 * heads):
            half, h = head // heads, head % heads
            q_ref, k_ref, v_ref = refs[3 * half : 3 * half + 3]
            q = q_ref[h]
            total = None
            for j in blocks:
                at = pl.ds(pl.multiple_of((i + j) * BLOCK, BLOCK), BLOCK)
                p = jnp.exp2(dot_right(q, k_ref[h, at]) * c).astype(LOW)
                term = dot(p, v_ref[h, at])
                total = term if total is None else total + term
            norm = total[:, hd : hd + 1]
            out = (total * (1.0 / norm)).astype(LOW)
            mix_ref[:, hd * head : hd * (head + 1)] = out[:, :hd]
            rest = jnp.log2(norm) * (1.0 / c)
            first = rest.astype(LOW).astype(WIDE)
            rest = rest - first
            second = rest.astype(LOW).astype(WIDE)
            third = rest - second
            logs = jnp.where(lane == hd + 8, first, jnp.where(lane == hd + 9, second, third))
            marked = jnp.where((lane >= hd + 8) & (lane < hd + 11), logs.astype(LOW), q)
            refs[7 + half][h] = marked

    near_blocks(run)


def attend(one, two, hd, c):
    heads, n, _ = one[0].shape
    full = pl.BlockSpec((heads, n, LANES), lambda i: (0, 0, 0), pipeline_mode=pl.Buffered(1))
    block = pl.BlockSpec((heads, BLOCK, LANES), lambda i: (0, i, 0))
    width = 2 * heads * hd
    return pl.pallas_call(
        partial(attend_kernel, hd, c),
        grid=(n // BLOCK,),
        in_specs=[block, full, full] * 2,
        out_specs=[pl.BlockSpec((BLOCK, width), lambda i: (i, 0)), block, block],
        out_shape=[jax.ShapeDtypeStruct((n, width), LOW)]
        + [jax.ShapeDtypeStruct((heads, n, LANES), LOW)] * 2,
        compiler_params=pltpu.CompilerParams(vmem_limit_bytes=56 * MIB),
        cost_estimate=pl.CostEstimate(
            flops=8 * n * 640 * LANES * heads,
            bytes_accessed=20 * MIB,
            transcendentals=2 * heads * n * 640,
        ),
        name="attend",
    )(*one, *two)


def spread_kernel(heads, hd, proj_at, ga_ref, w_ref, mix_ref, out_ref, grad_scr, mix_scr):
    width = heads * hd
    grad_scr[:, width:] = jnp.zeros((BLOCK, LANES), WIDE)
    mix_scr[:, width:] = jnp.zeros((BLOCK, LANES), WIDE)
    grad_scr[:, :width] = dot_right(ga_ref[:, :width], w_ref[:, proj_at : proj_at + width]).astype(LOW).astype(WIDE)
    mix_scr[:, :width] = mix_ref[...].astype(WIDE)
    lane = lax.broadcasted_iota(jnp.int32, (BLOCK, LANES), 1)
    ones = jnp.full((LANES, LANES), 1.0, LOW)
    for h in range(heads):
        at = hd * h
        grad = jnp.where(lane < hd, grad_scr[:, at : at + LANES], 0.0)
        product = grad * mix_scr[:, at : at + LANES]
        high = product.astype(LOW)
        rest = (product - high.astype(WIDE)).astype(LOW)
        delta = -(dot(high, ones) + dot(rest, ones))
        first = delta.astype(LOW)
        second = (delta - first.astype(WIDE)).astype(LOW)
        out_ref[h] = jnp.where(
            lane == hd, first, jnp.where(lane == hd + 1, second, grad.astype(LOW))
        )


def spread(ga, w, mix, heads, hd, proj_at):
    n = ga.shape[0]
    width = heads * hd
    row = pl.BlockSpec((BLOCK, width), lambda i: (i, 0))
    wide_row = pl.BlockSpec((BLOCK, ga.shape[1]), lambda i: (i, 0))
    return pl.pallas_call(
        partial(spread_kernel, heads, hd, proj_at),
        grid=(n // BLOCK,),
        in_specs=[wide_row, whole_block(w), row],
        out_specs=pl.BlockSpec((heads, BLOCK, LANES), lambda i: (0, i, 0)),
        out_shape=jax.ShapeDtypeStruct((heads, n, LANES), LOW),
        scratch_shapes=[
            pltpu.VMEM((BLOCK, width + LANES), WIDE),
            pltpu.VMEM((BLOCK, width + LANES), WIDE),
        ],
        compiler_params=pltpu.CompilerParams(vmem_limit_bytes=56 * MIB),
        cost_estimate=pl.CostEstimate(
            flops=2 * n * width * width, bytes_accessed=12 * MIB, transcendentals=0
        ),
        name="spread",
    )(ga, w, mix)


def back_kernel(
    hd, c, score_scale, core_ref, q_ref, k_ref, v_ref, do_ref, rq_ref, rk_ref, rot_ref, gq_ref, gk_ref,
    joint_ref, gain_ref, dq_scr, dk_scr, dv_scr, gain_scr,
):
    i = pl.program_id(0)
    n = pl.num_programs(0)
    heads = q_ref.shape[0]
    width = GROUP * hd
    tail = joint_ref.shape[2] - 3 * width
    core = core_ref[0]
    slots = (1 - core, core)

    @pl.when(i == 0)
    def _():
        dq_scr[...] = jnp.zeros(dq_scr.shape, WIDE)
        gain_scr[...] = jnp.zeros(gain_scr.shape, WIDE)

    ones = jnp.full((LANES, LANES), 1.0, LOW)

    def run(blocks):
        def body(h, carry):
            kk = k_ref[h]
            vv = v_ref[h]
            dk = dv = None
            for j in blocks:
                at = pl.ds(pl.multiple_of((i + j) * BLOCK, BLOCK), BLOCK)
                q = q_ref[h, at]
                do = do_ref[h, at]
                p = jnp.exp2(dot_right(kk, q) * c)
                term = dot(p.astype(LOW), do)
                dv = term if dv is None else dv + term
                ds = (p * dot_right(vv, do)).astype(LOW)
                term = dot(ds, q)
                dk = term if dk is None else dk + term
                dq_scr[h, at] += dot_left(ds, kk)
            dk_scr[h] = dk
            dv_scr[h] = dv
            return carry

        lax.fori_loop(0, heads, body, 0, unroll=2)

    near_blocks(run)

    def finish(dy, raw, rot, gain, row):
        raw = raw.astype(WIDE)
        dy = dy * score_scale
        up = pltpu.roll(dy, LANES - hd // 4, 1)
        down = pltpu.roll(dy, hd // 4, 1)
        d = dy * rot[0] - up * rot[1] - down * rot[2]
        r = lax.rsqrt(dot((raw * raw).astype(LOW), ones) * (1.0 / hd) + EPSILON)
        u = raw * r
        ud = u * d
        gain_scr[row] += jnp.sum(ud.reshape(BLOCK // 8, 8, LANES), axis=0)
        m = dot((ud * gain).astype(LOW), ones) * (1.0 / hd)
        return (r * (gain * d - u * m)).astype(LOW)

    here = pl.ds(pl.multiple_of(i * BLOCK, BLOCK), BLOCK)
    rot = [rot_ref[t, here] for t in range(3)]
    for slot in range(2):
        joint_ref[slot, here, 3 * width :] = jnp.zeros((BLOCK, tail), LOW)
    for h in range(heads):
        slot, at = slots[h // GROUP], hd * (h % GROUP)
        grad = finish(dk_scr[h], rk_ref[h], rot, gk_ref[...], 1)
        joint_ref[slot, here, width + at : width + at + hd] = grad[:, :hd]
        value = dv_scr[h].astype(LOW)
        joint_ref[slot, here, 2 * width + at : 2 * width + at + hd] = value[:, :hd]

    @pl.when(i == n - 1)
    def _():
        def rows(b, carry):
            at = pl.ds(pl.multiple_of(b * BLOCK, BLOCK), BLOCK)
            turn = [rot_ref[t, at] for t in range(3)]
            for h in range(heads):
                start = hd * (h % GROUP)
                grad = finish(dq_scr[h, at], rq_ref[h, at], turn, gq_ref[...], 0)
                joint_ref[slots[h // GROUP], at, start : start + hd] = grad[:, :hd]
            return carry

        lax.fori_loop(0, n, rows, 0)
        gain_ref[...] = gain_scr[...]


def attend_back(part, core, q2, k, v, do, rq, rk, rot, gq, gk, hd, c, score_scale):
    _, n, _ = q2.shape
    one = pl.Buffered(1)
    full = pl.BlockSpec((2 * GROUP, n, LANES), lambda i: (0, 0, 0), pipeline_mode=one)
    block = pl.BlockSpec((2 * GROUP, BLOCK, LANES), lambda i: (0, i, 0))
    small = pl.BlockSpec((1, LANES), lambda i: (0, 0))
    width = part_width(hd)
    return pl.pallas_call(
        partial(back_kernel, hd, c, score_scale),
        grid=(n // BLOCK,),
        in_specs=[
            pl.BlockSpec(memory_space=pltpu.SMEM),
            *(full, block, block),
            pl.BlockSpec((2 * GROUP, n, LANES), lambda i: (part, 0, 0), pipeline_mode=one),
            *(full, block, whole_block(rot), small, small),
        ],
        out_specs=[
            pl.BlockSpec((2, n, width), lambda i: (0, 0, 0), pipeline_mode=one),
            pl.BlockSpec((2, 8, LANES), lambda i: (0, 0, 0)),
        ],
        out_shape=[
            jax.ShapeDtypeStruct((2, n, width), LOW),
            jax.ShapeDtypeStruct((2, 8, LANES), WIDE),
        ],
        scratch_shapes=[
            pltpu.VMEM((2 * GROUP, n, LANES), WIDE),
            pltpu.VMEM((2 * GROUP, BLOCK, LANES), WIDE),
            pltpu.VMEM((2 * GROUP, BLOCK, LANES), WIDE),
            pltpu.VMEM((2, 8, LANES), WIDE),
        ],
        compiler_params=pltpu.CompilerParams(vmem_limit_bytes=56 * MIB),
        cost_estimate=pl.CostEstimate(
            flops=10 * n * 640 * LANES * 2 * GROUP,
            bytes_accessed=20 * MIB,
            transcendentals=2 * GROUP * n * 640,
        ),
        name="attend_back",
    )(core, q2, k, v, do, rq, rk, rot, gq, gk)


def normed_rows(values):
    centred = values - jnp.mean(values, axis=-1, keepdims=True)
    scale = lax.rsqrt(jnp.mean(centred * centred, axis=-1, keepdims=True) + EPSILON)
    return centred * scale, scale


def norm_back(normed, scale, grad):
    inner = jnp.mean(grad * normed, axis=-1, keepdims=True)
    return scale * (grad - jnp.mean(grad, axis=-1, keepdims=True) - normed * inner)


def add_sums(out_ref, at, hot, values):
    width = values.shape[1]
    term = dot_left(hot, values.astype(LOW))
    here = (slice(None), slice(at * width, (at + 1) * width))

    @pl.when(pl.program_id(0) == 0)
    def _():
        out_ref[here] = term

    @pl.when(pl.program_id(0) > 0)
    def _():
        out_ref[here] += term


def rows_of(array):
    if array.ndim == 3:
        return pl.BlockSpec((2, BLOCK, array.shape[2]), lambda i: (0, i, 0))
    return pl.BlockSpec((BLOCK, array.shape[1]), lambda i: (i, 0))


def call_rows(kernel, name, streamed, fixed, outs, sums=(), core=None, scratch=()):
    n = streamed[0].shape[-2]
    work = sum(2 * n * a.size for a in fixed if a.shape[0] > 256)
    moved = sum(a.size * a.dtype.itemsize for a in (*streamed, *fixed))
    scalars = () if core is None else (core,)
    return pl.pallas_call(
        kernel,
        grid=(n // BLOCK,),
        in_specs=[pl.BlockSpec(memory_space=pltpu.SMEM) for _ in scalars]
        + [rows_of(a) for a in streamed]
        + [whole_block(a) for a in fixed],
        out_specs=[pl.BlockSpec((BLOCK, w), lambda i: (i, 0)) for w, _ in outs]
        + [pl.BlockSpec(shape, lambda i: (0, 0)) for shape in sums],
        out_shape=[jax.ShapeDtypeStruct((n, w), t) for w, t in outs]
        + [jax.ShapeDtypeStruct(shape, WIDE) for shape in sums],
        scratch_shapes=[pltpu.VMEM(shape, WIDE) for shape in scratch],
        compiler_params=pltpu.CompilerParams(vmem_limit_bytes=56 * MIB),
        cost_estimate=pl.CostEstimate(flops=work, bytes_accessed=moved, transcendentals=0),
        name=name,
    )(*scalars, *streamed, *fixed)


def join_kernel(
    proj_at, mix_ref, x_ref, hot_ref, keep_ref, w_ref, mod_ref, att_ref, mid_ref, norm_ref
):
    width = x_ref.shape[1]
    hot = hot_ref[...]
    attended = dot(mix_ref[...], w_ref[:, proj_at : proj_at + width])
    att_ref[...] = attended.astype(LOW)
    gate = dot(hot, mod_ref[:, :width]) * keep_ref[...]
    middle = x_ref[...].astype(WIDE) + gate * attended
    mid_ref[...] = middle
    normed, _ = normed_rows(middle)
    scale = dot(hot, mod_ref[:, 2 * width : 3 * width])
    shift = dot(hot, mod_ref[:, width : 2 * width])
    norm_ref[...] = (normed * (1.0 + scale) + shift).astype(LOW)


def gate_kernel(x_ref, w_ref, out_ref):
    out_ref[...] = dot(x_ref[...], w_ref[...]).astype(LOW)


def up_kernel(x_ref, gate_ref, w_ref, up_ref, inner_ref):
    up = dot(x_ref[...], w_ref[...])
    up_ref[...] = up.astype(LOW)
    gate = gate_ref[...].astype(WIDE)
    inner_ref[...] = (gate * jax.nn.sigmoid(gate) * up).astype(LOW)


def down_kernel(
    inner_ref, mid_ref, grad_ref, hot_ref, keep_ref, w_ref, mod_ref, out_ref, back_ref, sum_ref
):
    width = mid_ref.shape[1]
    hot = hot_ref[...]
    returned = dot(inner_ref[...], w_ref[:, :width])
    gate = dot(hot, mod_ref[...]) * keep_ref[...]
    out_ref[...] = (mid_ref[...] + gate * returned).astype(LOW)
    upstream = grad_ref[...].astype(WIDE)
    back_ref[:, :width] = (upstream * gate).astype(LOW)
    if back_ref.shape[1] > width:
        back_ref[:, width:] = jnp.zeros((BLOCK, back_ref.shape[1] - width), LOW)
    add_sums(sum_ref, 0, hot, upstream * keep_ref[...] * returned)


def inner_back_kernel(core_ref, grad_ref, gate_ref, up_ref, w_ref, send_ref, keep_ref):
    grad = dot_right(grad_ref[...], w_ref[...])
    gate = gate_ref[...].astype(WIDE)
    sig = jax.nn.sigmoid(gate)
    act = gate * sig
    for_gate = (grad * up_ref[...].astype(WIDE) * (sig + act * (1.0 - sig))).astype(LOW)
    for_up = (grad * act).astype(LOW)

    @pl.when(core_ref[0] == 0)
    def _():
        send_ref[...] = for_up
        keep_ref[...] = for_gate

    @pl.when(core_ref[0] != 0)
    def _():
        send_ref[...] = for_gate
        keep_ref[...] = for_up


def middle_back_kernel(
    core_ref, send_ref, mine_ref, mid_ref, grad_ref, att_ref, hot_ref, keep_ref, wg_ref, wu_ref,
    mod_ref, out_ref, back_ref, sum_ref, total_ref,
):
    width = mid_ref.shape[1]
    hot = hot_ref[...]
    keep = keep_ref[...]

    @pl.when(core_ref[0] == 0)
    def _():
        total_ref[...] = dot_right(mine_ref[...], wg_ref[...])
        total_ref[...] += dot_right(send_ref[...], wu_ref[...])

    @pl.when(core_ref[0] != 0)
    def _():
        total_ref[...] = dot_right(send_ref[...], wg_ref[...])
        total_ref[...] += dot_right(mine_ref[...], wu_ref[...])

    grad = total_ref[...]
    normed, scale = normed_rows(mid_ref[...])
    turned = grad * (1.0 + dot(hot, mod_ref[:, 2 * width : 3 * width]))
    total = grad_ref[...].astype(WIDE) + norm_back(normed, scale, turned)
    out_ref[...] = total
    gate = dot(hot, mod_ref[:, :width]) * keep
    back_ref[:, :width] = (total * gate).astype(LOW)
    if back_ref.shape[1] > width:
        back_ref[:, width:] = jnp.zeros((BLOCK, back_ref.shape[1] - width), LOW)
    add_sums(sum_ref, 0, hot, total * keep * att_ref[...].astype(WIDE))
    add_sums(sum_ref, 1, hot, grad)
    add_sums(sum_ref, 2, hot, grad * normed)


def input_back_kernel(
    core_ref, one_ref, two_ref, mid_ref, x_ref, hot_ref, wo_ref, wt_ref, mod_ref, out_ref, sum_ref
):
    width = x_ref.shape[1]
    hot = hot_ref[...]
    step = one_ref.shape[2]
    core = core_ref[0]
    grad = None
    for ref, w_ref in ((one_ref, wo_ref), (two_ref, wt_ref)):
        term = dot_right(ref[1 - core], w_ref[:, :step]) + dot_right(ref[core], w_ref[:, step : 2 * step])
        grad = term if grad is None else grad + term
    normed, scale = normed_rows(x_ref[...].astype(WIDE))
    turned = grad * (1.0 + dot(hot, mod_ref[:, width : 2 * width]))
    out_ref[...] = mid_ref[...] + norm_back(normed, scale, turned)
    add_sums(sum_ref, 0, hot, grad)
    add_sums(sum_ref, 1, hot, grad * normed)


def finish_kernel(hd, core_ref, head_done, head_twin, tail_done, tail_twin, qkv_ref, proj_ref):
    step = part_width(hd)
    short = GROUP * hd
    total = qkv_ref.shape[1] // 3

    def write(sources):
        for part, source in enumerate(sources):
            values = source[:, :step].astype(WIDE)
            for kind in range(3):
                at = kind * total + part * short
                qkv_ref[:, at : at + short] = values[:, kind * short : (kind + 1) * short]
        half = sources[0].shape[1] - step
        proj_ref[:, :half] = sources[0][:, step:].astype(WIDE)
        rest = proj_ref.shape[1] - half
        proj_ref[:, half:] = sources[1][:, step : step + rest].astype(WIDE)

    @pl.when(core_ref[0] == 0)
    def _():
        write((head_done, head_twin, tail_done, tail_twin))

    @pl.when(core_ref[0] != 0)
    def _():
        write((head_twin, head_done, tail_twin, tail_done))


def finish(core, head, tail, hd, width):
    rows = head["done"].shape[0]
    return pl.pallas_call(
        partial(finish_kernel, hd),
        in_specs=[pl.BlockSpec(memory_space=pltpu.SMEM)]
        + [pl.BlockSpec(memory_space=pltpu.VMEM)] * 4,
        out_specs=[pl.BlockSpec(memory_space=pltpu.VMEM)] * 2,
        out_shape=[
            jax.ShapeDtypeStruct((rows, 3 * width), WIDE),
            jax.ShapeDtypeStruct((rows, width), WIDE),
        ],
        compiler_params=pltpu.CompilerParams(vmem_limit_bytes=40 * MIB),
        name="finish",
    )(core, head["done"], head["twin"], tail["done"], tail["twin"])


def turn_tables(row_place, column_place, hd):
    quarter = hd // 4
    inverse = 10000.0 ** (-jnp.arange(quarter, dtype=WIDE) / quarter)
    row_angle = row_place.astype(WIDE)[:, None] * inverse[None, :]
    column_angle = column_place.astype(WIDE)[:, None] * inverse[None, :]
    rest = jnp.zeros((row_place.shape[0], LANES - hd), WIDE)
    none = jnp.zeros_like(row_angle)
    rc, rs = jnp.cos(row_angle), jnp.sin(row_angle)
    cc, cs = jnp.cos(column_angle), jnp.sin(column_angle)
    return jnp.stack(
        [
            jnp.concatenate([rc, rc, cc, cc, rest], 1),
            jnp.concatenate([-rs, none, -cs, none, rest], 1),
            jnp.concatenate([none, rs, none, cs, rest], 1),
        ],
        0,
    )


def high_and_rest(values):
    high = values.astype(LOW)
    return jnp.concatenate([high, (values - high.astype(WIDE)).astype(LOW)], axis=0)


def pad_columns(array, width):
    return jnp.pad(array, ((0, 0), (0, width - array.shape[1])))


def to_parts(array, heads, hd):
    rows = array.shape[0]
    shaped = array.reshape(rows, 3, heads // GROUP, GROUP * hd).swapaxes(1, 2)
    shaped = shaped.reshape(rows, heads // GROUP, 3 * GROUP * hd)
    padded = jnp.pad(shaped, ((0, 0), (0, 0), (0, part_width(hd) - 3 * GROUP * hd)))
    return padded.reshape(rows, -1)


def from_parts(array, heads, hd):
    rows = array.shape[0]
    shaped = array.reshape(rows, heads // GROUP, -1)[:, :, : 3 * GROUP * hd]
    shaped = shaped.reshape(rows, heads // GROUP, 3, GROUP * hd).swapaxes(1, 2)
    return shaped.reshape(rows, -1)


def local(
    block_in,
    condition,
    item_lengths,
    item_widths,
    ada_weight,
    ada_bias,
    qkv_weight,
    query_gain,
    key_gain,
    proj_weight,
    gate_up_weight,
    down_weight,
    out_grad,
):
    _, n, width = block_in.shape
    items = item_lengths.shape[1]
    hd = query_gain.shape[0]
    heads = width // hd
    ff = down_weight.shape[0] * lax.axis_size("fsdp")
    score_scale = float(hd) ** (-0.5)
    c = score_scale * 1.4426950408889634
    shards = lax.axis_size("fsdp")
    fsdp_place = lax.axis_index("fsdp")
    odd = width + LANES if (width // LANES) % 2 else width

    qkv_parts = to_parts(qkv_weight, heads, hd)
    cut = qkv_parts.shape[1] // 2
    g_one = Gather(qkv_parts[:, :cut])
    g_two = Gather(jnp.concatenate([qkv_parts[:, cut:], pad_columns(proj_weight, odd)], axis=1))
    g_gate = Gather(gate_up_weight[:, :ff])
    g_up = Gather(gate_up_weight[:, ff:])
    g_down = Gather(pad_columns(down_weight, odd))
    gathers = [g_one, g_two, g_gate, g_up, g_down]
    core_place = (lax.axis_index("rep") % 2).astype(jnp.int32).reshape(1)

    cond_float = condition.astype(WIDE).reshape(items, width)
    cond_silu, silu_pull = jax.vjp(jax.nn.silu, cond_float)
    cond_act = cond_silu.astype(LOW)

    g_one.z()
    group_act = exchange(cond_act)
    member, segment, row_place, column_place = layout(item_lengths[0], item_widths[0], n)
    member_low = member.astype(LOW)
    keep = (segment < items - 1).astype(WIDE).reshape(n, 1)
    rot = turn_tables(row_place, column_place, hd)
    spare = jnp.zeros((n, LANES - hd - items), LOW)
    ones_at = jnp.zeros((n, LANES - hd - items), LOW).at[:, :3].set(-1.0)
    blank = jnp.zeros((n, hd), LOW)
    query_tail = jnp.concatenate([blank, member_low, spare], 1)
    key_tail = jnp.concatenate([blank, (member_low - 1.0) * MASK, ones_at], 1)
    value_tail = jnp.zeros((1, LANES), LOW).at[:, hd : hd + 2].set(1.0)
    gain_q = pad_columns(query_gain.astype(WIDE)[None, :], LANES)
    gain_k = pad_columns(key_gain.astype(WIDE)[None, :], LANES)
    hot = jnp.concatenate([member_low, member_low], axis=1)
    tables = (rot, query_tail, key_tail, hot, keep)
    group_act = hold(gathers, group_act)

    g_one.y()
    g_two.z()
    bias_row = lax.dynamic_update_slice(
        jnp.zeros((6 * width,), WIDE), ada_bias.astype(WIDE), (fsdp_place * ada_bias.shape[0],)
    )
    mod_part = (dot(group_act, ada_weight) + bias_row[None, :]).astype(LOW)
    mod_part, group_act, tables = hold(gathers, (mod_part, group_act, tables))

    early = 2 * width
    modulation = high_and_rest(sum_back(mod_part, items))
    g_one.x()
    g_one.core("own", "far")
    g_two.y()
    inputs_low = block_in[0]
    modulation, tables, inputs_low = hold(gathers, (modulation, tables, inputs_low))
    mod_a, mod_b = modulation[:, :early], modulation[:, early:]

    g_one.core("both")
    g_two.x()
    g_two.core("own", "far")
    g_gate.z()
    rot, query_tail, key_tail, hot, keep = tables
    set_out = (gain_q, gain_k, rot, query_tail, key_tail, value_tail, heads // 2, hd)
    one_full = g_one.whole()
    normed_a, q_one, k_one, v_one, rq_one, rk_one = prepare(
        True, inputs_low, hot, mod_a, one_full, *set_out
    )
    gathers = gathers[1:]
    normed_a, q_one, k_one, v_one, rq_one, rk_one, one_full = hold(
        gathers, (normed_a, q_one, k_one, v_one, rq_one, rk_one, one_full)
    )

    g_two.core("both")
    g_gate.y()
    g_up.z()
    two_full = g_two.whole()
    q_two, k_two, v_two, rq_two, rk_two = prepare(
        False, normed_a, hot, mod_a, two_full, *set_out
    )
    gathers = gathers[1:]
    normed_a, q_two, k_two, v_two, rq_two, rk_two, two_full, q_one, k_one, v_one = hold(
        gathers, (normed_a, q_two, k_two, v_two, rq_two, rk_two, two_full, q_one, k_one, v_one)
    )

    g_gate.x()
    g_gate.core("own", "far")
    g_up.y()
    g_down.z()
    mixed, q2_one, q2_two = attend((q_one, k_one, v_one), (q_two, k_two, v_two), hd, c)
    mixed, q2_one, q2_two = hold(gathers, (mixed, q2_one, q2_two))

    g_gate.core("both")
    g_up.x()
    g_up.core("own", "far")
    g_down.y()
    mod_mid = mod_b[:, : 3 * width]
    attended, middle, normed_b = call_rows(
        partial(join_kernel, cut), "join", (mixed, inputs_low, hot, keep), (two_full, mod_mid),
        ((width, LOW), (width, WIDE), (width, LOW)),
    )
    middle, normed_b, attended = hold(gathers, (middle, normed_b, attended))

    g_up.core("both")
    g_down.x()
    g_down.core("own", "far")
    gate_full = g_gate.whole()
    (gate,) = call_rows(gate_kernel, "gate", (normed_b,), (gate_full,), ((ff, LOW),))
    gathers = gathers[1:]
    gate, gate_full, normed_b = hold(gathers, (gate, gate_full, normed_b))

    g_down.core("both")
    up_full = g_up.whole()
    up, inner = call_rows(
        up_kernel, "up", (normed_b, gate), (up_full,), ((ff, LOW), (ff, LOW))
    )
    gathers = gathers[1:]
    inner, up, gate, up_full, middle = hold(gathers, (inner, up, gate, up_full, middle))

    down_full = g_down.whole()
    block_out, grad_returned, sums_gate_b = call_rows(
        down_kernel, "down", (inner, middle, out_grad[0], hot, keep),
        (down_full, mod_b[:, 3 * width :]), ((width, LOW), (odd, LOW)), ((2 * items, width),),
    )

    s_down = Scatter(inner, *column_halves(grad_returned))
    s_down.first()
    plans = [s_down]
    grad_returned, down_full, gate, up, gate_full, up_full, normed_b, middle, attended = hold(
        plans,
        (grad_returned, down_full, gate, up, gate_full, up_full, normed_b, middle, attended),
    )

    s_down.core()
    grad_send, grad_keep = call_rows(
        inner_back_kernel, "inner_back", (grad_returned, gate, up), (down_full,),
        ((ff, LOW), (ff, LOW)), core=core_place,
    )
    grad_send, grad_keep = hold(plans, (grad_send, grad_keep))

    s_down.second()
    s_wide = Scatter(normed_b, grad_send, grad_keep)
    s_wide.first()
    plans = [s_down, s_wide]
    grad_send, grad_keep = hold(plans, (grad_send, grad_keep))

    s_down.x()
    s_wide.core()
    grad_middle, grad_attended, sums_mid = call_rows(
        middle_back_kernel, "middle_back",
        (grad_send, grad_keep, middle, out_grad[0], attended, hot, keep),
        (gate_full, up_full, mod_mid), ((width, WIDE), (odd, LOW)), ((2 * items, 3 * width),),
        core=core_place, scratch=((BLOCK, width),),
    )
    s_proj = Scatter(mixed, *column_halves(grad_attended))
    plans = [s_down, s_wide, s_proj]
    grad_middle, grad_attended, sums_mid = hold(plans, (grad_middle, grad_attended, sums_mid))

    s_down.y()
    s_wide.second()
    s_proj.first()
    late_sums = jnp.concatenate([sums_mid[:items], sums_gate_b[:items]], axis=1).astype(LOW)
    grad_mixed = spread(grad_attended, two_full, mixed, heads, hd, cut)
    late_sums, grad_mixed = hold(plans, (late_sums, grad_mixed))

    back = partial(
        attend_back, core=core_place, rot=rot, gq=gain_q, gk=gain_k, hd=hd, c=c,
        score_scale=score_scale,
    )
    s_down.z()
    s_wide.x()
    s_proj.core()
    joint_one, gains_0 = back(
        0, q2=q2_one, k=k_one, v=v_one, do=grad_mixed, rq=rq_one, rk=rk_one
    )
    s_head = Scatter(normed_a, joint_one[0], joint_one[1])
    s_head.first()
    s_proj.second()
    plans = plans + [s_head]
    joint_one, gains_0, grad_mixed, late_sums = hold(
        plans, (joint_one, gains_0, grad_mixed, late_sums)
    )

    s_head.core()
    s_wide.y()
    late_sums = hold([s_head], late_sums)
    s_down.last_x()
    s_head.second()
    s_head.join(s_proj)
    grad_mixed = hold([s_head], grad_mixed)
    s_head.x()
    late_group = gather_rows(late_sums)
    joint_two, gains_1 = back(
        1, q2=q2_two, k=k_two, v=v_two, do=grad_mixed, rq=rq_two, rk=rk_two
    )
    s_tail = Scatter(normed_a, joint_two[0], joint_two[1])
    s_tail.first()
    plans = [s_down, s_wide, s_head, s_tail]
    joint_one, joint_two, gains_1, late_group = hold(
        plans, (joint_one, joint_two, gains_1, late_group)
    )

    s_tail.core()
    s_down.last_core()
    s_wide.z()
    s_head.y()
    s_tail.second()
    joint_two = hold([s_tail], joint_two)
    s_tail.x()
    grad_input, sums_early = call_rows(
        input_back_kernel, "input_back",
        (joint_one, joint_two, grad_middle, inputs_low, hot),
        (one_full, two_full, mod_a), ((width, WIDE),), ((2 * items, 2 * width),),
        core=core_place,
    )
    plans = [s_down, s_wide, s_head, s_tail]
    grad_input, sums_early, late_group = hold(plans, (grad_input, sums_early, late_group))

    s_wide.last_x()
    s_head.z(apart=True)
    s_tail.y()
    early_sums = sums_early[:items]
    gain_row = jnp.sum(gains_0 + gains_1, axis=1)[:, :hd].reshape(1, 2 * hd)
    gain_high = gain_row.astype(LOW).astype(WIDE)
    gain_block = jnp.concatenate([gain_high, gain_row - gain_high], axis=0)
    gain_block = jnp.pad(gain_block, ((0, items - 2), (0, 2 * LANES - 2 * hd)))
    early_sums = jnp.concatenate([early_sums, gain_block], axis=1).astype(LOW)
    early_group = gather_rows(early_sums)
    act_far = across_x(group_act)
    late_far = across_x(late_group)
    shard_down = jnp.concatenate(s_down.halves(), axis=1)[:, :width]
    plans = [s_wide, s_head, s_tail]
    early_group, late_far, act_far, shard_down = hold(
        plans, (early_group, late_far, act_far, shard_down)
    )

    s_wide.last_core()
    s_head.last_x()
    s_tail.z(apart=True)
    early_far = across_x(early_group)
    every_act = across_replicas(group_act, act_far)
    late_every = across_replicas(late_group, late_far)
    shard_late = dot_left(every_act, late_every)
    cond_part = dot_right(early_group[:, :early], ada_weight[:, :early]) + dot_right(
        late_group, ada_weight[:, early:]
    )
    early_far, cond_part, shard_late, every_act, late_every = hold(
        plans, (early_far, cond_part, shard_late, every_act, late_every)
    )

    s_head.last_core()
    s_tail.last_x()
    cond_back = lax.all_to_all(cond_part.astype(LOW).reshape(shards, items, -1), "fsdp", 0, 0)
    early_every = across_replicas(early_group, early_far)
    shard_early = dot_left(every_act, early_every[:, :early])
    shard_wide = jnp.concatenate(s_wide.halves(), axis=1)
    shard_early, shard_wide = hold(plans, (shard_early, shard_wide))
    shard_ada = jnp.concatenate([shard_early, shard_late], axis=1)
    bias_sums = jnp.concatenate(
        [
            jnp.sum(early_every[:, :early].astype(WIDE), axis=0),
            jnp.sum(late_every.astype(WIDE), axis=0),
        ],
        axis=0,
    )
    shard_bias = lax.dynamic_slice(
        bias_sums, (fsdp_place * ada_bias.shape[0],), (ada_bias.shape[0],)
    )
    gain_sums = jnp.sum(early_every[:, early:].astype(WIDE), axis=0)[: 2 * hd]
    cond_back = hold(plans, cond_back)
    s_tail.last_core()
    grad_cond_act = cond_back.swapaxes(0, 1).reshape(items, width).astype(WIDE)
    grad_condition = silu_pull(grad_cond_act)[0]
    if s_head.fast:
        shard_qkv, shard_proj = finish(core_place, s_head.live, s_tail.live, hd, width)
    else:
        shard_qkv = jnp.concatenate(s_head.halves() + s_tail.halves(), axis=1)
        shard_qkv = from_parts(shard_qkv, heads, hd)
        shard_proj = jnp.concatenate(s_proj.halves(), axis=1)[:, :width]
    shard_gate_up = shard_wide
    return (
        block_out[None],
        grad_input[None],
        grad_condition[None],
        shard_ada,
        shard_bias,
        shard_qkv,
        gain_sums[:hd],
        gain_sums[hd:],
        shard_proj,
        shard_gate_up,
        shard_down,
    )


def solution(mesh):
    return jax.shard_map(
        local,
        mesh=mesh,
        in_specs=(
            P(("rep", "fsdp"), None, None),
            P(("rep", "fsdp"), None, None),
            P(("rep", "fsdp"), None),
            P(("rep", "fsdp"), None),
            P("fsdp", None),
            P("fsdp"),
            P("fsdp", None),
            P(),
            P(),
            P("fsdp", None),
            P("fsdp", None),
            P("fsdp", None),
            P(("rep", "fsdp"), None, None),
        ),
        out_specs=(
            P(("rep", "fsdp"), None, None),
            P(("rep", "fsdp"), None, None),
            P(("rep", "fsdp"), None, None),
            P("fsdp", None),
            P("fsdp"),
            P("fsdp", None),
            P(),
            P(),
            P("fsdp", None),
            P("fsdp", None),
            P("fsdp", None),
        ),
        check_vma=False,
    )
```

```python
import functools
from functools import partial

import jax
import jax.numpy as jnp
from jax import lax
from jax.experimental import pallas as pl
from jax.experimental.pallas import tpu as pltpu
from jax.sharding import PartitionSpec as P

EPSILON = 1e-06
WIDE = jnp.float32
LOW = jnp.bfloat16
AXES = ("rep", "fsdp")
HIGH_Z = 4
PARTS = 3
BLOCK = 256
LANES = 128
GROUP = 4
MASK = 4096.0
MIB = 2**20


def dot(left, right):
    return jnp.dot(left, right, preferred_element_type=WIDE)


def dot_left(left, right):
    return lax.dot_general(left, right, (((0,), (0,)), ((), ())), preferred_element_type=WIDE)


def dot_right(left, right):
    return lax.dot_general(left, right, (((1,), (1,)), ((), ())), preferred_element_type=WIDE)


def layer_norm(values):
    centred = values - jnp.mean(values, axis=-1, keepdims=True)
    return centred * lax.rsqrt(jnp.mean(centred * centred, axis=-1, keepdims=True) + EPSILON)


def modulated(values, shift_part, scale_part):
    return layer_norm(values) * (1.0 + scale_part) + shift_part


def layout(lengths_row, widths_row, length):
    seg_count = lengths_row.shape[0]
    item_ends = jnp.cumsum(lengths_row)
    item_starts = item_ends - lengths_row
    token_place = jnp.arange(length, dtype=jnp.int32)[:, None]
    member = ((token_place >= item_starts[None, :]) & (token_place < item_ends[None, :])).astype(
        jnp.int32
    )
    segment = jnp.sum(member * jnp.arange(seg_count, dtype=jnp.int32)[None, :], axis=1)
    offset = token_place[:, 0] - jnp.sum(member * item_starts[None, :], axis=1)
    across = jnp.sum(member * widths_row[None, :], axis=1)
    return (member, segment, offset // across, offset % across)


def device_index(x, core, z, y):
    return (x * 2 + core) * 8 + z * 2 + y


PLACES = [(x, c, z, y) for x in range(2) for c in range(2) for z in range(4) for y in range(2)]
TO_CORE = [(device_index(x, c, z, y), device_index(x, 1 - c, z, y)) for x, c, z, y in PLACES]
TO_X = [(device_index(x, c, z, y), device_index(1 - x, c, z, y)) for x, c, z, y in PLACES]
TO_Y = [(device_index(x, c, z, y), device_index(x, c, z, 1 - y)) for x, c, z, y in PLACES]
TO_Z = [
    [(device_index(x, c, z, y), device_index(x, c, (z + k) % 4, y)) for x, c, z, y in PLACES]
    for k in range(4)
]
Z_GROUPS = [[0, 2, 4, 6], [1, 3, 5, 7]]


def coordinates():
    replica = lax.axis_index("rep")
    shard = lax.axis_index("fsdp")
    return replica // 2, replica % 2, shard // 2, shard % 2


def is_fast():
    return lax.axis_size("rep") == 4 and lax.axis_size("fsdp") == 8


def pick(operand, index, axis):
    return lax.dynamic_index_in_dim(operand, index, axis, keepdims=False)


def over_z(operand):
    return lax.all_to_all(operand, "fsdp", 0, 0, axis_index_groups=Z_GROUPS)


def hold(plans, values):
    flat, tree = jax.tree.flatten(([plan.live for plan in plans], values))
    flat = lax.optimization_barrier(flat)
    lives, values = jax.tree.unflatten(tree, flat)
    for plan, live in zip(plans, lives):
        plan.live = live
    return values


def place_pieces(shape, apart, where, pieces, out, sems):
    x, core, z, y = where[0], where[1], where[2], where[3]
    a0, a1, ax, b0, b1, bx = pieces
    rows, half = shape[0] // 8, shape[1] // 2
    h = rows // PARTS
    copies = []
    for p0, p1, px, c in ((a0, a1, ax, core), (b0, b1, bx, 1 - core)):
        for q in range(HIGH_Z):
            for source, yy, third in (
                (p0.at[q, 0], y, x),
                (p0.at[q, 1], y, 2),
                (p1.at[q, 0], 1 - y, x),
                (p1.at[q, 1], 1 - y, 2),
                (px.at[q, 0], y, 1 - x),
                (px.at[q, 1], 1 - y, 1 - x),
            ):
                zz = (z + HIGH_Z - q) % HIGH_Z if apart else q
                row = pl.multiple_of((2 * zz + yy) * rows + third * h, 16)
                column = pl.multiple_of(c * half, LANES)
                target = out.at[pl.ds(row, h), pl.ds(column, half)]
                copy = pltpu.make_async_copy(source, target, sems.at[len(copies)])
                copy.start()
                copies.append(copy)
    for copy in copies:
        copy.wait()


def placing(kernel, shape, apart, before, after):
    def run(where, *refs):
        pieces, refs = refs[:6], refs[6:]
        inputs, rest = refs[: before + after], refs[before + after :]
        *rest, laid, sems, out_sem = rest
        outs, full, scratch = rest[0], rest[1], rest[2:]
        step = pl.program_id(0)

        @pl.when(step == 0)
        def _():
            place_pieces(shape, apart, where, pieces, laid, sems)
            pltpu.make_async_copy(laid, full, out_sem).start()

        kernel(*inputs[:before], laid, *inputs[before:], *outs, *scratch)

        @pl.when(step == pl.num_programs(0) - 1)
        def _():
            pltpu.make_async_copy(laid, full, out_sem).wait()

    return run


def call_placed(kernel, gather, args, specs, before, out_shape, out_specs, scratch, **options):
    if not gather.fast:
        weight = gather.whole()
        args = (*args[:before], weight, *args[before:])
        specs = [*specs[:before], whole_block(weight), *specs[before:]]
        got = pl.pallas_call(
            kernel, in_specs=specs, out_shape=out_shape, out_specs=out_specs,
            scratch_shapes=scratch, **options,
        )(*args)
        return (*got, weight)
    shape = (8 * gather.rows, gather.width)
    count = len(out_shape)
    inner = placing(kernel, shape, gather.apart, before, len(args) - before)

    def run(*refs):
        at = 7 + len(args)
        inner(*refs[:at], refs[at : at + count], *refs[at + count :])

    any_space = pl.BlockSpec(memory_space=pl.ANY)
    live = gather.live
    pieces = [live[k] for k in ("own", "far", "both", "twin_own", "twin_far", "twin_both")]
    return pl.pallas_call(
        run,
        in_specs=[pl.BlockSpec(memory_space=pltpu.SMEM)] + [any_space] * 6 + list(specs),
        out_shape=list(out_shape) + [jax.ShapeDtypeStruct(shape, LOW)],
        out_specs=list(out_specs) + [any_space],
        scratch_shapes=list(scratch)
        + [pltpu.VMEM(shape, LOW), pltpu.SemaphoreType.DMA((48,)), pltpu.SemaphoreType.DMA],
        **options,
    )(jnp.stack(coordinates()).astype(jnp.int32), *pieces, *args)


class Gather:
    def __init__(self, weight):
        self.rows, self.width = weight.shape
        self.live = {"weight": weight}
        self.fast = is_fast() and self.rows % 48 == 0

    def z(self, apart=False):
        if not self.fast:
            return
        self.apart = apart
        x, core, _, _ = coordinates()
        h, half = self.rows // PARTS, self.width // 2
        weight = self.live.pop("weight")
        mine = lax.dynamic_slice_in_dim(weight, core * half, half, 1).reshape(PARTS, h, half)
        base = jnp.stack([pick(mine, x, 0), mine[2]], 0)
        if apart:
            lines = [base] + [lax.ppermute(base, AXES, TO_Z[k]) for k in (1, 2, 3)]
            self.live["own"] = jnp.stack(lines, 0)
            return
        self.live["own"] = over_z(jnp.broadcast_to(base, (HIGH_Z, 2, h, half)))

    def y(self):
        if self.fast:
            self.live["far"] = lax.ppermute(self.live["own"], AXES, TO_Y)

    def x(self):
        if self.fast:
            ends = jnp.stack([self.live["own"][:, 0], self.live["far"][:, 0]], 1)
            self.live["both"] = lax.ppermute(ends, AXES, TO_X)

    def core(self, *names):
        if self.fast:
            for name in names:
                self.live["twin_" + name] = lax.ppermute(self.live[name], AXES, TO_CORE)

    def whole(self):
        return lax.all_gather(self.live["weight"], "fsdp", axis=0, tiled=True)


class Scatter:
    def __init__(self, left, send=None, keep=None, pair=None):
        self.left, self.fast = left, is_fast() and left.shape[1] % 384 == 0
        self.live = {"send": send, "keep": keep} if pair is None else {"pair": pair}

    def operand(self, name):
        if "pair" in self.live:
            return self.live["pair"][("send", "keep").index(name)]
        return self.live[name]

    def first(self):
        live = self.live
        if self.fast:
            live["out"] = dot_left(self.left, self.operand("send")).astype(LOW)
            live.pop("send", None)

    def core(self):
        if self.fast:
            self.live["got"] = lax.ppermute(self.live.pop("out"), AXES, TO_CORE)

    def second(self):
        live = self.live
        if self.fast:
            product = dot_left(self.left, self.operand("keep"))
            live["kept"] = (product + live.pop("got").astype(WIDE)).astype(LOW)
            live.pop("keep", None)

    def join(self, other):
        if self.fast:
            kept = [self.live["kept"], other.live.pop("kept")]
            self.live["kept"] = jnp.concatenate(kept, axis=1)

    def view(self):
        rows, half = self.live["kept"].shape
        return self.live["kept"].reshape(HIGH_Z, 2, PARTS, rows // 24, half)

    def cut(self, start, sizes):
        view = self.view()
        return lax.dynamic_slice(view, (*start, 0, 0), (*sizes, *view.shape[3:])).reshape(
            tuple(k for k in sizes if k > 1) + view.shape[3:]
        )

    def x(self, half=None):
        if not self.fast:
            return
        x, _, _, _ = coordinates()
        if half is None:
            self.live["side"] = lax.ppermute(
                self.cut((0, 0, 1 - x), (HIGH_Z, 2, 1)), AXES, TO_X
            )
        else:
            self.live["side_" + str(half)] = lax.ppermute(
                self.cut((2 * half, 0, 1 - x), (2, 2, 1)), AXES, TO_X
            )

    def own(self, index):
        x, _, _, _ = coordinates()
        live = self.live
        sides = [live["side"]] if "side" in live else [live["side_0"], live["side_1"]]
        sides = [pick(side, index, 1) for side in sides]
        side = jnp.concatenate(sides, 0) if len(sides) > 1 else sides[0]
        mine = self.cut((0, index, x), (HIGH_Z, 1, 1))
        return (mine.astype(WIDE) + side.astype(WIDE)).astype(LOW)

    def common(self, index):
        return self.cut((0, index, 2), (HIGH_Z, 1, 1))

    def y_common(self):
        if self.fast:
            _, _, _, y = coordinates()
            self.live["far_common"] = lax.ppermute(self.common(1 - y), AXES, TO_Y)

    def y_own(self):
        if self.fast:
            _, _, _, y = coordinates()
            self.live["far_own"] = lax.ppermute(self.own(1 - y), AXES, TO_Y)

    def y_both(self):
        if self.fast:
            _, _, _, y = coordinates()
            both = jnp.stack([self.own(1 - y), self.common(1 - y)], 1)
            self.live["far_both"] = lax.ppermute(both, AXES, TO_Y)

    def line(self, name):
        _, _, _, y = coordinates()
        mine = self.common(y) if name == "common" else self.own(y)
        if "far_both" in self.live:
            far = self.live["far_both"][:, 1 if name == "common" else 0]
        else:
            far = self.live.pop("far_" + name)
        return (mine.astype(WIDE) + far.astype(WIDE)).astype(LOW)

    def z_common(self):
        if self.fast:
            self.live["sum_common"] = {"all": over_z(self.line("common"))}

    def z_own(self, apart=False):
        if not self.fast:
            return
        line = self.line("own")
        self.forget()
        if not apart:
            self.live["sum_own"] = {"all": over_z(line)}
            return
        _, _, z, _ = coordinates()
        lines = {"0": pick(line, z, 0)}
        for k in (2, 1, 3):
            lines[str(k)] = lax.ppermute(pick(line, (z + k) % 4, 0), AXES, TO_Z[k])
        self.live["sum_own"] = lines

    def z_both(self):
        if self.fast:
            lines = jnp.stack([self.line("own"), self.line("common")], 1)
            self.forget()
            self.live["sum_both"] = {"all": over_z(lines)}

    def forget(self):
        for name in ("kept", "side", "side_0", "side_1", "far_both"):
            self.live.pop(name, None)

    def total(self, name):
        lines = self.live.pop(name)
        if "all" in lines:
            return jnp.sum(lines["all"].astype(WIDE), axis=0).astype(LOW)
        wide = [lines[k].astype(WIDE) for k in ("0", "1", "2", "3")]
        return (wide[0] + wide[1] + wide[2] + wide[3]).astype(LOW)

    def last_x(self):
        if self.fast:
            if "sum_both" in self.live:
                part = self.total("sum_both")
            else:
                part = jnp.stack([self.total("sum_own"), self.total("sum_common")], 0)
            self.live = {"part": part, "other": lax.ppermute(part, AXES, TO_X)}

    def last_core(self):
        if self.fast:
            x, _, _, _ = coordinates()
            part, other = self.live["part"], self.live["other"]
            shared = (part[1].astype(WIDE) + other[1].astype(WIDE)).astype(LOW)
            first = jnp.where(x == 0, part[0], other[0])
            second = jnp.where(x == 0, other[0], part[0])
            done = jnp.concatenate([first, second, shared], 0)
            self.live = {"done": done, "twin": lax.ppermute(done, AXES, TO_CORE)}

    def halves(self):
        if self.fast:
            _, core, _, _ = coordinates()
            done, twin = self.live["done"], self.live["twin"]
            first = jnp.where(core == 0, done, twin)
            second = jnp.where(core == 0, twin, done)
            return first.astype(WIDE), second.astype(WIDE)
        _, core, _, _ = coordinates()
        left = self.left
        keep, send = self.operand("keep"), self.operand("send")
        first = jnp.where(core == 0, keep, send)
        second = jnp.where(core == 0, send, keep)
        sums = []
        for columns in (first, second):
            grad = dot_left(left, columns).astype(LOW)
            part = lax.psum_scatter(grad, "fsdp", scatter_dimension=0, tiled=True)
            sums.append(lax.psum(part, "rep").astype(WIDE))
        return sums[0], sums[1]


def column_halves(array):
    _, core, _, _ = coordinates()
    half = array.shape[1] // 2
    send = lax.dynamic_slice_in_dim(array, (1 - core) * half, half, 1)
    keep = lax.dynamic_slice_in_dim(array, core * half, half, 1)
    return send, keep


def across_x(rows):
    return lax.ppermute(rows, AXES, TO_X) if is_fast() else rows


def across_replicas(rows, far):
    if not is_fast():
        return lax.all_gather(rows, "rep", axis=0, tiled=True)
    x, core, _, _ = coordinates()
    count, width = rows.shape
    line = jnp.stack([jnp.where(x == 0, rows, far), jnp.where(x == 0, far, rows)], 0)
    twin = lax.ppermute(line, AXES, TO_CORE)
    every = [jnp.where(core == 0, line, twin), jnp.where(core == 0, twin, line)]
    return jnp.stack(every, 1).reshape(4 * count, width)


def gather_rows(rows):
    shards = lax.axis_size("fsdp")
    count, width = rows.shape
    group = lax.all_to_all(jnp.broadcast_to(rows, (shards, count, width)), "fsdp", 0, 0)
    return group.reshape(shards * count, width)


def exchange(rows):
    shards = lax.axis_size("fsdp")
    count, width = rows.shape
    shaped = rows.reshape(count, shards, width // shards).swapaxes(0, 1)
    return lax.all_to_all(shaped, "fsdp", 0, 0).reshape(shards * count, width // shards)


def sum_back(partial_rows, count):
    shards = lax.axis_size("fsdp")
    shaped = partial_rows.astype(LOW).reshape(shards, count, -1)
    got = lax.all_to_all(shaped, "fsdp", 0, 0)
    return jnp.sum(got.astype(WIDE), axis=0)


def whole_block(array):
    return pl.BlockSpec(
        array.shape, lambda i: (0,) * array.ndim, pipeline_mode=pl.Buffered(1)
    )


def part_width(hd):
    return -(-3 * GROUP * hd // LANES) * LANES


def prepare_kernel(
    first, heads, hd, x_ref, hot_ref, mod_ref, w_ref, gq_ref, gk_ref, rot_ref, qt_ref, kt_ref,
    vt_ref, *refs
):
    normed_ref, q_ref, k_ref, v_ref, rq_ref, rk_ref, wide_ref = refs if first else (x_ref, *refs)
    step = part_width(hd)
    if first:
        width = x_ref.shape[1]
        hot = hot_ref[...]
        shift = dot(hot, mod_ref[:, :width])
        scale = dot(hot, mod_ref[:, width:])
        normed, _ = normed_rows(x_ref[...].astype(WIDE))
        normed = (normed * (1.0 + scale) + shift).astype(LOW)
        normed_ref[...] = normed
    else:
        normed = x_ref[...]
    cosine, plus, minus = rot_ref[0], rot_ref[1], rot_ref[2]
    lane = lax.broadcasted_iota(jnp.int32, (BLOCK, LANES), 1)
    inside = lane < hd
    ones = jnp.full((LANES, LANES), 1.0, LOW)
    wide_ref[:, step:] = jnp.zeros((BLOCK, LANES), WIDE)
    for part in range(heads // GROUP):
        wide_ref[:, :step] = dot(normed, w_ref[:, part * step : (part + 1) * step])
        for kind, (g_ref, t_ref, o_ref, r_ref) in enumerate(
            (
                (gq_ref, qt_ref, q_ref, rq_ref),
                (gk_ref, kt_ref, k_ref, rk_ref),
                (None, vt_ref, v_ref, None),
            )
        ):
            tail = t_ref[...]
            for g in range(GROUP):
                h = part * GROUP + g
                at = (kind * GROUP + g) * hd
                raw = jnp.where(inside, wide_ref[:, at : at + LANES], 0.0)
                if kind < 2:
                    r_ref[h] = raw.astype(LOW)
                    total = dot((raw * raw).astype(LOW), ones)
                    u = raw * lax.rsqrt(total * (1.0 / hd) + EPSILON) * g_ref[...]
                    up = pltpu.roll(u, LANES - hd // 4, 1)
                    down = pltpu.roll(u, hd // 4, 1)
                    raw = u * cosine + up * plus + down * minus
                o_ref[h] = raw.astype(LOW) + tail


def prepare(first, x, hot, mod, gather, gq, gk, rot, qt, kt, vt, heads, hd):
    n, width = x.shape
    rows = pl.BlockSpec((BLOCK, width), lambda i: (i, 0))
    head_spec = pl.BlockSpec((heads, BLOCK, LANES), lambda i: (0, i, 0))
    tail = pl.BlockSpec((BLOCK, LANES), lambda i: (i, 0))
    normed_spec, normed_shape = [rows], [jax.ShapeDtypeStruct((n, width), LOW)]
    return call_placed(
        partial(prepare_kernel, first, heads, hd),
        gather,
        (x, hot, mod, gq, gk, rot, qt, kt, vt),
        [
            rows,
            pl.BlockSpec((BLOCK, hot.shape[1]), lambda i: (i, 0)),
            whole_block(mod),
            whole_block(gq),
            whole_block(gk),
            pl.BlockSpec((3, BLOCK, LANES), lambda i: (0, i, 0)),
            tail,
            tail,
            pl.BlockSpec((1, LANES), lambda i: (0, 0)),
        ],
        3,
        (normed_shape if first else []) + [jax.ShapeDtypeStruct((heads, n, LANES), LOW)] * 5,
        (normed_spec if first else []) + [head_spec] * 5,
        [pltpu.VMEM((BLOCK, part_width(hd) + LANES), WIDE)],
        grid=(n // BLOCK,),
        compiler_params=pltpu.CompilerParams(vmem_limit_bytes=56 * MIB),
        cost_estimate=pl.CostEstimate(
            flops=12 * n * width * width // 2, bytes_accessed=20 * MIB, transcendentals=0
        ),
        name="prepare",
    )


def near_blocks(run):
    i = pl.program_id(0)
    n = pl.num_programs(0)

    @pl.when(i == 0)
    def _():
        run(pl.ds(0, 2 * BLOCK))

    @pl.when(i == n - 1)
    def _():
        run(pl.ds(pl.multiple_of((i - 1) * BLOCK, BLOCK), 2 * BLOCK))

    @pl.when((i > 0) & (i < n - 1))
    def _():
        run(pl.ds(pl.multiple_of((i - 1) * BLOCK, BLOCK), 3 * BLOCK))


def attend_kernel(hd, c, *refs):
    mix_ref = refs[6]
    lane = lax.broadcasted_iota(jnp.int32, (BLOCK, LANES), 1)
    heads = refs[0].shape[0]

    def run(at):
        for head in range(2 * heads):
            half, h = head // heads, head % heads
            q_ref, k_ref, v_ref = refs[3 * half : 3 * half + 3]
            q = q_ref[h]
            p = jnp.exp2(dot_right(q, k_ref[h, at]) * c).astype(LOW)
            total = dot(p, v_ref[h, at])
            norm = total[:, hd : hd + 1]
            out = (total * (1.0 / norm)).astype(LOW)
            mix_ref[:, hd * head : hd * (head + 1)] = out[:, :hd]
            rest = jnp.log2(norm) * (1.0 / c)
            first = rest.astype(LOW).astype(WIDE)
            rest = rest - first
            second = rest.astype(LOW).astype(WIDE)
            third = rest - second
            logs = jnp.where(lane == hd + 8, first, jnp.where(lane == hd + 9, second, third))
            marked = jnp.where((lane >= hd + 8) & (lane < hd + 11), logs.astype(LOW), q)
            refs[7 + half][h] = marked

    near_blocks(run)


def attend(one, two, hd, c):
    heads, n, _ = one[0].shape
    full = pl.BlockSpec((heads, n, LANES), lambda i: (0, 0, 0), pipeline_mode=pl.Buffered(1))
    block = pl.BlockSpec((heads, BLOCK, LANES), lambda i: (0, i, 0))
    width = 2 * heads * hd
    return pl.pallas_call(
        partial(attend_kernel, hd, c),
        grid=(n // BLOCK,),
        in_specs=[block, full, full] * 2,
        out_specs=[pl.BlockSpec((BLOCK, width), lambda i: (i, 0)), block, block],
        out_shape=[jax.ShapeDtypeStruct((n, width), LOW)]
        + [jax.ShapeDtypeStruct((heads, n, LANES), LOW)] * 2,
        compiler_params=pltpu.CompilerParams(vmem_limit_bytes=56 * MIB),
        cost_estimate=pl.CostEstimate(
            flops=8 * n * 640 * LANES * heads,
            bytes_accessed=20 * MIB,
            transcendentals=2 * heads * n * 640,
        ),
        name="attend",
    )(*one, *two)


def spread_kernel(heads, hd, proj_at, ga_ref, w_ref, mix_ref, out_ref, grad_scr, mix_scr):
    width = heads * hd
    grad_scr[:, width:] = jnp.zeros((BLOCK, LANES), WIDE)
    mix_scr[:, width:] = jnp.zeros((BLOCK, LANES), WIDE)
    grad_scr[:, :width] = dot_right(ga_ref[:, :width], w_ref[:, proj_at : proj_at + width]).astype(LOW).astype(WIDE)
    mix_scr[:, :width] = mix_ref[...].astype(WIDE)
    lane = lax.broadcasted_iota(jnp.int32, (BLOCK, LANES), 1)
    ones = jnp.full((LANES, LANES), 1.0, LOW)
    for h in range(heads):
        at = hd * h
        grad = jnp.where(lane < hd, grad_scr[:, at : at + LANES], 0.0)
        product = grad * mix_scr[:, at : at + LANES]
        high = product.astype(LOW)
        rest = (product - high.astype(WIDE)).astype(LOW)
        delta = -(dot(high, ones) + dot(rest, ones))
        first = delta.astype(LOW)
        second = (delta - first.astype(WIDE)).astype(LOW)
        out_ref[h] = jnp.where(
            lane == hd, first, jnp.where(lane == hd + 1, second, grad.astype(LOW))
        )


def spread(ga, w, mix, heads, hd, proj_at):
    n = ga.shape[0]
    width = heads * hd
    row = pl.BlockSpec((BLOCK, width), lambda i: (i, 0))
    wide_row = pl.BlockSpec((BLOCK, ga.shape[1]), lambda i: (i, 0))
    return pl.pallas_call(
        partial(spread_kernel, heads, hd, proj_at),
        grid=(n // BLOCK,),
        in_specs=[wide_row, whole_block(w), row],
        out_specs=pl.BlockSpec((heads, BLOCK, LANES), lambda i: (0, i, 0)),
        out_shape=jax.ShapeDtypeStruct((heads, n, LANES), LOW),
        scratch_shapes=[
            pltpu.VMEM((BLOCK, width + LANES), WIDE),
            pltpu.VMEM((BLOCK, width + LANES), WIDE),
        ],
        compiler_params=pltpu.CompilerParams(vmem_limit_bytes=56 * MIB),
        cost_estimate=pl.CostEstimate(
            flops=2 * n * width * width, bytes_accessed=12 * MIB, transcendentals=0
        ),
        name="spread",
    )(ga, w, mix)


def back_kernel(
    hd, c, score_scale, part, core_ref, q_ref, k_ref, v_ref, do_ref, rq_ref, rk_ref, rot_ref, gq_ref, gk_ref,
    *refs,
):
    out_ref, gain_ref, joint_ref, dq_scr, dk_scr, dv_scr, gain_scr, out_sem = refs[part:]
    i = pl.program_id(0)
    n = pl.num_programs(0)
    heads = q_ref.shape[0]
    width = GROUP * hd
    tail = joint_ref.shape[1] - 3 * width
    slot = core_ref[0] if part else 1 - core_ref[0]

    @pl.when(i == 0)
    def _():
        dq_scr[...] = jnp.zeros(dq_scr.shape, WIDE)
        gain_scr[...] = jnp.zeros(gain_scr.shape, WIDE)

    ones = jnp.full((LANES, LANES), 1.0, LOW)

    def run(at):
        def body(h, carry):
            kk = k_ref[h]
            vv = v_ref[h]
            q = q_ref[h, at]
            do = do_ref[h, at]
            p = jnp.exp2(dot_right(kk, q) * c)
            dv_scr[h] = dot(p.astype(LOW), do)
            ds = (p * dot_right(vv, do)).astype(LOW)
            dk_scr[h] = dot(ds, q)
            dq_scr[h, at] += dot_left(ds, kk)
            return carry

        lax.fori_loop(0, heads, body, 0, unroll=GROUP)

    near_blocks(run)

    def finish(dy, raw, rot, gain, row):
        raw = raw.astype(WIDE)
        dy = dy * score_scale
        up = pltpu.roll(dy, LANES - hd // 4, 1)
        down = pltpu.roll(dy, hd // 4, 1)
        d = dy * rot[0] - up * rot[1] - down * rot[2]
        r = lax.rsqrt(dot((raw * raw).astype(LOW), ones) * (1.0 / hd) + EPSILON)
        u = raw * r
        ud = u * d
        gain_scr[row] += jnp.sum(ud.reshape(BLOCK // 8, 8, LANES), axis=0)
        m = dot((ud * gain).astype(LOW), ones) * (1.0 / hd)
        return (r * (gain * d - u * m)).astype(LOW)

    here = pl.ds(pl.multiple_of(i * BLOCK, BLOCK), BLOCK)
    rot = [rot_ref[t, here] for t in range(3)]
    joint_ref[here, 3 * width :] = jnp.zeros((BLOCK, tail), LOW)
    for h in range(heads):
        at = hd * h
        grad = finish(dk_scr[h], rk_ref[h], rot, gk_ref[...], 1)
        joint_ref[here, width + at : width + at + hd] = grad[:, :hd]
        value = dv_scr[h].astype(LOW)
        joint_ref[here, 2 * width + at : 2 * width + at + hd] = value[:, :hd]

    @pl.when(i == n - 1)
    def _():
        def rows(b, carry):
            at = pl.ds(pl.multiple_of(b * BLOCK, BLOCK), BLOCK)
            turn = [rot_ref[t, at] for t in range(3)]
            for h in range(heads):
                start = hd * h
                grad = finish(dq_scr[h, at], rq_ref[h, at], turn, gq_ref[...], 0)
                joint_ref[at, start : start + hd] = grad[:, :hd]
            return carry

        lax.fori_loop(0, n, rows, 0)
        gain_ref[...] = gain_scr[...]
        copy = pltpu.make_async_copy(joint_ref, out_ref.at[slot], out_sem)
        copy.start()
        copy.wait()


def attend_back(half, part, before, core, q2, k, v, do, rq, rk, rot, gq, gk, hd, c, score_scale):
    _, n, _ = q2.shape
    one = pl.Buffered(1)
    full = pl.BlockSpec((GROUP, n, LANES), lambda i: (part, 0, 0), pipeline_mode=one)
    block = pl.BlockSpec((GROUP, BLOCK, LANES), lambda i: (part, i, 0))
    small = pl.BlockSpec((1, LANES), lambda i: (0, 0))
    any_space = pl.BlockSpec(memory_space=pl.ANY)
    width = part_width(hd)
    at = 2 * half + part
    return pl.pallas_call(
        partial(back_kernel, hd, c, score_scale, part),
        grid=(n // BLOCK,),
        in_specs=[
            pl.BlockSpec(memory_space=pltpu.SMEM),
            *(full, block, block),
            pl.BlockSpec((GROUP, n, LANES), lambda i: (at, 0, 0), pipeline_mode=one),
            *(full, block, whole_block(rot), small, small),
            *([any_space] if part else []),
        ],
        out_specs=[any_space, pl.BlockSpec((2, 8, LANES), lambda i: (0, 0, 0))],
        out_shape=[
            jax.ShapeDtypeStruct((2, n, width), LOW),
            jax.ShapeDtypeStruct((2, 8, LANES), WIDE),
        ],
        scratch_shapes=[
            pltpu.VMEM((n, width), LOW),
            pltpu.VMEM((GROUP, n, LANES), WIDE),
            pltpu.VMEM((GROUP, BLOCK, LANES), WIDE),
            pltpu.VMEM((GROUP, BLOCK, LANES), WIDE),
            pltpu.VMEM((2, 8, LANES), WIDE),
            pltpu.SemaphoreType.DMA,
        ],
        input_output_aliases={10: 0} if part else {},
        compiler_params=pltpu.CompilerParams(vmem_limit_bytes=56 * MIB),
        cost_estimate=pl.CostEstimate(
            flops=10 * n * 640 * LANES * GROUP,
            bytes_accessed=10 * MIB,
            transcendentals=GROUP * n * 640,
        ),
        name="attend_back",
    )(core, q2, k, v, do, rq, rk, rot, gq, gk, *([before] if part else []))


def normed_rows(values):
    centred = values - jnp.mean(values, axis=-1, keepdims=True)
    scale = lax.rsqrt(jnp.mean(centred * centred, axis=-1, keepdims=True) + EPSILON)
    return centred * scale, scale


def norm_back(normed, scale, grad):
    inner = jnp.mean(grad * normed, axis=-1, keepdims=True)
    return scale * (grad - jnp.mean(grad, axis=-1, keepdims=True) - normed * inner)


def add_sums(out_ref, at, hot, values):
    width = values.shape[1]
    term = dot_left(hot, values.astype(LOW))
    here = (slice(None), slice(at * width, (at + 1) * width))

    @pl.when(pl.program_id(0) == 0)
    def _():
        out_ref[here] = term

    @pl.when(pl.program_id(0) > 0)
    def _():
        out_ref[here] += term


def rows_of(array):
    if array.ndim == 3:
        return pl.BlockSpec((2, BLOCK, array.shape[2]), lambda i: (0, i, 0))
    return pl.BlockSpec((BLOCK, array.shape[1]), lambda i: (i, 0))


def call_rows(
    kernel, name, streamed, fixed, outs, sums=(), core=None, scratch=(), gather=None
):
    n = streamed[0].shape[-2]
    work = sum(2 * n * a.size for a in fixed if a.shape[0] > 256)
    moved = sum(a.size * a.dtype.itemsize for a in (*streamed, *fixed))
    scalars = () if core is None else (core,)
    args = (*scalars, *streamed, *fixed)
    specs = [pl.BlockSpec(memory_space=pltpu.SMEM) for _ in scalars]
    specs += [rows_of(a) for a in streamed] + [whole_block(a) for a in fixed]
    out_specs = [pl.BlockSpec((BLOCK, w), lambda i: (i, 0)) for w, _ in outs]
    out_specs += [pl.BlockSpec(shape, lambda i: (0, 0)) for shape in sums]
    out_shape = [jax.ShapeDtypeStruct((n, w), t) for w, t in outs]
    out_shape += [jax.ShapeDtypeStruct(shape, WIDE) for shape in sums]
    scratch = [pltpu.VMEM(shape, WIDE) for shape in scratch]
    if gather is not None:
        work += 2 * n * gather.rows * lax.axis_size("fsdp") * gather.width
    options = dict(
        grid=(n // BLOCK,),
        compiler_params=pltpu.CompilerParams(vmem_limit_bytes=56 * MIB),
        cost_estimate=pl.CostEstimate(flops=work, bytes_accessed=moved, transcendentals=0),
        name=name,
    )
    if gather is not None:
        before = len(scalars) + len(streamed)
        return call_placed(
            kernel, gather, args, specs, before, out_shape, out_specs, scratch, **options
        )
    return pl.pallas_call(
        kernel, in_specs=specs, out_specs=out_specs, out_shape=out_shape, scratch_shapes=scratch,
        **options,
    )(*args)


def join_kernel(
    proj_at, mix_ref, x_ref, hot_ref, keep_ref, w_ref, mod_ref, att_ref, mid_ref, norm_ref
):
    width = x_ref.shape[1]
    hot = hot_ref[...]
    attended = dot(mix_ref[...], w_ref[:, proj_at : proj_at + width])
    att_ref[...] = attended.astype(LOW)
    gate = dot(hot, mod_ref[:, :width]) * keep_ref[...]
    middle = x_ref[...].astype(WIDE) + gate * attended
    mid_ref[...] = middle
    normed, _ = normed_rows(middle)
    scale = dot(hot, mod_ref[:, 2 * width : 3 * width])
    shift = dot(hot, mod_ref[:, width : 2 * width])
    norm_ref[...] = (normed * (1.0 + scale) + shift).astype(LOW)


def gate_kernel(x_ref, w_ref, out_ref):
    out_ref[...] = dot(x_ref[...], w_ref[:, : out_ref.shape[1]]).astype(LOW)


def up_kernel(x_ref, gate_ref, w_ref, up_ref, inner_ref):
    up = dot(x_ref[...], w_ref[...])
    up_ref[...] = up.astype(LOW)
    gate = gate_ref[...].astype(WIDE)
    inner_ref[...] = (gate * jax.nn.sigmoid(gate) * up).astype(LOW)


def down_kernel(
    inner_ref, mid_ref, grad_ref, hot_ref, keep_ref, w_ref, mod_ref, out_ref, back_ref, sum_ref
):
    width = mid_ref.shape[1]
    hot = hot_ref[...]
    returned = dot(inner_ref[...], w_ref[:, :width])
    gate = dot(hot, mod_ref[...]) * keep_ref[...]
    out_ref[...] = (mid_ref[...] + gate * returned).astype(LOW)
    upstream = grad_ref[...].astype(WIDE)
    back_ref[:, :width] = (upstream * gate).astype(LOW)
    if back_ref.shape[1] > width:
        back_ref[:, width:] = jnp.zeros((BLOCK, back_ref.shape[1] - width), LOW)
    add_sums(sum_ref, 0, hot, upstream * keep_ref[...] * returned)


def inner_back_kernel(core_ref, grad_ref, gate_ref, up_ref, w_ref, send_ref, keep_ref):
    grad = dot_right(grad_ref[...], w_ref[...])
    gate = gate_ref[...].astype(WIDE)
    sig = jax.nn.sigmoid(gate)
    act = gate * sig
    for_gate = (grad * up_ref[...].astype(WIDE) * (sig + act * (1.0 - sig))).astype(LOW)
    for_up = (grad * act).astype(LOW)

    @pl.when(core_ref[0] == 0)
    def _():
        send_ref[...] = for_up
        keep_ref[...] = for_gate

    @pl.when(core_ref[0] != 0)
    def _():
        send_ref[...] = for_gate
        keep_ref[...] = for_up


def middle_back_kernel(
    core_ref, send_ref, mine_ref, mid_ref, grad_ref, att_ref, hot_ref, keep_ref, wg_ref, wu_ref,
    mod_ref, out_ref, back_ref, sum_ref, total_ref,
):
    width = mid_ref.shape[1]
    hot = hot_ref[...]
    keep = keep_ref[...]

    @pl.when(core_ref[0] == 0)
    def _():
        total_ref[...] = dot_right(mine_ref[...], wg_ref[:, : mine_ref.shape[1]])
        total_ref[...] += dot_right(send_ref[...], wu_ref[...])

    @pl.when(core_ref[0] != 0)
    def _():
        total_ref[...] = dot_right(send_ref[...], wg_ref[:, : send_ref.shape[1]])
        total_ref[...] += dot_right(mine_ref[...], wu_ref[...])

    grad = total_ref[...]
    normed, scale = normed_rows(mid_ref[...])
    turned = grad * (1.0 + dot(hot, mod_ref[:, 2 * width : 3 * width]))
    total = grad_ref[...].astype(WIDE) + norm_back(normed, scale, turned)
    out_ref[...] = total
    gate = dot(hot, mod_ref[:, :width]) * keep
    back_ref[:, :width] = (total * gate).astype(LOW)
    if back_ref.shape[1] > width:
        back_ref[:, width:] = jnp.zeros((BLOCK, back_ref.shape[1] - width), LOW)
    add_sums(sum_ref, 0, hot, total * keep * att_ref[...].astype(WIDE))
    add_sums(sum_ref, 1, hot, grad)
    add_sums(sum_ref, 2, hot, grad * normed)


def input_back_kernel(
    core_ref, one_ref, two_ref, mid_ref, x_ref, hot_ref, wo_ref, wt_ref, mod_ref, out_ref, sum_ref
):
    width = x_ref.shape[1]
    hot = hot_ref[...]
    step = one_ref.shape[2]
    core = core_ref[0]
    grad = None
    for ref, w_ref in ((one_ref, wo_ref), (two_ref, wt_ref)):
        term = dot_right(ref[1 - core], w_ref[:, :step]) + dot_right(ref[core], w_ref[:, step : 2 * step])
        grad = term if grad is None else grad + term
    normed, scale = normed_rows(x_ref[...].astype(WIDE))
    turned = grad * (1.0 + dot(hot, mod_ref[:, width : 2 * width]))
    out_ref[...] = mid_ref[...] + norm_back(normed, scale, turned)
    add_sums(sum_ref, 0, hot, grad)
    add_sums(sum_ref, 1, hot, grad * normed)


def finish_kernel(hd, core_ref, head_done, head_twin, tail_done, tail_twin, qkv_ref, proj_ref):
    step = part_width(hd)
    short = GROUP * hd
    total = qkv_ref.shape[1] // 3

    def write(sources):
        for part, source in enumerate(sources):
            values = source[:, :step].astype(WIDE)
            for kind in range(3):
                at = kind * total + part * short
                qkv_ref[:, at : at + short] = values[:, kind * short : (kind + 1) * short]
        half = sources[0].shape[1] - step
        proj_ref[:, :half] = sources[0][:, step:].astype(WIDE)
        rest = proj_ref.shape[1] - half
        proj_ref[:, half:] = sources[1][:, step : step + rest].astype(WIDE)

    @pl.when(core_ref[0] == 0)
    def _():
        write((head_done, head_twin, tail_done, tail_twin))

    @pl.when(core_ref[0] != 0)
    def _():
        write((head_twin, head_done, tail_twin, tail_done))


def finish(core, head, tail, hd, width):
    rows = head["done"].shape[0]
    return pl.pallas_call(
        partial(finish_kernel, hd),
        in_specs=[pl.BlockSpec(memory_space=pltpu.SMEM)]
        + [pl.BlockSpec(memory_space=pltpu.VMEM)] * 4,
        out_specs=[pl.BlockSpec(memory_space=pltpu.VMEM)] * 2,
        out_shape=[
            jax.ShapeDtypeStruct((rows, 3 * width), WIDE),
            jax.ShapeDtypeStruct((rows, width), WIDE),
        ],
        compiler_params=pltpu.CompilerParams(vmem_limit_bytes=40 * MIB),
        name="finish",
    )(core, head["done"], head["twin"], tail["done"], tail["twin"])


def turn_tables(row_place, column_place, hd):
    quarter = hd // 4
    inverse = 10000.0 ** (-jnp.arange(quarter, dtype=WIDE) / quarter)
    row_angle = row_place.astype(WIDE)[:, None] * inverse[None, :]
    column_angle = column_place.astype(WIDE)[:, None] * inverse[None, :]
    rest = jnp.zeros((row_place.shape[0], LANES - hd), WIDE)
    none = jnp.zeros_like(row_angle)
    rc, rs = jnp.cos(row_angle), jnp.sin(row_angle)
    cc, cs = jnp.cos(column_angle), jnp.sin(column_angle)
    return jnp.stack(
        [
            jnp.concatenate([rc, rc, cc, cc, rest], 1),
            jnp.concatenate([-rs, none, -cs, none, rest], 1),
            jnp.concatenate([none, rs, none, cs, rest], 1),
        ],
        0,
    )


def high_and_rest(values):
    high = values.astype(LOW)
    return jnp.concatenate([high, (values - high.astype(WIDE)).astype(LOW)], axis=0)


def pad_columns(array, width):
    return jnp.pad(array, ((0, 0), (0, width - array.shape[1])))


def to_parts(array, heads, hd):
    rows = array.shape[0]
    shaped = array.reshape(rows, 3, heads // GROUP, GROUP * hd).swapaxes(1, 2)
    shaped = shaped.reshape(rows, heads // GROUP, 3 * GROUP * hd)
    padded = jnp.pad(shaped, ((0, 0), (0, 0), (0, part_width(hd) - 3 * GROUP * hd)))
    return padded.reshape(rows, -1)


def from_parts(array, heads, hd):
    rows = array.shape[0]
    shaped = array.reshape(rows, heads // GROUP, -1)[:, :, : 3 * GROUP * hd]
    shaped = shaped.reshape(rows, heads // GROUP, 3, GROUP * hd).swapaxes(1, 2)
    return shaped.reshape(rows, -1)


def local(
    block_in,
    condition,
    item_lengths,
    item_widths,
    ada_weight,
    ada_bias,
    qkv_weight,
    query_gain,
    key_gain,
    proj_weight,
    gate_up_weight,
    down_weight,
    out_grad,
):
    _, n, width = block_in.shape
    items = item_lengths.shape[1]
    hd = query_gain.shape[0]
    heads = width // hd
    ff = down_weight.shape[0] * lax.axis_size("fsdp")
    score_scale = float(hd) ** (-0.5)
    c = score_scale * 1.4426950408889634
    shards = lax.axis_size("fsdp")
    fsdp_place = lax.axis_index("fsdp")
    odd = width + LANES if (width // LANES) % 2 else width

    qkv_parts = to_parts(qkv_weight, heads, hd)
    cut = qkv_parts.shape[1] // 2
    g_one = Gather(qkv_parts[:, :cut])
    g_two = Gather(jnp.concatenate([qkv_parts[:, cut:], pad_columns(proj_weight, odd)], axis=1))
    g_gate = Gather(gate_up_weight[:, :ff])
    g_up = Gather(gate_up_weight[:, ff:])
    g_down = Gather(pad_columns(down_weight, odd))
    gathers = [g_one, g_two, g_gate, g_up, g_down]
    core_place = (lax.axis_index("rep") % 2).astype(jnp.int32).reshape(1)

    cond_float = condition.astype(WIDE).reshape(items, width)
    cond_silu, silu_pull = jax.vjp(jax.nn.silu, cond_float)
    cond_act = cond_silu.astype(LOW)

    g_one.z()
    group_act = exchange(cond_act)
    member, segment, row_place, column_place = layout(item_lengths[0], item_widths[0], n)
    member_low = member.astype(LOW)
    keep = (segment < items - 1).astype(WIDE).reshape(n, 1)
    rot = turn_tables(row_place, column_place, hd)
    spare = jnp.zeros((n, LANES - hd - items), LOW)
    ones_at = jnp.zeros((n, LANES - hd - items), LOW).at[:, :3].set(-1.0)
    blank = jnp.zeros((n, hd), LOW)
    query_tail = jnp.concatenate([blank, member_low, spare], 1)
    key_tail = jnp.concatenate([blank, (member_low - 1.0) * MASK, ones_at], 1)
    value_tail = jnp.zeros((1, LANES), LOW).at[:, hd : hd + 2].set(1.0)
    gain_q = pad_columns(query_gain.astype(WIDE)[None, :], LANES)
    gain_k = pad_columns(key_gain.astype(WIDE)[None, :], LANES)
    hot = jnp.concatenate([member_low, member_low], axis=1)
    tables = (rot, query_tail, key_tail, hot, keep)
    group_act = hold(gathers, group_act)

    g_one.y()
    g_two.z()
    bias_row = lax.dynamic_update_slice(
        jnp.zeros((6 * width,), WIDE), ada_bias.astype(WIDE), (fsdp_place * ada_bias.shape[0],)
    )
    mod_part = (dot(group_act, ada_weight) + bias_row[None, :]).astype(LOW)
    mod_part, group_act, tables = hold(gathers, (mod_part, group_act, tables))

    early = 2 * width
    modulation = high_and_rest(sum_back(mod_part, items))
    g_one.x()
    g_one.core("own", "far")
    g_two.y()
    inputs_low = block_in[0]
    modulation, tables, inputs_low = hold(gathers, (modulation, tables, inputs_low))
    mod_a, mod_b = modulation[:, :early], modulation[:, early:]

    g_one.core("both")
    g_two.x()
    g_two.core("own", "far")
    g_gate.z()
    rot, query_tail, key_tail, hot, keep = tables
    set_out = (gain_q, gain_k, rot, query_tail, key_tail, value_tail, heads // 2, hd)
    normed_a, q_one, k_one, v_one, rq_one, rk_one, one_full = prepare(
        True, inputs_low, hot, mod_a, g_one, *set_out
    )
    gathers = gathers[1:]
    normed_a, q_one, k_one, v_one, rq_one, rk_one, one_full = hold(
        gathers, (normed_a, q_one, k_one, v_one, rq_one, rk_one, one_full)
    )

    g_two.core("both")
    g_gate.y()
    g_up.z()
    q_two, k_two, v_two, rq_two, rk_two, two_full = prepare(
        False, normed_a, hot, mod_a, g_two, *set_out
    )
    gathers = gathers[1:]
    normed_a, q_two, k_two, v_two, rq_two, rk_two, two_full, q_one, k_one, v_one = hold(
        gathers, (normed_a, q_two, k_two, v_two, rq_two, rk_two, two_full, q_one, k_one, v_one)
    )

    g_gate.x()
    g_gate.core("own", "far")
    g_up.y()
    g_down.z()
    mixed, q2_one, q2_two = attend((q_one, k_one, v_one), (q_two, k_two, v_two), hd, c)
    mixed, q2_one, q2_two = hold(gathers, (mixed, q2_one, q2_two))

    g_gate.core("both")
    g_up.x()
    g_up.core("own", "far")
    g_down.y()
    mod_mid = mod_b[:, : 3 * width]
    attended, middle, normed_b = call_rows(
        partial(join_kernel, cut), "join", (mixed, inputs_low, hot, keep), (two_full, mod_mid),
        ((width, LOW), (width, WIDE), (width, LOW)),
    )
    middle, normed_b, attended = hold([g_gate], (middle, normed_b, attended))

    gate, gate_full = call_rows(
        gate_kernel, "gate", (normed_b,), (), ((ff, LOW),), gather=g_gate
    )
    gathers = [g_up, g_down]
    gate, gate_full, normed_b, middle, attended = hold(
        gathers, (gate, gate_full, normed_b, middle, attended)
    )

    g_up.core("both")
    g_down.x()
    g_down.core("own", "far")
    normed_b = hold([g_up], normed_b)
    up, inner, up_full = call_rows(
        up_kernel, "up", (normed_b, gate), (), ((ff, LOW), (ff, LOW)), gather=g_up
    )
    gathers = [g_down]
    inner, up, gate, up_full, middle = hold(gathers, (inner, up, gate, up_full, middle))

    g_down.core("both")
    block_out, grad_returned, sums_gate_b, down_full = call_rows(
        down_kernel, "down", (inner, middle, out_grad[0], hot, keep), (mod_b[:, 3 * width :],),
        ((width, LOW), (odd, LOW)), ((2 * items, width),), gather=g_down,
    )

    s_down = Scatter(inner, *column_halves(grad_returned))
    s_down.first()
    plans = [s_down]
    grad_returned, down_full, gate, up, gate_full, up_full, normed_b, middle, attended = hold(
        plans,
        (grad_returned, down_full, gate, up, gate_full, up_full, normed_b, middle, attended),
    )

    s_down.core()
    grad_send, grad_keep = call_rows(
        inner_back_kernel, "inner_back", (grad_returned, gate, up), (down_full,),
        ((ff, LOW), (ff, LOW)), core=core_place,
    )
    grad_send, grad_keep = hold(plans, (grad_send, grad_keep))

    s_down.second()
    s_wide = Scatter(normed_b, grad_send, grad_keep)
    s_wide.first()
    plans = [s_down, s_wide]
    grad_send, grad_keep = hold(plans, (grad_send, grad_keep))

    s_down.x()
    s_wide.core()
    grad_middle, grad_attended, sums_mid = call_rows(
        middle_back_kernel, "middle_back",
        (grad_send, grad_keep, middle, out_grad[0], attended, hot, keep),
        (gate_full, up_full, mod_mid), ((width, WIDE), (odd, LOW)), ((2 * items, 3 * width),),
        core=core_place, scratch=((BLOCK, width),),
    )
    s_proj = Scatter(mixed, *column_halves(grad_attended))
    plans = [s_down, s_wide, s_proj]
    grad_middle, grad_attended, sums_mid = hold(plans, (grad_middle, grad_attended, sums_mid))

    s_wide.second()
    grad_attended = hold([s_wide], grad_attended)
    s_wide.x(0)
    s_down.y_both()
    s_proj.first()
    late_sums = jnp.concatenate([sums_mid[:items], sums_gate_b[:items]], axis=1).astype(LOW)
    grad_mixed = spread(grad_attended, two_full, mixed, heads, hd, cut)
    late_sums, grad_mixed = hold([s_down, s_wide, s_proj], (late_sums, grad_mixed))

    back = partial(
        attend_back, core=core_place, rot=rot, gq=gain_q, gk=gain_k, hd=hd, c=c,
        score_scale=score_scale,
    )
    one = dict(q2=q2_one, k=k_one, v=v_one, rq=rq_one, rk=rk_one)
    two = dict(q2=q2_two, k=k_two, v=v_two, rq=rq_two, rk=rk_two)
    s_down.z_both()
    s_wide.x(1)
    s_wide.y_common()
    s_proj.core()
    joint_one, gains_0 = back(0, 0, None, do=grad_mixed, **one)
    joint_one, gains_0, grad_mixed = hold([s_down, s_wide, s_proj], (joint_one, gains_0, grad_mixed))

    s_down.last_x()
    s_wide.y_own()
    s_wide.z_common()
    s_proj.second()
    joint_one, gains_1 = back(0, 1, joint_one, do=grad_mixed, **one)
    s_head = Scatter(normed_a, pair=joint_one)
    s_head.first()
    gains_1, grad_mixed = hold([s_down, s_wide, s_proj, s_head], (gains_1, grad_mixed))

    s_head.core()
    s_down.last_core()
    s_wide.z_own()
    joint_two, gains_2 = back(1, 0, None, do=grad_mixed, **two)
    s_head.second()
    s_head.join(s_proj)
    joint_two, gains_2, grad_mixed, late_sums = hold(
        [s_down, s_wide, s_head], (joint_two, gains_2, grad_mixed, late_sums)
    )

    s_head.x()
    s_head.y_common()
    s_wide.last_x()
    late_group = gather_rows(late_sums)
    joint_two, gains_3 = back(1, 1, joint_two, do=grad_mixed, **two)
    s_tail = Scatter(normed_a, pair=joint_two)
    s_tail.first()
    gains_3, late_group = hold([s_wide, s_head, s_tail], (gains_3, late_group))

    s_tail.core()
    s_head.y_own()
    s_head.z_common()
    s_tail.second()
    grad_middle = hold([s_tail], grad_middle)
    s_tail.x()
    s_wide.last_core()
    grad_input, sums_early = call_rows(
        input_back_kernel, "input_back",
        (s_head.live["pair"], s_tail.live["pair"], grad_middle, inputs_low, hot),
        (one_full, two_full, mod_a), ((width, WIDE),), ((2 * items, 2 * width),),
        core=core_place,
    )
    if s_head.fast:
        s_head.live.pop("pair")
        s_tail.live.pop("pair")
    plans = [s_down, s_wide, s_head, s_tail]
    grad_input, sums_early, late_group = hold(plans, (grad_input, sums_early, late_group))

    s_head.z_own(apart=True)
    s_tail.y_both()
    early_sums = sums_early[:items]
    gains = gains_0 + gains_1 + gains_2 + gains_3
    gain_row = jnp.sum(gains, axis=1)[:, :hd].reshape(1, 2 * hd)
    gain_high = gain_row.astype(LOW).astype(WIDE)
    gain_block = jnp.concatenate([gain_high, gain_row - gain_high], axis=0)
    gain_block = jnp.pad(gain_block, ((0, items - 2), (0, 2 * LANES - 2 * hd)))
    early_sums = jnp.concatenate([early_sums, gain_block], axis=1).astype(LOW)
    early_group = gather_rows(early_sums)
    act_far = across_x(group_act)
    late_far = across_x(late_group)
    shard_down = jnp.concatenate(s_down.halves(), axis=1)[:, :width]
    shard_wide = jnp.concatenate(s_wide.halves(), axis=1)
    plans = [s_head, s_tail]
    early_group, late_far, act_far, shard_down, shard_wide = hold(
        plans, (early_group, late_far, act_far, shard_down, shard_wide)
    )

    s_head.last_x()
    s_tail.z_both()
    early_far = across_x(early_group)
    every_act = across_replicas(group_act, act_far)
    late_every = across_replicas(late_group, late_far)
    shard_late = dot_left(every_act, late_every)
    cond_part = dot_right(early_group[:, :early], ada_weight[:, :early]) + dot_right(
        late_group, ada_weight[:, early:]
    )
    early_far, cond_part, shard_late, every_act, late_every = hold(
        plans, (early_far, cond_part, shard_late, every_act, late_every)
    )

    s_head.last_core()
    s_tail.last_x()
    cond_back = lax.all_to_all(cond_part.astype(LOW).reshape(shards, items, -1), "fsdp", 0, 0)
    early_every = across_replicas(early_group, early_far)
    shard_early = dot_left(every_act, early_every[:, :early])
    shard_early = hold(plans, shard_early)
    shard_ada = jnp.concatenate([shard_early, shard_late], axis=1)
    bias_sums = jnp.concatenate(
        [
            jnp.sum(early_every[:, :early].astype(WIDE), axis=0),
            jnp.sum(late_every.astype(WIDE), axis=0),
        ],
        axis=0,
    )
    shard_bias = lax.dynamic_slice(
        bias_sums, (fsdp_place * ada_bias.shape[0],), (ada_bias.shape[0],)
    )
    gain_sums = jnp.sum(early_every[:, early:].astype(WIDE), axis=0)[: 2 * hd]
    cond_back = hold(plans, cond_back)
    s_tail.last_core()
    grad_cond_act = cond_back.swapaxes(0, 1).reshape(items, width).astype(WIDE)
    grad_condition = silu_pull(grad_cond_act)[0]
    if s_head.fast:
        shard_qkv, shard_proj = finish(core_place, s_head.live, s_tail.live, hd, width)
    else:
        shard_qkv = jnp.concatenate(s_head.halves() + s_tail.halves(), axis=1)
        shard_qkv = from_parts(shard_qkv, heads, hd)
        shard_proj = jnp.concatenate(s_proj.halves(), axis=1)[:, :width]
    shard_gate_up = shard_wide
    return (
        block_out[None],
        grad_input[None],
        grad_condition[None],
        shard_ada,
        shard_bias,
        shard_qkv,
        gain_sums[:hd],
        gain_sums[hd:],
        shard_proj,
        shard_gate_up,
        shard_down,
    )


def solution(mesh):
    return jax.shard_map(
        local,
        mesh=mesh,
        in_specs=(
            P(("rep", "fsdp"), None, None),
            P(("rep", "fsdp"), None, None),
            P(("rep", "fsdp"), None),
            P(("rep", "fsdp"), None),
            P("fsdp", None),
            P("fsdp"),
            P("fsdp", None),
            P(),
            P(),
            P("fsdp", None),
            P("fsdp", None),
            P("fsdp", None),
            P(("rep", "fsdp"), None, None),
        ),
        out_specs=(
            P(("rep", "fsdp"), None, None),
            P(("rep", "fsdp"), None, None),
            P(("rep", "fsdp"), None, None),
            P("fsdp", None),
            P("fsdp"),
            P("fsdp", None),
            P(),
            P(),
            P("fsdp", None),
            P("fsdp", None),
            P("fsdp", None),
        ),
        check_vma=False,
    )
```

```python
import functools
from functools import partial

import jax
import jax.numpy as jnp
from jax import lax
from jax.experimental import pallas as pl
from jax.experimental.pallas import tpu as pltpu
from jax.sharding import PartitionSpec as P

EPSILON = 1e-06
WIDE = jnp.float32
LOW = jnp.bfloat16
AXES = ("rep", "fsdp")
HIGH_Z = 4
PARTS = 3
BLOCK = 256
LANES = 128
GROUP = 4
MASK = 4096.0
MIB = 2**20


def dot(left, right):
    return jnp.dot(left, right, preferred_element_type=WIDE)


def dot_left(left, right):
    return lax.dot_general(left, right, (((0,), (0,)), ((), ())), preferred_element_type=WIDE)


def dot_right(left, right):
    return lax.dot_general(left, right, (((1,), (1,)), ((), ())), preferred_element_type=WIDE)


def layer_norm(values):
    centred = values - jnp.mean(values, axis=-1, keepdims=True)
    return centred * lax.rsqrt(jnp.mean(centred * centred, axis=-1, keepdims=True) + EPSILON)


def modulated(values, shift_part, scale_part):
    return layer_norm(values) * (1.0 + scale_part) + shift_part


def layout(lengths_row, widths_row, length):
    seg_count = lengths_row.shape[0]
    item_ends = jnp.cumsum(lengths_row)
    item_starts = item_ends - lengths_row
    token_place = jnp.arange(length, dtype=jnp.int32)[:, None]
    member = ((token_place >= item_starts[None, :]) & (token_place < item_ends[None, :])).astype(
        jnp.int32
    )
    segment = jnp.sum(member * jnp.arange(seg_count, dtype=jnp.int32)[None, :], axis=1)
    offset = token_place[:, 0] - jnp.sum(member * item_starts[None, :], axis=1)
    across = jnp.sum(member * widths_row[None, :], axis=1)
    return (member, segment, offset // across, offset % across)


def device_index(x, core, z, y):
    return (x * 2 + core) * 8 + z * 2 + y


PLACES = [(x, c, z, y) for x in range(2) for c in range(2) for z in range(4) for y in range(2)]
TO_CORE = [(device_index(x, c, z, y), device_index(x, 1 - c, z, y)) for x, c, z, y in PLACES]
TO_X = [(device_index(x, c, z, y), device_index(1 - x, c, z, y)) for x, c, z, y in PLACES]
TO_Y = [(device_index(x, c, z, y), device_index(x, c, z, 1 - y)) for x, c, z, y in PLACES]
TO_Z = [
    [(device_index(x, c, z, y), device_index(x, c, (z + k) % 4, y)) for x, c, z, y in PLACES]
    for k in range(4)
]
Z_GROUPS = [[0, 2, 4, 6], [1, 3, 5, 7]]


def coordinates():
    replica = lax.axis_index("rep")
    shard = lax.axis_index("fsdp")
    return replica // 2, replica % 2, shard // 2, shard % 2


def is_fast():
    return lax.axis_size("rep") == 4 and lax.axis_size("fsdp") == 8


def pick(operand, index, axis):
    return lax.dynamic_index_in_dim(operand, index, axis, keepdims=False)


def over_z(operand):
    return lax.all_to_all(operand, "fsdp", 0, 0, axis_index_groups=Z_GROUPS)


def hold(plans, values):
    flat, tree = jax.tree.flatten(([plan.live for plan in plans], values))
    flat = lax.optimization_barrier(flat)
    lives, values = jax.tree.unflatten(tree, flat)
    for plan, live in zip(plans, lives):
        plan.live = live
    return values


def place_pieces(shape, apart, where, pieces, out, sems):
    x, core, z, y = where[0], where[1], where[2], where[3]
    a0, a1, ax, b0, b1, bx = pieces
    rows, half = shape[0] // 8, shape[1] // 2
    h = rows // PARTS
    copies = []
    for p0, p1, px, c in ((a0, a1, ax, core), (b0, b1, bx, 1 - core)):
        for q in range(HIGH_Z):
            for source, yy, third in (
                (p0.at[q, 0], y, x),
                (p0.at[q, 1], y, 2),
                (p1.at[q, 0], 1 - y, x),
                (p1.at[q, 1], 1 - y, 2),
                (px.at[q, 0], y, 1 - x),
                (px.at[q, 1], 1 - y, 1 - x),
            ):
                zz = (z + HIGH_Z - q) % HIGH_Z if apart else q
                row = pl.multiple_of((2 * zz + yy) * rows + third * h, 16)
                column = pl.multiple_of(c * half, LANES)
                target = out.at[pl.ds(row, h), pl.ds(column, half)]
                copy = pltpu.make_async_copy(source, target, sems.at[len(copies)])
                copy.start()
                copies.append(copy)
    for copy in copies:
        copy.wait()


def placing(kernel, shape, apart, before, after):
    def run(where, *refs):
        pieces, refs = refs[:6], refs[6:]
        inputs, rest = refs[: before + after], refs[before + after :]
        *rest, laid, sems, out_sem = rest
        outs, full, scratch = rest[0], rest[1], rest[2:]
        step = pl.program_id(0)

        @pl.when(step == 0)
        def _():
            place_pieces(shape, apart, where, pieces, laid, sems)
            pltpu.make_async_copy(laid, full, out_sem).start()

        kernel(*inputs[:before], laid, *inputs[before:], *outs, *scratch)

        @pl.when(step == pl.num_programs(0) - 1)
        def _():
            pltpu.make_async_copy(laid, full, out_sem).wait()

    return run


def call_placed(kernel, gather, args, specs, before, out_shape, out_specs, scratch, **options):
    if not gather.fast:
        weight = gather.whole()
        args = (*args[:before], weight, *args[before:])
        specs = [*specs[:before], whole_block(weight), *specs[before:]]
        got = pl.pallas_call(
            kernel, in_specs=specs, out_shape=out_shape, out_specs=out_specs,
            scratch_shapes=scratch, **options,
        )(*args)
        return (*got, weight)
    shape = (8 * gather.rows, gather.width)
    count = len(out_shape)
    inner = placing(kernel, shape, gather.apart, before, len(args) - before)

    def run(*refs):
        at = 7 + len(args)
        inner(*refs[:at], refs[at : at + count], *refs[at + count :])

    any_space = pl.BlockSpec(memory_space=pl.ANY)
    live = gather.live
    pieces = [live[k] for k in ("own", "far", "both", "twin_own", "twin_far", "twin_both")]
    return pl.pallas_call(
        run,
        in_specs=[pl.BlockSpec(memory_space=pltpu.SMEM)] + [any_space] * 6 + list(specs),
        out_shape=list(out_shape) + [jax.ShapeDtypeStruct(shape, LOW)],
        out_specs=list(out_specs) + [any_space],
        scratch_shapes=list(scratch)
        + [pltpu.VMEM(shape, LOW), pltpu.SemaphoreType.DMA((48,)), pltpu.SemaphoreType.DMA],
        **options,
    )(jnp.stack(coordinates()).astype(jnp.int32), *pieces, *args)


class Gather:
    def __init__(self, weight):
        self.rows, self.width = weight.shape
        self.live = {"weight": weight}
        self.fast = is_fast() and self.rows % 48 == 0

    def z(self, apart=False):
        if not self.fast:
            return
        self.apart = apart
        x, core, _, _ = coordinates()
        h, half = self.rows // PARTS, self.width // 2
        weight = self.live.pop("weight")
        mine = lax.dynamic_slice_in_dim(weight, core * half, half, 1).reshape(PARTS, h, half)
        base = jnp.stack([pick(mine, x, 0), mine[2]], 0)
        if apart:
            lines = [base] + [lax.ppermute(base, AXES, TO_Z[k]) for k in (1, 2, 3)]
            self.live["own"] = jnp.stack(lines, 0)
            return
        self.live["own"] = over_z(jnp.broadcast_to(base, (HIGH_Z, 2, h, half)))

    def y(self):
        if self.fast:
            self.live["far"] = lax.ppermute(self.live["own"], AXES, TO_Y)

    def x(self):
        if self.fast:
            ends = jnp.stack([self.live["own"][:, 0], self.live["far"][:, 0]], 1)
            self.live["both"] = lax.ppermute(ends, AXES, TO_X)

    def core(self, *names):
        if self.fast:
            for name in names:
                self.live["twin_" + name] = lax.ppermute(self.live[name], AXES, TO_CORE)

    def whole(self):
        return lax.all_gather(self.live["weight"], "fsdp", axis=0, tiled=True)


class Scatter:
    def __init__(self, left, send=None, keep=None, pair=None):
        self.left, self.fast = left, is_fast() and left.shape[1] % 384 == 0
        self.live = {"send": send, "keep": keep} if pair is None else {"pair": pair}

    def operand(self, name):
        if "pair" in self.live:
            return self.live["pair"][("send", "keep").index(name)]
        return self.live[name]

    def first(self):
        live = self.live
        if self.fast:
            live["out"] = dot_left(self.left, self.operand("send")).astype(LOW)
            live.pop("send", None)

    def core(self):
        if self.fast:
            self.live["got"] = lax.ppermute(self.live.pop("out"), AXES, TO_CORE)

    def second(self):
        live = self.live
        if self.fast:
            product = dot_left(self.left, self.operand("keep"))
            live["kept"] = (product + live.pop("got").astype(WIDE)).astype(LOW)
            live.pop("keep", None)

    def join(self, other):
        if self.fast:
            kept = [self.live["kept"], other.live.pop("kept")]
            self.live["kept"] = jnp.concatenate(kept, axis=1)

    def view(self):
        rows, half = self.live["kept"].shape
        return self.live["kept"].reshape(HIGH_Z, 2, PARTS, rows // 24, half)

    def cut(self, start, sizes):
        view = self.view()
        return lax.dynamic_slice(view, (*start, 0, 0), (*sizes, *view.shape[3:])).reshape(
            tuple(k for k in sizes if k > 1) + view.shape[3:]
        )

    def x(self, half=None):
        if not self.fast:
            return
        x, _, _, _ = coordinates()
        if half is None:
            self.live["side"] = lax.ppermute(
                self.cut((0, 0, 1 - x), (HIGH_Z, 2, 1)), AXES, TO_X
            )
        else:
            self.live["side_" + str(half)] = lax.ppermute(
                self.cut((2 * half, 0, 1 - x), (2, 2, 1)), AXES, TO_X
            )

    def own(self, index):
        x, _, _, _ = coordinates()
        live = self.live
        sides = [live["side"]] if "side" in live else [live["side_0"], live["side_1"]]
        sides = [pick(side, index, 1) for side in sides]
        side = jnp.concatenate(sides, 0) if len(sides) > 1 else sides[0]
        mine = self.cut((0, index, x), (HIGH_Z, 1, 1))
        return (mine.astype(WIDE) + side.astype(WIDE)).astype(LOW)

    def common(self, index):
        return self.cut((0, index, 2), (HIGH_Z, 1, 1))

    def y_common(self):
        if self.fast:
            _, _, _, y = coordinates()
            self.live["far_common"] = lax.ppermute(self.common(1 - y), AXES, TO_Y)

    def y_own(self):
        if self.fast:
            _, _, _, y = coordinates()
            self.live["far_own"] = lax.ppermute(self.own(1 - y), AXES, TO_Y)

    def y_both(self):
        if self.fast:
            _, _, _, y = coordinates()
            both = jnp.stack([self.own(1 - y), self.common(1 - y)], 1)
            self.live["far_both"] = lax.ppermute(both, AXES, TO_Y)

    def line(self, name):
        _, _, _, y = coordinates()
        mine = self.common(y) if name == "common" else self.own(y)
        if "far_both" in self.live:
            far = self.live["far_both"][:, 1 if name == "common" else 0]
        else:
            far = self.live.pop("far_" + name)
        return (mine.astype(WIDE) + far.astype(WIDE)).astype(LOW)

    def z_common(self):
        if self.fast:
            self.live["sum_common"] = {"all": over_z(self.line("common"))}

    def z_own(self, apart=False):
        if not self.fast:
            return
        line = self.line("own")
        self.forget()
        if not apart:
            self.live["sum_own"] = {"all": over_z(line)}
            return
        _, _, z, _ = coordinates()
        lines = {"0": pick(line, z, 0)}
        for k in (2, 1, 3):
            lines[str(k)] = lax.ppermute(pick(line, (z + k) % 4, 0), AXES, TO_Z[k])
        self.live["sum_own"] = lines

    def z_both(self):
        if self.fast:
            lines = jnp.stack([self.line("own"), self.line("common")], 1)
            self.forget()
            self.live["sum_both"] = {"all": over_z(lines)}

    def forget(self):
        for name in ("kept", "side", "side_0", "side_1", "far_both"):
            self.live.pop(name, None)

    def total(self, name):
        lines = self.live.pop(name)
        if "all" in lines:
            return jnp.sum(lines["all"].astype(WIDE), axis=0).astype(LOW)
        wide = [lines[k].astype(WIDE) for k in ("0", "1", "2", "3")]
        return (wide[0] + wide[1] + wide[2] + wide[3]).astype(LOW)

    def last_x(self):
        if self.fast:
            if "sum_both" in self.live:
                part = self.total("sum_both")
            else:
                part = jnp.stack([self.total("sum_own"), self.total("sum_common")], 0)
            self.live = {"part": part, "other": lax.ppermute(part, AXES, TO_X)}

    def last_core(self):
        if self.fast:
            x, _, _, _ = coordinates()
            part, other = self.live["part"], self.live["other"]
            shared = (part[1].astype(WIDE) + other[1].astype(WIDE)).astype(LOW)
            first = jnp.where(x == 0, part[0], other[0])
            second = jnp.where(x == 0, other[0], part[0])
            done = jnp.concatenate([first, second, shared], 0)
            self.live = {"done": done, "twin": lax.ppermute(done, AXES, TO_CORE)}

    def halves(self):
        if self.fast:
            _, core, _, _ = coordinates()
            done, twin = self.live["done"], self.live["twin"]
            first = jnp.where(core == 0, done, twin)
            second = jnp.where(core == 0, twin, done)
            return first.astype(WIDE), second.astype(WIDE)
        _, core, _, _ = coordinates()
        left = self.left
        keep, send = self.operand("keep"), self.operand("send")
        first = jnp.where(core == 0, keep, send)
        second = jnp.where(core == 0, send, keep)
        sums = []
        for columns in (first, second):
            grad = dot_left(left, columns).astype(LOW)
            part = lax.psum_scatter(grad, "fsdp", scatter_dimension=0, tiled=True)
            sums.append(lax.psum(part, "rep").astype(WIDE))
        return sums[0], sums[1]


def column_halves(array):
    _, core, _, _ = coordinates()
    half = array.shape[1] // 2
    send = lax.dynamic_slice_in_dim(array, (1 - core) * half, half, 1)
    keep = lax.dynamic_slice_in_dim(array, core * half, half, 1)
    return send, keep


def across_x(rows):
    return lax.ppermute(rows, AXES, TO_X) if is_fast() else rows


def across_replicas(rows, far):
    if not is_fast():
        return lax.all_gather(rows, "rep", axis=0, tiled=True)
    x, core, _, _ = coordinates()
    count, width = rows.shape
    line = jnp.stack([jnp.where(x == 0, rows, far), jnp.where(x == 0, far, rows)], 0)
    twin = lax.ppermute(line, AXES, TO_CORE)
    every = [jnp.where(core == 0, line, twin), jnp.where(core == 0, twin, line)]
    return jnp.stack(every, 1).reshape(4 * count, width)


def gather_rows(rows):
    shards = lax.axis_size("fsdp")
    count, width = rows.shape
    group = lax.all_to_all(jnp.broadcast_to(rows, (shards, count, width)), "fsdp", 0, 0)
    return group.reshape(shards * count, width)


def exchange(rows):
    shards = lax.axis_size("fsdp")
    count, width = rows.shape
    shaped = rows.reshape(count, shards, width // shards).swapaxes(0, 1)
    return lax.all_to_all(shaped, "fsdp", 0, 0).reshape(shards * count, width // shards)


def sum_back(partial_rows, count):
    shards = lax.axis_size("fsdp")
    shaped = partial_rows.astype(LOW).reshape(shards, count, -1)
    got = lax.all_to_all(shaped, "fsdp", 0, 0)
    return jnp.sum(got.astype(WIDE), axis=0)


def whole_block(array):
    return pl.BlockSpec(
        array.shape, lambda i: (0,) * array.ndim, pipeline_mode=pl.Buffered(1)
    )


def part_width(hd):
    return -(-3 * GROUP * hd // LANES) * LANES


def prepare_kernel(
    first, heads, hd, x_ref, hot_ref, mod_ref, w_ref, gq_ref, gk_ref, rot_ref, qt_ref, kt_ref,
    vt_ref, *refs
):
    normed_ref, q_ref, k_ref, v_ref, rq_ref, rk_ref, wide_ref = refs if first else (x_ref, *refs)
    step = part_width(hd)
    if first:
        width = x_ref.shape[1]
        hot = hot_ref[...]
        shift = dot(hot, mod_ref[:, :width])
        scale = dot(hot, mod_ref[:, width : 2 * width])
        normed, _ = normed_rows(x_ref[...].astype(WIDE))
        normed = (normed * (1.0 + scale) + shift).astype(LOW)
        normed_ref[...] = normed
    else:
        normed = x_ref[...]
    cosine, plus, minus = rot_ref[0], rot_ref[1], rot_ref[2]
    lane = lax.broadcasted_iota(jnp.int32, (BLOCK, LANES), 1)
    inside = lane < hd
    ones = jnp.full((LANES, LANES), 1.0, LOW)
    wide_ref[:, step:] = jnp.zeros((BLOCK, LANES), WIDE)
    for part in range(heads // GROUP):
        wide_ref[:, :step] = dot(normed, w_ref[:, part * step : (part + 1) * step])
        for kind, (g_ref, t_ref, o_ref, r_ref) in enumerate(
            (
                (gq_ref, qt_ref, q_ref, rq_ref),
                (gk_ref, kt_ref, k_ref, rk_ref),
                (None, vt_ref, v_ref, None),
            )
        ):
            tail = t_ref[...]
            for g in range(GROUP):
                h = part * GROUP + g
                at = (kind * GROUP + g) * hd
                raw = jnp.where(inside, wide_ref[:, at : at + LANES], 0.0)
                if kind < 2:
                    r_ref[h] = raw.astype(LOW)
                    total = dot((raw * raw).astype(LOW), ones)
                    u = raw * lax.rsqrt(total * (1.0 / hd) + EPSILON) * g_ref[...]
                    up = pltpu.roll(u, LANES - hd // 4, 1)
                    down = pltpu.roll(u, hd // 4, 1)
                    raw = u * cosine + up * plus + down * minus
                o_ref[h] = raw.astype(LOW) + tail


def prepare(first, x, hot, mod, gather, gq, gk, rot, qt, kt, vt, heads, hd):
    n, width = x.shape
    rows = pl.BlockSpec((BLOCK, width), lambda i: (i, 0))
    head_spec = pl.BlockSpec((heads, BLOCK, LANES), lambda i: (0, i, 0))
    tail = pl.BlockSpec((BLOCK, LANES), lambda i: (i, 0))
    normed_spec, normed_shape = [rows], [jax.ShapeDtypeStruct((n, width), LOW)]
    return call_placed(
        partial(prepare_kernel, first, heads, hd),
        gather,
        (x, hot, mod, gq, gk, rot, qt, kt, vt),
        [
            rows,
            pl.BlockSpec((BLOCK, hot.shape[1]), lambda i: (i, 0)),
            whole_block(mod),
            whole_block(gq),
            whole_block(gk),
            pl.BlockSpec((3, BLOCK, LANES), lambda i: (0, i, 0)),
            tail,
            tail,
            pl.BlockSpec((1, LANES), lambda i: (0, 0)),
        ],
        3,
        (normed_shape if first else []) + [jax.ShapeDtypeStruct((heads, n, LANES), LOW)] * 5,
        (normed_spec if first else []) + [head_spec] * 5,
        [pltpu.VMEM((BLOCK, part_width(hd) + LANES), WIDE)],
        grid=(n // BLOCK,),
        compiler_params=pltpu.CompilerParams(vmem_limit_bytes=56 * MIB),
        cost_estimate=pl.CostEstimate(
            flops=12 * n * width * width // 2, bytes_accessed=20 * MIB, transcendentals=0
        ),
        name="prepare",
    )


def near_blocks(run):
    i = pl.program_id(0)
    n = pl.num_programs(0)

    @pl.when(i == 0)
    def _():
        run(pl.ds(0, 2 * BLOCK))

    @pl.when(i == n - 1)
    def _():
        run(pl.ds(pl.multiple_of((i - 1) * BLOCK, BLOCK), 2 * BLOCK))

    @pl.when((i > 0) & (i < n - 1))
    def _():
        run(pl.ds(pl.multiple_of((i - 1) * BLOCK, BLOCK), 3 * BLOCK))


def attend_kernel(hd, c, *refs):
    mix_ref = refs[6]
    lane = lax.broadcasted_iota(jnp.int32, (BLOCK, LANES), 1)
    heads = refs[0].shape[0]

    def run(at):
        for head in range(2 * heads):
            half, h = head // heads, head % heads
            q_ref, k_ref, v_ref = refs[3 * half : 3 * half + 3]
            q = q_ref[h]
            p = jnp.exp2(dot_right(q, k_ref[h, at]) * c).astype(LOW)
            total = dot(p, v_ref[h, at])
            norm = total[:, hd : hd + 1]
            out = (total * (1.0 / norm)).astype(LOW)
            mix_ref[:, hd * head : hd * (head + 1)] = out[:, :hd]
            rest = jnp.log2(norm) * (1.0 / c)
            first = rest.astype(LOW).astype(WIDE)
            rest = rest - first
            second = rest.astype(LOW).astype(WIDE)
            third = rest - second
            logs = jnp.where(lane == hd + 8, first, jnp.where(lane == hd + 9, second, third))
            marked = jnp.where((lane >= hd + 8) & (lane < hd + 11), logs.astype(LOW), q)
            refs[7 + half][h] = marked

    near_blocks(run)


def attend(one, two, hd, c):
    heads, n, _ = one[0].shape
    full = pl.BlockSpec((heads, n, LANES), lambda i: (0, 0, 0), pipeline_mode=pl.Buffered(1))
    block = pl.BlockSpec((heads, BLOCK, LANES), lambda i: (0, i, 0))
    width = 2 * heads * hd
    return pl.pallas_call(
        partial(attend_kernel, hd, c),
        grid=(n // BLOCK,),
        in_specs=[block, full, full] * 2,
        out_specs=[pl.BlockSpec((BLOCK, width), lambda i: (i, 0)), block, block],
        out_shape=[jax.ShapeDtypeStruct((n, width), LOW)]
        + [jax.ShapeDtypeStruct((heads, n, LANES), LOW)] * 2,
        compiler_params=pltpu.CompilerParams(vmem_limit_bytes=56 * MIB),
        cost_estimate=pl.CostEstimate(
            flops=8 * n * 640 * LANES * heads,
            bytes_accessed=20 * MIB,
            transcendentals=2 * heads * n * 640,
        ),
        name="attend",
    )(*one, *two)


def spread_kernel(heads, hd, proj_at, ga_ref, w_ref, mix_ref, out_ref, grad_scr, mix_scr):
    width = heads * hd
    grad_scr[:, width:] = jnp.zeros((BLOCK, LANES), WIDE)
    mix_scr[:, width:] = jnp.zeros((BLOCK, LANES), WIDE)
    grad_scr[:, :width] = dot_right(ga_ref[:, :width], w_ref[:, proj_at : proj_at + width]).astype(LOW).astype(WIDE)
    mix_scr[:, :width] = mix_ref[...].astype(WIDE)
    lane = lax.broadcasted_iota(jnp.int32, (BLOCK, LANES), 1)
    ones = jnp.full((LANES, LANES), 1.0, LOW)
    for h in range(heads):
        at = hd * h
        grad = jnp.where(lane < hd, grad_scr[:, at : at + LANES], 0.0)
        product = grad * mix_scr[:, at : at + LANES]
        high = product.astype(LOW)
        rest = (product - high.astype(WIDE)).astype(LOW)
        delta = -(dot(high, ones) + dot(rest, ones))
        first = delta.astype(LOW)
        second = (delta - first.astype(WIDE)).astype(LOW)
        out_ref[h] = jnp.where(
            lane == hd, first, jnp.where(lane == hd + 1, second, grad.astype(LOW))
        )


def spread(ga, w, mix, heads, hd, proj_at):
    n = ga.shape[0]
    width = heads * hd
    row = pl.BlockSpec((BLOCK, width), lambda i: (i, 0))
    wide_row = pl.BlockSpec((BLOCK, ga.shape[1]), lambda i: (i, 0))
    return pl.pallas_call(
        partial(spread_kernel, heads, hd, proj_at),
        grid=(n // BLOCK,),
        in_specs=[wide_row, whole_block(w), row],
        out_specs=pl.BlockSpec((heads, BLOCK, LANES), lambda i: (0, i, 0)),
        out_shape=jax.ShapeDtypeStruct((heads, n, LANES), LOW),
        scratch_shapes=[
            pltpu.VMEM((BLOCK, width + LANES), WIDE),
            pltpu.VMEM((BLOCK, width + LANES), WIDE),
        ],
        compiler_params=pltpu.CompilerParams(vmem_limit_bytes=56 * MIB),
        cost_estimate=pl.CostEstimate(
            flops=2 * n * width * width, bytes_accessed=12 * MIB, transcendentals=0
        ),
        name="spread",
    )(ga, w, mix)


def back_kernel(
    hd, c, score_scale, part, core_ref, q_ref, k_ref, v_ref, do_ref, rq_ref, rk_ref, rot_ref, gq_ref, gk_ref,
    *refs,
):
    out_ref, gain_ref, joint_ref, dq_scr, dk_scr, dv_scr, gain_scr, out_sem = refs[part:]
    i = pl.program_id(0)
    n = pl.num_programs(0)
    heads = q_ref.shape[0]
    width = GROUP * hd
    tail = joint_ref.shape[1] - 3 * width
    slot = core_ref[0] if part else 1 - core_ref[0]

    @pl.when(i == 0)
    def _():
        dq_scr[...] = jnp.zeros(dq_scr.shape, WIDE)
        gain_scr[...] = jnp.zeros(gain_scr.shape, WIDE)

    ones = jnp.full((LANES, LANES), 1.0, LOW)

    def run(at):
        def body(h, carry):
            kk = k_ref[h]
            vv = v_ref[h]
            q = q_ref[h, at]
            do = do_ref[h, at]
            p = jnp.exp2(dot_right(kk, q) * c)
            dv_scr[h] = dot(p.astype(LOW), do)
            ds = (p * dot_right(vv, do)).astype(LOW)
            dk_scr[h] = dot(ds, q)
            dq_scr[h, at] += dot_left(ds, kk)
            return carry

        lax.fori_loop(0, heads, body, 0, unroll=GROUP)

    near_blocks(run)

    def finish(dy, raw, rot, gain, row):
        raw = raw.astype(WIDE)
        dy = dy * score_scale
        up = pltpu.roll(dy, LANES - hd // 4, 1)
        down = pltpu.roll(dy, hd // 4, 1)
        d = dy * rot[0] - up * rot[1] - down * rot[2]
        r = lax.rsqrt(dot((raw * raw).astype(LOW), ones) * (1.0 / hd) + EPSILON)
        u = raw * r
        ud = u * d
        gain_scr[row] += jnp.sum(ud.reshape(BLOCK // 8, 8, LANES), axis=0)
        m = dot((ud * gain).astype(LOW), ones) * (1.0 / hd)
        return (r * (gain * d - u * m)).astype(LOW)

    here = pl.ds(pl.multiple_of(i * BLOCK, BLOCK), BLOCK)
    rot = [rot_ref[t, here] for t in range(3)]
    joint_ref[here, 3 * width :] = jnp.zeros((BLOCK, tail), LOW)
    for h in range(heads):
        at = hd * h
        grad = finish(dk_scr[h], rk_ref[h], rot, gk_ref[...], 1)
        joint_ref[here, width + at : width + at + hd] = grad[:, :hd]
        value = dv_scr[h].astype(LOW)
        joint_ref[here, 2 * width + at : 2 * width + at + hd] = value[:, :hd]

    @pl.when(i == n - 1)
    def _():
        def rows(b, carry):
            at = pl.ds(pl.multiple_of(b * BLOCK, BLOCK), BLOCK)
            turn = [rot_ref[t, at] for t in range(3)]
            for h in range(heads):
                start = hd * h
                grad = finish(dq_scr[h, at], rq_ref[h, at], turn, gq_ref[...], 0)
                joint_ref[at, start : start + hd] = grad[:, :hd]
            return carry

        lax.fori_loop(0, n, rows, 0)
        gain_ref[...] = gain_scr[...]
        copy = pltpu.make_async_copy(joint_ref, out_ref.at[slot], out_sem)
        copy.start()
        copy.wait()


def attend_back(half, part, before, core, q2, k, v, do, rq, rk, rot, gq, gk, hd, c, score_scale):
    _, n, _ = q2.shape
    one = pl.Buffered(1)
    full = pl.BlockSpec((GROUP, n, LANES), lambda i: (part, 0, 0), pipeline_mode=one)
    block = pl.BlockSpec((GROUP, BLOCK, LANES), lambda i: (part, i, 0))
    small = pl.BlockSpec((1, LANES), lambda i: (0, 0))
    any_space = pl.BlockSpec(memory_space=pl.ANY)
    width = part_width(hd)
    at = 2 * half + part
    return pl.pallas_call(
        partial(back_kernel, hd, c, score_scale, part),
        grid=(n // BLOCK,),
        in_specs=[
            pl.BlockSpec(memory_space=pltpu.SMEM),
            *(full, block, block),
            pl.BlockSpec((GROUP, n, LANES), lambda i: (at, 0, 0), pipeline_mode=one),
            *(full, block, whole_block(rot), small, small),
            *([any_space] if part else []),
        ],
        out_specs=[any_space, pl.BlockSpec((2, 8, LANES), lambda i: (0, 0, 0))],
        out_shape=[
            jax.ShapeDtypeStruct((2, n, width), LOW),
            jax.ShapeDtypeStruct((2, 8, LANES), WIDE),
        ],
        scratch_shapes=[
            pltpu.VMEM((n, width), LOW),
            pltpu.VMEM((GROUP, n, LANES), WIDE),
            pltpu.VMEM((GROUP, BLOCK, LANES), WIDE),
            pltpu.VMEM((GROUP, BLOCK, LANES), WIDE),
            pltpu.VMEM((2, 8, LANES), WIDE),
            pltpu.SemaphoreType.DMA,
        ],
        input_output_aliases={10: 0} if part else {},
        compiler_params=pltpu.CompilerParams(vmem_limit_bytes=56 * MIB),
        cost_estimate=pl.CostEstimate(
            flops=10 * n * 640 * LANES * GROUP,
            bytes_accessed=10 * MIB,
            transcendentals=GROUP * n * 640,
        ),
        name="attend_back",
    )(core, q2, k, v, do, rq, rk, rot, gq, gk, *([before] if part else []))


def normed_rows(values):
    centred = values - jnp.mean(values, axis=-1, keepdims=True)
    scale = lax.rsqrt(jnp.mean(centred * centred, axis=-1, keepdims=True) + EPSILON)
    return centred * scale, scale


def norm_back(normed, scale, grad):
    inner = jnp.mean(grad * normed, axis=-1, keepdims=True)
    return scale * (grad - jnp.mean(grad, axis=-1, keepdims=True) - normed * inner)


def add_sums(out_ref, at, hot, values):
    width = values.shape[1]
    term = dot_left(hot, values.astype(LOW))
    here = (slice(None), slice(at * width, (at + 1) * width))

    @pl.when(pl.program_id(0) == 0)
    def _():
        out_ref[here] = term

    @pl.when(pl.program_id(0) > 0)
    def _():
        out_ref[here] += term


def rows_of(array):
    if array.ndim == 3:
        return pl.BlockSpec((2, BLOCK, array.shape[2]), lambda i: (0, i, 0))
    return pl.BlockSpec((BLOCK, array.shape[1]), lambda i: (i, 0))


def call_rows(
    kernel, name, streamed, fixed, outs, sums=(), core=None, scratch=(), gather=None
):
    n = streamed[0].shape[-2]
    work = sum(2 * n * a.size for a in fixed if a.shape[0] > 256)
    moved = sum(a.size * a.dtype.itemsize for a in (*streamed, *fixed))
    scalars = () if core is None else (core,)
    args = (*scalars, *streamed, *fixed)
    specs = [pl.BlockSpec(memory_space=pltpu.SMEM) for _ in scalars]
    specs += [rows_of(a) for a in streamed] + [whole_block(a) for a in fixed]
    out_specs = [pl.BlockSpec((BLOCK, w), lambda i: (i, 0)) for w, _ in outs]
    out_specs += [pl.BlockSpec(shape, lambda i: (0, 0)) for shape in sums]
    out_shape = [jax.ShapeDtypeStruct((n, w), t) for w, t in outs]
    out_shape += [jax.ShapeDtypeStruct(shape, WIDE) for shape in sums]
    scratch = [pltpu.VMEM(shape, WIDE) for shape in scratch]
    if gather is not None:
        work += 2 * n * gather.rows * lax.axis_size("fsdp") * gather.width
    options = dict(
        grid=(n // BLOCK,),
        compiler_params=pltpu.CompilerParams(vmem_limit_bytes=56 * MIB),
        cost_estimate=pl.CostEstimate(flops=work, bytes_accessed=moved, transcendentals=0),
        name=name,
    )
    if gather is not None:
        before = len(scalars) + len(streamed)
        return call_placed(
            kernel, gather, args, specs, before, out_shape, out_specs, scratch, **options
        )
    return pl.pallas_call(
        kernel, in_specs=specs, out_specs=out_specs, out_shape=out_shape, scratch_shapes=scratch,
        **options,
    )(*args)


def join_kernel(
    proj_at, mix_ref, x_ref, hot_ref, keep_ref, w_ref, mod_ref, att_ref, mid_ref, norm_ref
):
    width = x_ref.shape[1]
    hot = hot_ref[...]
    attended = dot(mix_ref[...], w_ref[:, proj_at : proj_at + width])
    att_ref[...] = attended.astype(LOW)
    gate = dot(hot, mod_ref[:, 2 * width : 3 * width]) * keep_ref[...]
    middle = x_ref[...].astype(WIDE) + gate * attended
    mid_ref[...] = middle
    normed, _ = normed_rows(middle)
    scale = dot(hot, mod_ref[:, 4 * width : 5 * width])
    shift = dot(hot, mod_ref[:, 3 * width : 4 * width])
    norm_ref[...] = (normed * (1.0 + scale) + shift).astype(LOW)


def gate_kernel(x_ref, w_ref, out_ref):
    out_ref[...] = dot(x_ref[...], w_ref[:, : out_ref.shape[1]]).astype(LOW)


def up_kernel(x_ref, gate_ref, w_ref, up_ref, inner_ref):
    up = dot(x_ref[...], w_ref[...])
    up_ref[...] = up.astype(LOW)
    gate = gate_ref[...].astype(WIDE)
    inner_ref[...] = (gate * jax.nn.sigmoid(gate) * up).astype(LOW)


def down_kernel(
    inner_ref, mid_ref, grad_ref, hot_ref, keep_ref, w_ref, mod_ref, out_ref, back_ref, sum_ref
):
    width = mid_ref.shape[1]
    hot = hot_ref[...]
    returned = dot(inner_ref[...], w_ref[:, :width])
    gate = dot(hot, mod_ref[:, 5 * width : 6 * width]) * keep_ref[...]
    out_ref[...] = (mid_ref[...] + gate * returned).astype(LOW)
    upstream = grad_ref[...].astype(WIDE)
    back_ref[:, :width] = (upstream * gate).astype(LOW)
    if back_ref.shape[1] > width:
        back_ref[:, width:] = jnp.zeros((BLOCK, back_ref.shape[1] - width), LOW)
    add_sums(sum_ref, 0, hot, upstream * keep_ref[...] * returned)


def inner_back_kernel(core_ref, grad_ref, gate_ref, up_ref, w_ref, send_ref, keep_ref):
    grad = dot_right(grad_ref[...], w_ref[...])
    gate = gate_ref[...].astype(WIDE)
    sig = jax.nn.sigmoid(gate)
    act = gate * sig
    for_gate = (grad * up_ref[...].astype(WIDE) * (sig + act * (1.0 - sig))).astype(LOW)
    for_up = (grad * act).astype(LOW)

    @pl.when(core_ref[0] == 0)
    def _():
        send_ref[...] = for_up
        keep_ref[...] = for_gate

    @pl.when(core_ref[0] != 0)
    def _():
        send_ref[...] = for_gate
        keep_ref[...] = for_up


def middle_back_kernel(
    core_ref, send_ref, mine_ref, mid_ref, grad_ref, att_ref, hot_ref, keep_ref, wg_ref, wu_ref,
    mod_ref, out_ref, back_ref, sum_ref, total_ref,
):
    width = mid_ref.shape[1]
    hot = hot_ref[...]
    keep = keep_ref[...]

    @pl.when(core_ref[0] == 0)
    def _():
        total_ref[...] = dot_right(mine_ref[...], wg_ref[:, : mine_ref.shape[1]])
        total_ref[...] += dot_right(send_ref[...], wu_ref[...])

    @pl.when(core_ref[0] != 0)
    def _():
        total_ref[...] = dot_right(send_ref[...], wg_ref[:, : send_ref.shape[1]])
        total_ref[...] += dot_right(mine_ref[...], wu_ref[...])

    grad = total_ref[...]
    normed, scale = normed_rows(mid_ref[...])
    turned = grad * (1.0 + dot(hot, mod_ref[:, 4 * width : 5 * width]))
    total = grad_ref[...].astype(WIDE) + norm_back(normed, scale, turned)
    out_ref[...] = total
    gate = dot(hot, mod_ref[:, 2 * width : 3 * width]) * keep
    back_ref[:, :width] = (total * gate).astype(LOW)
    if back_ref.shape[1] > width:
        back_ref[:, width:] = jnp.zeros((BLOCK, back_ref.shape[1] - width), LOW)
    add_sums(sum_ref, 0, hot, total * keep * att_ref[...].astype(WIDE))
    add_sums(sum_ref, 1, hot, grad)
    add_sums(sum_ref, 2, hot, grad * normed)


def input_back_kernel(
    core_ref, one_ref, two_ref, mid_ref, x_ref, hot_ref, wo_ref, wt_ref, mod_ref, out_ref, sum_ref
):
    width = x_ref.shape[1]
    hot = hot_ref[...]
    step = one_ref.shape[2]
    core = core_ref[0]
    grad = None
    for ref, w_ref in ((one_ref, wo_ref), (two_ref, wt_ref)):
        term = dot_right(ref[1 - core], w_ref[:, :step]) + dot_right(ref[core], w_ref[:, step : 2 * step])
        grad = term if grad is None else grad + term
    normed, scale = normed_rows(x_ref[...].astype(WIDE))
    turned = grad * (1.0 + dot(hot, mod_ref[:, width : 2 * width]))
    out_ref[...] = mid_ref[...] + norm_back(normed, scale, turned)
    add_sums(sum_ref, 0, hot, grad)
    add_sums(sum_ref, 1, hot, grad * normed)


def finish_kernel(hd, core_ref, head_done, head_twin, tail_done, tail_twin, qkv_ref, proj_ref):
    step = part_width(hd)
    short = GROUP * hd
    total = qkv_ref.shape[1] // 3

    def write(sources):
        for part, source in enumerate(sources):
            values = source[:, :step].astype(WIDE)
            for kind in range(3):
                at = kind * total + part * short
                qkv_ref[:, at : at + short] = values[:, kind * short : (kind + 1) * short]
        half = sources[0].shape[1] - step
        proj_ref[:, :half] = sources[0][:, step:].astype(WIDE)
        rest = proj_ref.shape[1] - half
        proj_ref[:, half:] = sources[1][:, step : step + rest].astype(WIDE)

    @pl.when(core_ref[0] == 0)
    def _():
        write((head_done, head_twin, tail_done, tail_twin))

    @pl.when(core_ref[0] != 0)
    def _():
        write((head_twin, head_done, tail_twin, tail_done))


def finish(core, head, tail, hd, width):
    rows = head["done"].shape[0]
    return pl.pallas_call(
        partial(finish_kernel, hd),
        in_specs=[pl.BlockSpec(memory_space=pltpu.SMEM)]
        + [pl.BlockSpec(memory_space=pltpu.VMEM)] * 4,
        out_specs=[pl.BlockSpec(memory_space=pltpu.VMEM)] * 2,
        out_shape=[
            jax.ShapeDtypeStruct((rows, 3 * width), WIDE),
            jax.ShapeDtypeStruct((rows, width), WIDE),
        ],
        compiler_params=pltpu.CompilerParams(vmem_limit_bytes=40 * MIB),
        name="finish",
    )(core, head["done"], head["twin"], tail["done"], tail["twin"])


def turn_tables(row_place, column_place, hd):
    quarter = hd // 4
    inverse = 10000.0 ** (-jnp.arange(quarter, dtype=WIDE) / quarter)
    row_angle = row_place.astype(WIDE)[:, None] * inverse[None, :]
    column_angle = column_place.astype(WIDE)[:, None] * inverse[None, :]
    rest = jnp.zeros((row_place.shape[0], LANES - hd), WIDE)
    none = jnp.zeros_like(row_angle)
    rc, rs = jnp.cos(row_angle), jnp.sin(row_angle)
    cc, cs = jnp.cos(column_angle), jnp.sin(column_angle)
    return jnp.stack(
        [
            jnp.concatenate([rc, rc, cc, cc, rest], 1),
            jnp.concatenate([-rs, none, -cs, none, rest], 1),
            jnp.concatenate([none, rs, none, cs, rest], 1),
        ],
        0,
    )


def high_and_rest(values):
    high = values.astype(LOW)
    return jnp.concatenate([high, (values - high.astype(WIDE)).astype(LOW)], axis=0)


def pad_columns(array, width):
    return jnp.pad(array, ((0, 0), (0, width - array.shape[1])))


def to_parts(array, heads, hd):
    rows = array.shape[0]
    shaped = array.reshape(rows, 3, heads // GROUP, GROUP * hd).swapaxes(1, 2)
    shaped = shaped.reshape(rows, heads // GROUP, 3 * GROUP * hd)
    padded = jnp.pad(shaped, ((0, 0), (0, 0), (0, part_width(hd) - 3 * GROUP * hd)))
    return padded.reshape(rows, -1)


def from_parts(array, heads, hd):
    rows = array.shape[0]
    shaped = array.reshape(rows, heads // GROUP, -1)[:, :, : 3 * GROUP * hd]
    shaped = shaped.reshape(rows, heads // GROUP, 3, GROUP * hd).swapaxes(1, 2)
    return shaped.reshape(rows, -1)


def local(
    block_in,
    condition,
    item_lengths,
    item_widths,
    ada_weight,
    ada_bias,
    qkv_weight,
    query_gain,
    key_gain,
    proj_weight,
    gate_up_weight,
    down_weight,
    out_grad,
):
    _, n, width = block_in.shape
    items = item_lengths.shape[1]
    hd = query_gain.shape[0]
    heads = width // hd
    ff = down_weight.shape[0] * lax.axis_size("fsdp")
    score_scale = float(hd) ** (-0.5)
    c = score_scale * 1.4426950408889634
    shards = lax.axis_size("fsdp")
    fsdp_place = lax.axis_index("fsdp")
    odd = width + LANES if (width // LANES) % 2 else width

    qkv_parts = to_parts(qkv_weight, heads, hd)
    cut = qkv_parts.shape[1] // 2
    g_one = Gather(qkv_parts[:, :cut])
    g_two = Gather(jnp.concatenate([qkv_parts[:, cut:], pad_columns(proj_weight, odd)], axis=1))
    g_gate = Gather(gate_up_weight[:, :ff])
    g_up = Gather(gate_up_weight[:, ff:])
    g_down = Gather(pad_columns(down_weight, odd))
    gathers = [g_one, g_two, g_gate, g_up, g_down]
    core_place = (lax.axis_index("rep") % 2).astype(jnp.int32).reshape(1)

    cond_float = condition.astype(WIDE).reshape(items, width)
    cond_silu, silu_pull = jax.vjp(jax.nn.silu, cond_float)
    cond_act = cond_silu.astype(LOW)

    g_one.z()
    group_act = exchange(cond_act)
    member, segment, row_place, column_place = layout(item_lengths[0], item_widths[0], n)
    member_low = member.astype(LOW)
    keep = (segment < items - 1).astype(WIDE).reshape(n, 1)
    rot = turn_tables(row_place, column_place, hd)
    spare = jnp.zeros((n, LANES - hd - items), LOW)
    ones_at = jnp.zeros((n, LANES - hd - items), LOW).at[:, :3].set(-1.0)
    blank = jnp.zeros((n, hd), LOW)
    query_tail = jnp.concatenate([blank, member_low, spare], 1)
    key_tail = jnp.concatenate([blank, (member_low - 1.0) * MASK, ones_at], 1)
    value_tail = jnp.zeros((1, LANES), LOW).at[:, hd : hd + 2].set(1.0)
    gain_q = pad_columns(query_gain.astype(WIDE)[None, :], LANES)
    gain_k = pad_columns(key_gain.astype(WIDE)[None, :], LANES)
    hot = jnp.concatenate([member_low, member_low], axis=1)
    tables = (rot, query_tail, key_tail, hot, keep)
    group_act = hold(gathers, group_act)

    g_one.y()
    g_two.z()
    bias_row = lax.dynamic_update_slice(
        jnp.zeros((6 * width,), WIDE), ada_bias.astype(WIDE), (fsdp_place * ada_bias.shape[0],)
    )
    mod_part = (dot(group_act, ada_weight) + bias_row[None, :]).astype(LOW)
    act_far = across_x(group_act)
    mod_part, group_act, act_far, tables = hold(gathers, (mod_part, group_act, act_far, tables))

    early = 2 * width
    modulation = high_and_rest(sum_back(mod_part, items))
    g_one.x()
    g_one.core("own", "far")
    g_two.y()
    inputs_low = block_in[0]
    every_act = across_replicas(group_act, act_far)
    modulation, tables, inputs_low, every_act = hold(
        gathers, (modulation, tables, inputs_low, every_act)
    )

    g_one.core("both")
    g_two.x()
    g_two.core("own", "far")
    g_gate.z()
    rot, query_tail, key_tail, hot, keep = tables
    set_out = (gain_q, gain_k, rot, query_tail, key_tail, value_tail, heads // 2, hd)
    normed_a, q_one, k_one, v_one, rq_one, rk_one, one_full = prepare(
        True, inputs_low, hot, modulation, g_one, *set_out
    )
    gathers = gathers[1:]
    normed_a, q_one, k_one, v_one, rq_one, rk_one, one_full = hold(
        gathers, (normed_a, q_one, k_one, v_one, rq_one, rk_one, one_full)
    )

    g_two.core("both")
    g_gate.y()
    g_up.z()
    q_two, k_two, v_two, rq_two, rk_two, two_full = prepare(
        False, normed_a, hot, modulation, g_two, *set_out
    )
    gathers = gathers[1:]
    normed_a, q_two, k_two, v_two, rq_two, rk_two, two_full, q_one, k_one, v_one = hold(
        gathers, (normed_a, q_two, k_two, v_two, rq_two, rk_two, two_full, q_one, k_one, v_one)
    )

    g_gate.x()
    g_gate.core("own", "far")
    g_up.y()
    g_down.z()
    mixed, q2_one, q2_two = attend((q_one, k_one, v_one), (q_two, k_two, v_two), hd, c)
    mixed, q2_one, q2_two = hold(gathers, (mixed, q2_one, q2_two))

    g_gate.core("both")
    g_up.x()
    g_up.core("own", "far")
    g_down.y()
    attended, middle, normed_b = call_rows(
        partial(join_kernel, cut), "join", (mixed, inputs_low, hot, keep), (two_full, modulation),
        ((width, LOW), (width, WIDE), (width, LOW)),
    )
    middle, normed_b, attended = hold([g_gate], (middle, normed_b, attended))

    gate, gate_full = call_rows(
        gate_kernel, "gate", (normed_b,), (), ((ff, LOW),), gather=g_gate
    )
    gathers = [g_up, g_down]
    gate, gate_full, normed_b, middle, attended = hold(
        gathers, (gate, gate_full, normed_b, middle, attended)
    )

    g_up.core("both")
    g_down.x()
    g_down.core("own", "far")
    normed_b = hold([g_up], normed_b)
    up, inner, up_full = call_rows(
        up_kernel, "up", (normed_b, gate), (), ((ff, LOW), (ff, LOW)), gather=g_up
    )
    gathers = [g_down]
    inner, up, gate, up_full, middle = hold(gathers, (inner, up, gate, up_full, middle))

    g_down.core("both")
    block_out, grad_returned, sums_gate_b, down_full = call_rows(
        down_kernel, "down", (inner, middle, out_grad[0], hot, keep), (modulation,),
        ((width, LOW), (odd, LOW)), ((2 * items, width),), gather=g_down,
    )

    s_down = Scatter(inner, *column_halves(grad_returned))
    s_down.first()
    plans = [s_down]
    grad_returned, down_full, gate, up, gate_full, up_full, normed_b, middle, attended = hold(
        plans,
        (grad_returned, down_full, gate, up, gate_full, up_full, normed_b, middle, attended),
    )

    s_down.core()
    grad_send, grad_keep = call_rows(
        inner_back_kernel, "inner_back", (grad_returned, gate, up), (down_full,),
        ((ff, LOW), (ff, LOW)), core=core_place,
    )
    grad_send, grad_keep = hold(plans, (grad_send, grad_keep))

    s_down.second()
    s_wide = Scatter(normed_b, grad_send, grad_keep)
    s_wide.first()
    plans = [s_down, s_wide]
    grad_send, grad_keep = hold(plans, (grad_send, grad_keep))

    s_down.x()
    s_wide.core()
    grad_middle, grad_attended, sums_mid = call_rows(
        middle_back_kernel, "middle_back",
        (grad_send, grad_keep, middle, out_grad[0], attended, hot, keep),
        (gate_full, up_full, modulation), ((width, WIDE), (odd, LOW)), ((2 * items, 3 * width),),
        core=core_place, scratch=((BLOCK, width),),
    )
    s_proj = Scatter(mixed, *column_halves(grad_attended))
    plans = [s_down, s_wide, s_proj]
    grad_middle, grad_attended, sums_mid = hold(plans, (grad_middle, grad_attended, sums_mid))

    s_wide.second()
    grad_attended = hold([s_wide], grad_attended)
    s_wide.x(0)
    s_down.y_both()
    s_proj.first()
    late_sums = jnp.concatenate([sums_mid[:items], sums_gate_b[:items]], axis=1).astype(LOW)
    grad_mixed = spread(grad_attended, two_full, mixed, heads, hd, cut)
    late_sums, grad_mixed = hold([s_down, s_wide, s_proj], (late_sums, grad_mixed))

    back = partial(
        attend_back, core=core_place, rot=rot, gq=gain_q, gk=gain_k, hd=hd, c=c,
        score_scale=score_scale,
    )
    one = dict(q2=q2_one, k=k_one, v=v_one, rq=rq_one, rk=rk_one)
    two = dict(q2=q2_two, k=k_two, v=v_two, rq=rq_two, rk=rk_two)
    s_down.z_both()
    s_wide.x(1)
    s_wide.y_common()
    s_proj.core()
    joint_one, gains_0 = back(0, 0, None, do=grad_mixed, **one)
    joint_one, gains_0, grad_mixed = hold([s_down, s_wide, s_proj], (joint_one, gains_0, grad_mixed))

    s_down.last_x()
    s_wide.y_own()
    s_wide.z_common()
    s_proj.second()
    joint_one, gains_1 = back(0, 1, joint_one, do=grad_mixed, **one)
    s_head = Scatter(normed_a, pair=joint_one)
    s_head.first()
    gains_1, grad_mixed = hold([s_down, s_wide, s_proj, s_head], (gains_1, grad_mixed))

    s_head.core()
    s_down.last_core()
    s_wide.z_own()
    joint_two, gains_2 = back(1, 0, None, do=grad_mixed, **two)
    s_head.second()
    s_head.join(s_proj)
    joint_two, gains_2, grad_mixed, late_sums = hold(
        [s_down, s_wide, s_head], (joint_two, gains_2, grad_mixed, late_sums)
    )

    s_head.x()
    s_head.y_common()
    s_wide.last_x()
    late_group = gather_rows(late_sums)
    joint_two, gains_3 = back(1, 1, joint_two, do=grad_mixed, **two)
    s_tail = Scatter(normed_a, pair=joint_two)
    s_tail.first()
    shard_down = jnp.concatenate(s_down.halves(), axis=1)[:, :width]
    gains_3, late_group, shard_down = hold(
        [s_wide, s_head, s_tail], (gains_3, late_group, shard_down)
    )

    s_tail.core()
    s_head.y_own()
    s_head.z_common()
    s_tail.second()
    grad_middle = hold([s_tail], grad_middle)
    s_tail.x()
    s_wide.last_core()
    grad_input, sums_early = call_rows(
        input_back_kernel, "input_back",
        (s_head.live["pair"], s_tail.live["pair"], grad_middle, inputs_low, hot),
        (one_full, two_full, modulation), ((width, WIDE),), ((2 * items, 2 * width),),
        core=core_place,
    )
    if s_head.fast:
        s_head.live.pop("pair")
        s_tail.live.pop("pair")
    plans = [s_wide, s_head, s_tail]
    grad_input, sums_early, late_group = hold(plans, (grad_input, sums_early, late_group))

    s_head.z_own(apart=True)
    s_tail.y_both()
    early_sums = sums_early[:items]
    gains = gains_0 + gains_1 + gains_2 + gains_3
    gain_row = jnp.sum(gains, axis=1)[:, :hd].reshape(1, 2 * hd)
    gain_high = gain_row.astype(LOW).astype(WIDE)
    gain_block = jnp.concatenate([gain_high, gain_row - gain_high], axis=0)
    gain_block = jnp.pad(gain_block, ((0, items - 2), (0, 2 * LANES - 2 * hd)))
    early_sums = jnp.concatenate([early_sums, gain_block], axis=1).astype(LOW)
    early_group = gather_rows(early_sums)
    late_far = across_x(late_group)
    plans = [s_wide, s_head, s_tail]
    early_group, late_far = hold(plans, (early_group, late_far))

    s_head.last_x()
    s_tail.z_both()
    early_far = across_x(early_group)
    late_every = across_replicas(late_group, late_far)
    shard_late = dot_left(every_act, jnp.pad(late_every, ((0, 0), (early, 0))))
    shard_wide = jnp.concatenate(s_wide.halves(), axis=1)
    plans = [s_head, s_tail]
    cond_part = dot_right(early_group[:, :early], ada_weight[:, :early]) + dot_right(
        late_group, ada_weight[:, early:]
    )
    early_far, cond_part, shard_late, late_every, shard_wide = hold(
        plans, (early_far, cond_part, shard_late, late_every, shard_wide)
    )

    s_head.last_core()
    s_tail.last_x()
    cond_back = lax.all_to_all(cond_part.astype(LOW).reshape(shards, items, -1), "fsdp", 0, 0)
    early_every = across_replicas(early_group, early_far)
    shard_early = dot_left(every_act, early_every[:, :early])
    shard_early = hold(plans, shard_early)
    shard_ada = lax.dynamic_update_slice(shard_late, shard_early, (0, 0))
    bias_sums = jnp.concatenate(
        [
            jnp.sum(early_every[:, :early].astype(WIDE), axis=0),
            jnp.sum(late_every.astype(WIDE), axis=0),
        ],
        axis=0,
    )
    shard_bias = lax.dynamic_slice(
        bias_sums, (fsdp_place * ada_bias.shape[0],), (ada_bias.shape[0],)
    )
    gain_sums = jnp.sum(early_every[:, early:].astype(WIDE), axis=0)[: 2 * hd]
    cond_back = hold(plans, cond_back)
    s_tail.last_core()
    grad_cond_act = cond_back.swapaxes(0, 1).reshape(items, width).astype(WIDE)
    grad_condition = silu_pull(grad_cond_act)[0]
    if s_head.fast:
        shard_qkv, shard_proj = finish(core_place, s_head.live, s_tail.live, hd, width)
    else:
        shard_qkv = jnp.concatenate(s_head.halves() + s_tail.halves(), axis=1)
        shard_qkv = from_parts(shard_qkv, heads, hd)
        shard_proj = jnp.concatenate(s_proj.halves(), axis=1)[:, :width]
    shard_gate_up = shard_wide
    return (
        block_out[None],
        grad_input[None],
        grad_condition[None],
        shard_ada,
        shard_bias,
        shard_qkv,
        gain_sums[:hd],
        gain_sums[hd:],
        shard_proj,
        shard_gate_up,
        shard_down,
    )


def solution(mesh):
    return jax.shard_map(
        local,
        mesh=mesh,
        in_specs=(
            P(("rep", "fsdp"), None, None),
            P(("rep", "fsdp"), None, None),
            P(("rep", "fsdp"), None),
            P(("rep", "fsdp"), None),
            P("fsdp", None),
            P("fsdp"),
            P("fsdp", None),
            P(),
            P(),
            P("fsdp", None),
            P("fsdp", None),
            P("fsdp", None),
            P(("rep", "fsdp"), None, None),
        ),
        out_specs=(
            P(("rep", "fsdp"), None, None),
            P(("rep", "fsdp"), None, None),
            P(("rep", "fsdp"), None, None),
            P("fsdp", None),
            P("fsdp"),
            P("fsdp", None),
            P(),
            P(),
            P("fsdp", None),
            P("fsdp", None),
            P("fsdp", None),
        ),
        check_vma=False,
    )
```

```python
import functools
from functools import partial

import jax
import jax.numpy as jnp
from jax import lax
from jax.experimental import pallas as pl
from jax.experimental.pallas import tpu as pltpu
from jax.sharding import PartitionSpec as P

EPSILON = 1e-06
WIDE = jnp.float32
LOW = jnp.bfloat16
AXES = ("rep", "fsdp")
HIGH_Z = 4
PARTS = 3
BLOCK = 256
LANES = 128
GROUP = 4
MASK = 4096.0
MIB = 2**20


def dot(left, right):
    return jnp.dot(left, right, preferred_element_type=WIDE)


def dot_left(left, right):
    return lax.dot_general(left, right, (((0,), (0,)), ((), ())), preferred_element_type=WIDE)


def dot_right(left, right):
    return lax.dot_general(left, right, (((1,), (1,)), ((), ())), preferred_element_type=WIDE)


def layer_norm(values):
    centred = values - jnp.mean(values, axis=-1, keepdims=True)
    return centred * lax.rsqrt(jnp.mean(centred * centred, axis=-1, keepdims=True) + EPSILON)


def modulated(values, shift_part, scale_part):
    return layer_norm(values) * (1.0 + scale_part) + shift_part


def layout(lengths_row, widths_row, length):
    seg_count = lengths_row.shape[0]
    item_ends = jnp.cumsum(lengths_row)
    item_starts = item_ends - lengths_row
    token_place = jnp.arange(length, dtype=jnp.int32)[:, None]
    member = ((token_place >= item_starts[None, :]) & (token_place < item_ends[None, :])).astype(
        jnp.int32
    )
    segment = jnp.sum(member * jnp.arange(seg_count, dtype=jnp.int32)[None, :], axis=1)
    offset = token_place[:, 0] - jnp.sum(member * item_starts[None, :], axis=1)
    across = jnp.sum(member * widths_row[None, :], axis=1)
    return (member, segment, offset // across, offset % across)


def device_index(x, core, z, y):
    return (x * 2 + core) * 8 + z * 2 + y


PLACES = [(x, c, z, y) for x in range(2) for c in range(2) for z in range(4) for y in range(2)]
TO_CORE = [(device_index(x, c, z, y), device_index(x, 1 - c, z, y)) for x, c, z, y in PLACES]
TO_X = [(device_index(x, c, z, y), device_index(1 - x, c, z, y)) for x, c, z, y in PLACES]
TO_Y = [(device_index(x, c, z, y), device_index(x, c, z, 1 - y)) for x, c, z, y in PLACES]
TO_Z = [
    [(device_index(x, c, z, y), device_index(x, c, (z + k) % 4, y)) for x, c, z, y in PLACES]
    for k in range(4)
]
Z_GROUPS = [[0, 2, 4, 6], [1, 3, 5, 7]]


def coordinates():
    replica = lax.axis_index("rep")
    shard = lax.axis_index("fsdp")
    return replica // 2, replica % 2, shard // 2, shard % 2


def is_fast():
    return lax.axis_size("rep") == 4 and lax.axis_size("fsdp") == 8


def pick(operand, index, axis):
    return lax.dynamic_index_in_dim(operand, index, axis, keepdims=False)


def over_z(operand):
    return lax.all_to_all(operand, "fsdp", 0, 0, axis_index_groups=Z_GROUPS)


def hold(plans, values):
    flat, tree = jax.tree.flatten(([plan.live for plan in plans], values))
    flat = lax.optimization_barrier(flat)
    lives, values = jax.tree.unflatten(tree, flat)
    for plan, live in zip(plans, lives):
        plan.live = live
    return values


def place_pieces(shape, apart, where, pieces, out, sems):
    x, core, z, y = where[0], where[1], where[2], where[3]
    a0, a1, ax, b0, b1, bx = pieces
    rows, half = shape[0] // 8, shape[1] // 2
    h = rows // PARTS
    copies = []
    for p0, p1, px, c in ((a0, a1, ax, core), (b0, b1, bx, 1 - core)):
        for q in range(HIGH_Z):
            for source, yy, third in (
                (p0.at[q, 0], y, x),
                (p0.at[q, 1], y, 2),
                (p1.at[q, 0], 1 - y, x),
                (p1.at[q, 1], 1 - y, 2),
                (px.at[q, 0], y, 1 - x),
                (px.at[q, 1], 1 - y, 1 - x),
            ):
                zz = (z + HIGH_Z - q) % HIGH_Z if apart else q
                row = pl.multiple_of((2 * zz + yy) * rows + third * h, 16)
                column = pl.multiple_of(c * half, LANES)
                target = out.at[pl.ds(row, h), pl.ds(column, half)]
                copy = pltpu.make_async_copy(source, target, sems.at[len(copies)])
                copy.start()
                copies.append(copy)
    for copy in copies:
        copy.wait()


def placing(kernel, shape, apart, before, after):
    def run(where, *refs):
        pieces, refs = refs[:6], refs[6:]
        inputs, rest = refs[: before + after], refs[before + after :]
        *rest, laid, sems, out_sem = rest
        outs, full, scratch = rest[0], rest[1], rest[2:]
        step = pl.program_id(0)

        @pl.when(step == 0)
        def _():
            place_pieces(shape, apart, where, pieces, laid, sems)
            pltpu.make_async_copy(laid, full, out_sem).start()

        kernel(*inputs[:before], laid, *inputs[before:], *outs, *scratch)

        @pl.when(step == pl.num_programs(0) - 1)
        def _():
            pltpu.make_async_copy(laid, full, out_sem).wait()

    return run


def call_placed(kernel, gather, args, specs, before, out_shape, out_specs, scratch, **options):
    if not gather.fast:
        weight = gather.whole()
        args = (*args[:before], weight, *args[before:])
        specs = [*specs[:before], whole_block(weight), *specs[before:]]
        got = pl.pallas_call(
            kernel, in_specs=specs, out_shape=out_shape, out_specs=out_specs,
            scratch_shapes=scratch, **options,
        )(*args)
        return (*got, weight)
    shape = (8 * gather.rows, gather.width)
    count = len(out_shape)
    inner = placing(kernel, shape, gather.apart, before, len(args) - before)

    def run(*refs):
        at = 7 + len(args)
        inner(*refs[:at], refs[at : at + count], *refs[at + count :])

    any_space = pl.BlockSpec(memory_space=pl.ANY)
    live = gather.live
    pieces = [live[k] for k in ("own", "far", "both", "twin_own", "twin_far", "twin_both")]
    return pl.pallas_call(
        run,
        in_specs=[pl.BlockSpec(memory_space=pltpu.SMEM)] + [any_space] * 6 + list(specs),
        out_shape=list(out_shape) + [jax.ShapeDtypeStruct(shape, LOW)],
        out_specs=list(out_specs) + [any_space],
        scratch_shapes=list(scratch)
        + [pltpu.VMEM(shape, LOW), pltpu.SemaphoreType.DMA((48,)), pltpu.SemaphoreType.DMA],
        **options,
    )(jnp.stack(coordinates()).astype(jnp.int32), *pieces, *args)


class Gather:
    def __init__(self, weight):
        self.rows, self.width = weight.shape
        self.live = {"weight": weight}
        self.fast = is_fast() and self.rows % 48 == 0

    def z(self, apart=False):
        if not self.fast:
            return
        self.apart = apart
        x, core, _, _ = coordinates()
        h, half = self.rows // PARTS, self.width // 2
        weight = self.live.pop("weight")
        mine = lax.dynamic_slice_in_dim(weight, core * half, half, 1).reshape(PARTS, h, half)
        base = jnp.stack([pick(mine, x, 0), mine[2]], 0)
        if apart:
            lines = [base] + [lax.ppermute(base, AXES, TO_Z[k]) for k in (1, 2, 3)]
            self.live["own"] = jnp.stack(lines, 0)
            return
        self.live["own"] = over_z(jnp.broadcast_to(base, (HIGH_Z, 2, h, half)))

    def y(self):
        if self.fast:
            self.live["far"] = lax.ppermute(self.live["own"], AXES, TO_Y)

    def x(self):
        if self.fast:
            ends = jnp.concatenate([self.live["own"][:, :1], self.live["far"][:, :1]], 1)
            self.live["both"] = lax.ppermute(ends, AXES, TO_X)

    def core(self, *names):
        if self.fast:
            for name in names:
                self.live["twin_" + name] = lax.ppermute(self.live[name], AXES, TO_CORE)

    def whole(self):
        return lax.all_gather(self.live["weight"], "fsdp", axis=0, tiled=True)


class Scatter:
    def __init__(self, left, send=None, keep=None, pair=None):
        self.left, self.fast = left, is_fast() and left.shape[1] % 384 == 0
        self.live = {"send": send, "keep": keep} if pair is None else {"pair": pair}

    def operand(self, name):
        if "pair" in self.live:
            return self.live["pair"][("send", "keep").index(name)]
        return self.live[name]

    def first(self):
        live = self.live
        if self.fast:
            live["out"] = dot_left(self.left, self.operand("send")).astype(LOW)
            live.pop("send", None)

    def core(self):
        if self.fast:
            self.live["got"] = lax.ppermute(self.live.pop("out"), AXES, TO_CORE)

    def second(self):
        live = self.live
        if self.fast:
            product = dot_left(self.left, self.operand("keep"))
            live["kept"] = (product + live.pop("got").astype(WIDE)).astype(LOW)
            live.pop("keep", None)

    def join(self, other):
        if self.fast:
            kept = [self.live["kept"], other.live.pop("kept")]
            self.live["kept"] = jnp.concatenate(kept, axis=1)

    def view(self):
        rows, half = self.live["kept"].shape
        return self.live["kept"].reshape(HIGH_Z, 2, PARTS, rows // 24, half)

    def cut(self, start, sizes):
        view = self.view()
        return lax.dynamic_slice(view, (*start, 0, 0), (*sizes, *view.shape[3:])).reshape(
            tuple(k for k in sizes if k > 1) + view.shape[3:]
        )

    def x(self, half=None):
        if not self.fast:
            return
        x, _, _, _ = coordinates()
        if half is None:
            self.live["side"] = lax.ppermute(
                self.cut((0, 0, 1 - x), (HIGH_Z, 2, 1)), AXES, TO_X
            )
        else:
            self.live["side_" + str(half)] = lax.ppermute(
                self.cut((2 * half, 0, 1 - x), (2, 2, 1)), AXES, TO_X
            )

    def own(self, index):
        x, _, _, _ = coordinates()
        live = self.live
        sides = [live["side"]] if "side" in live else [live["side_0"], live["side_1"]]
        sides = [pick(side, index, 1) for side in sides]
        side = jnp.concatenate(sides, 0) if len(sides) > 1 else sides[0]
        mine = self.cut((0, index, x), (HIGH_Z, 1, 1))
        return (mine.astype(WIDE) + side.astype(WIDE)).astype(LOW)

    def common(self, index):
        return self.cut((0, index, 2), (HIGH_Z, 1, 1))

    def y_common(self):
        if self.fast:
            _, _, _, y = coordinates()
            self.live["far_common"] = lax.ppermute(self.common(1 - y), AXES, TO_Y)

    def y_own(self):
        if self.fast:
            _, _, _, y = coordinates()
            self.live["far_own"] = lax.ppermute(self.own(1 - y), AXES, TO_Y)

    def y_both(self):
        if self.fast:
            _, _, _, y = coordinates()
            both = jnp.stack([self.own(1 - y), self.common(1 - y)], 1)
            self.live["far_both"] = lax.ppermute(both, AXES, TO_Y)

    def line(self, name):
        _, _, _, y = coordinates()
        mine = self.common(y) if name == "common" else self.own(y)
        if "far_both" in self.live:
            far = self.live["far_both"][:, 1 if name == "common" else 0]
        else:
            far = self.live.pop("far_" + name)
        return (mine.astype(WIDE) + far.astype(WIDE)).astype(LOW)

    def z_common(self):
        if self.fast:
            self.live["sum_common"] = {"all": over_z(self.line("common"))}

    def z_own(self, apart=False):
        if not self.fast:
            return
        line = self.line("own")
        self.forget()
        if not apart:
            self.live["sum_own"] = {"all": over_z(line)}
            return
        _, _, z, _ = coordinates()
        lines = {"0": pick(line, z, 0)}
        for k in (2, 1, 3):
            lines[str(k)] = lax.ppermute(pick(line, (z + k) % 4, 0), AXES, TO_Z[k])
        self.live["sum_own"] = lines

    def z_both(self):
        if self.fast:
            lines = jnp.stack([self.line("own"), self.line("common")], 1)
            self.forget()
            self.live["sum_both"] = {"all": over_z(lines)}

    def forget(self):
        for name in ("kept", "side", "side_0", "side_1", "far_both"):
            self.live.pop(name, None)

    def total(self, name):
        lines = self.live.pop(name)
        if "all" in lines:
            return jnp.sum(lines["all"].astype(WIDE), axis=0).astype(LOW)
        wide = [lines[k].astype(WIDE) for k in ("0", "1", "2", "3")]
        return (wide[0] + wide[1] + wide[2] + wide[3]).astype(LOW)

    def last_x(self):
        if self.fast:
            if "sum_both" in self.live:
                part = self.total("sum_both")
            else:
                part = jnp.stack([self.total("sum_own"), self.total("sum_common")], 0)
            self.live = {"part": part, "other": lax.ppermute(part, AXES, TO_X)}

    def last_core(self):
        if self.fast:
            x, _, _, _ = coordinates()
            part, other = self.live["part"], self.live["other"]
            shared = (part[1].astype(WIDE) + other[1].astype(WIDE)).astype(LOW)
            first = jnp.where(x == 0, part[0], other[0])
            second = jnp.where(x == 0, other[0], part[0])
            done = jnp.concatenate([first, second, shared], 0)
            self.live = {"done": done, "twin": lax.ppermute(done, AXES, TO_CORE)}

    def halves(self):
        if self.fast:
            _, core, _, _ = coordinates()
            done, twin = self.live["done"], self.live["twin"]
            first = jnp.where(core == 0, done, twin)
            second = jnp.where(core == 0, twin, done)
            return first.astype(WIDE), second.astype(WIDE)
        _, core, _, _ = coordinates()
        left = self.left
        keep, send = self.operand("keep"), self.operand("send")
        first = jnp.where(core == 0, keep, send)
        second = jnp.where(core == 0, send, keep)
        sums = []
        for columns in (first, second):
            grad = dot_left(left, columns).astype(LOW)
            part = lax.psum_scatter(grad, "fsdp", scatter_dimension=0, tiled=True)
            sums.append(lax.psum(part, "rep").astype(WIDE))
        return sums[0], sums[1]


def column_halves(array):
    _, core, _, _ = coordinates()
    half = array.shape[1] // 2
    send = lax.dynamic_slice_in_dim(array, (1 - core) * half, half, 1)
    keep = lax.dynamic_slice_in_dim(array, core * half, half, 1)
    return send, keep


def across_x(rows):
    return lax.ppermute(rows, AXES, TO_X) if is_fast() else rows


def across_replicas(rows, far):
    if not is_fast():
        return lax.all_gather(rows, "rep", axis=0, tiled=True)
    x, core, _, _ = coordinates()
    count, width = rows.shape
    line = jnp.stack([jnp.where(x == 0, rows, far), jnp.where(x == 0, far, rows)], 0)
    twin = lax.ppermute(line, AXES, TO_CORE)
    every = [jnp.where(core == 0, line, twin), jnp.where(core == 0, twin, line)]
    return jnp.stack(every, 1).reshape(4 * count, width)


def gather_rows(rows):
    shards = lax.axis_size("fsdp")
    count, width = rows.shape
    group = lax.all_to_all(jnp.broadcast_to(rows, (shards, count, width)), "fsdp", 0, 0)
    return group.reshape(shards * count, width)


def exchange(rows):
    shards = lax.axis_size("fsdp")
    count, width = rows.shape
    shaped = rows.reshape(count, shards, width // shards).swapaxes(0, 1)
    return lax.all_to_all(shaped, "fsdp", 0, 0).reshape(shards * count, width // shards)


def sum_back(partial_rows, count):
    shards = lax.axis_size("fsdp")
    shaped = partial_rows.astype(LOW).reshape(shards, count, -1)
    got = lax.all_to_all(shaped, "fsdp", 0, 0)
    return jnp.sum(got.astype(WIDE), axis=0)


def whole_block(array):
    return pl.BlockSpec(
        array.shape, lambda i: (0,) * array.ndim, pipeline_mode=pl.Buffered(1)
    )


def part_width(hd):
    return -(-3 * GROUP * hd // LANES) * LANES


def prepare_kernel(
    first, heads, hd, x_ref, hot_ref, mod_ref, w_ref, gq_ref, gk_ref, rot_ref, qt_ref, kt_ref,
    vt_ref, *refs
):
    normed_ref, q_ref, k_ref, v_ref, rq_ref, rk_ref, wide_ref = refs if first else (x_ref, *refs)
    step = part_width(hd)
    if first:
        width = x_ref.shape[1]
        hot = hot_ref[...]
        shift = dot(hot, mod_ref[:, :width])
        scale = dot(hot, mod_ref[:, width : 2 * width])
        normed, _ = normed_rows(x_ref[...].astype(WIDE))
        normed = (normed * (1.0 + scale) + shift).astype(LOW)
        normed_ref[...] = normed
    else:
        normed = x_ref[...]
    cosine, plus, minus = rot_ref[0], rot_ref[1], rot_ref[2]
    lane = lax.broadcasted_iota(jnp.int32, (BLOCK, LANES), 1)
    inside = lane < hd
    ones = jnp.full((LANES, LANES), 1.0, LOW)
    wide_ref[:, step:] = jnp.zeros((BLOCK, LANES), WIDE)
    for part in range(heads // GROUP):
        wide_ref[:, :step] = dot(normed, w_ref[:, part * step : (part + 1) * step])
        for kind, (g_ref, t_ref, o_ref, r_ref) in enumerate(
            (
                (gq_ref, qt_ref, q_ref, rq_ref),
                (gk_ref, kt_ref, k_ref, rk_ref),
                (None, vt_ref, v_ref, None),
            )
        ):
            tail = t_ref[...]
            for g in range(GROUP):
                h = part * GROUP + g
                at = (kind * GROUP + g) * hd
                raw = jnp.where(inside, wide_ref[:, at : at + LANES], 0.0)
                if kind < 2:
                    r_ref[h] = raw.astype(LOW)
                    total = dot((raw * raw).astype(LOW), ones)
                    u = raw * lax.rsqrt(total * (1.0 / hd) + EPSILON) * g_ref[...]
                    up = pltpu.roll(u, LANES - hd // 4, 1)
                    down = pltpu.roll(u, hd // 4, 1)
                    raw = u * cosine + up * plus + down * minus
                o_ref[h] = raw.astype(LOW) + tail


def prepare(first, x, hot, mod, gather, gq, gk, rot, qt, kt, vt, heads, hd):
    n, width = x.shape
    rows = pl.BlockSpec((BLOCK, width), lambda i: (i, 0))
    head_spec = pl.BlockSpec((heads, BLOCK, LANES), lambda i: (0, i, 0))
    tail = pl.BlockSpec((BLOCK, LANES), lambda i: (i, 0))
    normed_spec, normed_shape = [rows], [jax.ShapeDtypeStruct((n, width), LOW)]
    return call_placed(
        partial(prepare_kernel, first, heads, hd),
        gather,
        (x, hot, mod, gq, gk, rot, qt, kt, vt),
        [
            rows,
            pl.BlockSpec((BLOCK, hot.shape[1]), lambda i: (i, 0)),
            whole_block(mod),
            whole_block(gq),
            whole_block(gk),
            pl.BlockSpec((3, BLOCK, LANES), lambda i: (0, i, 0)),
            tail,
            tail,
            pl.BlockSpec((1, LANES), lambda i: (0, 0)),
        ],
        3,
        (normed_shape if first else []) + [jax.ShapeDtypeStruct((heads, n, LANES), LOW)] * 5,
        (normed_spec if first else []) + [head_spec] * 5,
        [pltpu.VMEM((BLOCK, part_width(hd) + LANES), WIDE)],
        grid=(n // BLOCK,),
        compiler_params=pltpu.CompilerParams(vmem_limit_bytes=56 * MIB),
        cost_estimate=pl.CostEstimate(
            flops=12 * n * width * width // 2, bytes_accessed=20 * MIB, transcendentals=0
        ),
        name="prepare",
    )


def near_blocks(run):
    i = pl.program_id(0)
    n = pl.num_programs(0)

    @pl.when(i == 0)
    def _():
        run(pl.ds(0, 2 * BLOCK))

    @pl.when(i == n - 1)
    def _():
        run(pl.ds(pl.multiple_of((i - 1) * BLOCK, BLOCK), 2 * BLOCK))

    @pl.when((i > 0) & (i < n - 1))
    def _():
        run(pl.ds(pl.multiple_of((i - 1) * BLOCK, BLOCK), 3 * BLOCK))


def attend_kernel(hd, c, *refs):
    mix_ref = refs[6]
    lane = lax.broadcasted_iota(jnp.int32, (BLOCK, LANES), 1)
    heads = refs[0].shape[0]

    def run(at):
        for head in range(2 * heads):
            half, h = head // heads, head % heads
            q_ref, k_ref, v_ref = refs[3 * half : 3 * half + 3]
            q = q_ref[h]
            p = jnp.exp2(dot_right(q, k_ref[h, at]) * c).astype(LOW)
            total = dot(p, v_ref[h, at])
            norm = total[:, hd : hd + 1]
            out = (total * (1.0 / norm)).astype(LOW)
            mix_ref[:, hd * head : hd * (head + 1)] = out[:, :hd]
            rest = jnp.log2(norm) * (1.0 / c)
            first = rest.astype(LOW).astype(WIDE)
            rest = rest - first
            second = rest.astype(LOW).astype(WIDE)
            third = rest - second
            logs = jnp.where(lane == hd + 8, first, jnp.where(lane == hd + 9, second, third))
            marked = jnp.where((lane >= hd + 8) & (lane < hd + 11), logs.astype(LOW), q)
            refs[7 + half][h] = marked

    near_blocks(run)


def attend(one, two, hd, c):
    heads, n, _ = one[0].shape
    full = pl.BlockSpec((heads, n, LANES), lambda i: (0, 0, 0), pipeline_mode=pl.Buffered(1))
    block = pl.BlockSpec((heads, BLOCK, LANES), lambda i: (0, i, 0))
    width = 2 * heads * hd
    return pl.pallas_call(
        partial(attend_kernel, hd, c),
        grid=(n // BLOCK,),
        in_specs=[block, full, full] * 2,
        out_specs=[pl.BlockSpec((BLOCK, width), lambda i: (i, 0)), block, block],
        out_shape=[jax.ShapeDtypeStruct((n, width), LOW)]
        + [jax.ShapeDtypeStruct((heads, n, LANES), LOW)] * 2,
        compiler_params=pltpu.CompilerParams(vmem_limit_bytes=56 * MIB),
        cost_estimate=pl.CostEstimate(
            flops=8 * n * 640 * LANES * heads,
            bytes_accessed=20 * MIB,
            transcendentals=2 * heads * n * 640,
        ),
        name="attend",
    )(*one, *two)


def spread_kernel(heads, hd, proj_at, ga_ref, w_ref, mix_ref, out_ref, grad_scr, mix_scr):
    width = heads * hd
    grad_scr[:, width:] = jnp.zeros((BLOCK, LANES), WIDE)
    mix_scr[:, width:] = jnp.zeros((BLOCK, LANES), WIDE)
    grad_scr[:, :width] = dot_right(ga_ref[:, :width], w_ref[:, proj_at : proj_at + width]).astype(LOW).astype(WIDE)
    mix_scr[:, :width] = mix_ref[...].astype(WIDE)
    lane = lax.broadcasted_iota(jnp.int32, (BLOCK, LANES), 1)
    ones = jnp.full((LANES, LANES), 1.0, LOW)
    for h in range(heads):
        at = hd * h
        grad = jnp.where(lane < hd, grad_scr[:, at : at + LANES], 0.0)
        product = grad * mix_scr[:, at : at + LANES]
        high = product.astype(LOW)
        rest = (product - high.astype(WIDE)).astype(LOW)
        delta = -(dot(high, ones) + dot(rest, ones))
        first = delta.astype(LOW)
        second = (delta - first.astype(WIDE)).astype(LOW)
        out_ref[h] = jnp.where(
            lane == hd, first, jnp.where(lane == hd + 1, second, grad.astype(LOW))
        )


def spread(ga, w, mix, heads, hd, proj_at):
    n = ga.shape[0]
    width = heads * hd
    row = pl.BlockSpec((BLOCK, width), lambda i: (i, 0))
    wide_row = pl.BlockSpec((BLOCK, ga.shape[1]), lambda i: (i, 0))
    return pl.pallas_call(
        partial(spread_kernel, heads, hd, proj_at),
        grid=(n // BLOCK,),
        in_specs=[wide_row, whole_block(w), row],
        out_specs=pl.BlockSpec((heads, BLOCK, LANES), lambda i: (0, i, 0)),
        out_shape=jax.ShapeDtypeStruct((heads, n, LANES), LOW),
        scratch_shapes=[
            pltpu.VMEM((BLOCK, width + LANES), WIDE),
            pltpu.VMEM((BLOCK, width + LANES), WIDE),
        ],
        compiler_params=pltpu.CompilerParams(vmem_limit_bytes=56 * MIB),
        cost_estimate=pl.CostEstimate(
            flops=2 * n * width * width, bytes_accessed=12 * MIB, transcendentals=0
        ),
        name="spread",
    )(ga, w, mix)


def back_kernel(
    hd, c, score_scale, part, core_ref, q_ref, k_ref, v_ref, do_ref, rq_ref, rk_ref, rot_ref, gq_ref, gk_ref,
    *refs,
):
    out_ref, gain_ref, joint_ref, dq_scr, dk_scr, dv_scr, gain_scr, out_sem = refs[part:]
    i = pl.program_id(0)
    n = pl.num_programs(0)
    heads = q_ref.shape[0]
    width = GROUP * hd
    tail = joint_ref.shape[1] - 3 * width
    slot = core_ref[0] if part else 1 - core_ref[0]

    @pl.when(i == 0)
    def _():
        dq_scr[...] = jnp.zeros(dq_scr.shape, WIDE)
        gain_scr[...] = jnp.zeros(gain_scr.shape, WIDE)

    ones = jnp.full((LANES, LANES), 1.0, LOW)

    def run(at):
        def body(h, carry):
            kk = k_ref[h]
            vv = v_ref[h]
            q = q_ref[h, at]
            do = do_ref[h, at]
            p = jnp.exp2(dot_right(kk, q) * c)
            dv_scr[h] = dot(p.astype(LOW), do)
            ds = (p * dot_right(vv, do)).astype(LOW)
            dk_scr[h] = dot(ds, q)
            dq_scr[h, at] += dot_left(ds, kk)
            return carry

        lax.fori_loop(0, heads, body, 0, unroll=GROUP)

    near_blocks(run)

    def finish(dy, raw, rot, gain, row):
        raw = raw.astype(WIDE)
        dy = dy * score_scale
        up = pltpu.roll(dy, LANES - hd // 4, 1)
        down = pltpu.roll(dy, hd // 4, 1)
        d = dy * rot[0] - up * rot[1] - down * rot[2]
        r = lax.rsqrt(dot((raw * raw).astype(LOW), ones) * (1.0 / hd) + EPSILON)
        u = raw * r
        ud = u * d
        gain_scr[row] += jnp.sum(ud.reshape(BLOCK // 8, 8, LANES), axis=0)
        m = dot((ud * gain).astype(LOW), ones) * (1.0 / hd)
        return (r * (gain * d - u * m)).astype(LOW)

    here = pl.ds(pl.multiple_of(i * BLOCK, BLOCK), BLOCK)
    rot = [rot_ref[t, here] for t in range(3)]
    joint_ref[here, 3 * width :] = jnp.zeros((BLOCK, tail), LOW)
    for h in range(heads):
        at = hd * h
        grad = finish(dk_scr[h], rk_ref[h], rot, gk_ref[...], 1)
        joint_ref[here, width + at : width + at + hd] = grad[:, :hd]
        value = dv_scr[h].astype(LOW)
        joint_ref[here, 2 * width + at : 2 * width + at + hd] = value[:, :hd]

    @pl.when(i == n - 1)
    def _():
        def rows(b, carry):
            at = pl.ds(pl.multiple_of(b * BLOCK, BLOCK), BLOCK)
            turn = [rot_ref[t, at] for t in range(3)]
            for h in range(heads):
                start = hd * h
                grad = finish(dq_scr[h, at], rq_ref[h, at], turn, gq_ref[...], 0)
                joint_ref[at, start : start + hd] = grad[:, :hd]
            return carry

        lax.fori_loop(0, n, rows, 0)
        gain_ref[...] = gain_scr[...]
        copy = pltpu.make_async_copy(joint_ref, out_ref.at[slot], out_sem)
        copy.start()
        copy.wait()


def attend_back(half, part, before, core, q2, k, v, do, rq, rk, rot, gq, gk, hd, c, score_scale):
    _, n, _ = q2.shape
    one = pl.Buffered(1)
    full = pl.BlockSpec((GROUP, n, LANES), lambda i: (part, 0, 0), pipeline_mode=one)
    block = pl.BlockSpec((GROUP, BLOCK, LANES), lambda i: (part, i, 0))
    small = pl.BlockSpec((1, LANES), lambda i: (0, 0))
    any_space = pl.BlockSpec(memory_space=pl.ANY)
    width = part_width(hd)
    at = 2 * half + part
    return pl.pallas_call(
        partial(back_kernel, hd, c, score_scale, part),
        grid=(n // BLOCK,),
        in_specs=[
            pl.BlockSpec(memory_space=pltpu.SMEM),
            *(full, block, block),
            pl.BlockSpec((GROUP, n, LANES), lambda i: (at, 0, 0), pipeline_mode=one),
            *(full, block, whole_block(rot), small, small),
            *([any_space] if part else []),
        ],
        out_specs=[any_space, pl.BlockSpec((2, 8, LANES), lambda i: (0, 0, 0))],
        out_shape=[
            jax.ShapeDtypeStruct((2, n, width), LOW),
            jax.ShapeDtypeStruct((2, 8, LANES), WIDE),
        ],
        scratch_shapes=[
            pltpu.VMEM((n, width), LOW),
            pltpu.VMEM((GROUP, n, LANES), WIDE),
            pltpu.VMEM((GROUP, BLOCK, LANES), WIDE),
            pltpu.VMEM((GROUP, BLOCK, LANES), WIDE),
            pltpu.VMEM((2, 8, LANES), WIDE),
            pltpu.SemaphoreType.DMA,
        ],
        input_output_aliases={10: 0} if part else {},
        compiler_params=pltpu.CompilerParams(vmem_limit_bytes=56 * MIB),
        cost_estimate=pl.CostEstimate(
            flops=10 * n * 640 * LANES * GROUP,
            bytes_accessed=10 * MIB,
            transcendentals=GROUP * n * 640,
        ),
        name="attend_back",
    )(core, q2, k, v, do, rq, rk, rot, gq, gk, *([before] if part else []))


def normed_rows(values):
    centred = values - jnp.mean(values, axis=-1, keepdims=True)
    scale = lax.rsqrt(jnp.mean(centred * centred, axis=-1, keepdims=True) + EPSILON)
    return centred * scale, scale


def norm_back(normed, scale, grad):
    inner = jnp.mean(grad * normed, axis=-1, keepdims=True)
    return scale * (grad - jnp.mean(grad, axis=-1, keepdims=True) - normed * inner)


def add_sums(out_ref, at, hot, values):
    width = values.shape[1]
    term = dot_left(hot, values.astype(LOW))
    here = (slice(None), slice(at * width, (at + 1) * width))

    @pl.when(pl.program_id(0) == 0)
    def _():
        out_ref[here] = term

    @pl.when(pl.program_id(0) > 0)
    def _():
        out_ref[here] += term


def rows_of(array):
    if array.ndim == 3:
        return pl.BlockSpec((2, BLOCK, array.shape[2]), lambda i: (0, i, 0))
    return pl.BlockSpec((BLOCK, array.shape[1]), lambda i: (i, 0))


def call_rows(
    kernel, name, streamed, fixed, outs, sums=(), core=None, scratch=(), gather=None
):
    n = streamed[0].shape[-2]
    work = sum(2 * n * a.size for a in fixed if a.shape[0] > 256)
    moved = sum(a.size * a.dtype.itemsize for a in (*streamed, *fixed))
    scalars = () if core is None else (core,)
    args = (*scalars, *streamed, *fixed)
    specs = [pl.BlockSpec(memory_space=pltpu.SMEM) for _ in scalars]
    specs += [rows_of(a) for a in streamed] + [whole_block(a) for a in fixed]
    out_specs = [pl.BlockSpec((BLOCK, w), lambda i: (i, 0)) for w, _ in outs]
    out_specs += [pl.BlockSpec(shape, lambda i: (0, 0)) for shape in sums]
    out_shape = [jax.ShapeDtypeStruct((n, w), t) for w, t in outs]
    out_shape += [jax.ShapeDtypeStruct(shape, WIDE) for shape in sums]
    scratch = [pltpu.VMEM(shape, WIDE) for shape in scratch]
    if gather is not None:
        work += 2 * n * gather.rows * lax.axis_size("fsdp") * gather.width
    options = dict(
        grid=(n // BLOCK,),
        compiler_params=pltpu.CompilerParams(vmem_limit_bytes=56 * MIB),
        cost_estimate=pl.CostEstimate(flops=work, bytes_accessed=moved, transcendentals=0),
        name=name,
    )
    if gather is not None:
        before = len(scalars) + len(streamed)
        return call_placed(
            kernel, gather, args, specs, before, out_shape, out_specs, scratch, **options
        )
    return pl.pallas_call(
        kernel, in_specs=specs, out_specs=out_specs, out_shape=out_shape, scratch_shapes=scratch,
        **options,
    )(*args)


def join_kernel(
    proj_at, mix_ref, x_ref, hot_ref, keep_ref, w_ref, mod_ref, att_ref, mid_ref, norm_ref
):
    width = x_ref.shape[1]
    hot = hot_ref[...]
    attended = dot(mix_ref[...], w_ref[:, proj_at : proj_at + width])
    att_ref[...] = attended.astype(LOW)
    gate = dot(hot, mod_ref[:, 2 * width : 3 * width]) * keep_ref[...]
    middle = x_ref[...].astype(WIDE) + gate * attended
    mid_ref[...] = middle
    normed, _ = normed_rows(middle)
    scale = dot(hot, mod_ref[:, 4 * width : 5 * width])
    shift = dot(hot, mod_ref[:, 3 * width : 4 * width])
    norm_ref[...] = (normed * (1.0 + scale) + shift).astype(LOW)


def gate_kernel(x_ref, w_ref, out_ref):
    out_ref[...] = dot(x_ref[...], w_ref[:, : out_ref.shape[1]]).astype(LOW)


def up_kernel(x_ref, gate_ref, w_ref, up_ref, inner_ref):
    up = dot(x_ref[...], w_ref[...])
    up_ref[...] = up.astype(LOW)
    gate = gate_ref[...].astype(WIDE)
    inner_ref[...] = (gate * jax.nn.sigmoid(gate) * up).astype(LOW)


def down_kernel(
    inner_ref, mid_ref, grad_ref, hot_ref, keep_ref, w_ref, mod_ref, out_ref, back_ref, sum_ref
):
    width = mid_ref.shape[1]
    hot = hot_ref[...]
    returned = dot(inner_ref[...], w_ref[:, :width])
    gate = dot(hot, mod_ref[:, 5 * width : 6 * width]) * keep_ref[...]
    out_ref[...] = (mid_ref[...] + gate * returned).astype(LOW)
    upstream = grad_ref[...].astype(WIDE)
    back_ref[:, :width] = (upstream * gate).astype(LOW)
    if back_ref.shape[1] > width:
        back_ref[:, width:] = jnp.zeros((BLOCK, back_ref.shape[1] - width), LOW)
    add_sums(sum_ref, 0, hot, upstream * keep_ref[...] * returned)


def inner_back_kernel(core_ref, grad_ref, gate_ref, up_ref, w_ref, send_ref, keep_ref):
    grad = dot_right(grad_ref[...], w_ref[...])
    gate = gate_ref[...].astype(WIDE)
    sig = jax.nn.sigmoid(gate)
    act = gate * sig
    for_gate = (grad * up_ref[...].astype(WIDE) * (sig + act * (1.0 - sig))).astype(LOW)
    for_up = (grad * act).astype(LOW)

    @pl.when(core_ref[0] == 0)
    def _():
        send_ref[...] = for_up
        keep_ref[...] = for_gate

    @pl.when(core_ref[0] != 0)
    def _():
        send_ref[...] = for_gate
        keep_ref[...] = for_up


def middle_back_kernel(
    core_ref, send_ref, mine_ref, mid_ref, grad_ref, att_ref, hot_ref, keep_ref, wg_ref, wu_ref,
    mod_ref, out_ref, back_ref, sum_ref, total_ref,
):
    width = mid_ref.shape[1]
    hot = hot_ref[...]
    keep = keep_ref[...]

    @pl.when(core_ref[0] == 0)
    def _():
        total_ref[...] = dot_right(mine_ref[...], wg_ref[:, : mine_ref.shape[1]])
        total_ref[...] += dot_right(send_ref[...], wu_ref[...])

    @pl.when(core_ref[0] != 0)
    def _():
        total_ref[...] = dot_right(send_ref[...], wg_ref[:, : send_ref.shape[1]])
        total_ref[...] += dot_right(mine_ref[...], wu_ref[...])

    grad = total_ref[...]
    normed, scale = normed_rows(mid_ref[...])
    turned = grad * (1.0 + dot(hot, mod_ref[:, 4 * width : 5 * width]))
    total = grad_ref[...].astype(WIDE) + norm_back(normed, scale, turned)
    out_ref[...] = total
    gate = dot(hot, mod_ref[:, 2 * width : 3 * width]) * keep
    back_ref[:, :width] = (total * gate).astype(LOW)
    if back_ref.shape[1] > width:
        back_ref[:, width:] = jnp.zeros((BLOCK, back_ref.shape[1] - width), LOW)
    add_sums(sum_ref, 0, hot, total * keep * att_ref[...].astype(WIDE))
    add_sums(sum_ref, 1, hot, grad)
    add_sums(sum_ref, 2, hot, grad * normed)


def input_back_kernel(
    core_ref, one_ref, two_ref, mid_ref, x_ref, hot_ref, wo_ref, wt_ref, mod_ref, out_ref, sum_ref
):
    width = x_ref.shape[1]
    hot = hot_ref[...]
    step = one_ref.shape[2]
    core = core_ref[0]
    grad = None
    for ref, w_ref in ((one_ref, wo_ref), (two_ref, wt_ref)):
        term = dot_right(ref[1 - core], w_ref[:, :step]) + dot_right(ref[core], w_ref[:, step : 2 * step])
        grad = term if grad is None else grad + term
    normed, scale = normed_rows(x_ref[...].astype(WIDE))
    turned = grad * (1.0 + dot(hot, mod_ref[:, width : 2 * width]))
    out_ref[...] = mid_ref[...] + norm_back(normed, scale, turned)
    add_sums(sum_ref, 0, hot, grad)
    add_sums(sum_ref, 1, hot, grad * normed)


def finish_kernel(hd, core_ref, head_done, head_twin, tail_done, tail_twin, qkv_ref, proj_ref):
    step = part_width(hd)
    short = GROUP * hd
    total = qkv_ref.shape[1] // 3

    def write(sources):
        for part, source in enumerate(sources):
            values = source[:, :step].astype(WIDE)
            for kind in range(3):
                at = kind * total + part * short
                qkv_ref[:, at : at + short] = values[:, kind * short : (kind + 1) * short]
        half = sources[0].shape[1] - step
        proj_ref[:, :half] = sources[0][:, step:].astype(WIDE)
        rest = proj_ref.shape[1] - half
        proj_ref[:, half:] = sources[1][:, step : step + rest].astype(WIDE)

    @pl.when(core_ref[0] == 0)
    def _():
        write((head_done, head_twin, tail_done, tail_twin))

    @pl.when(core_ref[0] != 0)
    def _():
        write((head_twin, head_done, tail_twin, tail_done))


def finish(core, head, tail, hd, width):
    rows = head["done"].shape[0]
    return pl.pallas_call(
        partial(finish_kernel, hd),
        in_specs=[pl.BlockSpec(memory_space=pltpu.SMEM)]
        + [pl.BlockSpec(memory_space=pltpu.VMEM)] * 4,
        out_specs=[pl.BlockSpec(memory_space=pltpu.VMEM)] * 2,
        out_shape=[
            jax.ShapeDtypeStruct((rows, 3 * width), WIDE),
            jax.ShapeDtypeStruct((rows, width), WIDE),
        ],
        compiler_params=pltpu.CompilerParams(vmem_limit_bytes=40 * MIB),
        name="finish",
    )(core, head["done"], head["twin"], tail["done"], tail["twin"])


def turn_tables(row_place, column_place, hd):
    quarter = hd // 4
    inverse = 10000.0 ** (-jnp.arange(quarter, dtype=WIDE) / quarter)
    row_angle = row_place.astype(WIDE)[:, None] * inverse[None, :]
    column_angle = column_place.astype(WIDE)[:, None] * inverse[None, :]
    rest = jnp.zeros((row_place.shape[0], LANES - hd), WIDE)
    none = jnp.zeros_like(row_angle)
    rc, rs = jnp.cos(row_angle), jnp.sin(row_angle)
    cc, cs = jnp.cos(column_angle), jnp.sin(column_angle)
    return jnp.stack(
        [
            jnp.concatenate([rc, rc, cc, cc, rest], 1),
            jnp.concatenate([-rs, none, -cs, none, rest], 1),
            jnp.concatenate([none, rs, none, cs, rest], 1),
        ],
        0,
    )


def high_and_rest(values):
    high = values.astype(LOW)
    return jnp.concatenate([high, (values - high.astype(WIDE)).astype(LOW)], axis=0)


def pad_columns(array, width):
    return jnp.pad(array, ((0, 0), (0, width - array.shape[1])))


def to_parts(array, heads, hd):
    rows = array.shape[0]
    shaped = array.reshape(rows, 3, heads // GROUP, GROUP * hd).swapaxes(1, 2)
    shaped = shaped.reshape(rows, heads // GROUP, 3 * GROUP * hd)
    padded = jnp.pad(shaped, ((0, 0), (0, 0), (0, part_width(hd) - 3 * GROUP * hd)))
    return padded.reshape(rows, -1)


def from_parts(array, heads, hd):
    rows = array.shape[0]
    shaped = array.reshape(rows, heads // GROUP, -1)[:, :, : 3 * GROUP * hd]
    shaped = shaped.reshape(rows, heads // GROUP, 3, GROUP * hd).swapaxes(1, 2)
    return shaped.reshape(rows, -1)


def local(
    block_in,
    condition,
    item_lengths,
    item_widths,
    ada_weight,
    ada_bias,
    qkv_weight,
    query_gain,
    key_gain,
    proj_weight,
    gate_up_weight,
    down_weight,
    out_grad,
):
    _, n, width = block_in.shape
    items = item_lengths.shape[1]
    hd = query_gain.shape[0]
    heads = width // hd
    ff = down_weight.shape[0] * lax.axis_size("fsdp")
    score_scale = float(hd) ** (-0.5)
    c = score_scale * 1.4426950408889634
    shards = lax.axis_size("fsdp")
    fsdp_place = lax.axis_index("fsdp")
    odd = width + LANES if (width // LANES) % 2 else width

    qkv_parts = to_parts(qkv_weight, heads, hd)
    cut = qkv_parts.shape[1] // 2
    g_one = Gather(qkv_parts[:, :cut])
    g_two = Gather(jnp.concatenate([qkv_parts[:, cut:], pad_columns(proj_weight, odd)], axis=1))
    g_gate = Gather(gate_up_weight[:, :ff])
    g_up = Gather(gate_up_weight[:, ff:])
    g_down = Gather(pad_columns(down_weight, odd))
    gathers = [g_one, g_two, g_gate, g_up, g_down]
    core_place = (lax.axis_index("rep") % 2).astype(jnp.int32).reshape(1)

    cond_float = condition.astype(WIDE).reshape(items, width)
    cond_silu, silu_pull = jax.vjp(jax.nn.silu, cond_float)
    cond_act = cond_silu.astype(LOW)

    g_one.z()
    group_act = exchange(cond_act)
    member, segment, row_place, column_place = layout(item_lengths[0], item_widths[0], n)
    member_low = member.astype(LOW)
    keep = (segment < items - 1).astype(WIDE).reshape(n, 1)
    rot = turn_tables(row_place, column_place, hd)
    spare = jnp.zeros((n, LANES - hd - items), LOW)
    ones_at = jnp.zeros((n, LANES - hd - items), LOW).at[:, :3].set(-1.0)
    blank = jnp.zeros((n, hd), LOW)
    query_tail = jnp.concatenate([blank, member_low, spare], 1)
    key_tail = jnp.concatenate([blank, (member_low - 1.0) * MASK, ones_at], 1)
    value_tail = jnp.zeros((1, LANES), LOW).at[:, hd : hd + 2].set(1.0)
    gain_q = pad_columns(query_gain.astype(WIDE)[None, :], LANES)
    gain_k = pad_columns(key_gain.astype(WIDE)[None, :], LANES)
    hot = jnp.concatenate([member_low, member_low], axis=1)
    tables = (rot, query_tail, key_tail, hot, keep)
    group_act = hold(gathers, group_act)

    g_one.y()
    g_two.z()
    bias_row = lax.dynamic_update_slice(
        jnp.zeros((6 * width,), WIDE), ada_bias.astype(WIDE), (fsdp_place * ada_bias.shape[0],)
    )
    mod_part = (dot(group_act, ada_weight) + bias_row[None, :]).astype(LOW)
    act_far = across_x(group_act)
    mod_part, group_act, act_far, tables = hold(gathers, (mod_part, group_act, act_far, tables))

    early = 2 * width
    modulation = high_and_rest(sum_back(mod_part, items))
    g_one.x()
    g_one.core("own", "far")
    g_two.y()
    inputs_low = block_in[0]
    every_act = across_replicas(group_act, act_far)
    modulation, tables, inputs_low, every_act = hold(
        gathers, (modulation, tables, inputs_low, every_act)
    )

    g_one.core("both")
    g_two.x()
    g_two.core("own", "far")
    g_gate.z()
    rot, query_tail, key_tail, hot, keep = tables
    set_out = (gain_q, gain_k, rot, query_tail, key_tail, value_tail, heads // 2, hd)
    normed_a, q_one, k_one, v_one, rq_one, rk_one, one_full = prepare(
        True, inputs_low, hot, modulation, g_one, *set_out
    )
    gathers = gathers[1:]
    normed_a, q_one, k_one, v_one, rq_one, rk_one, one_full = hold(
        gathers, (normed_a, q_one, k_one, v_one, rq_one, rk_one, one_full)
    )

    g_two.core("both")
    g_gate.y()
    g_up.z()
    q_two, k_two, v_two, rq_two, rk_two, two_full = prepare(
        False, normed_a, hot, modulation, g_two, *set_out
    )
    gathers = gathers[1:]
    normed_a, q_two, k_two, v_two, rq_two, rk_two, two_full, q_one, k_one, v_one = hold(
        gathers, (normed_a, q_two, k_two, v_two, rq_two, rk_two, two_full, q_one, k_one, v_one)
    )

    g_gate.x()
    g_gate.core("own", "far")
    g_up.y()
    g_down.z()
    mixed, q2_one, q2_two = attend((q_one, k_one, v_one), (q_two, k_two, v_two), hd, c)
    mixed, q2_one, q2_two = hold(gathers, (mixed, q2_one, q2_two))

    g_gate.core("both")
    g_up.x()
    g_up.core("own", "far")
    g_down.y()
    attended, middle, normed_b = call_rows(
        partial(join_kernel, cut), "join", (mixed, inputs_low, hot, keep), (two_full, modulation),
        ((width, LOW), (width, WIDE), (width, LOW)),
    )
    middle, normed_b, attended = hold([g_gate], (middle, normed_b, attended))

    gate, gate_full = call_rows(
        gate_kernel, "gate", (normed_b,), (), ((ff, LOW),), gather=g_gate
    )
    gathers = [g_up, g_down]
    gate, gate_full, normed_b, middle, attended = hold(
        gathers, (gate, gate_full, normed_b, middle, attended)
    )

    g_up.core("both")
    g_down.x()
    g_down.core("own", "far")
    normed_b = hold([g_up], normed_b)
    up, inner, up_full = call_rows(
        up_kernel, "up", (normed_b, gate), (), ((ff, LOW), (ff, LOW)), gather=g_up
    )
    gathers = [g_down]
    inner, up, gate, up_full, middle = hold(gathers, (inner, up, gate, up_full, middle))

    g_down.core("both")
    block_out, grad_returned, sums_gate_b, down_full = call_rows(
        down_kernel, "down", (inner, middle, out_grad[0], hot, keep), (modulation,),
        ((width, LOW), (odd, LOW)), ((2 * items, width),), gather=g_down,
    )

    s_down = Scatter(inner, *column_halves(grad_returned))
    s_down.first()
    plans = [s_down]
    grad_returned, down_full, gate, up, gate_full, up_full, normed_b, middle, attended = hold(
        plans,
        (grad_returned, down_full, gate, up, gate_full, up_full, normed_b, middle, attended),
    )

    s_down.core()
    grad_send, grad_keep = call_rows(
        inner_back_kernel, "inner_back", (grad_returned, gate, up), (down_full,),
        ((ff, LOW), (ff, LOW)), core=core_place,
    )
    grad_send, grad_keep = hold(plans, (grad_send, grad_keep))

    s_down.second()
    s_wide = Scatter(normed_b, grad_send, grad_keep)
    s_wide.first()
    plans = [s_down, s_wide]
    grad_send, grad_keep = hold(plans, (grad_send, grad_keep))

    s_down.x()
    s_wide.core()
    grad_middle, grad_attended, sums_mid = call_rows(
        middle_back_kernel, "middle_back",
        (grad_send, grad_keep, middle, out_grad[0], attended, hot, keep),
        (gate_full, up_full, modulation), ((width, WIDE), (odd, LOW)), ((2 * items, 3 * width),),
        core=core_place, scratch=((BLOCK, width),),
    )
    s_proj = Scatter(mixed, *column_halves(grad_attended))
    plans = [s_down, s_wide, s_proj]
    grad_middle, grad_attended, sums_mid = hold(plans, (grad_middle, grad_attended, sums_mid))

    s_wide.second()
    grad_attended = hold([s_wide], grad_attended)
    s_wide.x(0)
    s_down.y_both()
    s_proj.first()
    late_sums = jnp.concatenate([sums_mid[:items], sums_gate_b[:items]], axis=1).astype(LOW)
    grad_mixed = spread(grad_attended, two_full, mixed, heads, hd, cut)
    late_sums, grad_mixed = hold([s_down, s_wide, s_proj], (late_sums, grad_mixed))

    back = partial(
        attend_back, core=core_place, rot=rot, gq=gain_q, gk=gain_k, hd=hd, c=c,
        score_scale=score_scale,
    )
    one = dict(q2=q2_one, k=k_one, v=v_one, rq=rq_one, rk=rk_one)
    two = dict(q2=q2_two, k=k_two, v=v_two, rq=rq_two, rk=rk_two)
    s_down.z_both()
    s_wide.x(1)
    s_wide.y_common()
    s_proj.core()
    joint_one, gains_0 = back(0, 0, None, do=grad_mixed, **one)
    joint_one, gains_0, grad_mixed = hold([s_down, s_wide, s_proj], (joint_one, gains_0, grad_mixed))

    s_down.last_x()
    s_wide.y_own()
    s_wide.z_common()
    s_proj.second()
    joint_one, gains_1 = back(0, 1, joint_one, do=grad_mixed, **one)
    s_head = Scatter(normed_a, pair=joint_one)
    s_head.first()
    gains_1, grad_mixed = hold([s_down, s_wide, s_proj, s_head], (gains_1, grad_mixed))

    s_head.core()
    s_down.last_core()
    s_wide.z_own()
    joint_two, gains_2 = back(1, 0, None, do=grad_mixed, **two)
    s_head.second()
    s_head.join(s_proj)
    joint_two, gains_2, grad_mixed, late_sums = hold(
        [s_down, s_wide, s_head], (joint_two, gains_2, grad_mixed, late_sums)
    )

    s_head.x()
    s_head.y_common()
    late_group = gather_rows(late_sums)
    joint_two, gains_3 = back(1, 1, joint_two, do=grad_mixed, **two)
    s_tail = Scatter(normed_a, pair=joint_two)
    s_tail.first()
    shard_down = jnp.concatenate(s_down.halves(), axis=1)[:, :width]
    gains_3, late_group, shard_down = hold(
        [s_wide, s_head, s_tail], (gains_3, late_group, shard_down)
    )

    s_tail.core()
    s_wide.last_x()
    s_head.y_own()
    s_head.z_common()
    s_tail.second()
    grad_middle = hold([s_tail], grad_middle)
    s_tail.x()
    grad_input, sums_early = call_rows(
        input_back_kernel, "input_back",
        (s_head.live["pair"], s_tail.live["pair"], grad_middle, inputs_low, hot),
        (one_full, two_full, modulation), ((width, WIDE),), ((2 * items, 2 * width),),
        core=core_place,
    )
    if s_head.fast:
        s_head.live.pop("pair")
        s_tail.live.pop("pair")
    plans = [s_wide, s_head, s_tail]
    grad_input, sums_early, late_group = hold(plans, (grad_input, sums_early, late_group))

    s_wide.last_core()
    s_head.z_own(apart=True)
    s_tail.y_both()
    early_sums = sums_early[:items]
    gains = gains_0 + gains_1 + gains_2 + gains_3
    gain_row = jnp.sum(gains, axis=1)[:, :hd].reshape(1, 2 * hd)
    gain_high = gain_row.astype(LOW).astype(WIDE)
    gain_block = jnp.concatenate([gain_high, gain_row - gain_high], axis=0)
    gain_block = jnp.pad(gain_block, ((0, items - 2), (0, 2 * LANES - 2 * hd)))
    early_sums = jnp.concatenate([early_sums, gain_block], axis=1).astype(LOW)
    early_group = gather_rows(early_sums)
    late_far = across_x(late_group)
    plans = [s_wide, s_head, s_tail]
    early_group, late_far = hold(plans, (early_group, late_far))

    s_head.last_x()
    s_tail.z_both()
    early_far = across_x(early_group)
    late_every = across_replicas(late_group, late_far)
    shard_late = dot_left(every_act, jnp.pad(late_every, ((0, 0), (early, 0))))
    shard_wide = jnp.concatenate(s_wide.halves(), axis=1)
    plans = [s_head, s_tail]
    cond_part = dot_right(early_group[:, :early], ada_weight[:, :early]) + dot_right(
        late_group, ada_weight[:, early:]
    )
    early_far, cond_part, shard_late, late_every, shard_wide = hold(
        plans, (early_far, cond_part, shard_late, late_every, shard_wide)
    )

    s_head.last_core()
    s_tail.last_x()
    cond_back = lax.all_to_all(cond_part.astype(LOW).reshape(shards, items, -1), "fsdp", 0, 0)
    early_every = across_replicas(early_group, early_far)
    shard_early = dot_left(every_act, early_every[:, :early])
    shard_early = hold(plans, shard_early)
    shard_ada = lax.dynamic_update_slice(shard_late, shard_early, (0, 0))
    bias_sums = jnp.concatenate(
        [
            jnp.sum(early_every[:, :early].astype(WIDE), axis=0),
            jnp.sum(late_every.astype(WIDE), axis=0),
        ],
        axis=0,
    )
    shard_bias = lax.dynamic_slice(
        bias_sums, (fsdp_place * ada_bias.shape[0],), (ada_bias.shape[0],)
    )
    gain_sums = jnp.sum(early_every[:, early:].astype(WIDE), axis=0)[: 2 * hd]
    cond_back = hold(plans, cond_back)
    s_tail.last_core()
    grad_cond_act = cond_back.swapaxes(0, 1).reshape(items, width).astype(WIDE)
    grad_condition = silu_pull(grad_cond_act)[0]
    if s_head.fast:
        shard_qkv, shard_proj = finish(core_place, s_head.live, s_tail.live, hd, width)
    else:
        shard_qkv = jnp.concatenate(s_head.halves() + s_tail.halves(), axis=1)
        shard_qkv = from_parts(shard_qkv, heads, hd)
        shard_proj = jnp.concatenate(s_proj.halves(), axis=1)[:, :width]
    shard_gate_up = shard_wide
    return (
        block_out[None],
        grad_input[None],
        grad_condition[None],
        shard_ada,
        shard_bias,
        shard_qkv,
        gain_sums[:hd],
        gain_sums[hd:],
        shard_proj,
        shard_gate_up,
        shard_down,
    )


def solution(mesh):
    return jax.shard_map(
        local,
        mesh=mesh,
        in_specs=(
            P(("rep", "fsdp"), None, None),
            P(("rep", "fsdp"), None, None),
            P(("rep", "fsdp"), None),
            P(("rep", "fsdp"), None),
            P("fsdp", None),
            P("fsdp"),
            P("fsdp", None),
            P(),
            P(),
            P("fsdp", None),
            P("fsdp", None),
            P("fsdp", None),
            P(("rep", "fsdp"), None, None),
        ),
        out_specs=(
            P(("rep", "fsdp"), None, None),
            P(("rep", "fsdp"), None, None),
            P(("rep", "fsdp"), None, None),
            P("fsdp", None),
            P("fsdp"),
            P("fsdp", None),
            P(),
            P(),
            P("fsdp", None),
            P("fsdp", None),
            P("fsdp", None),
        ),
        check_vma=False,
    )
```

```python
import functools
from functools import partial

import jax
import jax.numpy as jnp
from jax import lax
from jax.experimental import pallas as pl
from jax.experimental.pallas import tpu as pltpu
from jax.sharding import PartitionSpec as P

EPSILON = 1e-06
WIDE = jnp.float32
LOW = jnp.bfloat16
AXES = ("rep", "fsdp")
HIGH_Z = 4
PARTS = 3
BLOCK = 256
LANES = 128
GROUP = 4
MASK = 4096.0
MIB = 2**20


def dot(left, right):
    return jnp.dot(left, right, preferred_element_type=WIDE)


def dot_left(left, right):
    return lax.dot_general(left, right, (((0,), (0,)), ((), ())), preferred_element_type=WIDE)


def dot_right(left, right):
    return lax.dot_general(left, right, (((1,), (1,)), ((), ())), preferred_element_type=WIDE)


def layer_norm(values):
    centred = values - jnp.mean(values, axis=-1, keepdims=True)
    return centred * lax.rsqrt(jnp.mean(centred * centred, axis=-1, keepdims=True) + EPSILON)


def modulated(values, shift_part, scale_part):
    return layer_norm(values) * (1.0 + scale_part) + shift_part


def layout(lengths_row, widths_row, length):
    seg_count = lengths_row.shape[0]
    item_ends = jnp.cumsum(lengths_row)
    item_starts = item_ends - lengths_row
    token_place = jnp.arange(length, dtype=jnp.int32)[:, None]
    member = ((token_place >= item_starts[None, :]) & (token_place < item_ends[None, :])).astype(
        jnp.int32
    )
    segment = jnp.sum(member * jnp.arange(seg_count, dtype=jnp.int32)[None, :], axis=1)
    offset = token_place[:, 0] - jnp.sum(member * item_starts[None, :], axis=1)
    across = jnp.sum(member * widths_row[None, :], axis=1)
    return (member, segment, offset // across, offset % across)


def device_index(x, core, z, y):
    return (x * 2 + core) * 8 + z * 2 + y


PLACES = [(x, c, z, y) for x in range(2) for c in range(2) for z in range(4) for y in range(2)]
TO_CORE = [(device_index(x, c, z, y), device_index(x, 1 - c, z, y)) for x, c, z, y in PLACES]
TO_X = [(device_index(x, c, z, y), device_index(1 - x, c, z, y)) for x, c, z, y in PLACES]
TO_Y = [(device_index(x, c, z, y), device_index(x, c, z, 1 - y)) for x, c, z, y in PLACES]
TO_Z = [
    [(device_index(x, c, z, y), device_index(x, c, (z + k) % 4, y)) for x, c, z, y in PLACES]
    for k in range(4)
]
Z_GROUPS = [[0, 2, 4, 6], [1, 3, 5, 7]]


def coordinates():
    replica = lax.axis_index("rep")
    shard = lax.axis_index("fsdp")
    return replica // 2, replica % 2, shard // 2, shard % 2


def is_fast():
    return lax.axis_size("rep") == 4 and lax.axis_size("fsdp") == 8


def pick(operand, index, axis):
    return lax.dynamic_index_in_dim(operand, index, axis, keepdims=False)


def over_z(operand):
    return lax.all_to_all(operand, "fsdp", 0, 0, axis_index_groups=Z_GROUPS)


def hold(plans, values):
    flat, tree = jax.tree.flatten(([plan.live for plan in plans], values))
    flat = lax.optimization_barrier(flat)
    lives, values = jax.tree.unflatten(tree, flat)
    for plan, live in zip(plans, lives):
        plan.live = live
    return values


def place_pieces(shape, apart, where, pieces, out, sems):
    x, core, z, y = where[0], where[1], where[2], where[3]
    a0, a1, ax, b0, b1, bx = pieces
    rows, half = shape[0] // 8, shape[1] // 2
    h = rows // PARTS
    copies = []
    for p0, p1, px, c in ((a0, a1, ax, core), (b0, b1, bx, 1 - core)):
        for q in range(HIGH_Z):
            for source, yy, third in (
                (p0.at[q, 0], y, x),
                (p0.at[q, 1], y, 2),
                (p1.at[q, 0], 1 - y, x),
                (p1.at[q, 1], 1 - y, 2),
                (px.at[q, 0], y, 1 - x),
                (px.at[q, 1], 1 - y, 1 - x),
            ):
                zz = (z + HIGH_Z - q) % HIGH_Z if apart else q
                row = pl.multiple_of((2 * zz + yy) * rows + third * h, 16)
                column = pl.multiple_of(c * half, LANES)
                target = out.at[pl.ds(row, h), pl.ds(column, half)]
                copy = pltpu.make_async_copy(source, target, sems.at[len(copies)])
                copy.start()
                copies.append(copy)
    for copy in copies:
        copy.wait()


def placing(kernel, shape, apart, before, after):
    def run(where, *refs):
        pieces, refs = refs[:6], refs[6:]
        inputs, rest = refs[: before + after], refs[before + after :]
        *rest, laid, sems, out_sem = rest
        outs, full, scratch = rest[0], rest[1], rest[2:]
        step = pl.program_id(0)

        @pl.when(step == 0)
        def _():
            place_pieces(shape, apart, where, pieces, laid, sems)
            pltpu.make_async_copy(laid, full, out_sem).start()

        kernel(*inputs[:before], laid, *inputs[before:], *outs, *scratch)

        @pl.when(step == pl.num_programs(0) - 1)
        def _():
            pltpu.make_async_copy(laid, full, out_sem).wait()

    return run


def call_placed(kernel, gather, args, specs, before, out_shape, out_specs, scratch, **options):
    if not gather.fast:
        weight = gather.whole()
        args = (*args[:before], weight, *args[before:])
        specs = [*specs[:before], whole_block(weight), *specs[before:]]
        got = pl.pallas_call(
            kernel, in_specs=specs, out_shape=out_shape, out_specs=out_specs,
            scratch_shapes=scratch, **options,
        )(*args)
        return (*got, weight)
    shape = (8 * gather.rows, gather.width)
    count = len(out_shape)
    inner = placing(kernel, shape, gather.apart, before, len(args) - before)

    def run(*refs):
        at = 7 + len(args)
        inner(*refs[:at], refs[at : at + count], *refs[at + count :])

    any_space = pl.BlockSpec(memory_space=pl.ANY)
    live = gather.live
    pieces = [live[k] for k in ("own", "far", "both", "twin_own", "twin_far", "twin_both")]
    return pl.pallas_call(
        run,
        in_specs=[pl.BlockSpec(memory_space=pltpu.SMEM)] + [any_space] * 6 + list(specs),
        out_shape=list(out_shape) + [jax.ShapeDtypeStruct(shape, LOW)],
        out_specs=list(out_specs) + [any_space],
        scratch_shapes=list(scratch)
        + [pltpu.VMEM(shape, LOW), pltpu.SemaphoreType.DMA((48,)), pltpu.SemaphoreType.DMA],
        **options,
    )(jnp.stack(coordinates()).astype(jnp.int32), *pieces, *args)


class Gather:
    def __init__(self, weight):
        self.rows, self.width = weight.shape
        self.live = {"weight": weight}
        self.fast = is_fast() and self.rows % 48 == 0

    def z(self, apart=False):
        if not self.fast:
            return
        self.apart = apart
        x, core, _, _ = coordinates()
        h, half = self.rows // PARTS, self.width // 2
        weight = self.live.pop("weight")
        mine = lax.dynamic_slice_in_dim(weight, core * half, half, 1).reshape(PARTS, h, half)
        base = jnp.stack([pick(mine, x, 0), mine[2]], 0)
        if apart:
            lines = [base] + [lax.ppermute(base, AXES, TO_Z[k]) for k in (1, 2, 3)]
            self.live["own"] = jnp.stack(lines, 0)
            return
        self.live["own"] = over_z(jnp.broadcast_to(base, (HIGH_Z, 2, h, half)))

    def y(self):
        if self.fast:
            self.live["far"] = lax.ppermute(self.live["own"], AXES, TO_Y)

    def x(self):
        if self.fast:
            ends = jnp.concatenate([self.live["own"][:, :1], self.live["far"][:, :1]], 1)
            self.live["both"] = lax.ppermute(ends, AXES, TO_X)

    def core(self, *names):
        if self.fast:
            for name in names:
                self.live["twin_" + name] = lax.ppermute(self.live[name], AXES, TO_CORE)

    def whole(self):
        return lax.all_gather(self.live["weight"], "fsdp", axis=0, tiled=True)


class Scatter:
    def __init__(self, left, send=None, keep=None, pair=None):
        self.left, self.fast = left, is_fast() and left.shape[1] % 384 == 0
        self.live = {"send": send, "keep": keep} if pair is None else {"pair": pair}

    def operand(self, name):
        if "pair" in self.live:
            return self.live["pair"][("send", "keep").index(name)]
        return self.live[name]

    def first(self):
        live = self.live
        if self.fast:
            live["out"] = dot_left(self.left, self.operand("send")).astype(LOW)
            live.pop("send", None)

    def core(self):
        if self.fast:
            self.live["got"] = lax.ppermute(self.live.pop("out"), AXES, TO_CORE)

    def second(self):
        live = self.live
        if self.fast:
            product = dot_left(self.left, self.operand("keep"))
            live["kept"] = (product + live.pop("got").astype(WIDE)).astype(LOW)
            live.pop("keep", None)

    def join(self, other):
        if self.fast:
            kept = [self.live["kept"], other.live.pop("kept")]
            self.live["kept"] = jnp.concatenate(kept, axis=1)

    def view(self):
        rows, half = self.live["kept"].shape
        return self.live["kept"].reshape(HIGH_Z, 2, PARTS, rows // 24, half)

    def cut(self, start, sizes):
        view = self.view()
        return lax.dynamic_slice(view, (*start, 0, 0), (*sizes, *view.shape[3:])).reshape(
            tuple(k for k in sizes if k > 1) + view.shape[3:]
        )

    def x(self, half=None):
        if not self.fast:
            return
        x, _, _, _ = coordinates()
        if half is None:
            self.live["side"] = lax.ppermute(
                self.cut((0, 0, 1 - x), (HIGH_Z, 2, 1)), AXES, TO_X
            )
        else:
            self.live["side_" + str(half)] = lax.ppermute(
                self.cut((2 * half, 0, 1 - x), (2, 2, 1)), AXES, TO_X
            )

    def own(self, index):
        x, _, _, _ = coordinates()
        live = self.live
        sides = [live["side"]] if "side" in live else [live["side_0"], live["side_1"]]
        sides = [pick(side, index, 1) for side in sides]
        side = jnp.concatenate(sides, 0) if len(sides) > 1 else sides[0]
        mine = self.cut((0, index, x), (HIGH_Z, 1, 1))
        return (mine.astype(WIDE) + side.astype(WIDE)).astype(LOW)

    def common(self, index):
        return self.cut((0, index, 2), (HIGH_Z, 1, 1))

    def y_common(self):
        if self.fast:
            _, _, _, y = coordinates()
            self.live["far_common"] = lax.ppermute(self.common(1 - y), AXES, TO_Y)

    def y_own(self):
        if self.fast:
            _, _, _, y = coordinates()
            self.live["far_own"] = lax.ppermute(self.own(1 - y), AXES, TO_Y)

    def y_both(self):
        if self.fast:
            _, _, _, y = coordinates()
            both = jnp.stack([self.own(1 - y), self.common(1 - y)], 1)
            self.live["far_both"] = lax.ppermute(both, AXES, TO_Y)

    def line(self, name):
        _, _, _, y = coordinates()
        mine = self.common(y) if name == "common" else self.own(y)
        if "far_both" in self.live:
            far = self.live["far_both"][:, 1 if name == "common" else 0]
        else:
            far = self.live.pop("far_" + name)
        return (mine.astype(WIDE) + far.astype(WIDE)).astype(LOW)

    def z_common(self):
        if self.fast:
            self.live["sum_common"] = {"all": over_z(self.line("common"))}

    def z_own(self, apart=False):
        if not self.fast:
            return
        line = self.line("own")
        self.forget()
        if not apart:
            self.live["sum_own"] = {"all": over_z(line)}
            return
        _, _, z, _ = coordinates()
        lines = {"0": pick(line, z, 0)}
        for k in (2, 1, 3):
            lines[str(k)] = lax.ppermute(pick(line, (z + k) % 4, 0), AXES, TO_Z[k])
        self.live["sum_own"] = lines

    def z_both(self):
        if self.fast:
            lines = jnp.stack([self.line("own"), self.line("common")], 1)
            self.forget()
            self.live["sum_both"] = {"all": over_z(lines)}

    def forget(self):
        for name in ("kept", "side", "side_0", "side_1", "far_both"):
            self.live.pop(name, None)

    def total(self, name):
        lines = self.live.pop(name)
        if "all" in lines:
            return jnp.sum(lines["all"].astype(WIDE), axis=0).astype(LOW)
        wide = [lines[k].astype(WIDE) for k in ("0", "1", "2", "3")]
        return (wide[0] + wide[1] + wide[2] + wide[3]).astype(LOW)

    def last_x(self):
        if self.fast:
            if "sum_both" in self.live:
                part = self.total("sum_both")
            else:
                part = jnp.stack([self.total("sum_own"), self.total("sum_common")], 0)
            self.live = {"part": part, "other": lax.ppermute(part, AXES, TO_X)}

    def last_core(self):
        if self.fast:
            x, _, _, _ = coordinates()
            part, other = self.live["part"], self.live["other"]
            shared = (part[1].astype(WIDE) + other[1].astype(WIDE)).astype(LOW)
            first = jnp.where(x == 0, part[0], other[0])
            second = jnp.where(x == 0, other[0], part[0])
            done = jnp.concatenate([first, second, shared], 0)
            self.live = {"done": done, "twin": lax.ppermute(done, AXES, TO_CORE)}

    def halves(self):
        if self.fast:
            _, core, _, _ = coordinates()
            done, twin = self.live["done"], self.live["twin"]
            first = jnp.where(core == 0, done, twin)
            second = jnp.where(core == 0, twin, done)
            return first.astype(WIDE), second.astype(WIDE)
        _, core, _, _ = coordinates()
        left = self.left
        keep, send = self.operand("keep"), self.operand("send")
        first = jnp.where(core == 0, keep, send)
        second = jnp.where(core == 0, send, keep)
        sums = []
        for columns in (first, second):
            grad = dot_left(left, columns).astype(LOW)
            part = lax.psum_scatter(grad, "fsdp", scatter_dimension=0, tiled=True)
            sums.append(lax.psum(part, "rep").astype(WIDE))
        return sums[0], sums[1]


def column_halves(array):
    _, core, _, _ = coordinates()
    half = array.shape[1] // 2
    send = lax.dynamic_slice_in_dim(array, (1 - core) * half, half, 1)
    keep = lax.dynamic_slice_in_dim(array, core * half, half, 1)
    return send, keep


def across_x(rows):
    return lax.ppermute(rows, AXES, TO_X) if is_fast() else rows


def across_replicas(rows, far):
    if not is_fast():
        return lax.all_gather(rows, "rep", axis=0, tiled=True)
    x, core, _, _ = coordinates()
    count, width = rows.shape
    line = jnp.stack([jnp.where(x == 0, rows, far), jnp.where(x == 0, far, rows)], 0)
    twin = lax.ppermute(line, AXES, TO_CORE)
    every = [jnp.where(core == 0, line, twin), jnp.where(core == 0, twin, line)]
    return jnp.stack(every, 1).reshape(4 * count, width)


def gather_rows(rows):
    shards = lax.axis_size("fsdp")
    count, width = rows.shape
    group = lax.all_to_all(jnp.broadcast_to(rows, (shards, count, width)), "fsdp", 0, 0)
    return group.reshape(shards * count, width)


def exchange(rows):
    shards = lax.axis_size("fsdp")
    count, width = rows.shape
    shaped = rows.reshape(count, shards, width // shards).swapaxes(0, 1)
    return lax.all_to_all(shaped, "fsdp", 0, 0).reshape(shards * count, width // shards)


def sum_back(partial_rows, count):
    shards = lax.axis_size("fsdp")
    shaped = partial_rows.astype(LOW).reshape(shards, count, -1)
    got = lax.all_to_all(shaped, "fsdp", 0, 0)
    return jnp.sum(got.astype(WIDE), axis=0)


def whole_block(array):
    return pl.BlockSpec(
        array.shape, lambda i: (0,) * array.ndim, pipeline_mode=pl.Buffered(1)
    )


def part_width(hd):
    return -(-3 * GROUP * hd // LANES) * LANES


def prepare_kernel(
    first, heads, hd, x_ref, hot_ref, mod_ref, w_ref, gq_ref, gk_ref, rot_ref, qt_ref, kt_ref,
    vt_ref, *refs
):
    normed_ref, q_ref, k_ref, v_ref, rq_ref, rk_ref, wide_ref = refs if first else (x_ref, *refs)
    step = part_width(hd)
    if first:
        width = x_ref.shape[1]
        hot = hot_ref[...]
        shift = dot(hot, mod_ref[:, :width])
        scale = dot(hot, mod_ref[:, width : 2 * width])
        normed, _ = normed_rows(x_ref[...].astype(WIDE))
        normed = (normed * (1.0 + scale) + shift).astype(LOW)
        normed_ref[...] = normed
    else:
        normed = x_ref[...]
    cosine, plus, minus = rot_ref[0], rot_ref[1], rot_ref[2]
    lane = lax.broadcasted_iota(jnp.int32, (BLOCK, LANES), 1)
    inside = lane < hd
    ones = jnp.full((LANES, LANES), 1.0, LOW)
    wide_ref[:, step:] = jnp.zeros((BLOCK, LANES), WIDE)
    for part in range(heads // GROUP):
        wide_ref[:, :step] = dot(normed, w_ref[:, part * step : (part + 1) * step])
        for kind, (g_ref, t_ref, o_ref, r_ref) in enumerate(
            (
                (gq_ref, qt_ref, q_ref, rq_ref),
                (gk_ref, kt_ref, k_ref, rk_ref),
                (None, vt_ref, v_ref, None),
            )
        ):
            tail = t_ref[...]
            for g in range(GROUP):
                h = part * GROUP + g
                at = (kind * GROUP + g) * hd
                raw = jnp.where(inside, wide_ref[:, at : at + LANES], 0.0)
                if kind < 2:
                    r_ref[h] = raw.astype(LOW)
                    total = dot((raw * raw).astype(LOW), ones)
                    u = raw * lax.rsqrt(total * (1.0 / hd) + EPSILON) * g_ref[...]
                    up = pltpu.roll(u, LANES - hd // 4, 1)
                    down = pltpu.roll(u, hd // 4, 1)
                    raw = u * cosine + up * plus + down * minus
                o_ref[h] = raw.astype(LOW) + tail


def prepare(first, x, hot, mod, gather, gq, gk, rot, qt, kt, vt, heads, hd):
    n, width = x.shape
    rows = pl.BlockSpec((BLOCK, width), lambda i: (i, 0))
    head_spec = pl.BlockSpec((heads, BLOCK, LANES), lambda i: (0, i, 0))
    tail = pl.BlockSpec((BLOCK, LANES), lambda i: (i, 0))
    normed_spec, normed_shape = [rows], [jax.ShapeDtypeStruct((n, width), LOW)]
    return call_placed(
        partial(prepare_kernel, first, heads, hd),
        gather,
        (x, hot, mod, gq, gk, rot, qt, kt, vt),
        [
            rows,
            pl.BlockSpec((BLOCK, hot.shape[1]), lambda i: (i, 0)),
            whole_block(mod),
            whole_block(gq),
            whole_block(gk),
            pl.BlockSpec((3, BLOCK, LANES), lambda i: (0, i, 0)),
            tail,
            tail,
            pl.BlockSpec((1, LANES), lambda i: (0, 0)),
        ],
        3,
        (normed_shape if first else []) + [jax.ShapeDtypeStruct((heads, n, LANES), LOW)] * 5,
        (normed_spec if first else []) + [head_spec] * 5,
        [pltpu.VMEM((BLOCK, part_width(hd) + LANES), WIDE)],
        grid=(n // BLOCK,),
        compiler_params=pltpu.CompilerParams(vmem_limit_bytes=56 * MIB),
        cost_estimate=pl.CostEstimate(
            flops=12 * n * width * width // 2, bytes_accessed=20 * MIB, transcendentals=0
        ),
        name="prepare",
    )


def near_blocks(run):
    i = pl.program_id(0)
    n = pl.num_programs(0)

    @pl.when(i == 0)
    def _():
        run(pl.ds(0, 2 * BLOCK))

    @pl.when(i == n - 1)
    def _():
        run(pl.ds(pl.multiple_of((i - 1) * BLOCK, BLOCK), 2 * BLOCK))

    @pl.when((i > 0) & (i < n - 1))
    def _():
        run(pl.ds(pl.multiple_of((i - 1) * BLOCK, BLOCK), 3 * BLOCK))


def attend_kernel(hd, c, *refs):
    mix_ref = refs[6]
    lane = lax.broadcasted_iota(jnp.int32, (BLOCK, LANES), 1)
    heads = refs[0].shape[0]

    def run(at):
        for head in range(2 * heads):
            half, h = head // heads, head % heads
            q_ref, k_ref, v_ref = refs[3 * half : 3 * half + 3]
            q = q_ref[h]
            p = jnp.exp2(dot_right(q, k_ref[h, at]) * c).astype(LOW)
            total = dot(p, v_ref[h, at])
            norm = total[:, hd : hd + 1]
            out = (total * (1.0 / norm)).astype(LOW)
            mix_ref[:, hd * head : hd * (head + 1)] = out[:, :hd]
            rest = jnp.log2(norm) * (1.0 / c)
            first = rest.astype(LOW).astype(WIDE)
            rest = rest - first
            second = rest.astype(LOW).astype(WIDE)
            third = rest - second
            logs = jnp.where(lane == hd + 8, first, jnp.where(lane == hd + 9, second, third))
            marked = jnp.where((lane >= hd + 8) & (lane < hd + 11), logs.astype(LOW), q)
            refs[7 + half][h] = marked

    near_blocks(run)


def attend(one, two, hd, c):
    heads, n, _ = one[0].shape
    full = pl.BlockSpec((heads, n, LANES), lambda i: (0, 0, 0), pipeline_mode=pl.Buffered(1))
    block = pl.BlockSpec((heads, BLOCK, LANES), lambda i: (0, i, 0))
    width = 2 * heads * hd
    return pl.pallas_call(
        partial(attend_kernel, hd, c),
        grid=(n // BLOCK,),
        in_specs=[block, full, full] * 2,
        out_specs=[pl.BlockSpec((BLOCK, width), lambda i: (i, 0)), block, block],
        out_shape=[jax.ShapeDtypeStruct((n, width), LOW)]
        + [jax.ShapeDtypeStruct((heads, n, LANES), LOW)] * 2,
        compiler_params=pltpu.CompilerParams(vmem_limit_bytes=56 * MIB),
        cost_estimate=pl.CostEstimate(
            flops=8 * n * 640 * LANES * heads,
            bytes_accessed=20 * MIB,
            transcendentals=2 * heads * n * 640,
        ),
        name="attend",
    )(*one, *two)


def spread_kernel(heads, hd, proj_at, ga_ref, w_ref, mix_ref, out_ref, grad_scr, mix_scr):
    width = heads * hd
    grad_scr[:, width:] = jnp.zeros((BLOCK, LANES), WIDE)
    mix_scr[:, width:] = jnp.zeros((BLOCK, LANES), WIDE)
    grad_scr[:, :width] = dot_right(ga_ref[:, :width], w_ref[:, proj_at : proj_at + width]).astype(LOW).astype(WIDE)
    mix_scr[:, :width] = mix_ref[...].astype(WIDE)
    lane = lax.broadcasted_iota(jnp.int32, (BLOCK, LANES), 1)
    ones = jnp.full((LANES, LANES), 1.0, LOW)
    for h in range(heads):
        at = hd * h
        grad = jnp.where(lane < hd, grad_scr[:, at : at + LANES], 0.0)
        product = grad * mix_scr[:, at : at + LANES]
        high = product.astype(LOW)
        rest = (product - high.astype(WIDE)).astype(LOW)
        delta = -(dot(high, ones) + dot(rest, ones))
        first = delta.astype(LOW)
        second = (delta - first.astype(WIDE)).astype(LOW)
        out_ref[h] = jnp.where(
            lane == hd, first, jnp.where(lane == hd + 1, second, grad.astype(LOW))
        )


def spread(ga, w, mix, heads, hd, proj_at):
    n = ga.shape[0]
    width = heads * hd
    row = pl.BlockSpec((BLOCK, width), lambda i: (i, 0))
    wide_row = pl.BlockSpec((BLOCK, ga.shape[1]), lambda i: (i, 0))
    return pl.pallas_call(
        partial(spread_kernel, heads, hd, proj_at),
        grid=(n // BLOCK,),
        in_specs=[wide_row, whole_block(w), row],
        out_specs=pl.BlockSpec((heads, BLOCK, LANES), lambda i: (0, i, 0)),
        out_shape=jax.ShapeDtypeStruct((heads, n, LANES), LOW),
        scratch_shapes=[
            pltpu.VMEM((BLOCK, width + LANES), WIDE),
            pltpu.VMEM((BLOCK, width + LANES), WIDE),
        ],
        compiler_params=pltpu.CompilerParams(vmem_limit_bytes=56 * MIB),
        cost_estimate=pl.CostEstimate(
            flops=2 * n * width * width, bytes_accessed=12 * MIB, transcendentals=0
        ),
        name="spread",
    )(ga, w, mix)


def back_kernel(
    hd, c, score_scale, part, core_ref, q_ref, k_ref, v_ref, do_ref, rq_ref, rk_ref, rot_ref, gq_ref, gk_ref,
    *refs,
):
    out_ref, gain_ref, joint_ref, dq_scr, dk_scr, dv_scr, gain_scr, out_sem = refs[part:]
    i = pl.program_id(0)
    n = pl.num_programs(0)
    heads = q_ref.shape[0]
    width = GROUP * hd
    tail = joint_ref.shape[1] - 3 * width
    slot = core_ref[0] if part else 1 - core_ref[0]

    @pl.when(i == 0)
    def _():
        dq_scr[...] = jnp.zeros(dq_scr.shape, WIDE)
        gain_scr[...] = jnp.zeros(gain_scr.shape, WIDE)

    ones = jnp.full((LANES, LANES), 1.0, LOW)

    def run(at):
        def body(h, carry):
            kk = k_ref[h]
            vv = v_ref[h]
            q = q_ref[h, at]
            do = do_ref[h, at]
            p = jnp.exp2(dot_right(kk, q) * c)
            dv_scr[h] = dot(p.astype(LOW), do)
            ds = (p * dot_right(vv, do)).astype(LOW)
            dk_scr[h] = dot(ds, q)
            dq_scr[h, at] += dot_left(ds, kk)
            return carry

        lax.fori_loop(0, heads, body, 0, unroll=GROUP)

    near_blocks(run)

    def finish(dy, raw, rot, gain, row):
        raw = raw.astype(WIDE)
        dy = dy * score_scale
        up = pltpu.roll(dy, LANES - hd // 4, 1)
        down = pltpu.roll(dy, hd // 4, 1)
        d = dy * rot[0] - up * rot[1] - down * rot[2]
        r = lax.rsqrt(dot((raw * raw).astype(LOW), ones) * (1.0 / hd) + EPSILON)
        u = raw * r
        ud = u * d
        gain_scr[row] += jnp.sum(ud.reshape(BLOCK // 8, 8, LANES), axis=0)
        m = dot((ud * gain).astype(LOW), ones) * (1.0 / hd)
        return (r * (gain * d - u * m)).astype(LOW)

    here = pl.ds(pl.multiple_of(i * BLOCK, BLOCK), BLOCK)
    rot = [rot_ref[t, here] for t in range(3)]
    joint_ref[here, 3 * width :] = jnp.zeros((BLOCK, tail), LOW)
    for h in range(heads):
        at = hd * h
        grad = finish(dk_scr[h], rk_ref[h], rot, gk_ref[...], 1)
        joint_ref[here, width + at : width + at + hd] = grad[:, :hd]
        value = dv_scr[h].astype(LOW)
        joint_ref[here, 2 * width + at : 2 * width + at + hd] = value[:, :hd]

    @pl.when(i == n - 1)
    def _():
        def rows(b, carry):
            at = pl.ds(pl.multiple_of(b * BLOCK, BLOCK), BLOCK)
            turn = [rot_ref[t, at] for t in range(3)]
            for h in range(heads):
                start = hd * h
                grad = finish(dq_scr[h, at], rq_ref[h, at], turn, gq_ref[...], 0)
                joint_ref[at, start : start + hd] = grad[:, :hd]
            return carry

        lax.fori_loop(0, n, rows, 0)
        gain_ref[...] = gain_scr[...]
        copy = pltpu.make_async_copy(joint_ref, out_ref.at[slot], out_sem)
        copy.start()
        copy.wait()


def attend_back(half, part, before, core, q2, k, v, do, rq, rk, rot, gq, gk, hd, c, score_scale):
    _, n, _ = q2.shape
    one = pl.Buffered(1)
    full = pl.BlockSpec((GROUP, n, LANES), lambda i: (part, 0, 0), pipeline_mode=one)
    block = pl.BlockSpec((GROUP, BLOCK, LANES), lambda i: (part, i, 0))
    small = pl.BlockSpec((1, LANES), lambda i: (0, 0))
    any_space = pl.BlockSpec(memory_space=pl.ANY)
    width = part_width(hd)
    at = 2 * half + part
    return pl.pallas_call(
        partial(back_kernel, hd, c, score_scale, part),
        grid=(n // BLOCK,),
        in_specs=[
            pl.BlockSpec(memory_space=pltpu.SMEM),
            *(full, block, block),
            pl.BlockSpec((GROUP, n, LANES), lambda i: (at, 0, 0), pipeline_mode=one),
            *(full, block, whole_block(rot), small, small),
            *([any_space] if part else []),
        ],
        out_specs=[any_space, pl.BlockSpec((2, 8, LANES), lambda i: (0, 0, 0))],
        out_shape=[
            jax.ShapeDtypeStruct((2, n, width), LOW),
            jax.ShapeDtypeStruct((2, 8, LANES), WIDE),
        ],
        scratch_shapes=[
            pltpu.VMEM((n, width), LOW),
            pltpu.VMEM((GROUP, n, LANES), WIDE),
            pltpu.VMEM((GROUP, BLOCK, LANES), WIDE),
            pltpu.VMEM((GROUP, BLOCK, LANES), WIDE),
            pltpu.VMEM((2, 8, LANES), WIDE),
            pltpu.SemaphoreType.DMA,
        ],
        input_output_aliases={10: 0} if part else {},
        compiler_params=pltpu.CompilerParams(vmem_limit_bytes=56 * MIB),
        cost_estimate=pl.CostEstimate(
            flops=10 * n * 640 * LANES * GROUP,
            bytes_accessed=10 * MIB,
            transcendentals=GROUP * n * 640,
        ),
        name="attend_back",
    )(core, q2, k, v, do, rq, rk, rot, gq, gk, *([before] if part else []))


def normed_rows(values):
    centred = values - jnp.mean(values, axis=-1, keepdims=True)
    scale = lax.rsqrt(jnp.mean(centred * centred, axis=-1, keepdims=True) + EPSILON)
    return centred * scale, scale


def norm_back(normed, scale, grad):
    inner = jnp.mean(grad * normed, axis=-1, keepdims=True)
    return scale * (grad - jnp.mean(grad, axis=-1, keepdims=True) - normed * inner)


def add_sums(out_ref, at, hot, values):
    width = values.shape[1]
    term = dot_left(hot, values.astype(LOW))
    here = (slice(None), slice(at * width, (at + 1) * width))

    @pl.when(pl.program_id(0) == 0)
    def _():
        out_ref[here] = term

    @pl.when(pl.program_id(0) > 0)
    def _():
        out_ref[here] += term


def rows_of(array):
    if array.ndim == 3:
        return pl.BlockSpec((2, BLOCK, array.shape[2]), lambda i: (0, i, 0))
    return pl.BlockSpec((BLOCK, array.shape[1]), lambda i: (i, 0))


def call_rows(
    kernel, name, streamed, fixed, outs, sums=(), core=None, scratch=(), gather=None
):
    n = streamed[0].shape[-2]
    work = sum(2 * n * a.size for a in fixed if a.shape[0] > 256)
    moved = sum(a.size * a.dtype.itemsize for a in (*streamed, *fixed))
    scalars = () if core is None else (core,)
    args = (*scalars, *streamed, *fixed)
    specs = [pl.BlockSpec(memory_space=pltpu.SMEM) for _ in scalars]
    specs += [rows_of(a) for a in streamed] + [whole_block(a) for a in fixed]
    out_specs = [pl.BlockSpec((BLOCK, w), lambda i: (i, 0)) for w, _ in outs]
    out_specs += [pl.BlockSpec(shape, lambda i: (0, 0)) for shape in sums]
    out_shape = [jax.ShapeDtypeStruct((n, w), t) for w, t in outs]
    out_shape += [jax.ShapeDtypeStruct(shape, WIDE) for shape in sums]
    scratch = [pltpu.VMEM(shape, WIDE) for shape in scratch]
    if gather is not None:
        work += 2 * n * gather.rows * lax.axis_size("fsdp") * gather.width
    options = dict(
        grid=(n // BLOCK,),
        compiler_params=pltpu.CompilerParams(vmem_limit_bytes=56 * MIB),
        cost_estimate=pl.CostEstimate(flops=work, bytes_accessed=moved, transcendentals=0),
        name=name,
    )
    if gather is not None:
        before = len(scalars) + len(streamed)
        return call_placed(
            kernel, gather, args, specs, before, out_shape, out_specs, scratch, **options
        )
    return pl.pallas_call(
        kernel, in_specs=specs, out_specs=out_specs, out_shape=out_shape, scratch_shapes=scratch,
        **options,
    )(*args)


def join_kernel(
    proj_at, mix_ref, x_ref, hot_ref, keep_ref, w_ref, mod_ref, att_ref, mid_ref, norm_ref
):
    width = x_ref.shape[1]
    hot = hot_ref[...]
    attended = dot(mix_ref[...], w_ref[:, proj_at : proj_at + width])
    att_ref[...] = attended.astype(LOW)
    gate = dot(hot, mod_ref[:, 2 * width : 3 * width]) * keep_ref[...]
    middle = x_ref[...].astype(WIDE) + gate * attended
    mid_ref[...] = middle
    normed, _ = normed_rows(middle)
    scale = dot(hot, mod_ref[:, 4 * width : 5 * width])
    shift = dot(hot, mod_ref[:, 3 * width : 4 * width])
    norm_ref[...] = (normed * (1.0 + scale) + shift).astype(LOW)


def gate_kernel(x_ref, w_ref, out_ref):
    out_ref[...] = dot(x_ref[...], w_ref[:, : out_ref.shape[1]]).astype(LOW)


def up_kernel(x_ref, gate_ref, w_ref, up_ref, inner_ref):
    up = dot(x_ref[...], w_ref[...])
    up_ref[...] = up.astype(LOW)
    gate = gate_ref[...].astype(WIDE)
    inner_ref[...] = (gate * jax.nn.sigmoid(gate) * up).astype(LOW)


def down_kernel(
    inner_ref, mid_ref, grad_ref, hot_ref, keep_ref, w_ref, mod_ref, out_ref, back_ref, sum_ref
):
    width = mid_ref.shape[1]
    hot = hot_ref[...]
    returned = dot(inner_ref[...], w_ref[:, :width])
    gate = dot(hot, mod_ref[:, 5 * width : 6 * width]) * keep_ref[...]
    out_ref[...] = (mid_ref[...] + gate * returned).astype(LOW)
    upstream = grad_ref[...].astype(WIDE)
    back_ref[:, :width] = (upstream * gate).astype(LOW)
    if back_ref.shape[1] > width:
        back_ref[:, width:] = jnp.zeros((BLOCK, back_ref.shape[1] - width), LOW)
    add_sums(sum_ref, 0, hot, upstream * keep_ref[...] * returned)


def inner_back_kernel(core_ref, grad_ref, gate_ref, up_ref, w_ref, send_ref, keep_ref):
    grad = dot_right(grad_ref[...], w_ref[...])
    gate = gate_ref[...].astype(WIDE)
    sig = jax.nn.sigmoid(gate)
    act = gate * sig
    for_gate = (grad * up_ref[...].astype(WIDE) * (sig + act * (1.0 - sig))).astype(LOW)
    for_up = (grad * act).astype(LOW)

    @pl.when(core_ref[0] == 0)
    def _():
        send_ref[...] = for_up
        keep_ref[...] = for_gate

    @pl.when(core_ref[0] != 0)
    def _():
        send_ref[...] = for_gate
        keep_ref[...] = for_up


def middle_back_kernel(
    core_ref, send_ref, mine_ref, mid_ref, grad_ref, att_ref, hot_ref, keep_ref, wg_ref, wu_ref,
    mod_ref, out_ref, back_ref, sum_ref, total_ref,
):
    width = mid_ref.shape[1]
    hot = hot_ref[...]
    keep = keep_ref[...]

    @pl.when(core_ref[0] == 0)
    def _():
        total_ref[...] = dot_right(mine_ref[...], wg_ref[:, : mine_ref.shape[1]])
        total_ref[...] += dot_right(send_ref[...], wu_ref[...])

    @pl.when(core_ref[0] != 0)
    def _():
        total_ref[...] = dot_right(send_ref[...], wg_ref[:, : send_ref.shape[1]])
        total_ref[...] += dot_right(mine_ref[...], wu_ref[...])

    grad = total_ref[...]
    normed, scale = normed_rows(mid_ref[...])
    turned = grad * (1.0 + dot(hot, mod_ref[:, 4 * width : 5 * width]))
    total = grad_ref[...].astype(WIDE) + norm_back(normed, scale, turned)
    out_ref[...] = total
    gate = dot(hot, mod_ref[:, 2 * width : 3 * width]) * keep
    back_ref[:, :width] = (total * gate).astype(LOW)
    if back_ref.shape[1] > width:
        back_ref[:, width:] = jnp.zeros((BLOCK, back_ref.shape[1] - width), LOW)
    add_sums(sum_ref, 0, hot, total * keep * att_ref[...].astype(WIDE))
    add_sums(sum_ref, 1, hot, grad)
    add_sums(sum_ref, 2, hot, grad * normed)


def input_back_kernel(
    core_ref, one_ref, two_ref, mid_ref, x_ref, hot_ref, wo_ref, wt_ref, mod_ref, out_ref, sum_ref
):
    width = x_ref.shape[1]
    hot = hot_ref[...]
    step = one_ref.shape[2]
    core = core_ref[0]
    grad = None
    for ref, w_ref in ((one_ref, wo_ref), (two_ref, wt_ref)):
        term = dot_right(ref[1 - core], w_ref[:, :step]) + dot_right(ref[core], w_ref[:, step : 2 * step])
        grad = term if grad is None else grad + term
    normed, scale = normed_rows(x_ref[...].astype(WIDE))
    turned = grad * (1.0 + dot(hot, mod_ref[:, width : 2 * width]))
    out_ref[...] = mid_ref[...] + norm_back(normed, scale, turned)
    add_sums(sum_ref, 0, hot, grad)
    add_sums(sum_ref, 1, hot, grad * normed)


def finish_kernel(hd, core_ref, head_done, head_twin, tail_done, tail_twin, qkv_ref, proj_ref):
    step = part_width(hd)
    short = GROUP * hd
    total = qkv_ref.shape[1] // 3

    def write(sources):
        for part, source in enumerate(sources):
            values = source[:, :step].astype(WIDE)
            for kind in range(3):
                at = kind * total + part * short
                qkv_ref[:, at : at + short] = values[:, kind * short : (kind + 1) * short]
        half = sources[0].shape[1] - step
        proj_ref[:, :half] = sources[0][:, step:].astype(WIDE)
        rest = proj_ref.shape[1] - half
        proj_ref[:, half:] = sources[1][:, step : step + rest].astype(WIDE)

    @pl.when(core_ref[0] == 0)
    def _():
        write((head_done, head_twin, tail_done, tail_twin))

    @pl.when(core_ref[0] != 0)
    def _():
        write((head_twin, head_done, tail_twin, tail_done))


def finish(core, head, tail, hd, width):
    rows = head["done"].shape[0]
    return pl.pallas_call(
        partial(finish_kernel, hd),
        in_specs=[pl.BlockSpec(memory_space=pltpu.SMEM)]
        + [pl.BlockSpec(memory_space=pltpu.VMEM)] * 4,
        out_specs=[pl.BlockSpec(memory_space=pltpu.VMEM)] * 2,
        out_shape=[
            jax.ShapeDtypeStruct((rows, 3 * width), WIDE),
            jax.ShapeDtypeStruct((rows, width), WIDE),
        ],
        compiler_params=pltpu.CompilerParams(vmem_limit_bytes=40 * MIB),
        name="finish",
    )(core, head["done"], head["twin"], tail["done"], tail["twin"])


def turn_tables(row_place, column_place, hd):
    quarter = hd // 4
    inverse = 10000.0 ** (-jnp.arange(quarter, dtype=WIDE) / quarter)
    row_angle = row_place.astype(WIDE)[:, None] * inverse[None, :]
    column_angle = column_place.astype(WIDE)[:, None] * inverse[None, :]
    rest = jnp.zeros((row_place.shape[0], LANES - hd), WIDE)
    none = jnp.zeros_like(row_angle)
    rc, rs = jnp.cos(row_angle), jnp.sin(row_angle)
    cc, cs = jnp.cos(column_angle), jnp.sin(column_angle)
    return jnp.stack(
        [
            jnp.concatenate([rc, rc, cc, cc, rest], 1),
            jnp.concatenate([-rs, none, -cs, none, rest], 1),
            jnp.concatenate([none, rs, none, cs, rest], 1),
        ],
        0,
    )


def high_and_rest(values):
    high = values.astype(LOW)
    return jnp.concatenate([high, (values - high.astype(WIDE)).astype(LOW)], axis=0)


def pad_columns(array, width):
    return jnp.pad(array, ((0, 0), (0, width - array.shape[1])))


def to_parts(array, heads, hd):
    rows = array.shape[0]
    shaped = array.reshape(rows, 3, heads // GROUP, GROUP * hd).swapaxes(1, 2)
    shaped = shaped.reshape(rows, heads // GROUP, 3 * GROUP * hd)
    padded = jnp.pad(shaped, ((0, 0), (0, 0), (0, part_width(hd) - 3 * GROUP * hd)))
    return padded.reshape(rows, -1)


def from_parts(array, heads, hd):
    rows = array.shape[0]
    shaped = array.reshape(rows, heads // GROUP, -1)[:, :, : 3 * GROUP * hd]
    shaped = shaped.reshape(rows, heads // GROUP, 3, GROUP * hd).swapaxes(1, 2)
    return shaped.reshape(rows, -1)


def local(
    block_in,
    condition,
    item_lengths,
    item_widths,
    ada_weight,
    ada_bias,
    qkv_weight,
    query_gain,
    key_gain,
    proj_weight,
    gate_up_weight,
    down_weight,
    out_grad,
):
    _, n, width = block_in.shape
    items = item_lengths.shape[1]
    hd = query_gain.shape[0]
    heads = width // hd
    ff = down_weight.shape[0] * lax.axis_size("fsdp")
    score_scale = float(hd) ** (-0.5)
    c = score_scale * 1.4426950408889634
    shards = lax.axis_size("fsdp")
    fsdp_place = lax.axis_index("fsdp")
    odd = width + LANES if (width // LANES) % 2 else width

    qkv_parts = to_parts(qkv_weight, heads, hd)
    cut = qkv_parts.shape[1] // 2
    g_one = Gather(qkv_parts[:, :cut])
    g_two = Gather(jnp.concatenate([qkv_parts[:, cut:], pad_columns(proj_weight, odd)], axis=1))
    g_gate = Gather(gate_up_weight[:, :ff])
    g_up = Gather(gate_up_weight[:, ff:])
    g_down = Gather(pad_columns(down_weight, odd))
    gathers = [g_one, g_two, g_gate, g_up, g_down]
    core_place = (lax.axis_index("rep") % 2).astype(jnp.int32).reshape(1)

    cond_float = condition.astype(WIDE).reshape(items, width)
    cond_silu, silu_pull = jax.vjp(jax.nn.silu, cond_float)
    cond_act = cond_silu.astype(LOW)

    g_one.z()
    group_act = exchange(cond_act)
    member, segment, row_place, column_place = layout(item_lengths[0], item_widths[0], n)
    member_low = member.astype(LOW)
    keep = (segment < items - 1).astype(WIDE).reshape(n, 1)
    rot = turn_tables(row_place, column_place, hd)
    spare = jnp.zeros((n, LANES - hd - items), LOW)
    ones_at = jnp.zeros((n, LANES - hd - items), LOW).at[:, :3].set(-1.0)
    blank = jnp.zeros((n, hd), LOW)
    query_tail = jnp.concatenate([blank, member_low, spare], 1)
    key_tail = jnp.concatenate([blank, (member_low - 1.0) * MASK, ones_at], 1)
    value_tail = jnp.zeros((1, LANES), LOW).at[:, hd : hd + 2].set(1.0)
    gain_q = pad_columns(query_gain.astype(WIDE)[None, :], LANES)
    gain_k = pad_columns(key_gain.astype(WIDE)[None, :], LANES)
    hot = jnp.concatenate([member_low, member_low], axis=1)
    tables = (rot, query_tail, key_tail, hot, keep)
    group_act = hold(gathers, group_act)

    g_one.y()
    g_two.z()
    bias_row = lax.dynamic_update_slice(
        jnp.zeros((6 * width,), WIDE), ada_bias.astype(WIDE), (fsdp_place * ada_bias.shape[0],)
    )
    mod_part = (dot(group_act, ada_weight) + bias_row[None, :]).astype(LOW)
    act_far = across_x(group_act)
    mod_part, group_act, act_far, tables = hold(gathers, (mod_part, group_act, act_far, tables))

    early = 2 * width
    modulation = high_and_rest(sum_back(mod_part, items))
    g_one.x()
    g_one.core("own", "far")
    g_two.y()
    inputs_low = block_in[0]
    every_act = across_replicas(group_act, act_far)
    every_act = hold(gathers[1:], every_act)

    g_one.core("both")
    g_two.x()
    g_two.core("own", "far")
    g_gate.z()
    rot, query_tail, key_tail, hot, keep = tables
    set_out = (gain_q, gain_k, rot, query_tail, key_tail, value_tail, heads // 2, hd)
    normed_a, q_one, k_one, v_one, rq_one, rk_one, one_full = prepare(
        True, inputs_low, hot, modulation, g_one, *set_out
    )
    gathers = gathers[1:]
    normed_a, q_one, k_one, v_one, rq_one, rk_one, one_full = hold(
        gathers, (normed_a, q_one, k_one, v_one, rq_one, rk_one, one_full)
    )

    g_two.core("both")
    g_gate.y()
    g_up.z()
    q_two, k_two, v_two, rq_two, rk_two, two_full = prepare(
        False, normed_a, hot, modulation, g_two, *set_out
    )
    gathers = gathers[1:]
    normed_a, q_two, k_two, v_two, rq_two, rk_two, two_full, q_one, k_one, v_one = hold(
        gathers, (normed_a, q_two, k_two, v_two, rq_two, rk_two, two_full, q_one, k_one, v_one)
    )

    g_gate.x()
    g_gate.core("own", "far")
    g_up.y()
    g_down.z()
    mixed, q2_one, q2_two = attend((q_one, k_one, v_one), (q_two, k_two, v_two), hd, c)
    mixed, q2_one, q2_two = hold(gathers, (mixed, q2_one, q2_two))

    g_gate.core("both")
    g_up.x()
    g_up.core("own", "far")
    g_down.y()
    attended, middle, normed_b = call_rows(
        partial(join_kernel, cut), "join", (mixed, inputs_low, hot, keep), (two_full, modulation),
        ((width, LOW), (width, WIDE), (width, LOW)),
    )
    middle, normed_b, attended = hold([g_gate], (middle, normed_b, attended))

    gate, gate_full = call_rows(
        gate_kernel, "gate", (normed_b,), (), ((ff, LOW),), gather=g_gate
    )
    gathers = [g_up, g_down]
    gate, gate_full, normed_b, middle, attended = hold(
        gathers, (gate, gate_full, normed_b, middle, attended)
    )

    g_up.core("both")
    g_down.x()
    g_down.core("own", "far")
    normed_b = hold([g_up], normed_b)
    up, inner, up_full = call_rows(
        up_kernel, "up", (normed_b, gate), (), ((ff, LOW), (ff, LOW)), gather=g_up
    )
    gathers = [g_down]
    inner, up, gate, up_full, middle = hold(gathers, (inner, up, gate, up_full, middle))

    g_down.core("both")
    block_out, grad_returned, sums_gate_b, down_full = call_rows(
        down_kernel, "down", (inner, middle, out_grad[0], hot, keep), (modulation,),
        ((width, LOW), (odd, LOW)), ((2 * items, width),), gather=g_down,
    )

    s_down = Scatter(inner, *column_halves(grad_returned))
    s_down.first()
    plans = [s_down]
    grad_returned, down_full, gate, up, gate_full, up_full, normed_b, middle, attended = hold(
        plans,
        (grad_returned, down_full, gate, up, gate_full, up_full, normed_b, middle, attended),
    )

    s_down.core()
    grad_send, grad_keep = call_rows(
        inner_back_kernel, "inner_back", (grad_returned, gate, up), (down_full,),
        ((ff, LOW), (ff, LOW)), core=core_place,
    )
    grad_send, grad_keep = hold(plans, (grad_send, grad_keep))

    s_down.second()
    s_wide = Scatter(normed_b, grad_send, grad_keep)
    s_wide.first()
    plans = [s_down, s_wide]
    grad_send, grad_keep = hold(plans, (grad_send, grad_keep))

    s_down.x()
    s_wide.core()
    grad_middle, grad_attended, sums_mid = call_rows(
        middle_back_kernel, "middle_back",
        (grad_send, grad_keep, middle, out_grad[0], attended, hot, keep),
        (gate_full, up_full, modulation), ((width, WIDE), (odd, LOW)), ((2 * items, 3 * width),),
        core=core_place, scratch=((BLOCK, width),),
    )
    s_proj = Scatter(mixed, *column_halves(grad_attended))
    plans = [s_down, s_wide, s_proj]
    grad_middle, grad_attended, sums_mid = hold(plans, (grad_middle, grad_attended, sums_mid))

    s_wide.second()
    grad_attended = hold([s_wide], grad_attended)
    s_wide.x(0)
    s_down.y_both()
    s_proj.first()
    late_sums = jnp.concatenate([sums_mid[:items], sums_gate_b[:items]], axis=1).astype(LOW)
    grad_mixed = spread(grad_attended, two_full, mixed, heads, hd, cut)
    late_sums, grad_mixed = hold([s_down, s_wide, s_proj], (late_sums, grad_mixed))

    back = partial(
        attend_back, core=core_place, rot=rot, gq=gain_q, gk=gain_k, hd=hd, c=c,
        score_scale=score_scale,
    )
    one = dict(q2=q2_one, k=k_one, v=v_one, rq=rq_one, rk=rk_one)
    two = dict(q2=q2_two, k=k_two, v=v_two, rq=rq_two, rk=rk_two)
    s_down.z_both()
    s_wide.x(1)
    s_wide.y_common()
    s_proj.core()
    joint_one, gains_0 = back(0, 0, None, do=grad_mixed, **one)
    joint_one, gains_0, grad_mixed = hold([s_down, s_wide, s_proj], (joint_one, gains_0, grad_mixed))

    s_down.last_x()
    s_wide.y_own()
    s_wide.z_common()
    s_proj.second()
    joint_one, gains_1 = back(0, 1, joint_one, do=grad_mixed, **one)
    s_head = Scatter(normed_a, pair=joint_one)
    s_head.first()
    gains_1, grad_mixed = hold([s_down, s_wide, s_proj, s_head], (gains_1, grad_mixed))

    s_head.core()
    s_down.last_core()
    s_wide.z_own()
    joint_two, gains_2 = back(1, 0, None, do=grad_mixed, **two)
    s_head.second()
    s_head.join(s_proj)
    joint_two, gains_2, grad_mixed, late_sums = hold(
        [s_down, s_wide, s_head], (joint_two, gains_2, grad_mixed, late_sums)
    )

    s_head.x()
    s_head.y_common()
    late_group = gather_rows(late_sums)
    joint_two, gains_3 = back(1, 1, joint_two, do=grad_mixed, **two)
    s_tail = Scatter(normed_a, pair=joint_two)
    s_tail.first()
    shard_down = jnp.concatenate(s_down.halves(), axis=1)[:, :width]
    gains_3, late_group, shard_down = hold(
        [s_wide, s_head, s_tail], (gains_3, late_group, shard_down)
    )

    s_tail.core()
    s_wide.last_x()
    s_head.y_own()
    s_head.z_common()
    s_tail.second()
    grad_middle = hold([s_tail], grad_middle)
    s_tail.x()
    grad_input, sums_early = call_rows(
        input_back_kernel, "input_back",
        (s_head.live["pair"], s_tail.live["pair"], grad_middle, inputs_low, hot),
        (one_full, two_full, modulation), ((width, WIDE),), ((2 * items, 2 * width),),
        core=core_place,
    )
    if s_head.fast:
        s_head.live.pop("pair")
        s_tail.live.pop("pair")
    plans = [s_wide, s_head, s_tail]
    grad_input, sums_early, late_group = hold(plans, (grad_input, sums_early, late_group))

    s_wide.last_core()
    s_head.z_own(apart=True)
    s_tail.y_both()
    early_sums = sums_early[:items]
    gains = gains_0 + gains_1 + gains_2 + gains_3
    gain_row = jnp.sum(gains, axis=1)[:, :hd].reshape(1, 2 * hd)
    gain_high = gain_row.astype(LOW).astype(WIDE)
    gain_block = jnp.concatenate([gain_high, gain_row - gain_high], axis=0)
    gain_block = jnp.pad(gain_block, ((0, items - 2), (0, 2 * LANES - 2 * hd)))
    early_sums = jnp.concatenate([early_sums, gain_block], axis=1).astype(LOW)
    early_group = gather_rows(early_sums)
    late_far = across_x(late_group)
    plans = [s_wide, s_head, s_tail]
    early_group, late_far = hold(plans, (early_group, late_far))

    s_head.last_x()
    s_tail.z_both()
    early_far = across_x(early_group)
    late_every = across_replicas(late_group, late_far)
    shard_late = dot_left(every_act, jnp.pad(late_every, ((0, 0), (early, 0))))
    shard_wide = jnp.concatenate(s_wide.halves(), axis=1)
    plans = [s_head, s_tail]
    cond_part = dot_right(early_group[:, :early], ada_weight[:, :early]) + dot_right(
        late_group, ada_weight[:, early:]
    )
    early_far, cond_part, shard_late, late_every, shard_wide = hold(
        plans, (early_far, cond_part, shard_late, late_every, shard_wide)
    )

    s_head.last_core()
    s_tail.last_x()
    cond_back = lax.all_to_all(cond_part.astype(LOW).reshape(shards, items, -1), "fsdp", 0, 0)
    early_every = across_replicas(early_group, early_far)
    shard_early = dot_left(every_act, early_every[:, :early])
    shard_early = hold(plans, shard_early)
    shard_ada = lax.dynamic_update_slice(shard_late, shard_early, (0, 0))
    bias_sums = jnp.concatenate(
        [
            jnp.sum(early_every[:, :early].astype(WIDE), axis=0),
            jnp.sum(late_every.astype(WIDE), axis=0),
        ],
        axis=0,
    )
    shard_bias = lax.dynamic_slice(
        bias_sums, (fsdp_place * ada_bias.shape[0],), (ada_bias.shape[0],)
    )
    gain_sums = jnp.sum(early_every[:, early:].astype(WIDE), axis=0)[: 2 * hd]
    cond_back = hold(plans, cond_back)
    s_tail.last_core()
    grad_cond_act = cond_back.swapaxes(0, 1).reshape(items, width).astype(WIDE)
    grad_condition = silu_pull(grad_cond_act)[0]
    if s_head.fast:
        shard_qkv, shard_proj = finish(core_place, s_head.live, s_tail.live, hd, width)
    else:
        shard_qkv = jnp.concatenate(s_head.halves() + s_tail.halves(), axis=1)
        shard_qkv = from_parts(shard_qkv, heads, hd)
        shard_proj = jnp.concatenate(s_proj.halves(), axis=1)[:, :width]
    shard_gate_up = shard_wide
    return (
        block_out[None],
        grad_input[None],
        grad_condition[None],
        shard_ada,
        shard_bias,
        shard_qkv,
        gain_sums[:hd],
        gain_sums[hd:],
        shard_proj,
        shard_gate_up,
        shard_down,
    )


def solution(mesh):
    return jax.shard_map(
        local,
        mesh=mesh,
        in_specs=(
            P(("rep", "fsdp"), None, None),
            P(("rep", "fsdp"), None, None),
            P(("rep", "fsdp"), None),
            P(("rep", "fsdp"), None),
            P("fsdp", None),
            P("fsdp"),
            P("fsdp", None),
            P(),
            P(),
            P("fsdp", None),
            P("fsdp", None),
            P("fsdp", None),
            P(("rep", "fsdp"), None, None),
        ),
        out_specs=(
            P(("rep", "fsdp"), None, None),
            P(("rep", "fsdp"), None, None),
            P(("rep", "fsdp"), None, None),
            P("fsdp", None),
            P("fsdp"),
            P("fsdp", None),
            P(),
            P(),
            P("fsdp", None),
            P("fsdp", None),
            P("fsdp", None),
        ),
        check_vma=False,
    )
```
